32 devices in a mesh: seq: 8 (over y, x, core), wt: 4 (over z).
Axes of the slice: x: 2, y: 2, z: 4, core: 2. Of those that a mesh axis runs over, the one named last changes fastest.
Arguments:
- tokens: bfloat16 [8192, 1024], P(('wt', 'seq')), may hold values from -6 to 6
- cotangent: bfloat16 [8192, 1024], P(('wt', 'seq')), may hold values from -6 to 6
- w_qkv: bfloat16 [1024, 3072], P('wt'), may hold values from -0.1875 to 0.1875
- qv_bias: float32 [2, 1024], replicated, may hold values from -3 to 3
- w_out: bfloat16 [1024, 1024], P('wt'), may hold values from -1 to 1
- out_bias: float32 [1024], replicated, may hold values from -3 to 3
- norm1_gain: float32 [1024], replicated, may hold values from 0.1 to 1.9
- norm1_bias: float32 [1024], replicated, may hold values from -1.75 to 1.75
- w_fc1: bfloat16 [1024, 4096], P('wt'), may hold values from -0.1875 to 0.1875
- fc1_bias: float32 [4096], replicated, may hold values from -3 to 3
- w_fc2: bfloat16 [4096, 1024], P('wt'), may hold values from -0.09375 to 0.09375
- fc2_bias: float32 [1024], replicated, may hold values from -3 to 3
- norm2_gain: float32 [1024], replicated, may hold values from 0.1 to 1.9
- norm2_bias: float32 [1024], replicated, may hold values from -1.75 to 1.75
- doc_lengths: int32 [4, 4], P('wt'), may hold values from 1 to 1024, as said below
- adapter_ids: int32 [4, 4], P('wt'), may hold values from 0 to 7
- attn_down: bfloat16 [4, 8, 1024, 16], replicated, may hold values from -0.1875 to 0.1875
- attn_up: bfloat16 [4, 8, 16, 1024], replicated, may hold values from -1.5 to 1.5
- fc1_down: bfloat16 [8, 1024, 16], replicated, may hold values from -0.1875 to 0.1875
- fc1_up: bfloat16 [8, 16, 4096], replicated, may hold values from -1.5 to 1.5
- fc2_down: bfloat16 [8, 4096, 16], replicated, may hold values from -0.09375 to 0.09375
- fc2_up: bfloat16 [8, 16, 1024], replicated, may hold values from -1.5 to 1.5
Outputs:
- output: float32 [8192, 1024], P(('wt', 'seq'))
- input_grad: float32 [8192, 1024], P(('wt', 'seq'))
- grad_attn_down: float32 [4, 8, 1024, 16], replicated
- grad_attn_up: float32 [4, 8, 16, 1024], replicated
- grad_fc1_down: float32 [8, 1024, 16], replicated
- grad_fc1_up: float32 [8, 16, 4096], replicated
- grad_fc2_down: float32 [8, 4096, 16], replicated
- grad_fc2_up: float32 [8, 16, 1024], replicated
The draws below stay inside these ranges and needn't reach their ends.
Inputs may be any that keep to these rules, and one draw needn't show every extreme that they name: `doc_lengths`: row s lists in order the lengths of the 4 documents of group s and sums to 2048; in every row exactly one document has 1024 tokens and every other document has fewer.
All inputs are finite; a program needn't handle non-finite values.
Results may differ from the reference program's by a relative error of at most 0.018.
The reference program's roundings to bfloat16 on the way count: a program that leaves them out, or rounds other values in their place, can miss the bound.
Values may be sent and summed in bfloat16 or wider, within the bound.
A program may use at most 128 MiB of HBM per device.

```python
import jax
import jax.numpy as jnp
from jax import lax

D = 1024
HEADS = 16
HEAD_DIM = 64
FF = 4096
RANK = 16
ADAPTERS = 8
STRETCH = 2048
DOC_MOST = 1024
DOCS = 4
STRETCHES = 4
TOKENS = 8192


def group_lengths(key):
    key_cut, key_place = jax.random.split(key, 2)
    piece_count = DOCS - 1
    remaining = STRETCH - DOC_MOST
    base_size = remaining // piece_count
    quarter = base_size // 4
    inner = jnp.arange(1, piece_count, dtype=jnp.int32)
    cuts = inner * remaining // piece_count + jax.random.randint(key_cut, (piece_count - 1,), -quarter, quarter + 1)
    bounds = jnp.concatenate([jnp.zeros((1,), jnp.int32), cuts.astype(jnp.int32), jnp.full((1,), remaining, jnp.int32)])
    pieces = bounds[1:] - bounds[:-1]
    place = jax.random.randint(key_place, (), 0, DOCS)
    doc_index = jnp.arange(DOCS, dtype=jnp.int32)
    before_piece = pieces[jnp.clip(doc_index, 0, piece_count - 1)]
    after_piece = pieces[jnp.clip(doc_index - 1, 0, piece_count - 1)]
    return jnp.where(doc_index < place, before_piece, jnp.where(doc_index == place, DOC_MOST, after_piece)).astype(jnp.int32)


def draw_doc_lengths(key, part):
    key = jax.random.fold_in(key, 7)
    return jax.vmap(group_lengths)(jax.random.split(key, STRETCHES))


def touch_ends(array, stream_key, least, largest):
    extent = array.shape
    spot = [jax.random.randint(jax.random.fold_in(stream_key, axis), (), 0, extent[axis]) for axis in range(len(extent))]
    array = array.at[tuple(spot)].set(least)
    longest = extent.index(max(extent))
    spot[longest] = (spot[longest] + 1) % extent[longest]
    return array.at[tuple(spot)].set(largest)


def block_levels(stream_key, shape, shards, smallest, top_value):
    def one(position, shards_of):
        draws = jax.random.uniform(jax.random.fold_in(jax.random.fold_in(stream_key, 6), position), (shards_of,), jnp.float32, smallest / len(shards), top_value / len(shards))
        return jnp.repeat(jnp.exp(draws), shape[position] // shards_of).reshape((-1,) + (1,) * (len(shape) - position - 1))

    level = one(*shards[0])
    for cut in shards[1:]:
        level = level * one(*cut)
    return level


def scatter_about(stream_key, extent, deviation, bound, cuts=(), held_as=jnp.bfloat16):
    result = jax.random.normal(stream_key, extent, jnp.float32) * deviation
    if len(cuts) > 0:
        result = block_levels(stream_key, extent, cuts, -0.22, 0.18) * result
    return jnp.clip(result, min=-bound, max=bound).astype(held_as)


def setup_inputs(seed: int = 0) -> dict:
    seeds = jax.random.split(jax.random.key(seed), 23)
    return {
        "tokens": scatter_about(seeds[0], (TOKENS, D), 1.0, 6.0, ((0, 32),)),
        "cotangent": scatter_about(seeds[1], (TOKENS, D), 1.0, 6.0, ((0, 32),)),
        "w_qkv": scatter_about(seeds[2], (D, 3 * D), D ** -0.5, 0.1875, ((0, 4),)),
        "qv_bias": scatter_about(seeds[3], (2, D), 0.5, 3.0, (), jnp.float32),
        "w_out": scatter_about(seeds[4], (D, D), (D // 32) ** -0.5, 1.0, ((0, 4),)),
        "out_bias": scatter_about(seeds[5], (D,), 0.5, 3.0, (), jnp.float32),
        "norm1_gain": jnp.clip(1.0 + 0.18 * jax.random.normal(seeds[6], (D,), jnp.float32), 0.1, 1.9),
        "norm1_bias": scatter_about(seeds[7], (D,), 0.3, 1.75, (), jnp.float32),
        "w_fc1": scatter_about(seeds[8], (D, FF), D ** -0.5, 0.1875, ((0, 4),)),
        "fc1_bias": scatter_about(seeds[9], (FF,), 0.5, 3.0, (), jnp.float32),
        "w_fc2": scatter_about(seeds[10], (FF, D), FF ** -0.5, 0.09375, ((0, 4),)),
        "fc2_bias": scatter_about(seeds[11], (D,), 0.5, 3.0, (), jnp.float32),
        "norm2_gain": jnp.clip(1.0 + 0.18 * jax.random.normal(seeds[12], (D,), jnp.float32), 0.1, 1.9),
        "norm2_bias": scatter_about(seeds[13], (D,), 0.3, 1.75, (), jnp.float32),
        "doc_lengths": draw_doc_lengths(jax.random.fold_in(seeds[22], 71), 0),
        "adapter_ids": touch_ends(jax.random.randint(seeds[15], (STRETCHES, DOCS), 0, ADAPTERS), jax.random.fold_in(seeds[15], 1), 0, ADAPTERS - 1).astype(jnp.int32),
        "attn_down": scatter_about(seeds[16], (4, ADAPTERS, D, RANK), D ** -0.5, 0.1875),
        "attn_up": scatter_about(seeds[17], (4, ADAPTERS, RANK, D), RANK ** -0.5, 1.5),
        "fc1_down": scatter_about(seeds[18], (ADAPTERS, D, RANK), D ** -0.5, 0.1875),
        "fc1_up": scatter_about(seeds[19], (ADAPTERS, RANK, FF), RANK ** -0.5, 1.5),
        "fc2_down": scatter_about(seeds[20], (ADAPTERS, FF, RANK), FF ** -0.5, 0.09375),
        "fc2_up": scatter_about(seeds[21], (ADAPTERS, RANK, D), RANK ** -0.5, 1.5),
    }


highest = lax.Precision.HIGHEST

@jax.custom_vjp
def low(v):
    return lax.optimization_barrier(v.astype(jnp.bfloat16)).astype(jnp.float32)

@jax.custom_vjp
def low_back(v):
    return v

def low_keep(v):
    return (low(v), None)

def low_pass(kept, grad):
    return (grad,)

def back_keep(v):
    return (v, None)

def back_low(kept, grad):
    return (low(grad),)
low.defvjp(low_keep, low_pass)
low_back.defvjp(back_keep, back_low)

def matmul(left, right):
    return jnp.dot(left, right, precision=highest, preferred_element_type=jnp.float32)

def layer_norm(value, gain, shift):
    mean = lax.optimization_barrier(jnp.mean(value, axis=-1, keepdims=True))
    centred = value - mean
    spread = lax.optimization_barrier(jnp.mean(centred * centred, axis=-1, keepdims=True))
    return centred * lax.rsqrt(spread + 1e-05) * gain + shift

def stack_down(down):
    return jnp.transpose(down, (1, 0, 2)).reshape(down.shape[1], down.shape[0] * down.shape[2])

def stack_up(up):
    return up.reshape(up.shape[0] * up.shape[1], up.shape[2])

def adapt(inputs, down, up, select):
    small = low(low_back(matmul(inputs, stack_down(down)) * select))
    return matmul(small, stack_up(up))

def attend_block(query_block, seg_block, keys, values, segment):
    raw_scores = low_back(jnp.einsum('qhd,khd->hqk', query_block, keys, precision=highest))
    same_doc = (seg_block[:, None] == segment[None, :])[None]
    scores = jnp.where(same_doc, raw_scores * HEAD_DIM ** (-0.5), -1e+30)
    row_top = lax.optimization_barrier(jnp.max(scores, axis=2, keepdims=True))
    log_total = row_top + jnp.log(lax.optimization_barrier(jnp.sum(jnp.exp(scores - row_top), axis=2, keepdims=True)))
    probs = low(jnp.exp(scores - log_total))
    return jnp.einsum('hqk,khd->qhd', probs, values, precision=highest)

def doc_tables(doc_lengths, adapter_ids):
    starts = (jnp.cumsum(doc_lengths, axis=1) - doc_lengths).astype(jnp.int32)
    positions = jnp.arange(STRETCH, dtype=jnp.int32)
    segment = (lax.optimization_barrier(jnp.sum((positions[None, :, None] >= starts[:, None, :]).astype(jnp.int32), axis=2)) - 1).astype(jnp.int32)
    doc_range = jnp.arange(DOCS, dtype=jnp.int32)
    chosen = lax.optimization_barrier(jnp.sum(jnp.where(segment[:, :, None] == doc_range[None, None, :], adapter_ids[:, None, :], 0), axis=2)).astype(jnp.int32)
    return (segment, chosen.reshape(TOKENS))

def reference(tokens, cotangent, w_qkv, qv_bias, w_out, out_bias, norm1_gain, norm1_bias, w_fc1, fc1_bias, w_fc2, fc2_bias, norm2_gain, norm2_bias, doc_lengths, adapter_ids, attn_down, attn_up, fc1_down, fc1_up, fc2_down, fc2_up):
    segment, chosen = doc_tables(doc_lengths, adapter_ids)
    lane_owner = jnp.arange(ADAPTERS * RANK, dtype=jnp.int32) // RANK
    select = (chosen[:, None] == lane_owner[None, :]).astype(jnp.float32)
    full_qkv = w_qkv.astype(jnp.float32)
    full_out = w_out.astype(jnp.float32)
    full_fc1 = w_fc1.astype(jnp.float32)
    full_fc2 = w_fc2.astype(jnp.float32)
    bias_qkv = jnp.concatenate([qv_bias[0], jnp.zeros((D,), jnp.float32), qv_bias[1]])
    block_rows = min(512, STRETCH)

    def attend_stretch(items):
        queries, keys, values, seg_row = items

        def one_block(pair):
            return jax.checkpoint(attend_block)(pair[0], pair[1], keys, values, seg_row)
        blocks = lax.map(one_block, (queries.reshape(STRETCH // block_rows, block_rows, HEADS, HEAD_DIM), seg_row.reshape(STRETCH // block_rows, block_rows)))
        return blocks.reshape(STRETCH, D)

    def layer(layer_in, down_attn, up_attn, down_fc1, up_fc1, down_fc2, up_fc2):
        qkv_main = matmul(layer_in, full_qkv) + bias_qkv
        adapters = jnp.concatenate([adapt(layer_in, down_attn[i], up_attn[i], select) for i in range(3)], axis=1)
        qkv = low(low_back(qkv_main + adapters))
        shaped = qkv.reshape(STRETCHES, STRETCH, 3, HEADS, HEAD_DIM)
        attended = lax.map(attend_stretch, (shaped[:, :, 0], shaped[:, :, 1], shaped[:, :, 2], segment))
        attended = low(low_back(attended.reshape(TOKENS, D)))
        z_value = low_back(matmul(attended, full_out) + out_bias + adapt(attended, down_attn[3], up_attn[3], select))
        first_norm = layer_norm(layer_in + z_value, norm1_gain, norm1_bias)
        first_low = low(first_norm)
        pre_act = low_back(matmul(first_low, full_fc1) + fc1_bias + adapt(first_low, down_fc1, up_fc1, select))
        act_low = low(jax.nn.gelu(pre_act, approximate=False))
        y_value = low_back(matmul(act_low, full_fc2) + fc2_bias + adapt(act_low, down_fc2, up_fc2, select))
        return layer_norm(first_norm + y_value, norm2_gain, norm2_bias)
    output, pullback = jax.vjp(layer, tokens.astype(jnp.float32), attn_down.astype(jnp.float32), attn_up.astype(jnp.float32), fc1_down.astype(jnp.float32), fc1_up.astype(jnp.float32), fc2_down.astype(jnp.float32), fc2_up.astype(jnp.float32))
    grads = pullback(cotangent.astype(jnp.float32))
    return (output, grads[0], grads[1], grads[2], grads[3], grads[4], grads[5], grads[6])
```

```python
import functools

import jax
import jax.numpy as jnp
from jax import lax
from jax.experimental import pallas as pl
from jax.experimental.pallas import tpu as pltpu
from jax.sharding import PartitionSpec as P

HEADS = 16
HEAD_DIM = 64
LANES = 128
PAIR = LANES // HEAD_DIM
MESH = pl.DeviceIdType.MESH
F32 = jnp.float32
BF16 = jnp.bfloat16
VMEM_LIMIT = 60 * 2**20


def dot_nn(a, b):
    return lax.dot_general(a, b, (((1,), (0,)), ((), ())), preferred_element_type=F32)


def dot_nt(a, b):
    return lax.dot_general(a, b, (((1,), (1,)), ((), ())), preferred_element_type=F32)


def dot_tn(a, b):
    return lax.dot_general(a, b, (((0,), (0,)), ((), ())), preferred_element_type=F32)


class Geometry:
    def __init__(self, rows, width):
        self.seq = lax.axis_size("seq")
        self.wt = lax.axis_size("wt")
        self.rows = rows
        self.width = width
        self.groups = width // LANES
        self.parts = self.seq // self.groups
        chips = self.seq // 2
        nx = 1
        while nx * nx < chips:
            nx *= 2
        self.nx = nx
        self.ny = chips // nx
        self.keys = self.seq * rows
        self.queries = self.groups * rows


def doc_bounds(len_ref):
    count = len_ref.shape[1]
    starts, ends = [], []
    at = jnp.int32(0)
    for i in range(count):
        starts.append(at)
        at = at + len_ref[0, i]
        ends.append(at)
    return starts, ends


def segment_from(positions, starts):
    seg = jnp.zeros_like(positions)
    for start in starts[1:]:
        seg = seg + (positions >= start).astype(jnp.int32)
    return seg


def select_from(positions, starts, ends, id_ref, rank):
    owner = lax.broadcasted_iota(jnp.int32, positions.shape, 1) // rank
    picked = jnp.zeros(positions.shape, F32)
    for i in range(len(starts)):
        inside = (positions >= starts[i]) & (positions < ends[i]) & (owner == id_ref[0, i])
        picked = jnp.where(inside, 1.0, picked)
    return picked


class Spread:
    KINDS = 9

    def __init__(self, geo, here, region, send, recv, unit):
        self.geo, self.here, self.region = geo, here, region
        self.send, self.recv, self.unit = send, recv, unit

    def copy(self, kind, src, dst, x, y, core):
        return pltpu.make_async_remote_copy(
            src_ref=src,
            dst_ref=dst,
            send_sem=self.send.at[kind, self.unit],
            recv_sem=self.recv.at[kind, self.unit],
            device_id=(((y * self.geo.nx) + x) * 2 + core, self.here[3]),
            device_id_type=MESH,
        )

    def others(self):
        nx, ny = self.geo.nx, self.geo.ny
        x, y, core, _ = self.here
        row = [((x + d) % nx, y) for d in range(1, nx)]
        col = [(x, (y + d) % ny) for d in range(1, ny)]
        return row, col

    def plan(self):
        x, y, core, _ = self.here
        row, col = self.others()
        plan = {kind: [] for kind in range(self.KINDS)}
        for tx, ty in row:
            plan[0].append(((x, y), None, (tx, ty, core)))
        for tx, ty in col:
            plan[1].append(((x, y), None, (tx, ty, core)))
        for ux, uy in row:
            for tx, ty in col:
                plan[2].append(((ux, uy), 0, (tx, ty, core)))
        for ux, uy in col:
            for tx, ty in row:
                plan[3].append(((ux, uy), 1, (tx, ty, core)))
        plan[4].append(((x, y), None, (x, y, 1 - core)))
        for ux, uy in row:
            plan[5].append(((ux, uy), None, (x, y, 1 - core)))
        for ux, uy in col:
            plan[6].append(((ux, uy), None, (x, y, 1 - core)))
        for ux, _ in row:
            for _, uy in col:
                plan[7].append(((ux, uy), 0, (x, y, 1 - core)))
                plan[8].append(((ux, uy), 1, (x, y, 1 - core)))
        return plan

    def go(self, kind, own=None):
        core = self.here[2]
        for (ux, uy), half, (tx, ty, tcore) in self.plan()[kind]:
            dst = self.region(ux, uy, core, half)
            src = dst if own is None else own
            self.copy(kind, src, dst, tx, ty, tcore).start()

    def arrivals(self, kind):
        x, y, core, _ = self.here
        row, col = self.others()
        if kind == 0:
            return [(u, None, core) for u in row]
        if kind == 1:
            return [(u, None, core) for u in col]
        if kind in (2, 3):
            return [((ux, uy), kind - 2, core) for ux, _ in row for _, uy in col]
        if kind == 4:
            return [((x, y), None, 1 - core)]
        if kind == 5:
            return [(u, None, 1 - core) for u in row]
        if kind == 6:
            return [(u, None, 1 - core) for u in col]
        return [((ux, uy), kind - 7, 1 - core) for ux, _ in row for _, uy in col]

    def wait(self, kind):
        x, y, core, _ = self.here
        for (ux, uy), half, whose in self.arrivals(kind):
            ref = self.region(ux, uy, whose, half)
            self.copy(kind, ref, ref, x, y, 1 - core).wait_recv()

    def wait_sends(self):
        x, y, core, _ = self.here
        for kind in range(self.KINDS):
            for (ux, uy), half, _ in self.plan()[kind]:
                ref = self.region(ux, uy, core, half)
                self.copy(kind, ref, ref, x, y, 1 - core).wait_send()


def device_here(geo):
    s = lax.axis_index("seq")
    core = s % 2
    chip = s // 2
    return chip % geo.nx, chip // geo.nx, core, lax.axis_index("wt")


def greet(geo):
    s, w = lax.axis_index("seq"), lax.axis_index("wt")
    barrier = pltpu.get_barrier_semaphore()
    for d in range(1, geo.seq):
        pl.semaphore_signal(barrier, inc=1, device_id=((s + d) % geo.seq, w), device_id_type=MESH)
    for d in range(1, geo.wt):
        pl.semaphore_signal(barrier, inc=1, device_id=(s, (w + d) % geo.wt), device_id_type=MESH)
    pl.semaphore_wait(barrier, geo.seq + geo.wt - 2)


def forward_kernel(
    geo,
    weight_count,
    rank,
    len_ref,
    id_ref,
    tokens_ref,
    wqkv_ref,
    down_ref,
    up_ref,
    bias_ref,
    *refs,
):
    weights_in = refs[:weight_count]
    att_ref, q_ref, k_ref, v_ref, o_ref, lse_ref, slice_ref, small_ref = refs[weight_count : weight_count + 8]
    weights_out = refs[weight_count + 8 : 2 * weight_count + 8]
    (
        tok_buf,
        seg_buf,
        att_buf,
        local_sem,
        send_sem,
        recv_sem,
        slice_send,
        slice_recv,
        line_send,
        line_recv,
        att_send,
        att_recv,
    ) = refs[2 * weight_count + 8 :]
    here = device_here(geo)
    x, y, core, w = here
    s = lax.axis_index("seq")
    part, g = s // geo.groups, s % geo.groups
    rows, width, wt = geo.rows, geo.width, geo.wt
    lanes = pl.ds(pl.multiple_of(g * LANES, LANES), LANES)

    own_tok = pltpu.make_async_copy(tokens_ref, tok_buf.at[s], local_sem.at[0])
    own_tok.start()
    shard = wqkv_ref.shape[0]
    own_slices = []
    for j in range(3):
        src = wqkv_ref.at[:, pl.ds(pl.multiple_of(j * width + g * LANES, LANES), LANES)]
        dst = slice_ref.at[pl.ds(pl.multiple_of(w * shard, shard), shard), pl.ds(j * LANES, LANES)]
        own_slices.append(pltpu.make_async_copy(src, dst, local_sem.at[1 + j]))
        own_slices[-1].start()
    own_weights = []
    for m in range(weight_count):
        height = weights_in[m].shape[0]
        dst = weights_out[m].at[pl.ds(pl.multiple_of(w * height, height), height)]
        own_weights.append(pltpu.make_async_copy(weights_in[m], dst, local_sem.at[4 + m]))

    greet(geo)

    def token_region(ux, uy, whose, half):
        block = tok_buf.at[(uy * geo.nx + ux) * 2 + whose]
        if half is None:
            return block
        return block.at[pl.ds(half * (rows // 2), rows // 2)]

    tok = Spread(geo, here, token_region, send_sem, recv_sem, 0)
    tok.go(0, own=tokens_ref)
    tok.go(1, own=tokens_ref)
    tok.go(4, own=tokens_ref)

    def slice_copy(j, d):
        src = wqkv_ref.at[:, pl.ds(pl.multiple_of(j * width + g * LANES, LANES), LANES)]
        dst = slice_ref.at[pl.ds(pl.multiple_of(w * shard, shard), shard), pl.ds(j * LANES, LANES)]
        return pltpu.make_async_remote_copy(
            src_ref=src,
            dst_ref=dst,
            send_sem=slice_send.at[j, d],
            recv_sem=slice_recv.at[j, d],
            device_id=(s, (w + d) % wt),
            device_id_type=MESH,
        )

    def slice_arrival(j, d):
        origin = (w + wt - d) % wt
        dst = slice_ref.at[pl.ds(pl.multiple_of(origin * shard, shard), shard), pl.ds(j * LANES, LANES)]
        return pltpu.make_async_remote_copy(
            src_ref=dst,
            dst_ref=dst,
            send_sem=slice_send.at[j, d],
            recv_sem=slice_recv.at[j, d],
            device_id=(s, origin),
            device_id_type=MESH,
        )

    for d in range(1, wt):
        for j in range(3):
            slice_copy(j, d).start()
    for copy in own_weights:
        copy.start()

    starts, ends = doc_bounds(len_ref)
    seg_buf[...] = segment_from(lax.broadcasted_iota(jnp.int32, seg_buf.shape, 1), starts)

    seq = geo.seq
    mine = s

    def unit_rows(m, p, unit, half=None):
        height = weights_in[m].shape[0]
        piece = height // seq
        if half is None:
            return weights_out[m].at[pl.ds(pl.multiple_of(p * height + unit * piece, piece), piece)]
        piece = piece // 2
        return weights_out[m].at[
            pl.ds(pl.multiple_of(p * height + unit * 2 * piece + half * piece, piece), piece)
        ]

    def line_copy(m, p, up, own):
        height = weights_in[m].shape[0]
        piece = height // seq
        dst = unit_rows(m, p, mine)
        src = weights_in[m].at[pl.ds(pl.multiple_of(mine * piece, piece), piece)] if own else dst
        target = w + 1 if up else w - 1
        return pltpu.make_async_remote_copy(
            src_ref=src,
            dst_ref=dst,
            send_sem=line_send.at[0 if up else 1, m * wt + p],
            recv_sem=line_recv.at[m * wt + p],
            device_id=(s, target),
            device_id_type=MESH,
        )

    def nth_plane(j):
        below, above = w, wt - 1 - w
        both = jnp.minimum(below, above)
        in_turn = j < 2 * both
        dist = jnp.where(in_turn, j // 2 + 1, j - both + 1)
        from_below = jnp.where(in_turn, j % 2 == 0, below > above)
        return jnp.where(from_below, w - dist, w + dist)

    def weight_spread(m, p):
        def region(ux, uy, whose, half):
            return unit_rows(m, p, (uy * geo.nx + ux) * 2 + whose, half)

        return Spread(geo, here, region, send_sem, recv_sem, 1 + m * wt + p)

    units = [(m, j) for m in range(weight_count) for j in range(wt - 1)]

    def start_lines():
        for m in range(weight_count):
            @pl.when(w < wt - 1)
            def _():
                line_copy(m, w, True, True).start()

            @pl.when(w > 0)
            def _():
                line_copy(m, w, False, True).start()

    def tick(i):
        if 0 <= i < len(units):
            m, j = units[i]
            p = nth_plane(j)
            line_copy(m, p, True, False).wait_recv()

            @pl.when((p < w) & (w < wt - 1))
            def _():
                line_copy(m, p, True, False).start()

            @pl.when((p > w) & (w > 0))
            def _():
                line_copy(m, p, False, False).start()

            spread = weight_spread(m, p)
            spread.go(0)
            spread.go(1)
            spread.go(4)
        if 0 <= i - 1 < len(units):
            m, j = units[i - 1]
            spread = weight_spread(m, nth_plane(j))
            spread.wait(0)
            spread.go(2)
            spread.go(5)
            spread.wait(1)
            spread.go(3)
            spread.go(6)
        if 0 <= i - 2 < len(units):
            m, j = units[i - 2]
            spread = weight_spread(m, nth_plane(j))
            spread.wait(2)
            spread.go(7)
            spread.wait(3)
            spread.go(8)

    tick_count = len(units) + 2 if units else 0

    nx, ny = geo.nx, geo.ny
    row_n, col_n, diag_n = 2 * (nx - 1), 2 * (ny - 1), 2 * (nx - 1) * (ny - 1)

    def block_owner(i):
        r = i - 2
        c = r - row_n
        d = c - col_n
        dx_row, k_row = r % max(nx - 1, 1) + 1, r // max(nx - 1, 1)
        dy_col, k_col = c % max(ny - 1, 1) + 1, c // max(ny - 1, 1)
        half = max(diag_n // 2, 1)
        k_diag, in_diag = d // half, d % half
        dx_diag, dy_diag = in_diag % max(nx - 1, 1) + 1, in_diag // max(nx - 1, 1) + 1
        dx = jnp.where(i < 2, 0, jnp.where(i < 2 + row_n, dx_row, jnp.where(i < 2 + row_n + col_n, 0, dx_diag)))
        dy = jnp.where(i < 2 + row_n, 0, jnp.where(i < 2 + row_n + col_n, dy_col, dy_diag))
        kk = jnp.where(i < 2, i, jnp.where(i < 2 + row_n, k_row, jnp.where(i < 2 + row_n + col_n, k_col, k_diag)))
        return (((y + dy) % ny) * nx + (x + dx) % nx) * 2 + (core + kk) % 2

    def project(i, carry):
        @pl.when(i == 0)
        def _():
            own_tok.wait()
            for copy in own_slices:
                copy.wait()
            for d in range(1, wt):
                for j in range(3):
                    slice_arrival(j, d).wait_recv()
            start_lines()

        @pl.when(i == 1)
        def _():
            tok.wait(4)

        @pl.when(i == 2)
        def _():
            tok.wait(0)
            tok.go(2)
            tok.go(5)
            tok.wait(1)
            tok.go(3)
            tok.go(6)

        @pl.when(i == 2 + row_n // 2)
        def _():
            tok.wait(5)

        @pl.when(i == 2 + row_n + col_n // 2)
        def _():
            tok.wait(6)

        @pl.when(i == 2 + row_n + col_n)
        def _():
            tok.wait(2)
            tok.go(7)
            tok.wait(3)
            tok.go(8)

        @pl.when(i == 2 + row_n + col_n + diag_n // 2)
        def _():
            tok.wait(7)
            tok.wait(8)

        t = block_owner(i)
        block = tok_buf[t]
        at = pl.ds(pl.multiple_of(t * rows, rows), rows)
        pos = t * rows + lax.broadcasted_iota(jnp.int32, (rows, LANES), 0)
        chosen = select_from(pos, starts, ends, id_ref, rank)
        main = dot_nn(block, slice_ref[...])
        small = dot_nt(block, down_ref[...])
        for j in range(3):
            cut = slice(j * LANES, (j + 1) * LANES)
            low = (small[:, cut] * chosen).astype(BF16)
            small_ref[at, cut] = low
            value = main[:, cut] + dot_nn(low, up_ref[cut, lanes])
            if j == 0:
                value = value + bias_ref[0:1, lanes]

                @pl.when(t // geo.groups == part)
                def _():
                    inner = pl.ds(pl.multiple_of((t % geo.groups) * rows, rows), rows)
                    q_ref[inner, :] = value.astype(BF16)
            elif j == 1:
                k_ref[at, :] = value.astype(BF16)
            else:
                v_ref[at, :] = (value + bias_ref[1:2, lanes]).astype(BF16)
        return carry

    lax.fori_loop(0, geo.seq, project, 0)

    scale = HEAD_DIM ** (-0.5)
    chunk = min(2048, geo.keys)
    chunks = geo.keys // chunk
    first_head = lax.broadcasted_iota(jnp.int32, (rows, LANES), 1) < HEAD_DIM

    def att_copy(b):
        return pltpu.make_async_remote_copy(
            src_ref=att_buf.at[b],
            dst_ref=att_ref.at[:, lanes],
            send_sem=att_send.at[b],
            recv_sem=att_recv.at[g],
            device_id=(part * geo.groups + b, w),
            device_id_type=MESH,
        )

    def attend(i, carry):
        for n in range(min(tick_count, geo.groups)):
            @pl.when(i == n)
            def _():
                tick(n)

        b = (g + 1 + i) % geo.groups
        inner = pl.ds(pl.multiple_of(b * rows, rows), rows)
        query = q_ref[inner, :] * jnp.asarray(scale, BF16)
        q_pos = (part * geo.groups + b) * rows + lax.broadcasted_iota(jnp.int32, (rows, 1), 0)
        q_seg = segment_from(q_pos, starts)
        results = []
        for h in range(PAIR):
            mask = first_head if h == 0 else jnp.logical_not(first_head)
            q_head = jnp.where(mask, query, jnp.zeros_like(query))

            def one(c, state):
                top, total, acc = state
                keys_at = pl.ds(pl.multiple_of(c * chunk, chunk), chunk)
                score = dot_nt(q_head, k_ref[keys_at, :])
                score = jnp.where(q_seg == seg_buf[:, keys_at], score, -1e30)
                peak = jnp.max(score, axis=1, keepdims=True)
                if top is not None:
                    peak = jnp.maximum(top, peak)
                weight = jnp.exp(score - peak)
                add = jnp.sum(weight, axis=1, keepdims=True)
                out = dot_nn(weight.astype(BF16), v_ref[keys_at, :])
                if top is not None:
                    fade = jnp.exp(top - peak)
                    add = add + total * fade
                    out = out + acc * fade
                return peak, add, out

            state = one(0, (None, None, None))
            if chunks > 1:
                state = lax.fori_loop(1, chunks, one, state)
            top, total, acc = state
            results.append((acc / total, top + jnp.log(total)))
        out = jnp.where(first_head, results[0][0], results[1][0])
        o_ref[inner, :] = out
        lse_ref[inner, :] = jnp.where(first_head, results[0][1], results[1][1])
        att_buf[b] = out.astype(BF16)

        @pl.when(b != g)
        def _():
            att_copy(b).start()

        return carry

    lax.fori_loop(0, geo.groups, attend, 0)
    own_att = pltpu.make_async_copy(att_buf.at[g], att_ref.at[:, lanes], local_sem.at[0])
    own_att.start()

    for n in range(geo.groups, tick_count):
        tick(n)

    for d in range(1, geo.groups):
        other = (g + d) % geo.groups
        cut = pl.ds(pl.multiple_of(other * LANES, LANES), LANES)
        pltpu.make_async_remote_copy(
            src_ref=att_ref.at[:, cut],
            dst_ref=att_ref.at[:, cut],
            send_sem=att_send.at[other],
            recv_sem=att_recv.at[other],
            device_id=(part * geo.groups + other, w),
            device_id_type=MESH,
        ).wait_recv()
        att_copy(other).wait_send()
    own_att.wait()
    tok.wait_sends()
    for d in range(1, wt):
        for j in range(3):
            slice_copy(j, d).wait_send()
    for m in range(weight_count):
        own_weights[m].wait()

        @pl.when(w < wt - 1)
        def _():
            line_copy(m, w, True, True).wait_send()

        @pl.when(w > 0)
        def _():
            line_copy(m, w, False, True).wait_send()

    for m, j in units:
        p = nth_plane(j)

        @pl.when((p < w) & (w < wt - 1))
        def _():
            line_copy(m, p, True, False).wait_send()

        @pl.when((p > w) & (w > 0))
        def _():
            line_copy(m, p, False, False).wait_send()

        spread = weight_spread(m, p)
        for kind in range(4, 9):
            spread.wait(kind)
        spread.wait_sends()


def forward_attention(geo, rank, lengths, ids, tokens, w_qkv, down, up, bias, weights):
    rows, width = geo.rows, geo.width
    count = len(weights)
    any_spec = pl.BlockSpec(memory_space=pl.ANY)
    vmem = pl.BlockSpec(memory_space=pltpu.VMEM)
    smem = pl.BlockSpec(memory_space=pltpu.SMEM)
    shapes = [
        jax.ShapeDtypeStruct((rows, width), BF16),
        jax.ShapeDtypeStruct((geo.queries, LANES), BF16),
        jax.ShapeDtypeStruct((geo.keys, LANES), BF16),
        jax.ShapeDtypeStruct((geo.keys, LANES), BF16),
        jax.ShapeDtypeStruct((geo.queries, LANES), F32),
        jax.ShapeDtypeStruct((geo.queries, LANES), F32),
        jax.ShapeDtypeStruct((width, 3 * LANES), BF16),
        jax.ShapeDtypeStruct((geo.keys, 3 * LANES), BF16),
    ] + [jax.ShapeDtypeStruct((v.shape[0] * geo.wt, v.shape[1]), BF16) for v in weights]
    units = 1 + count * geo.wt
    dma = pltpu.SemaphoreType.DMA
    results = pl.pallas_call(
        functools.partial(forward_kernel, geo, count, rank),
        out_shape=shapes,
        in_specs=[smem, smem, any_spec, any_spec, vmem, vmem, vmem] + [any_spec] * count,
        out_specs=[any_spec] + [vmem] * 7 + [any_spec] * count,
        scratch_shapes=[
            pltpu.VMEM((geo.seq, rows, width), BF16),
            pltpu.VMEM((1, geo.keys), jnp.int32),
            pltpu.VMEM((geo.groups, rows, LANES), BF16),
            dma((4 + count,)),
            dma((Spread.KINDS, units)),
            dma((Spread.KINDS, units)),
            dma((3, geo.wt)),
            dma((3, geo.wt)),
            dma((2, max(count, 1) * geo.wt)),
            dma((max(count, 1) * geo.wt,)),
            dma((geo.groups,)),
            dma((geo.groups,)),
        ],
        compiler_params=pltpu.CompilerParams(
            collective_id=0, has_side_effects=True, vmem_limit_bytes=VMEM_LIMIT
        ),
        name="gather_attend",
    )(lengths, ids, tokens, w_qkv, down, up, bias, *weights)
    return results[:8], results[8:]


def backward_kernel(geo, len_ref, part_ref, q_ref, k_ref, v_ref, o_ref, lse_ref, g_ref, dq_ref, dk_ref, dv_ref, dk_acc, dv_acc):
    rows = geo.rows
    part = part_ref[0, 0]
    scale = HEAD_DIM ** (-0.5)
    starts, ends = doc_bounds(len_ref)
    first_head = lax.broadcasted_iota(jnp.int32, (rows, LANES), 1) < HEAD_DIM
    dk_acc[...] = jnp.zeros_like(dk_acc)
    dv_acc[...] = jnp.zeros_like(dv_acc)

    def seg_of(position):
        seg = jnp.int32(0)
        for start in starts[1:]:
            seg = seg + (position >= start).astype(jnp.int32)
        return seg

    def pick(values, index):
        found = values[0]
        for i in range(1, len(values)):
            found = jnp.where(index == i, values[i], found)
        return found

    def query_block(b, carry):
        at = pl.ds(pl.multiple_of(b * rows, rows), rows)
        origin = (part * geo.groups + b) * rows
        query = q_ref[at, :] * jnp.asarray(scale, BF16)
        cot = g_ref[at, :]
        lse = lse_ref[at, :]
        both = cot.astype(F32) * o_ref[at, :]
        q_pos = origin + lax.broadcasted_iota(jnp.int32, (rows, 1), 0)
        q_seg = segment_from(q_pos, starts)
        heads = []
        for h in range(PAIR):
            mask = first_head if h == 0 else jnp.logical_not(first_head)
            zero = jnp.zeros_like(query)
            heads.append(
                (
                    jnp.where(mask, query, zero),
                    jnp.where(mask, cot, zero),
                    lse[:, h * HEAD_DIM : h * HEAD_DIM + 1],
                    jnp.sum(jnp.where(mask, both, 0.0), axis=1, keepdims=True),
                )
            )
        low = pick(starts, seg_of(origin)) // rows
        high = (pick(ends, seg_of(origin + rows - 1)) + rows - 1) // rows

        def key_block(c, accs):
            keys_at = pl.ds(pl.multiple_of(c * rows, rows), rows)
            key, value = k_ref[keys_at, :], v_ref[keys_at, :]
            k_pos = c * rows + lax.broadcasted_iota(jnp.int32, (1, rows), 1)
            same = q_seg == segment_from(k_pos, starts)
            new = []
            dk_parts, dv_parts = [], []
            for h in range(PAIR):
                q_head, g_head, lse_head, dot_head = heads[h]
                score = jnp.where(same, dot_nt(q_head, key), -1e30)
                prob = jnp.exp(score - lse_head)
                d_prob = dot_nt(g_head, value)
                raw = (prob * (d_prob - dot_head) * scale).astype(BF16)
                new.append(accs[h] + dot_nn(raw, key))
                dk_parts.append(dot_tn(raw, q_head))
                dv_parts.append(dot_tn(prob.astype(BF16), g_head))
            dk_acc[keys_at, :] += dk_parts[0] + dk_parts[1]
            dv_acc[keys_at, :] += dv_parts[0] + dv_parts[1]
            return tuple(new)

        zero = jnp.zeros((rows, LANES), F32)
        accs = lax.fori_loop(low, high, key_block, (zero, zero))
        dq_ref[at, :] = jnp.where(first_head, accs[0], accs[1]).astype(BF16)
        return carry

    lax.fori_loop(0, geo.groups, query_block, 0)
    dk_ref[...] = (dk_acc[...] * HEAD_DIM**0.5).astype(BF16)
    dv_ref[...] = dv_acc[...].astype(BF16)


def backward_attention(geo, lengths, part, q, k, v, o, lse, d_heads):
    smem = pl.BlockSpec(memory_space=pltpu.SMEM)
    vmem = pl.BlockSpec(memory_space=pltpu.VMEM)
    return pl.pallas_call(
        functools.partial(backward_kernel, geo),
        out_shape=[
            jax.ShapeDtypeStruct((geo.queries, LANES), BF16),
            jax.ShapeDtypeStruct((geo.keys, LANES), BF16),
            jax.ShapeDtypeStruct((geo.keys, LANES), BF16),
        ],
        in_specs=[smem, smem] + [vmem] * 6,
        out_specs=[vmem] * 3,
        scratch_shapes=[pltpu.VMEM((geo.keys, LANES), F32)] * 2,
        compiler_params=pltpu.CompilerParams(vmem_limit_bytes=VMEM_LIMIT),
        name="attend_back",
    )(lengths, part, q, k, v, o, lse, d_heads)


def layer_norm(value, gain, shift):
    mean = jnp.mean(value, axis=-1, keepdims=True)
    centred = value - mean
    spread = jnp.mean(centred * centred, axis=-1, keepdims=True)
    return centred * lax.rsqrt(spread + 1e-05) * gain + shift


def gelu_exact(value):
    return jax.nn.gelu(value, approximate=False)


def times_transposed(grad, weight):
    return lax.dot_general(
        grad, weight, (((1,), (1,)), ((), ())), preferred_element_type=jnp.float32
    )


def left_inner(left, right):
    return lax.dot_general(
        left, right, (((0,), (0,)), ((), ())), preferred_element_type=jnp.float32
    )


def stack_down(down):
    return jnp.transpose(down, (1, 0, 2)).reshape(down.shape[1], down.shape[0] * down.shape[2])


def stack_up(up):
    return up.reshape(up.shape[0] * up.shape[1], up.shape[2])


def unstack_down(stacked, adapter_count, rank_size):
    return jnp.transpose(stacked.reshape(stacked.shape[0], adapter_count, rank_size), (1, 0, 2))


def unstack_up(stacked, adapter_count, rank_size):
    return stacked.reshape(adapter_count, rank_size, stacked.shape[1])


def segment_of(positions, starts):
    return jnp.sum((positions[:, None] >= starts[None, :]).astype(jnp.int32), axis=1) - 1


def shards(
    tokens,
    cotangent,
    w_qkv,
    qv_bias,
    w_out,
    out_bias,
    norm1_gain,
    norm1_bias,
    w_fc1,
    fc1_bias,
    w_fc2,
    fc2_bias,
    norm2_gain,
    norm2_bias,
    doc_lengths,
    adapter_ids,
    attn_down,
    attn_up,
    fc1_down,
    fc1_up,
    fc2_down,
    fc2_up,
):
    tok_rows, model_width = tokens.shape
    adapter_count = attn_down.shape[1]
    rank_size = attn_down.shape[3]
    lane_count = adapter_count * rank_size
    seq_count = lax.axis_size("seq")
    geo = Geometry(tok_rows, model_width)
    seq_index = lax.axis_index("seq")
    part_index = seq_index // geo.groups
    head_index = seq_index % geo.groups
    lengths = doc_lengths[0]
    starts = jnp.cumsum(lengths) - lengths
    local_pos = seq_index * tok_rows + jnp.arange(tok_rows, dtype=jnp.int32)
    local_seg = segment_of(local_pos, starts)
    doc_range = jnp.arange(lengths.shape[0], dtype=jnp.int32)
    chosen = jnp.sum(
        jnp.where(local_seg[:, None] == doc_range[None, :], adapter_ids[0][None, :], 0), axis=1
    )
    lane_owner = jnp.arange(lane_count, dtype=jnp.int32) // rank_size
    select = (chosen[:, None] == lane_owner[None, :]).astype(jnp.float32)
    out_down = stack_down(attn_down[3])
    out_up = stack_up(attn_up[3])
    fc1_down_all = stack_down(fc1_down)
    fc1_up_all = stack_up(fc1_up)
    fc2_down_all = stack_down(fc2_down)
    fc2_up_all = stack_up(fc2_up)
    down_rows = jnp.transpose(attn_down, (0, 1, 3, 2)).reshape(4 * lane_count, model_width)
    up_rows = attn_up.reshape(4 * lane_count, model_width)
    weights = (w_out, w_fc1, w_fc2)
    inside = [v.shape[0] % (32 * seq_count) == 0 for v in weights]
    (attended_tok, q_heads, k_heads, v_heads, o_heads, lse_heads, w_slice, small_all), gathered = forward_attention(
        geo,
        rank_size,
        doc_lengths,
        adapter_ids,
        tokens,
        w_qkv,
        down_rows[: 3 * lane_count],
        up_rows[: 3 * lane_count],
        qv_bias,
        [v for v, here in zip(weights, inside) if here],
    )
    gathered = list(gathered)
    full_out, full_fc1, full_fc2 = [
        gathered.pop(0) if here else lax.all_gather(v, "wt", axis=0, tiled=True)
        for v, here in zip(weights, inside)
    ]
    out_main = jnp.dot(attended_tok, full_out, preferred_element_type=jnp.float32)
    small_out = (
        jnp.dot(attended_tok, out_down, preferred_element_type=jnp.float32) * select
    ).astype(jnp.bfloat16)
    z_value = out_main + out_bias + jnp.dot(small_out, out_up, preferred_element_type=jnp.float32)
    first_sum = tokens.astype(jnp.float32) + z_value
    first_norm, norm1_back = jax.vjp(
        lambda value: layer_norm(value, norm1_gain, norm1_bias), first_sum
    )
    first_low = first_norm.astype(jnp.bfloat16)
    fc1_main = jnp.dot(first_low, full_fc1, preferred_element_type=jnp.float32)
    small_fc1 = (
        jnp.dot(first_low, fc1_down_all, preferred_element_type=jnp.float32) * select
    ).astype(jnp.bfloat16)
    pre_act = (
        fc1_main + fc1_bias + jnp.dot(small_fc1, fc1_up_all, preferred_element_type=jnp.float32)
    )
    act_value, gelu_back = jax.vjp(gelu_exact, pre_act)
    act_low = act_value.astype(jnp.bfloat16)
    fc2_main = jnp.dot(act_low, full_fc2, preferred_element_type=jnp.float32)
    small_fc2 = (
        jnp.dot(act_low, fc2_down_all, preferred_element_type=jnp.float32) * select
    ).astype(jnp.bfloat16)
    y_value = (
        fc2_main + fc2_bias + jnp.dot(small_fc2, fc2_up_all, preferred_element_type=jnp.float32)
    )
    output, norm2_back = jax.vjp(
        lambda value: layer_norm(value, norm2_gain, norm2_bias), first_norm + y_value
    )
    d_second = norm2_back(cotangent.astype(jnp.float32))[0]
    d_y = d_second.astype(jnp.bfloat16)
    d_act = times_transposed(d_y, full_fc2)
    low_fc2 = (times_transposed(d_y, fc2_up_all) * select).astype(jnp.bfloat16)
    d_act = d_act + times_transposed(low_fc2, fc2_down_all)
    grad_fc2_up = left_inner(small_fc2, d_y)
    grad_fc2_down = left_inner(act_low, low_fc2)
    d_pre = gelu_back(d_act)[0].astype(jnp.bfloat16)
    d_first_low = times_transposed(d_pre, full_fc1)
    low_fc1 = (times_transposed(d_pre, fc1_up_all) * select).astype(jnp.bfloat16)
    d_first_low = d_first_low + times_transposed(low_fc1, fc1_down_all)
    grad_fc1_up = left_inner(small_fc1, d_pre)
    grad_fc1_down = left_inner(first_low, low_fc1)
    d_first = norm1_back(d_second + d_first_low)[0]
    d_z = d_first.astype(jnp.bfloat16)
    d_attended = times_transposed(d_z, full_out)
    low_out = (times_transposed(d_z, out_up) * select).astype(jnp.bfloat16)
    d_attended = (d_attended + times_transposed(low_out, out_down)).astype(jnp.bfloat16)
    grad_out_up = left_inner(small_out, d_z)
    grad_out_down = left_inner(attended_tok, low_out)
    blocks = [
        [p * geo.groups + i for i in range(geo.groups)] for p in range(geo.parts)
    ]
    d_heads = lax.all_to_all(
        d_attended.reshape(tok_rows, geo.groups, LANES),
        "seq",
        split_axis=1,
        concat_axis=0,
        axis_index_groups=blocks,
        tiled=True,
    ).reshape(geo.queries, LANES)
    d_q, d_k, d_v = backward_attention(
        geo, doc_lengths, part_index.reshape(1, 1), q_heads, k_heads, v_heads, o_heads, lse_heads, d_heads
    )
    if geo.parts > 1:
        d_q = lax.dynamic_update_slice_in_dim(
            jnp.zeros((geo.keys, LANES), BF16), d_q, part_index * geo.queries, 0
        )
    d_three = jnp.concatenate([d_q, d_k, d_v], axis=1)
    partial = times_transposed(d_three, w_slice).astype(BF16).reshape(seq_count, tok_rows, model_width)
    d_tokens = jnp.sum(
        lax.all_to_all(partial, "seq", split_axis=0, concat_axis=0, tiled=True).astype(F32), axis=0
    )
    up_slice = lax.dynamic_slice_in_dim(up_rows[: 3 * lane_count], head_index * LANES, LANES, 1)
    low_part = jnp.concatenate(
        [
            times_transposed(
                d_three[:, i * LANES : (i + 1) * LANES], up_slice[i * lane_count : (i + 1) * lane_count]
            )
            for i in range(3)
        ],
        axis=1,
    )
    low_sum = lax.psum_scatter(low_part, "seq", scatter_dimension=0, tiled=True)
    low_qkv = (low_sum * jnp.tile(select, (1, 3))).astype(BF16)
    input_grad = d_first + d_tokens + jnp.dot(
        low_qkv, down_rows[: 3 * lane_count], preferred_element_type=F32
    )
    grad_qkv_down = left_inner(low_qkv, tokens)
    grad_qkv_up = []
    for i in range(3):
        cut = slice(i * LANES, (i + 1) * LANES)
        own = left_inner(small_all[:, cut], d_three[:, cut])
        grad_qkv_up.append(
            lax.dynamic_update_slice_in_dim(
                jnp.zeros((lane_count, model_width), F32), own, head_index * LANES, 1
            )
        )
    grad_attn_down = jnp.stack(
        [
            jnp.transpose(
                grad_qkv_down[i * lane_count : (i + 1) * lane_count].reshape(
                    adapter_count, rank_size, model_width
                ),
                (0, 2, 1),
            )
            for i in range(3)
        ]
        + [unstack_down(grad_out_down, adapter_count, rank_size)]
    )
    grad_attn_up = jnp.stack(
        [
            unstack_up(piece_grad, adapter_count, rank_size)
            for piece_grad in grad_qkv_up + [grad_out_up]
        ]
    )
    summed = lax.psum(
        (
            grad_attn_down,
            grad_attn_up,
            unstack_down(grad_fc1_down, adapter_count, rank_size),
            unstack_up(grad_fc1_up, adapter_count, rank_size),
            unstack_down(grad_fc2_down, adapter_count, rank_size),
            unstack_up(grad_fc2_up, adapter_count, rank_size),
        ),
        ("seq", "wt"),
    )
    return (output, input_grad, summed[0], summed[1], summed[2], summed[3], summed[4], summed[5])


def solution(mesh):
    placed = (
        P(("wt", "seq"), None),
        P(("wt", "seq"), None),
        P("wt", None),
        P(),
        P("wt", None),
        P(),
        P(),
        P(),
        P("wt", None),
        P(),
        P("wt", None),
        P(),
        P(),
        P(),
        P("wt", None),
        P("wt", None),
        P(),
        P(),
        P(),
        P(),
        P(),
        P(),
    )
    return jax.shard_map(
        shards,
        mesh=mesh,
        in_specs=placed,
        out_specs=(P(("wt", "seq"), None), P(("wt", "seq"), None), P(), P(), P(), P(), P(), P()),
        check_vma=False,
    )
```

```python
import functools

import jax
import jax.numpy as jnp
from jax import lax
from jax.experimental import pallas as pl
from jax.experimental.pallas import tpu as pltpu
from jax.sharding import PartitionSpec as P

HEADS = 16
HEAD_DIM = 64
LANES = 128
PAIR = LANES // HEAD_DIM
MESH = pl.DeviceIdType.MESH
F32 = jnp.float32
BF16 = jnp.bfloat16
VMEM_LIMIT = 60 * 2**20


def dot_nn(a, b):
    return lax.dot_general(a, b, (((1,), (0,)), ((), ())), preferred_element_type=F32)


def dot_nt(a, b):
    return lax.dot_general(a, b, (((1,), (1,)), ((), ())), preferred_element_type=F32)


def dot_tn(a, b):
    return lax.dot_general(a, b, (((0,), (0,)), ((), ())), preferred_element_type=F32)


class Geometry:
    def __init__(self, rows, width):
        self.seq = lax.axis_size("seq")
        self.wt = lax.axis_size("wt")
        self.rows = rows
        self.width = width
        self.groups = width // LANES
        self.parts = self.seq // self.groups
        chips = self.seq // 2
        nx = 1
        while nx * nx < chips:
            nx *= 2
        self.nx = nx
        self.ny = chips // nx
        self.keys = self.seq * rows
        self.queries = self.groups * rows


def doc_bounds(len_ref):
    count = len_ref.shape[1]
    starts, ends = [], []
    at = jnp.int32(0)
    for i in range(count):
        starts.append(at)
        at = at + len_ref[0, i]
        ends.append(at)
    return starts, ends


def segment_from(positions, starts):
    seg = jnp.zeros_like(positions)
    for start in starts[1:]:
        seg = seg + (positions >= start).astype(jnp.int32)
    return seg


def select_from(positions, starts, ends, id_ref, rank):
    owner = lax.broadcasted_iota(jnp.int32, positions.shape, 1) // rank
    picked = jnp.zeros(positions.shape, F32)
    for i in range(len(starts)):
        inside = (positions >= starts[i]) & (positions < ends[i]) & (owner == id_ref[0, i])
        picked = jnp.where(inside, 1.0, picked)
    return picked


class Spread:
    KINDS = 9

    def __init__(self, geo, here, region, send, recv, unit, first=0):
        self.geo, self.here, self.region = geo, here, region
        self.send, self.recv, self.unit, self.first = send, recv, unit, first

    def copy(self, kind, src, dst, x, y, core):
        return pltpu.make_async_remote_copy(
            src_ref=src,
            dst_ref=dst,
            send_sem=self.send.at[kind, self.unit],
            recv_sem=self.recv.at[kind, self.unit],
            device_id=(self.first + ((y * self.geo.nx) + x) * 2 + core, self.here[3]),
            device_id_type=MESH,
        )

    def others(self):
        nx, ny = self.geo.nx, self.geo.ny
        x, y, core, _ = self.here
        row = [((x + d) % nx, y) for d in range(1, nx)]
        col = [(x, (y + d) % ny) for d in range(1, ny)]
        return row, col

    def plan(self):
        x, y, core, _ = self.here
        row, col = self.others()
        plan = {kind: [] for kind in range(self.KINDS)}
        for tx, ty in row:
            plan[0].append(((x, y), None, (tx, ty, core)))
        for tx, ty in col:
            plan[1].append(((x, y), None, (tx, ty, core)))
        for ux, uy in row:
            for tx, ty in col:
                plan[2].append(((ux, uy), 0, (tx, ty, core)))
        for ux, uy in col:
            for tx, ty in row:
                plan[3].append(((ux, uy), 1, (tx, ty, core)))
        plan[4].append(((x, y), None, (x, y, 1 - core)))
        for ux, uy in row:
            plan[5].append(((ux, uy), None, (x, y, 1 - core)))
        for ux, uy in col:
            plan[6].append(((ux, uy), None, (x, y, 1 - core)))
        for ux, _ in row:
            for _, uy in col:
                plan[7].append(((ux, uy), 0, (x, y, 1 - core)))
                plan[8].append(((ux, uy), 1, (x, y, 1 - core)))
        return plan

    def go(self, kind, own=None):
        core = self.here[2]
        for (ux, uy), half, (tx, ty, tcore) in self.plan()[kind]:
            dst = self.region(ux, uy, core, half)
            src = dst if own is None else own
            self.copy(kind, src, dst, tx, ty, tcore).start()

    def arrivals(self, kind):
        x, y, core, _ = self.here
        row, col = self.others()
        if kind == 0:
            return [(u, None, core) for u in row]
        if kind == 1:
            return [(u, None, core) for u in col]
        if kind in (2, 3):
            return [((ux, uy), kind - 2, core) for ux, _ in row for _, uy in col]
        if kind == 4:
            return [((x, y), None, 1 - core)]
        if kind == 5:
            return [(u, None, 1 - core) for u in row]
        if kind == 6:
            return [(u, None, 1 - core) for u in col]
        return [((ux, uy), kind - 7, 1 - core) for ux, _ in row for _, uy in col]

    def wait(self, kind):
        x, y, core, _ = self.here
        for (ux, uy), half, whose in self.arrivals(kind):
            ref = self.region(ux, uy, whose, half)
            self.copy(kind, ref, ref, x, y, 1 - core).wait_recv()

    def wait_sends(self):
        x, y, core, _ = self.here
        for kind in range(self.KINDS):
            for (ux, uy), half, _ in self.plan()[kind]:
                ref = self.region(ux, uy, core, half)
                self.copy(kind, ref, ref, x, y, 1 - core).wait_send()


def device_here(geo):
    s = lax.axis_index("seq")
    core = s % 2
    chip = s // 2
    return chip % geo.nx, chip // geo.nx, core, lax.axis_index("wt")


def greet(geo):
    s, w = lax.axis_index("seq"), lax.axis_index("wt")
    barrier = pltpu.get_barrier_semaphore()
    for d in range(1, geo.seq):
        pl.semaphore_signal(barrier, inc=1, device_id=((s + d) % geo.seq, w), device_id_type=MESH)
    for d in range(1, geo.wt):
        pl.semaphore_signal(barrier, inc=1, device_id=(s, (w + d) % geo.wt), device_id_type=MESH)
    pl.semaphore_wait(barrier, geo.seq + geo.wt - 2)


def forward_kernel(
    geo,
    weight_count,
    rank,
    len_ref,
    id_ref,
    tokens_ref,
    wqkv_ref,
    down_ref,
    up_ref,
    bias_ref,
    *refs,
):
    weights_in = refs[:weight_count]
    att_ref, q_ref, k_ref, v_ref, o_ref, lse_ref, slice_ref, small_ref = refs[weight_count : weight_count + 8]
    weights_out = refs[weight_count + 8 : 2 * weight_count + 8]
    (
        tok_buf,
        seg_buf,
        att_buf,
        local_sem,
        send_sem,
        recv_sem,
        slice_send,
        slice_recv,
        line_send,
        line_recv,
        att_send,
        att_recv,
    ) = refs[2 * weight_count + 8 :]
    here = device_here(geo)
    x, y, core, w = here
    s = lax.axis_index("seq")
    part, g = s // geo.groups, s % geo.groups
    rows, width, wt = geo.rows, geo.width, geo.wt
    lanes = pl.ds(pl.multiple_of(g * LANES, LANES), LANES)

    own_tok = pltpu.make_async_copy(tokens_ref, tok_buf.at[s], local_sem.at[0])
    own_tok.start()
    shard = wqkv_ref.shape[0]
    own_slices = []
    for j in range(3):
        src = wqkv_ref.at[:, pl.ds(pl.multiple_of(j * width + g * LANES, LANES), LANES)]
        dst = slice_ref.at[pl.ds(pl.multiple_of(w * shard, shard), shard), pl.ds(j * LANES, LANES)]
        own_slices.append(pltpu.make_async_copy(src, dst, local_sem.at[1 + j]))
        own_slices[-1].start()
    own_weights = []
    for m in range(weight_count):
        height = weights_in[m].shape[0]
        dst = weights_out[m].at[pl.ds(pl.multiple_of(w * height, height), height)]
        own_weights.append(pltpu.make_async_copy(weights_in[m], dst, local_sem.at[4 + m]))

    greet(geo)

    def token_region(ux, uy, whose, half):
        block = tok_buf.at[(uy * geo.nx + ux) * 2 + whose]
        if half is None:
            return block
        return block.at[pl.ds(half * (rows // 2), rows // 2)]

    tok = Spread(geo, here, token_region, send_sem, recv_sem, 0)
    tok.go(0, own=tokens_ref)
    tok.go(1, own=tokens_ref)
    tok.go(4, own=tokens_ref)

    def slice_copy(j, d):
        src = wqkv_ref.at[:, pl.ds(pl.multiple_of(j * width + g * LANES, LANES), LANES)]
        dst = slice_ref.at[pl.ds(pl.multiple_of(w * shard, shard), shard), pl.ds(j * LANES, LANES)]
        return pltpu.make_async_remote_copy(
            src_ref=src,
            dst_ref=dst,
            send_sem=slice_send.at[j, d],
            recv_sem=slice_recv.at[j, d],
            device_id=(s, (w + d) % wt),
            device_id_type=MESH,
        )

    def slice_arrival(j, d):
        origin = (w + wt - d) % wt
        dst = slice_ref.at[pl.ds(pl.multiple_of(origin * shard, shard), shard), pl.ds(j * LANES, LANES)]
        return pltpu.make_async_remote_copy(
            src_ref=dst,
            dst_ref=dst,
            send_sem=slice_send.at[j, d],
            recv_sem=slice_recv.at[j, d],
            device_id=(s, origin),
            device_id_type=MESH,
        )

    for d in range(1, wt):
        for j in range(3):
            slice_copy(j, d).start()
    for copy in own_weights:
        copy.start()

    starts, ends = doc_bounds(len_ref)
    seg_buf[...] = segment_from(lax.broadcasted_iota(jnp.int32, seg_buf.shape, 1), starts)

    seq = geo.seq
    mine = s

    def unit_rows(m, p, unit, half=None):
        height = weights_in[m].shape[0]
        piece = height // seq
        if half is None:
            return weights_out[m].at[pl.ds(pl.multiple_of(p * height + unit * piece, piece), piece)]
        piece = piece // 2
        return weights_out[m].at[
            pl.ds(pl.multiple_of(p * height + unit * 2 * piece + half * piece, piece), piece)
        ]

    def line_copy(m, p, up, own):
        height = weights_in[m].shape[0]
        piece = height // seq
        dst = unit_rows(m, p, mine)
        src = weights_in[m].at[pl.ds(pl.multiple_of(mine * piece, piece), piece)] if own else dst
        target = w + 1 if up else w - 1
        return pltpu.make_async_remote_copy(
            src_ref=src,
            dst_ref=dst,
            send_sem=line_send.at[0 if up else 1, m * wt + p],
            recv_sem=line_recv.at[m * wt + p],
            device_id=(s, target),
            device_id_type=MESH,
        )

    def nth_plane(j):
        below, above = w, wt - 1 - w
        both = jnp.minimum(below, above)
        in_turn = j < 2 * both
        dist = jnp.where(in_turn, j // 2 + 1, j - both + 1)
        from_below = jnp.where(in_turn, j % 2 == 0, below > above)
        return jnp.where(from_below, w - dist, w + dist)

    def weight_spread(m, p):
        def region(ux, uy, whose, half):
            return unit_rows(m, p, (uy * geo.nx + ux) * 2 + whose, half)

        return Spread(geo, here, region, send_sem, recv_sem, 1 + m * wt + p)

    units = [(m, j) for m in range(weight_count) for j in range(wt - 1)]

    def start_lines():
        for m in range(weight_count):
            @pl.when(w < wt - 1)
            def _():
                line_copy(m, w, True, True).start()

            @pl.when(w > 0)
            def _():
                line_copy(m, w, False, True).start()

    def tick(i):
        if 0 <= i < len(units):
            m, j = units[i]
            p = nth_plane(j)
            line_copy(m, p, True, False).wait_recv()

            @pl.when((p < w) & (w < wt - 1))
            def _():
                line_copy(m, p, True, False).start()

            @pl.when((p > w) & (w > 0))
            def _():
                line_copy(m, p, False, False).start()

            spread = weight_spread(m, p)
            spread.go(0)
            spread.go(1)
            spread.go(4)
        if 0 <= i - 1 < len(units):
            m, j = units[i - 1]
            spread = weight_spread(m, nth_plane(j))
            spread.wait(0)
            spread.go(2)
            spread.go(5)
            spread.wait(1)
            spread.go(3)
            spread.go(6)
        if 0 <= i - 2 < len(units):
            m, j = units[i - 2]
            spread = weight_spread(m, nth_plane(j))
            spread.wait(2)
            spread.go(7)
            spread.wait(3)
            spread.go(8)

    tick_count = len(units) + 2 if units else 0

    nx, ny = geo.nx, geo.ny
    row_n, col_n, diag_n = 2 * (nx - 1), 2 * (ny - 1), 2 * (nx - 1) * (ny - 1)

    def block_owner(i):
        r = i - 2
        c = r - row_n
        d = c - col_n
        dx_row, k_row = r % max(nx - 1, 1) + 1, r // max(nx - 1, 1)
        dy_col, k_col = c % max(ny - 1, 1) + 1, c // max(ny - 1, 1)
        half = max(diag_n // 2, 1)
        k_diag, in_diag = d // half, d % half
        dx_diag, dy_diag = in_diag % max(nx - 1, 1) + 1, in_diag // max(nx - 1, 1) + 1
        dx = jnp.where(i < 2, 0, jnp.where(i < 2 + row_n, dx_row, jnp.where(i < 2 + row_n + col_n, 0, dx_diag)))
        dy = jnp.where(i < 2 + row_n, 0, jnp.where(i < 2 + row_n + col_n, dy_col, dy_diag))
        kk = jnp.where(i < 2, i, jnp.where(i < 2 + row_n, k_row, jnp.where(i < 2 + row_n + col_n, k_col, k_diag)))
        return (((y + dy) % ny) * nx + (x + dx) % nx) * 2 + (core + kk) % 2

    def project(i, carry):
        @pl.when(i == 0)
        def _():
            own_tok.wait()
            for copy in own_slices:
                copy.wait()
            for d in range(1, wt):
                for j in range(3):
                    slice_arrival(j, d).wait_recv()
            start_lines()

        @pl.when(i == 1)
        def _():
            tok.wait(4)

        @pl.when(i == 2)
        def _():
            tok.wait(0)
            tok.go(2)
            tok.go(5)
            tok.wait(1)
            tok.go(3)
            tok.go(6)

        @pl.when(i == 2 + row_n // 2)
        def _():
            tok.wait(5)

        @pl.when(i == 2 + row_n + col_n // 2)
        def _():
            tok.wait(6)

        @pl.when(i == 2 + row_n + col_n)
        def _():
            tok.wait(2)
            tok.go(7)
            tok.wait(3)
            tok.go(8)

        @pl.when(i == 2 + row_n + col_n + diag_n // 2)
        def _():
            tok.wait(7)
            tok.wait(8)

        t = block_owner(i)
        block = tok_buf[t]
        at = pl.ds(pl.multiple_of(t * rows, rows), rows)
        pos = t * rows + lax.broadcasted_iota(jnp.int32, (rows, LANES), 0)
        chosen = select_from(pos, starts, ends, id_ref, rank)
        main = dot_nn(block, slice_ref[...])
        small = dot_nt(block, down_ref[...])
        for j in range(3):
            cut = slice(j * LANES, (j + 1) * LANES)
            low = (small[:, cut] * chosen).astype(BF16)
            small_ref[at, cut] = low
            value = main[:, cut] + dot_nn(low, up_ref[cut, lanes])
            if j == 0:
                value = value + bias_ref[0:1, lanes]

                @pl.when(t // geo.groups == part)
                def _():
                    inner = pl.ds(pl.multiple_of((t % geo.groups) * rows, rows), rows)
                    q_ref[inner, :] = value.astype(BF16)
            elif j == 1:
                k_ref[at, :] = value.astype(BF16)
            else:
                v_ref[at, :] = (value + bias_ref[1:2, lanes]).astype(BF16)
        return carry

    lax.fori_loop(0, geo.seq, project, 0)

    scale = HEAD_DIM ** (-0.5)
    chunk = min(2048, geo.keys)
    chunks = geo.keys // chunk
    first_head = lax.broadcasted_iota(jnp.int32, (rows, LANES), 1) < HEAD_DIM

    def att_copy(b):
        return pltpu.make_async_remote_copy(
            src_ref=att_buf.at[b],
            dst_ref=att_ref.at[:, lanes],
            send_sem=att_send.at[b],
            recv_sem=att_recv.at[g],
            device_id=(part * geo.groups + b, w),
            device_id_type=MESH,
        )

    def attend(i, carry):
        for n in range(min(tick_count, geo.groups)):
            @pl.when(i == n)
            def _():
                tick(n)

        b = (g + 1 + i) % geo.groups
        inner = pl.ds(pl.multiple_of(b * rows, rows), rows)
        query = q_ref[inner, :] * jnp.asarray(scale, BF16)
        q_pos = (part * geo.groups + b) * rows + lax.broadcasted_iota(jnp.int32, (rows, 1), 0)
        q_seg = segment_from(q_pos, starts)
        results = []
        for h in range(PAIR):
            mask = first_head if h == 0 else jnp.logical_not(first_head)
            q_head = jnp.where(mask, query, jnp.zeros_like(query))

            def one(c, state):
                top, total, acc = state
                keys_at = pl.ds(pl.multiple_of(c * chunk, chunk), chunk)
                score = dot_nt(q_head, k_ref[keys_at, :])
                score = jnp.where(q_seg == seg_buf[:, keys_at], score, -1e30)
                peak = jnp.max(score, axis=1, keepdims=True)
                if top is not None:
                    peak = jnp.maximum(top, peak)
                weight = jnp.exp(score - peak)
                add = jnp.sum(weight, axis=1, keepdims=True)
                out = dot_nn(weight.astype(BF16), v_ref[keys_at, :])
                if top is not None:
                    fade = jnp.exp(top - peak)
                    add = add + total * fade
                    out = out + acc * fade
                return peak, add, out

            state = one(0, (None, None, None))
            if chunks > 1:
                state = lax.fori_loop(1, chunks, one, state)
            top, total, acc = state
            results.append((acc / total, top + jnp.log(total)))
        out = jnp.where(first_head, results[0][0], results[1][0])
        o_ref[inner, :] = out
        lse_ref[inner, :] = jnp.where(first_head, results[0][1], results[1][1])
        att_buf[b] = out.astype(BF16)

        @pl.when(b != g)
        def _():
            att_copy(b).start()

        return carry

    lax.fori_loop(0, geo.groups, attend, 0)
    own_att = pltpu.make_async_copy(att_buf.at[g], att_ref.at[:, lanes], local_sem.at[0])
    own_att.start()

    for n in range(geo.groups, tick_count):
        tick(n)

    for d in range(1, geo.groups):
        other = (g + d) % geo.groups
        cut = pl.ds(pl.multiple_of(other * LANES, LANES), LANES)
        pltpu.make_async_remote_copy(
            src_ref=att_ref.at[:, cut],
            dst_ref=att_ref.at[:, cut],
            send_sem=att_send.at[other],
            recv_sem=att_recv.at[other],
            device_id=(part * geo.groups + other, w),
            device_id_type=MESH,
        ).wait_recv()
        att_copy(other).wait_send()
    own_att.wait()
    tok.wait_sends()
    for d in range(1, wt):
        for j in range(3):
            slice_copy(j, d).wait_send()
    for m in range(weight_count):
        own_weights[m].wait()

        @pl.when(w < wt - 1)
        def _():
            line_copy(m, w, True, True).wait_send()

        @pl.when(w > 0)
        def _():
            line_copy(m, w, False, True).wait_send()

    for m, j in units:
        p = nth_plane(j)

        @pl.when((p < w) & (w < wt - 1))
        def _():
            line_copy(m, p, True, False).wait_send()

        @pl.when((p > w) & (w > 0))
        def _():
            line_copy(m, p, False, False).wait_send()

        spread = weight_spread(m, p)
        for kind in range(4, 9):
            spread.wait(kind)
        spread.wait_sends()


def forward_attention(geo, rank, lengths, ids, tokens, w_qkv, down, up, bias, weights):
    rows, width = geo.rows, geo.width
    count = len(weights)
    any_spec = pl.BlockSpec(memory_space=pl.ANY)
    vmem = pl.BlockSpec(memory_space=pltpu.VMEM)
    smem = pl.BlockSpec(memory_space=pltpu.SMEM)
    shapes = [
        jax.ShapeDtypeStruct((rows, width), BF16),
        jax.ShapeDtypeStruct((geo.queries, LANES), BF16),
        jax.ShapeDtypeStruct((geo.keys, LANES), BF16),
        jax.ShapeDtypeStruct((geo.keys, LANES), BF16),
        jax.ShapeDtypeStruct((geo.queries, LANES), F32),
        jax.ShapeDtypeStruct((geo.queries, LANES), F32),
        jax.ShapeDtypeStruct((width, 3 * LANES), BF16),
        jax.ShapeDtypeStruct((geo.keys, 3 * LANES), BF16),
    ] + [jax.ShapeDtypeStruct((v.shape[0] * geo.wt, v.shape[1]), BF16) for v in weights]
    units = 1 + count * geo.wt
    dma = pltpu.SemaphoreType.DMA
    results = pl.pallas_call(
        functools.partial(forward_kernel, geo, count, rank),
        out_shape=shapes,
        in_specs=[smem, smem, any_spec, any_spec, vmem, vmem, vmem] + [any_spec] * count,
        out_specs=[any_spec] + [vmem] * 7 + [any_spec] * count,
        scratch_shapes=[
            pltpu.VMEM((geo.seq, rows, width), BF16),
            pltpu.VMEM((1, geo.keys), jnp.int32),
            pltpu.VMEM((geo.groups, rows, LANES), BF16),
            dma((4 + count,)),
            dma((Spread.KINDS, units)),
            dma((Spread.KINDS, units)),
            dma((3, geo.wt)),
            dma((3, geo.wt)),
            dma((2, max(count, 1) * geo.wt)),
            dma((max(count, 1) * geo.wt,)),
            dma((geo.groups,)),
            dma((geo.groups,)),
        ],
        compiler_params=pltpu.CompilerParams(
            collective_id=0, has_side_effects=True, vmem_limit_bytes=VMEM_LIMIT
        ),
        name="gather_attend",
    )(lengths, ids, tokens, w_qkv, down, up, bias, *weights)
    return results[:8], results[8:]


def backward_kernel(geo, len_ref, part_ref, q_ref, k_ref, v_ref, o_ref, lse_ref, g_ref, dq_ref, dk_ref, dv_ref, dk_acc, dv_acc):
    rows = geo.rows
    part = part_ref[0, 0]
    scale = HEAD_DIM ** (-0.5)
    starts, ends = doc_bounds(len_ref)
    first_head = lax.broadcasted_iota(jnp.int32, (rows, LANES), 1) < HEAD_DIM
    dk_acc[...] = jnp.zeros_like(dk_acc)
    dv_acc[...] = jnp.zeros_like(dv_acc)

    def seg_of(position):
        seg = jnp.int32(0)
        for start in starts[1:]:
            seg = seg + (position >= start).astype(jnp.int32)
        return seg

    def pick(values, index):
        found = values[0]
        for i in range(1, len(values)):
            found = jnp.where(index == i, values[i], found)
        return found

    def query_block(b, carry):
        at = pl.ds(pl.multiple_of(b * rows, rows), rows)
        origin = (part * geo.groups + b) * rows
        query = q_ref[at, :] * jnp.asarray(scale, BF16)
        cot = g_ref[at, :]
        lse = lse_ref[at, :]
        both = cot.astype(F32) * o_ref[at, :]
        q_pos = origin + lax.broadcasted_iota(jnp.int32, (rows, 1), 0)
        q_seg = segment_from(q_pos, starts)
        heads = []
        for h in range(PAIR):
            mask = first_head if h == 0 else jnp.logical_not(first_head)
            zero = jnp.zeros_like(query)
            heads.append(
                (
                    jnp.where(mask, query, zero),
                    jnp.where(mask, cot, zero),
                    lse[:, h * HEAD_DIM : h * HEAD_DIM + 1],
                    jnp.sum(jnp.where(mask, both, 0.0), axis=1, keepdims=True),
                )
            )
        low = pick(starts, seg_of(origin)) // rows
        high = (pick(ends, seg_of(origin + rows - 1)) + rows - 1) // rows

        def key_block(c, accs):
            keys_at = pl.ds(pl.multiple_of(c * rows, rows), rows)
            key, value = k_ref[keys_at, :], v_ref[keys_at, :]
            k_pos = c * rows + lax.broadcasted_iota(jnp.int32, (1, rows), 1)
            same = q_seg == segment_from(k_pos, starts)
            new = []
            dk_parts, dv_parts = [], []
            for h in range(PAIR):
                q_head, g_head, lse_head, dot_head = heads[h]
                score = jnp.where(same, dot_nt(q_head, key), -1e30)
                prob = jnp.exp(score - lse_head)
                d_prob = dot_nt(g_head, value)
                raw = (prob * (d_prob - dot_head) * scale).astype(BF16)
                new.append(accs[h] + dot_nn(raw, key))
                dk_parts.append(dot_tn(raw, q_head))
                dv_parts.append(dot_tn(prob.astype(BF16), g_head))
            dk_acc[keys_at, :] += dk_parts[0] + dk_parts[1]
            dv_acc[keys_at, :] += dv_parts[0] + dv_parts[1]
            return tuple(new)

        zero = jnp.zeros((rows, LANES), F32)
        accs = lax.fori_loop(low, high, key_block, (zero, zero))
        dq_ref[at, :] = jnp.where(first_head, accs[0], accs[1]).astype(BF16)
        return carry

    lax.fori_loop(0, geo.groups, query_block, 0)
    dk_ref[...] = (dk_acc[...] * HEAD_DIM**0.5).astype(BF16)
    dv_ref[...] = dv_acc[...].astype(BF16)


def backward_attention(geo, lengths, part, q, k, v, o, lse, d_heads):
    smem = pl.BlockSpec(memory_space=pltpu.SMEM)
    vmem = pl.BlockSpec(memory_space=pltpu.VMEM)
    return pl.pallas_call(
        functools.partial(backward_kernel, geo),
        out_shape=[
            jax.ShapeDtypeStruct((geo.queries, LANES), BF16),
            jax.ShapeDtypeStruct((geo.keys, LANES), BF16),
            jax.ShapeDtypeStruct((geo.keys, LANES), BF16),
        ],
        in_specs=[smem, smem] + [vmem] * 6,
        out_specs=[vmem] * 3,
        scratch_shapes=[pltpu.VMEM((geo.keys, LANES), F32)] * 2,
        compiler_params=pltpu.CompilerParams(vmem_limit_bytes=VMEM_LIMIT),
        name="attend_back",
    )(lengths, part, q, k, v, o, lse, d_heads)


class Block:
    def __init__(self, geo):
        chips = geo.groups // 2
        self.nx = min(geo.nx, chips)
        self.ny = chips // self.nx


class PairSum:
    def __init__(self, count, me, core, first, w, bufs, sems, make, stage=None):
        self.count, self.me, self.core, self.first, self.w = count, me, core, first, w
        self.near_out, self.near_in, self.far_in = bufs
        self.near_send, self.near_recv, self.far_send, self.far_recv = sems
        self.make = make
        self.slots = self.near_out.shape[0]
        self.stage = stage

    def slot(self, chip):
        return ((chip + self.count - self.me + self.count - 1) % self.count) % self.slots

    def near(self, chip):
        return pltpu.make_async_remote_copy(
            src_ref=self.near_out.at[self.slot(chip)],
            dst_ref=self.near_in.at[chip],
            send_sem=self.near_send.at[chip],
            recv_sem=self.near_recv.at[chip],
            device_id=(self.first + self.me * 2 + 1 - self.core, self.w),
            device_id_type=MESH,
        )

    def far(self, chip):
        return pltpu.make_async_remote_copy(
            src_ref=self.near_in.at[chip],
            dst_ref=self.far_in.at[self.me],
            send_sem=self.far_send.at[chip],
            recv_sem=self.far_recv.at[self.me],
            device_id=(self.first + chip * 2 + self.core, self.w),
            device_id_type=MESH,
        )

    def far_arrival(self, chip):
        return pltpu.make_async_remote_copy(
            src_ref=self.far_in.at[chip],
            dst_ref=self.far_in.at[chip],
            send_sem=self.far_send.at[chip],
            recv_sem=self.far_recv.at[chip],
            device_id=(self.first + chip * 2 + self.core, self.w),
            device_id_type=MESH,
        )

    def start(self):
        def step(d, carry):
            chip = (self.me + 1 + d) % self.count
            if self.slots < self.count:

                @pl.when(d >= self.slots)
                def _():
                    self.near((self.me + 1 + d - self.slots) % self.count).wait_send()

            self.near_out[d % self.slots] = self.make(chip, 1 - self.core).astype(BF16)
            self.near(chip).start()
            return carry

        lax.fori_loop(0, self.count, step, 0)

    def send(self):
        def step(d, carry):
            chip = (self.me + 1 + d) % self.count
            own = self.make(chip, self.core)
            self.near(chip).wait_recv()
            self.near_in[chip] = (own + self.near_in[chip].astype(F32)).astype(BF16)
            self.far(chip).start()
            return carry

        lax.fori_loop(0, self.count - 1, step, 0)

    def finish(self):
        total = self.make(self.me, self.core)
        self.near(self.me).wait_recv()
        total = total + self.near_in[self.me].astype(F32)
        if self.stage is None:
            for d in range(1, self.count):
                chip = (self.me + d) % self.count
                self.far_arrival(chip).wait_recv()
                total = total + self.far_in[chip].astype(F32)
            return total
        stage, sem = self.stage

        def fetch(d):
            chip = (self.me + d) % self.count
            return pltpu.make_async_copy(self.far_in.at[chip], stage.at[d % 2], sem.at[d % 2])

        self.far_arrival((self.me + 1) % self.count).wait_recv()
        fetch(1).start()
        for d in range(1, self.count):
            if d + 1 < self.count:
                self.far_arrival((self.me + d + 1) % self.count).wait_recv()
                fetch(d + 1).start()
            fetch(d).wait()
            total = total + stage[d % 2].astype(F32)
        return total

    def drain(self):
        for d in range(self.count):
            chip = (self.me + 1 + d) % self.count
            if d >= self.count - self.slots:
                self.near(chip).wait_send()
            if d < self.count - 1:
                self.far(chip).wait_send()


def closing_kernel(
    geo,
    rank,
    len_ref,
    id_ref,
    tokens_ref,
    first_ref,
    dq_ref,
    dk_ref,
    dv_ref,
    slice_ref,
    down_ref,
    up_ref,
    small_ref,
    out_down_ref,
    out_up_ref,
    fc1_down_ref,
    fc2_up_ref,
    fc1_up_ref,
    fc2_down_ref,
    grad_ref,
    sum1_ref,
    sum2_ref,
    tok_far,
    tok_out,
    tok_in,
    tok_stage,
    small_buf,
    set1_out,
    set1_in,
    set1_far,
    set2_out,
    set2_in,
    set2_far,
    down_acc,
    up_acc,
    mine1,
    mine2,
    place_buf,
    fold_buf,
    all1,
    all2,
    places,
    done1,
    done2,
    tok_sems,
    set1_sems,
    set2_sems,
    line_send,
    line_recv,
    spread_send,
    spread_recv,
    local_sem,
    stage_sem,
    small_sem,
):
    x, y, core, w = device_here(geo)
    s = lax.axis_index("seq")
    rows, width, wt, groups, parts = geo.rows, geo.width, geo.wt, geo.groups, geo.parts
    part, g = s // groups, s % groups
    docs = len_ref.shape[1]
    doc_rows = docs * rank
    lane_count = down_ref.shape[0] // 3
    lanes = pl.ds(pl.multiple_of(g * LANES, LANES), LANES)
    starts, ends = doc_bounds(len_ref)
    ids = [id_ref[0, d] for d in range(docs)]
    fresh = []
    for d in range(docs):
        seen = jnp.bool_(False)
        for e in range(d):
            seen = seen | (ids[e] == ids[d])
        fresh.append(jnp.where(seen, 0.0, 1.0))

    greet_all(geo)

    def iota(shape, dim):
        return lax.broadcasted_iota(jnp.int32, shape, dim)

    def zero_one(condition):
        return jnp.where(condition, 1.0, 0.0).astype(BF16)

    def chosen_of(t):
        pos = t * rows + iota((rows, LANES), 0)
        return select_from(pos, starts, ends, id_ref, rank)

    def fold(j):
        a, b = iota((lane_count, LANES), 0), iota((lane_count, LANES), 1)
        return zero_one((b >= j * rank) & (b < (j + 1) * rank) & (a % rank == b - j * rank))

    def make_tokens(chip, whose):
        t = chip * 2 + whose
        at = pl.ds(pl.multiple_of(t * rows, rows), rows)
        if parts == 1:
            d_q = dq_ref[at, :]
        else:
            inner = pl.ds(pl.multiple_of((t % groups) * rows, rows), rows)
            d_q = jnp.where(t // groups == part, dq_ref[inner, :], jnp.zeros((rows, LANES), BF16))
        pieces = [d_q, dk_ref[at, :], dv_ref[at, :]]
        chosen = chosen_of(t)
        total = jnp.zeros((rows, width), F32)
        low = jnp.zeros((rows, LANES), F32)
        for j in range(3):
            total = total + dot_nt(pieces[j], slice_ref[:, j * LANES : (j + 1) * LANES])
            part_low = dot_nt(pieces[j], up_ref[pl.ds(j * lane_count, lane_count), lanes])
            low = low + dot_nn((part_low * chosen).astype(BF16), fold(j))
        return jnp.concatenate([total, low], axis=1)

    tok = PairSum(
        geo.seq // 2, s // 2, core, 0, w, (tok_out, tok_in, tok_far), [tok_sems.at[i] for i in range(4)], make_tokens,
        (tok_stage, stage_sem),
    )

    singles = [out_down_ref, out_up_ref, fc1_down_ref, fc2_up_ref, fc1_up_ref, fc2_down_ref]

    def by_document(value):
        return dot_tn(fold_buf[...], value)[:doc_rows]

    def make_set1(chip, whose):
        owner = chip * 2 + whose
        cols = []
        for ref in singles:
            wide = ref.shape[1] // groups
            cols.append(by_document(ref[:, pl.ds(pl.multiple_of(owner * wide, LANES), wide)]))
        return jnp.concatenate(cols, axis=1)

    def make_set2(chip, whose):
        owner = chip * 2 + whose
        cut = pl.ds(pl.multiple_of(owner * LANES, LANES), LANES)
        return jnp.concatenate([down_acc[j * doc_rows : (j + 1) * doc_rows, cut] for j in range(3)], axis=1)

    chips = groups // 2
    set1 = PairSum(
        chips, g // 2, core, part * groups, w, (set1_out, set1_in, set1_far), [set1_sems.at[i] for i in range(4)], make_set1
    )
    set2 = PairSum(
        chips, g // 2, core, part * groups, w, (set2_out, set2_in, set2_far), [set2_sems.at[i] for i in range(4)], make_set2
    )

    def peer(n):
        plane = (w + n) % wt
        other = (part + n // wt) % parts
        return other * groups + g, plane, other * wt + plane

    mine_at = part * wt + w

    def line_copy(kind, n, src, dst_all):
        device, plane, _ = peer(n)
        return pltpu.make_async_remote_copy(
            src_ref=src,
            dst_ref=dst_all.at[mine_at],
            send_sem=line_send.at[kind, n],
            recv_sem=line_recv.at[kind, mine_at],
            device_id=(device, plane),
            device_id_type=MESH,
        )

    def line_arrival(kind, n, dst_all):
        device, plane, at = peer(n)
        return pltpu.make_async_remote_copy(
            src_ref=dst_all.at[at],
            dst_ref=dst_all.at[at],
            send_sem=line_send.at[kind, n],
            recv_sem=line_recv.at[kind, at],
            device_id=(device, plane),
            device_id_type=MESH,
        )

    peers = range(1, wt * parts)

    block = Block(geo)
    chip_here = g // 2
    here = (chip_here % block.nx, chip_here // block.nx, core, w)

    def region_of(ref):
        def region(ux, uy, whose, half):
            one = ref.at[(uy * block.nx + ux) * 2 + whose]
            if half is None:
                return one
            return one.at[pl.ds(half * (lane_count // 2), lane_count // 2)]

        return region

    spreads = [
        Spread(block, here, region_of(ref), spread_send, spread_recv, i, part * groups)
        for i, ref in enumerate((sum1_ref, sum2_ref))
    ]
    finals = [done1, done2]
    outs = [sum1_ref, sum2_ref]

    def place(kind, mine, dst_all):
        total = dot_nn(place_buf[:, :doc_rows], mine[...])
        for n in peers:
            line_arrival(kind, n, dst_all).wait_recv()
            if kind == 0:
                line_arrival(2, n, places).wait_recv()
            at = peer(n)[2]
            total = total + dot_nn(places[at][:, :doc_rows], dst_all[at])
        finals[kind][...] = total.astype(BF16)
        for way in (0, 1, 4):
            spreads[kind].go(way, own=finals[kind])
        pltpu.make_async_copy(finals[kind], outs[kind].at[g], local_sem.at[kind]).start()

    def pass_on(kind):
        spread = spreads[kind]
        spread.wait(0)
        spread.go(2)
        spread.go(5)
        spread.wait(1)
        spread.go(3)
        spread.go(6)

    def pass_last(kind):
        spread = spreads[kind]
        spread.wait(2)
        spread.go(7)
        spread.wait(3)
        spread.go(8)

    a, b = iota((lane_count, LANES), 0), iota((lane_count, LANES), 1)
    places_all = jnp.zeros((lane_count, LANES), F32)
    places_first = jnp.zeros((lane_count, LANES), F32)
    for d in range(docs):
        hit = (a // rank == ids[d]) & (b // rank == d) & (a % rank == b % rank)
        places_all = jnp.where(hit, 1.0, places_all)
        places_first = jnp.where(hit, fresh[d], places_first)
    place_buf[...] = places_all.astype(BF16)
    fold_buf[...] = places_first.astype(BF16)
    for n in peers:
        line_copy(2, n, place_buf, places).start()

    set1.start()
    tok.start()
    set1.send()
    tok.send()

    def small_copy(t):
        return pltpu.make_async_copy(
            small_ref.at[pl.ds(pl.multiple_of(t * rows, rows), rows)], small_buf.at[t % 2], small_sem.at[t % 2]
        )

    def add_up(t, carry):
        at = pl.ds(pl.multiple_of(t * rows, rows), rows)

        @pl.when(t + 1 < geo.seq)
        def _():
            small_copy(t + 1).start()

        small_copy(t).wait()
        for j in range(3):
            cut = slice(j * LANES, (j + 1) * LANES)
            if j == 0:
                if parts == 1:
                    value = dq_ref[at, :]
                else:
                    inner = pl.ds(pl.multiple_of((t % groups) * rows, rows), rows)
                    value = jnp.where(t // groups == part, dq_ref[inner, :], jnp.zeros((rows, LANES), BF16))
            else:
                value = (dk_ref if j == 1 else dv_ref)[at, :]
            up_acc[cut, :] += dot_tn(small_buf[t % 2][:, cut], value)
        return carry

    up_acc[...] = jnp.zeros_like(up_acc)
    small_copy(0).start()
    lax.fori_loop(0, geo.seq, add_up, 0)

    mine1[...] = set1.finish().astype(BF16)
    for n in peers:
        line_copy(0, n, mine1, all1).start()

    total = tok.finish()
    low = total[:, width:].astype(BF16)
    total = total[:, :width] + first_ref[...]
    chosen = chosen_of(s)
    pos = s * rows + iota((rows, doc_rows), 0)
    doc_of = iota((rows, doc_rows), 1) // rank
    in_doc = doc_of == segment_from(pos, starts)
    tokens = tokens_ref[...]
    for j in range(3):
        a, b = iota((LANES, lane_count), 0), iota((LANES, lane_count), 1)
        widen = zero_one((a >= j * rank) & (a < (j + 1) * rank) & (b % rank == a - j * rank))
        wide = (dot_nn(low, widen) * chosen).astype(BF16)
        total = total + dot_nn(wide, down_ref[j * lane_count : (j + 1) * lane_count, :])
        by_doc = dot_nn(low, widen[:, :doc_rows])
        by_doc = jnp.where(in_doc, by_doc, 0.0).astype(BF16)
        down_acc[j * doc_rows : (j + 1) * doc_rows, :] = dot_tn(by_doc, tokens)
    set2.start()
    grad_ref[...] = total
    set2.send()
    place(0, mine1, all1)
    for j in range(3):
        mine2[:, (3 + j) * LANES : (4 + j) * LANES] = by_document(
            up_acc[j * lane_count : (j + 1) * lane_count, :].astype(BF16)
        ).astype(BF16)
    mine2[:, : 3 * LANES] = set2.finish().astype(BF16)
    for n in peers:
        line_copy(1, n, mine2, all2).start()
    pass_on(0)
    pass_last(0)
    place(1, mine2, all2)
    pass_on(1)
    pass_last(1)
    for kind in range(2):
        for way in range(4, 9):
            spreads[kind].wait(way)
        spreads[kind].wait_sends()
        pltpu.make_async_copy(finals[kind], outs[kind].at[g], local_sem.at[kind]).wait()
    for n in peers:
        line_copy(0, n, mine1, all1).wait_send()
        line_copy(1, n, mine2, all2).wait_send()
        line_copy(2, n, place_buf, places).wait_send()
    tok.drain()
    set1.drain()
    set2.drain()


def greet_all(geo):
    s, w = lax.axis_index("seq"), lax.axis_index("wt")
    barrier = pltpu.get_barrier_semaphore()
    part, g = s // geo.groups, s % geo.groups
    for d in range(1, geo.seq):
        pl.semaphore_signal(barrier, inc=1, device_id=((s + d) % geo.seq, w), device_id_type=MESH)
    count = geo.seq - 1
    for d in range(1, geo.wt):
        for q in range(geo.parts):
            other = ((part + q) % geo.parts) * geo.groups + g
            pl.semaphore_signal(barrier, inc=1, device_id=(other, (w + d) % geo.wt), device_id_type=MESH)
            count += 1
    pl.semaphore_wait(barrier, count)


def closing(geo, rank, lengths, ids, tokens, d_first, dq, dk, dv, w_slice, down, up, small, grads):
    rows, width = geo.rows, geo.width
    docs = lengths.shape[1]
    doc_rows = docs * rank
    lane_count = down.shape[0] // 3
    set1 = sum(v.shape[1] for v in grads) // geo.groups
    set2 = 6 * LANES
    chips, near = geo.seq // 2, geo.groups // 2
    peers = geo.wt * geo.parts
    smem = pl.BlockSpec(memory_space=pltpu.SMEM)
    vmem = pl.BlockSpec(memory_space=pltpu.VMEM)
    any_spec = pl.BlockSpec(memory_space=pl.ANY)
    dma = pltpu.SemaphoreType.DMA
    wide = width + LANES
    return pl.pallas_call(
        functools.partial(closing_kernel, geo, rank),
        out_shape=[
            jax.ShapeDtypeStruct((rows, width), F32),
            jax.ShapeDtypeStruct((geo.groups, lane_count, set1), BF16),
            jax.ShapeDtypeStruct((geo.groups, lane_count, set2), BF16),
            jax.ShapeDtypeStruct((chips, rows, wide), BF16),
        ],
        in_specs=[smem, smem] + [vmem] * 8 + [any_spec] + [vmem] * len(grads),
        out_specs=[vmem, any_spec, any_spec, any_spec],
        scratch_shapes=[
            pltpu.VMEM((min(chips, 4), rows, wide), BF16),
            pltpu.VMEM((chips, rows, wide), BF16),
            pltpu.VMEM((2, rows, wide), BF16),
            pltpu.VMEM((2, rows, 3 * lane_count), BF16),
            pltpu.VMEM((near, doc_rows, set1), BF16),
            pltpu.VMEM((near, doc_rows, set1), BF16),
            pltpu.VMEM((near, doc_rows, set1), BF16),
            pltpu.VMEM((near, doc_rows, 3 * LANES), BF16),
            pltpu.VMEM((near, doc_rows, 3 * LANES), BF16),
            pltpu.VMEM((near, doc_rows, 3 * LANES), BF16),
            pltpu.VMEM((3 * doc_rows, width), F32),
            pltpu.VMEM((3 * lane_count, LANES), F32),
            pltpu.VMEM((doc_rows, set1), BF16),
            pltpu.VMEM((doc_rows, set2), BF16),
            pltpu.VMEM((lane_count, LANES), BF16),
            pltpu.VMEM((lane_count, LANES), BF16),
            pltpu.VMEM((peers, doc_rows, set1), BF16),
            pltpu.VMEM((peers, doc_rows, set2), BF16),
            pltpu.VMEM((peers, lane_count, LANES), BF16),
            pltpu.VMEM((lane_count, set1), BF16),
            pltpu.VMEM((lane_count, set2), BF16),
            dma((4, chips)),
            dma((4, near)),
            dma((4, near)),
            dma((3, peers)),
            dma((3, peers)),
            dma((Spread.KINDS, 2)),
            dma((Spread.KINDS, 2)),
            dma((2,)),
            dma((2,)),
            dma((2,)),
        ],
        compiler_params=pltpu.CompilerParams(
            collective_id=1, has_side_effects=True, vmem_limit_bytes=VMEM_LIMIT
        ),
        name="close",
    )(lengths, ids, tokens, d_first, dq, dk, dv, w_slice, down, up, small, *grads)


def unpack_kernel(one_ref, two_ref, down_ref, up_ref, fc1_down_ref, fc2_up_ref, fc1_up_ref, fc2_down_ref):
    for j in range(3):
        down_ref[j] = two_ref[0, :, j * LANES : (j + 1) * LANES].astype(F32)
        up_ref[j] = two_ref[0, :, (3 + j) * LANES : (4 + j) * LANES].astype(F32)
    at = 0
    for ref in (down_ref.at[3], up_ref.at[3], fc1_down_ref, fc2_up_ref, fc1_up_ref, fc2_down_ref):
        wide = ref.shape[1]
        ref[...] = one_ref[0, :, at : at + wide].astype(F32)
        at += wide


def unpack(geo, one, two, lane_count):
    groups = geo.groups
    thick = (one.shape[2] - 4 * LANES) // 2

    def whole(wide):
        return jax.ShapeDtypeStruct((lane_count, wide * groups), F32)

    def flat(wide):
        return pl.BlockSpec((lane_count, wide), lambda i: (0, i))

    four = jax.ShapeDtypeStruct((4, lane_count, LANES * groups), F32)
    four_spec = pl.BlockSpec((4, lane_count, LANES), lambda i: (0, 0, i))
    return pl.pallas_call(
        unpack_kernel,
        grid=(groups,),
        out_shape=[four, four, whole(LANES), whole(LANES), whole(thick), whole(thick)],
        in_specs=[
            pl.BlockSpec((1,) + one.shape[1:], lambda i: (i, 0, 0)),
            pl.BlockSpec((1,) + two.shape[1:], lambda i: (i, 0, 0)),
        ],
        out_specs=[four_spec, four_spec, flat(LANES), flat(LANES), flat(thick), flat(thick)],
        compiler_params=pltpu.CompilerParams(vmem_limit_bytes=VMEM_LIMIT // 2),
        name="unpack",
    )(one, two)


def layer_norm(value, gain, shift):
    mean = jnp.mean(value, axis=-1, keepdims=True)
    centred = value - mean
    spread = jnp.mean(centred * centred, axis=-1, keepdims=True)
    return centred * lax.rsqrt(spread + 1e-05) * gain + shift


def gelu_exact(value):
    return jax.nn.gelu(value, approximate=False)


def times_transposed(grad, weight):
    return lax.dot_general(
        grad, weight, (((1,), (1,)), ((), ())), preferred_element_type=jnp.float32
    )


def left_inner(left, right):
    return lax.dot_general(
        left, right, (((0,), (0,)), ((), ())), preferred_element_type=jnp.float32
    )


def stack_down(down):
    return jnp.transpose(down, (1, 0, 2)).reshape(down.shape[1], down.shape[0] * down.shape[2])


def stack_up(up):
    return up.reshape(up.shape[0] * up.shape[1], up.shape[2])


def unstack_down(stacked, adapter_count, rank_size):
    return jnp.transpose(stacked.reshape(stacked.shape[0], adapter_count, rank_size), (1, 0, 2))


def unstack_up(stacked, adapter_count, rank_size):
    return stacked.reshape(adapter_count, rank_size, stacked.shape[1])


def segment_of(positions, starts):
    return jnp.sum((positions[:, None] >= starts[None, :]).astype(jnp.int32), axis=1) - 1


def shards(
    tokens,
    cotangent,
    w_qkv,
    qv_bias,
    w_out,
    out_bias,
    norm1_gain,
    norm1_bias,
    w_fc1,
    fc1_bias,
    w_fc2,
    fc2_bias,
    norm2_gain,
    norm2_bias,
    doc_lengths,
    adapter_ids,
    attn_down,
    attn_up,
    fc1_down,
    fc1_up,
    fc2_down,
    fc2_up,
):
    tok_rows, model_width = tokens.shape
    adapter_count = attn_down.shape[1]
    rank_size = attn_down.shape[3]
    lane_count = adapter_count * rank_size
    seq_count = lax.axis_size("seq")
    geo = Geometry(tok_rows, model_width)
    seq_index = lax.axis_index("seq")
    part_index = seq_index // geo.groups
    head_index = seq_index % geo.groups
    lengths = doc_lengths[0]
    starts = jnp.cumsum(lengths) - lengths
    local_pos = seq_index * tok_rows + jnp.arange(tok_rows, dtype=jnp.int32)
    local_seg = segment_of(local_pos, starts)
    doc_range = jnp.arange(lengths.shape[0], dtype=jnp.int32)
    chosen = jnp.sum(
        jnp.where(local_seg[:, None] == doc_range[None, :], adapter_ids[0][None, :], 0), axis=1
    )
    lane_owner = jnp.arange(lane_count, dtype=jnp.int32) // rank_size
    select = (chosen[:, None] == lane_owner[None, :]).astype(jnp.float32)
    out_down = stack_down(attn_down[3])
    out_up = stack_up(attn_up[3])
    fc1_down_all = stack_down(fc1_down)
    fc1_up_all = stack_up(fc1_up)
    fc2_down_all = stack_down(fc2_down)
    fc2_up_all = stack_up(fc2_up)
    down_rows = jnp.transpose(attn_down, (0, 1, 3, 2)).reshape(4 * lane_count, model_width)
    up_rows = attn_up.reshape(4 * lane_count, model_width)
    weights = (w_out, w_fc1, w_fc2)
    inside = [v.shape[0] % (32 * seq_count) == 0 for v in weights]
    (attended_tok, q_heads, k_heads, v_heads, o_heads, lse_heads, w_slice, small_all), gathered = forward_attention(
        geo,
        rank_size,
        doc_lengths,
        adapter_ids,
        tokens,
        w_qkv,
        down_rows[: 3 * lane_count],
        up_rows[: 3 * lane_count],
        qv_bias,
        [v for v, here in zip(weights, inside) if here],
    )
    gathered = list(gathered)
    full_out, full_fc1, full_fc2 = [
        gathered.pop(0) if here else lax.all_gather(v, "wt", axis=0, tiled=True)
        for v, here in zip(weights, inside)
    ]
    out_main = jnp.dot(attended_tok, full_out, preferred_element_type=jnp.float32)
    small_out = (
        jnp.dot(attended_tok, out_down, preferred_element_type=jnp.float32) * select
    ).astype(jnp.bfloat16)
    z_value = out_main + out_bias + jnp.dot(small_out, out_up, preferred_element_type=jnp.float32)
    first_sum = tokens.astype(jnp.float32) + z_value
    first_norm, norm1_back = jax.vjp(
        lambda value: layer_norm(value, norm1_gain, norm1_bias), first_sum
    )
    first_low = first_norm.astype(jnp.bfloat16)
    fc1_main = jnp.dot(first_low, full_fc1, preferred_element_type=jnp.float32)
    small_fc1 = (
        jnp.dot(first_low, fc1_down_all, preferred_element_type=jnp.float32) * select
    ).astype(jnp.bfloat16)
    pre_act = (
        fc1_main + fc1_bias + jnp.dot(small_fc1, fc1_up_all, preferred_element_type=jnp.float32)
    )
    act_value, gelu_back = jax.vjp(gelu_exact, pre_act)
    act_low = act_value.astype(jnp.bfloat16)
    fc2_main = jnp.dot(act_low, full_fc2, preferred_element_type=jnp.float32)
    small_fc2 = (
        jnp.dot(act_low, fc2_down_all, preferred_element_type=jnp.float32) * select
    ).astype(jnp.bfloat16)
    y_value = (
        fc2_main + fc2_bias + jnp.dot(small_fc2, fc2_up_all, preferred_element_type=jnp.float32)
    )
    output, norm2_back = jax.vjp(
        lambda value: layer_norm(value, norm2_gain, norm2_bias), first_norm + y_value
    )
    d_second = norm2_back(cotangent.astype(jnp.float32))[0]
    d_y = d_second.astype(jnp.bfloat16)
    d_act = times_transposed(d_y, full_fc2)
    low_fc2 = (times_transposed(d_y, fc2_up_all) * select).astype(jnp.bfloat16)
    d_act = d_act + times_transposed(low_fc2, fc2_down_all)
    grad_fc2_up = left_inner(small_fc2, d_y)
    grad_fc2_down = left_inner(low_fc2, act_low)
    d_pre = gelu_back(d_act)[0].astype(jnp.bfloat16)
    d_first_low = times_transposed(d_pre, full_fc1)
    low_fc1 = (times_transposed(d_pre, fc1_up_all) * select).astype(jnp.bfloat16)
    d_first_low = d_first_low + times_transposed(low_fc1, fc1_down_all)
    grad_fc1_up = left_inner(small_fc1, d_pre)
    grad_fc1_down = left_inner(low_fc1, first_low)
    d_first = norm1_back(d_second + d_first_low)[0]
    d_z = d_first.astype(jnp.bfloat16)
    d_attended = times_transposed(d_z, full_out)
    low_out = (times_transposed(d_z, out_up) * select).astype(jnp.bfloat16)
    d_attended = (d_attended + times_transposed(low_out, out_down)).astype(jnp.bfloat16)
    grad_out_up = left_inner(small_out, d_z)
    grad_out_down = left_inner(low_out, attended_tok)
    blocks = [
        [p * geo.groups + i for i in range(geo.groups)] for p in range(geo.parts)
    ]
    d_heads = lax.all_to_all(
        d_attended.reshape(tok_rows, geo.groups, LANES),
        "seq",
        split_axis=1,
        concat_axis=0,
        axis_index_groups=blocks,
        tiled=True,
    ).reshape(geo.queries, LANES)
    d_q, d_k, d_v = backward_attention(
        geo, doc_lengths, part_index.reshape(1, 1), q_heads, k_heads, v_heads, o_heads, lse_heads, d_heads
    )
    set1 = [
        v.astype(BF16) for v in (grad_out_down, grad_out_up, grad_fc1_down, grad_fc2_up, grad_fc1_up, grad_fc2_down)
    ]
    input_grad, sum1, sum2, _ = closing(
        geo,
        rank_size,
        doc_lengths,
        adapter_ids,
        tokens,
        d_first,
        d_q,
        d_k,
        d_v,
        w_slice,
        down_rows[: 3 * lane_count],
        up_rows[: 3 * lane_count],
        small_all,
        set1,
    )

    down4, up4, fc1_down_sum, fc2_up_sum, fc1_up_sum, fc2_down_sum = unpack(geo, sum1, sum2, lane_count)

    def as_up(rows):
        return rows.reshape(rows.shape[:-2] + (adapter_count, rank_size, rows.shape[-1]))

    def as_down(rows):
        return jnp.swapaxes(as_up(rows), -1, -2)

    return (
        output,
        input_grad,
        as_down(down4),
        as_up(up4),
        as_down(fc1_down_sum),
        as_up(fc1_up_sum),
        as_down(fc2_down_sum),
        as_up(fc2_up_sum),
    )


def solution(mesh):
    placed = (
        P(("wt", "seq"), None),
        P(("wt", "seq"), None),
        P("wt", None),
        P(),
        P("wt", None),
        P(),
        P(),
        P(),
        P("wt", None),
        P(),
        P("wt", None),
        P(),
        P(),
        P(),
        P("wt", None),
        P("wt", None),
        P(),
        P(),
        P(),
        P(),
        P(),
        P(),
    )
    return jax.shard_map(
        shards,
        mesh=mesh,
        in_specs=placed,
        out_specs=(P(("wt", "seq"), None), P(("wt", "seq"), None), P(), P(), P(), P(), P(), P()),
        check_vma=False,
    )
```

```python
import functools

import jax
import jax.numpy as jnp
from jax import lax
from jax.experimental import pallas as pl
from jax.experimental.pallas import tpu as pltpu
from jax.sharding import PartitionSpec as P

HEADS = 16
HEAD_DIM = 64
LANES = 128
PAIR = LANES // HEAD_DIM
MESH = pl.DeviceIdType.MESH
F32 = jnp.float32
BF16 = jnp.bfloat16
VMEM_LIMIT = 60 * 2**20


def dot_nn(a, b):
    return lax.dot_general(a, b, (((1,), (0,)), ((), ())), preferred_element_type=F32)


def dot_nt(a, b):
    return lax.dot_general(a, b, (((1,), (1,)), ((), ())), preferred_element_type=F32)


def dot_tn(a, b):
    return lax.dot_general(a, b, (((0,), (0,)), ((), ())), preferred_element_type=F32)


class Geometry:
    def __init__(self, rows, width):
        self.seq = lax.axis_size("seq")
        self.wt = lax.axis_size("wt")
        self.rows = rows
        self.width = width
        self.groups = width // LANES
        self.parts = self.seq // self.groups
        chips = self.seq // 2
        nx = 1
        while nx * nx < chips:
            nx *= 2
        self.nx = nx
        self.ny = chips // nx
        self.keys = self.seq * rows
        self.queries = self.groups * rows


def doc_bounds(len_ref):
    count = len_ref.shape[1]
    starts, ends = [], []
    at = jnp.int32(0)
    for i in range(count):
        starts.append(at)
        at = at + len_ref[0, i]
        ends.append(at)
    return starts, ends


def segment_from(positions, starts):
    seg = jnp.zeros_like(positions)
    for start in starts[1:]:
        seg = seg + (positions >= start).astype(jnp.int32)
    return seg


def select_from(positions, starts, ends, id_ref, rank):
    owner = lax.broadcasted_iota(jnp.int32, positions.shape, 1) // rank
    picked = jnp.zeros(positions.shape, F32)
    for i in range(len(starts)):
        inside = (positions >= starts[i]) & (positions < ends[i]) & (owner == id_ref[0, i])
        picked = jnp.where(inside, 1.0, picked)
    return picked


class Spread:
    KINDS = 9

    def __init__(self, geo, here, region, send, recv, unit, first=0):
        self.geo, self.here, self.region = geo, here, region
        self.send, self.recv, self.unit, self.first = send, recv, unit, first

    def copy(self, kind, src, dst, x, y, core):
        return pltpu.make_async_remote_copy(
            src_ref=src,
            dst_ref=dst,
            send_sem=self.send.at[kind, self.unit],
            recv_sem=self.recv.at[kind, self.unit],
            device_id=(self.first + ((y * self.geo.nx) + x) * 2 + core, self.here[3]),
            device_id_type=MESH,
        )

    def others(self):
        nx, ny = self.geo.nx, self.geo.ny
        x, y, core, _ = self.here
        row = [((x + d) % nx, y) for d in range(1, nx)]
        col = [(x, (y + d) % ny) for d in range(1, ny)]
        return row, col

    def plan(self):
        x, y, core, _ = self.here
        row, col = self.others()
        plan = {kind: [] for kind in range(self.KINDS)}
        for tx, ty in row:
            plan[0].append(((x, y), None, (tx, ty, core)))
        for tx, ty in col:
            plan[1].append(((x, y), None, (tx, ty, core)))
        for ux, uy in row:
            for tx, ty in col:
                plan[2].append(((ux, uy), 0, (tx, ty, core)))
        for ux, uy in col:
            for tx, ty in row:
                plan[3].append(((ux, uy), 1, (tx, ty, core)))
        plan[4].append(((x, y), None, (x, y, 1 - core)))
        for ux, uy in row:
            plan[5].append(((ux, uy), None, (x, y, 1 - core)))
        for ux, uy in col:
            plan[6].append(((ux, uy), None, (x, y, 1 - core)))
        for ux, _ in row:
            for _, uy in col:
                plan[7].append(((ux, uy), 0, (x, y, 1 - core)))
                plan[8].append(((ux, uy), 1, (x, y, 1 - core)))
        return plan

    def go(self, kind, own=None):
        core = self.here[2]
        for (ux, uy), half, (tx, ty, tcore) in self.plan()[kind]:
            dst = self.region(ux, uy, core, half)
            src = dst if own is None else own
            self.copy(kind, src, dst, tx, ty, tcore).start()

    def arrivals(self, kind):
        x, y, core, _ = self.here
        row, col = self.others()
        if kind == 0:
            return [(u, None, core) for u in row]
        if kind == 1:
            return [(u, None, core) for u in col]
        if kind in (2, 3):
            return [((ux, uy), kind - 2, core) for ux, _ in row for _, uy in col]
        if kind == 4:
            return [((x, y), None, 1 - core)]
        if kind == 5:
            return [(u, None, 1 - core) for u in row]
        if kind == 6:
            return [(u, None, 1 - core) for u in col]
        return [((ux, uy), kind - 7, 1 - core) for ux, _ in row for _, uy in col]

    def wait(self, kind):
        x, y, core, _ = self.here
        for (ux, uy), half, whose in self.arrivals(kind):
            ref = self.region(ux, uy, whose, half)
            self.copy(kind, ref, ref, x, y, 1 - core).wait_recv()

    def wait_sends(self):
        x, y, core, _ = self.here
        for kind in range(self.KINDS):
            for (ux, uy), half, _ in self.plan()[kind]:
                ref = self.region(ux, uy, core, half)
                self.copy(kind, ref, ref, x, y, 1 - core).wait_send()


def device_here(geo):
    s = lax.axis_index("seq")
    core = s % 2
    chip = s // 2
    return chip % geo.nx, chip // geo.nx, core, lax.axis_index("wt")


def greet(geo):
    s, w = lax.axis_index("seq"), lax.axis_index("wt")
    barrier = pltpu.get_barrier_semaphore()
    for d in range(1, geo.seq):
        pl.semaphore_signal(barrier, inc=1, device_id=((s + d) % geo.seq, w), device_id_type=MESH)
    for d in range(1, geo.wt):
        pl.semaphore_signal(barrier, inc=1, device_id=(s, (w + d) % geo.wt), device_id_type=MESH)
    pl.semaphore_wait(barrier, geo.seq + geo.wt - 2)


def forward_kernel(
    geo,
    weight_count,
    rank,
    len_ref,
    id_ref,
    tokens_ref,
    wqkv_ref,
    down_ref,
    up_ref,
    bias_ref,
    *refs,
):
    weights_in = refs[:weight_count]
    att_ref, q_ref, k_ref, v_ref, o_ref, lse_ref, slice_ref, small_ref = refs[weight_count : weight_count + 8]
    weights_out = refs[weight_count + 8 : 2 * weight_count + 8]
    (
        tok_buf,
        seg_buf,
        att_buf,
        local_sem,
        send_sem,
        recv_sem,
        slice_send,
        slice_recv,
        line_send,
        line_recv,
        att_send,
        att_recv,
        *weights_buf,
    ) = refs[2 * weight_count + 8 :]
    here = device_here(geo)
    x, y, core, w = here
    s = lax.axis_index("seq")
    part, g = s // geo.groups, s % geo.groups
    rows, width, wt = geo.rows, geo.width, geo.wt
    lanes = pl.ds(pl.multiple_of(g * LANES, LANES), LANES)

    own_tok = pltpu.make_async_copy(tokens_ref, tok_buf.at[s], local_sem.at[0])
    own_tok.start()
    shard = wqkv_ref.shape[0]
    own_slices = []
    for j in range(3):
        src = wqkv_ref.at[:, pl.ds(pl.multiple_of(j * width + g * LANES, LANES), LANES)]
        dst = slice_ref.at[pl.ds(pl.multiple_of(w * shard, shard), shard), pl.ds(j * LANES, LANES)]
        own_slices.append(pltpu.make_async_copy(src, dst, local_sem.at[1 + j]))
        own_slices[-1].start()
    own_weights = []
    for m in range(weight_count):
        height = weights_in[m].shape[0]
        dst = weights_out[m].at[pl.ds(pl.multiple_of(w * height, height), height)]
        stage = weights_buf[m]
        pltpu.make_async_copy(weights_in[m], stage, local_sem.at[4 + m]).start()
        own_weights.append(
            (
                pltpu.make_async_copy(weights_in[m], stage, local_sem.at[4 + m]),
                pltpu.make_async_copy(stage, dst, local_sem.at[4 + m]),
            )
        )

    greet(geo)

    def token_region(ux, uy, whose, half):
        block = tok_buf.at[(uy * geo.nx + ux) * 2 + whose]
        if half is None:
            return block
        return block.at[pl.ds(half * (rows // 2), rows // 2)]

    tok = Spread(geo, here, token_region, send_sem, recv_sem, 0)
    tok.go(0, own=tokens_ref)
    tok.go(1, own=tokens_ref)
    tok.go(4, own=tokens_ref)

    def slice_copy(j, d):
        src = wqkv_ref.at[:, pl.ds(pl.multiple_of(j * width + g * LANES, LANES), LANES)]
        dst = slice_ref.at[pl.ds(pl.multiple_of(w * shard, shard), shard), pl.ds(j * LANES, LANES)]
        return pltpu.make_async_remote_copy(
            src_ref=src,
            dst_ref=dst,
            send_sem=slice_send.at[j, d],
            recv_sem=slice_recv.at[j, d],
            device_id=(s, (w + d) % wt),
            device_id_type=MESH,
        )

    def slice_arrival(j, d):
        origin = (w + wt - d) % wt
        dst = slice_ref.at[pl.ds(pl.multiple_of(origin * shard, shard), shard), pl.ds(j * LANES, LANES)]
        return pltpu.make_async_remote_copy(
            src_ref=dst,
            dst_ref=dst,
            send_sem=slice_send.at[j, d],
            recv_sem=slice_recv.at[j, d],
            device_id=(s, origin),
            device_id_type=MESH,
        )

    for d in range(1, wt):
        for j in range(3):
            slice_copy(j, d).start()
    starts, ends = doc_bounds(len_ref)
    seg_buf[...] = segment_from(lax.broadcasted_iota(jnp.int32, seg_buf.shape, 1), starts)

    seq = geo.seq
    mine = s

    def unit_rows(m, p, unit, half=None):
        height = weights_in[m].shape[0]
        piece = height // seq
        if half is None:
            return weights_out[m].at[pl.ds(pl.multiple_of(p * height + unit * piece, piece), piece)]
        piece = piece // 2
        return weights_out[m].at[
            pl.ds(pl.multiple_of(p * height + unit * 2 * piece + half * piece, piece), piece)
        ]

    def line_copy(m, p, up, own):
        height = weights_in[m].shape[0]
        piece = height // seq
        dst = unit_rows(m, p, mine)
        src = weights_in[m].at[pl.ds(pl.multiple_of(mine * piece, piece), piece)] if own else dst
        target = w + 1 if up else w - 1
        return pltpu.make_async_remote_copy(
            src_ref=src,
            dst_ref=dst,
            send_sem=line_send.at[0 if up else 1, m * wt + p],
            recv_sem=line_recv.at[m * wt + p],
            device_id=(s, target),
            device_id_type=MESH,
        )

    def nth_plane(j):
        below, above = w, wt - 1 - w
        both = jnp.minimum(below, above)
        in_turn = j < 2 * both
        dist = jnp.where(in_turn, j // 2 + 1, j - both + 1)
        from_below = jnp.where(in_turn, j % 2 == 0, below > above)
        return jnp.where(from_below, w - dist, w + dist)

    def weight_spread(m, p):
        def region(ux, uy, whose, half):
            return unit_rows(m, p, (uy * geo.nx + ux) * 2 + whose, half)

        return Spread(geo, here, region, send_sem, recv_sem, 1 + m * wt + p)

    units = [(m, j) for j in range(wt - 1) for m in range(weight_count)]

    def start_lines():
        for m in range(weight_count):
            @pl.when(w < wt - 1)
            def _():
                line_copy(m, w, True, True).start()

            @pl.when(w > 0)
            def _():
                line_copy(m, w, False, True).start()

    def tick(i):
        if 0 <= i < len(units):
            m, j = units[i]
            p = nth_plane(j)
            line_copy(m, p, True, False).wait_recv()

            @pl.when((p < w) & (w < wt - 1))
            def _():
                line_copy(m, p, True, False).start()

            @pl.when((p > w) & (w > 0))
            def _():
                line_copy(m, p, False, False).start()

            spread = weight_spread(m, p)
            spread.go(0)
            spread.go(1)
            spread.go(4)
        if 0 <= i - 1 < len(units):
            m, j = units[i - 1]
            spread = weight_spread(m, nth_plane(j))
            spread.wait(0)
            spread.go(2)
            spread.go(5)
            spread.wait(1)
            spread.go(3)
            spread.go(6)
        if 0 <= i - 2 < len(units):
            m, j = units[i - 2]
            spread = weight_spread(m, nth_plane(j))
            spread.wait(2)
            spread.go(7)
            spread.wait(3)
            spread.go(8)

    tick_count = len(units) + 2 if units else 0

    nx, ny = geo.nx, geo.ny
    row_n, col_n, diag_n = 2 * (nx - 1), 2 * (ny - 1), 2 * (nx - 1) * (ny - 1)

    def block_owner(i):
        r = i - 2
        c = r - row_n
        d = c - col_n
        dx_row, k_row = r % max(nx - 1, 1) + 1, r // max(nx - 1, 1)
        dy_col, k_col = c % max(ny - 1, 1) + 1, c // max(ny - 1, 1)
        half = max(diag_n // 2, 1)
        k_diag, in_diag = d // half, d % half
        dx_diag, dy_diag = in_diag % max(nx - 1, 1) + 1, in_diag // max(nx - 1, 1) + 1
        dx = jnp.where(i < 2, 0, jnp.where(i < 2 + row_n, dx_row, jnp.where(i < 2 + row_n + col_n, 0, dx_diag)))
        dy = jnp.where(i < 2 + row_n, 0, jnp.where(i < 2 + row_n + col_n, dy_col, dy_diag))
        kk = jnp.where(i < 2, i, jnp.where(i < 2 + row_n, k_row, jnp.where(i < 2 + row_n + col_n, k_col, k_diag)))
        return (((y + dy) % ny) * nx + (x + dx) % nx) * 2 + (core + kk) % 2

    def project(i, carry):
        @pl.when(i == 0)
        def _():
            own_tok.wait()
            for copy in own_slices:
                copy.wait()
            for fetch, store in own_weights:
                fetch.wait()
                store.start()
            for d in range(1, wt):
                for j in range(3):
                    slice_arrival(j, d).wait_recv()
            start_lines()

        @pl.when(i == 1)
        def _():
            tok.wait(4)

        @pl.when(i == 2)
        def _():
            tok.wait(0)
            tok.go(2)
            tok.go(5)
            tok.wait(1)
            tok.go(3)
            tok.go(6)

        @pl.when(i == 2 + row_n // 2)
        def _():
            tok.wait(5)

        @pl.when(i == 2 + row_n + col_n // 2)
        def _():
            tok.wait(6)

        @pl.when(i == 2 + row_n + col_n)
        def _():
            tok.wait(2)
            tok.go(7)
            tok.wait(3)
            tok.go(8)

        @pl.when(i == 2 + row_n + col_n + diag_n // 2)
        def _():
            tok.wait(7)
            tok.wait(8)

        t = block_owner(i)
        block = tok_buf[t]
        at = pl.ds(pl.multiple_of(t * rows, rows), rows)
        pos = t * rows + lax.broadcasted_iota(jnp.int32, (rows, LANES), 0)
        chosen = select_from(pos, starts, ends, id_ref, rank)
        main = dot_nn(block, slice_ref[...])
        small = dot_nt(block, down_ref[: 3 * LANES, :])
        for j in range(3):
            cut = slice(j * LANES, (j + 1) * LANES)
            low = (small[:, cut] * chosen).astype(BF16)
            small_ref[at, cut] = low
            value = main[:, cut] + dot_nn(low, up_ref[cut, lanes])
            if j == 0:
                value = value + bias_ref[0:1, lanes]

                @pl.when(t // geo.groups == part)
                def _():
                    inner = pl.ds(pl.multiple_of((t % geo.groups) * rows, rows), rows)
                    q_ref[inner, :] = value.astype(BF16)
            elif j == 1:
                k_ref[at, :] = value.astype(BF16)
            else:
                v_ref[at, :] = (value + bias_ref[1:2, lanes]).astype(BF16)
        return carry

    lax.fori_loop(0, geo.seq, project, 0)

    scale = HEAD_DIM ** (-0.5)
    chunk = min(2048, geo.keys)
    chunks = geo.keys // chunk
    first_head = lax.broadcasted_iota(jnp.int32, (rows, LANES), 1) < HEAD_DIM

    def att_copy(b):
        return pltpu.make_async_remote_copy(
            src_ref=att_buf.at[b],
            dst_ref=att_ref.at[:, lanes],
            send_sem=att_send.at[b],
            recv_sem=att_recv.at[g],
            device_id=(part * geo.groups + b, w),
            device_id_type=MESH,
        )

    def attend(i, carry):
        for n in range(min(tick_count, geo.groups)):
            @pl.when(i == n)
            def _():
                tick(n)

        b = (g + 1 + i) % geo.groups
        inner = pl.ds(pl.multiple_of(b * rows, rows), rows)
        query = q_ref[inner, :] * jnp.asarray(scale, BF16)
        q_pos = (part * geo.groups + b) * rows + lax.broadcasted_iota(jnp.int32, (rows, 1), 0)
        q_seg = segment_from(q_pos, starts)
        results = []
        for h in range(PAIR):
            mask = first_head if h == 0 else jnp.logical_not(first_head)
            q_head = jnp.where(mask, query, jnp.zeros_like(query))

            def one(c, state):
                top, total, acc = state
                keys_at = pl.ds(pl.multiple_of(c * chunk, chunk), chunk)
                score = dot_nt(q_head, k_ref[keys_at, :])
                score = jnp.where(q_seg == seg_buf[:, keys_at], score, -1e30)
                peak = jnp.max(score, axis=1, keepdims=True)
                if top is not None:
                    peak = jnp.maximum(top, peak)
                weight = jnp.exp(score - peak)
                add = jnp.sum(weight, axis=1, keepdims=True)
                out = dot_nn(weight.astype(BF16), v_ref[keys_at, :])
                if top is not None:
                    fade = jnp.exp(top - peak)
                    add = add + total * fade
                    out = out + acc * fade
                return peak, add, out

            state = one(0, (None, None, None))
            if chunks > 1:
                state = lax.fori_loop(1, chunks, one, state)
            top, total, acc = state
            results.append((acc / total, top + jnp.log(total)))
        out = jnp.where(first_head, results[0][0], results[1][0])
        o_ref[inner, :] = out
        lse_ref[inner, :] = jnp.where(first_head, results[0][1], results[1][1])
        att_buf[b] = out.astype(BF16)

        @pl.when(b != g)
        def _():
            att_copy(b).start()

        return carry

    lax.fori_loop(0, geo.groups, attend, 0)
    own_att = pltpu.make_async_copy(att_buf.at[g], att_ref.at[:, lanes], local_sem.at[0])
    own_att.start()

    for n in range(geo.groups, tick_count):
        tick(n)

    for d in range(1, geo.groups):
        other = (g + d) % geo.groups
        cut = pl.ds(pl.multiple_of(other * LANES, LANES), LANES)
        pltpu.make_async_remote_copy(
            src_ref=att_ref.at[:, cut],
            dst_ref=att_ref.at[:, cut],
            send_sem=att_send.at[other],
            recv_sem=att_recv.at[other],
            device_id=(part * geo.groups + other, w),
            device_id_type=MESH,
        ).wait_recv()
        att_copy(other).wait_send()
    own_att.wait()
    tok.wait_sends()
    for d in range(1, wt):
        for j in range(3):
            slice_copy(j, d).wait_send()
    for m in range(weight_count):
        own_weights[m][1].wait()

        @pl.when(w < wt - 1)
        def _():
            line_copy(m, w, True, True).wait_send()

        @pl.when(w > 0)
        def _():
            line_copy(m, w, False, True).wait_send()

    for m, j in units:
        p = nth_plane(j)

        @pl.when((p < w) & (w < wt - 1))
        def _():
            line_copy(m, p, True, False).wait_send()

        @pl.when((p > w) & (w > 0))
        def _():
            line_copy(m, p, False, False).wait_send()

        spread = weight_spread(m, p)
        for kind in range(4, 9):
            spread.wait(kind)
        spread.wait_sends()


def forward_attention(geo, rank, lengths, ids, tokens, w_qkv, down, up, bias, weights):
    rows, width = geo.rows, geo.width
    count = len(weights)
    any_spec = pl.BlockSpec(memory_space=pl.ANY)
    vmem = pl.BlockSpec(memory_space=pltpu.VMEM)
    smem = pl.BlockSpec(memory_space=pltpu.SMEM)
    shapes = [
        jax.ShapeDtypeStruct((rows, width), BF16),
        jax.ShapeDtypeStruct((geo.queries, LANES), BF16),
        jax.ShapeDtypeStruct((geo.keys, LANES), BF16),
        jax.ShapeDtypeStruct((geo.keys, LANES), BF16),
        jax.ShapeDtypeStruct((geo.queries, LANES), F32),
        jax.ShapeDtypeStruct((geo.queries, LANES), F32),
        jax.ShapeDtypeStruct((width, 3 * LANES), BF16),
        jax.ShapeDtypeStruct((geo.keys, 3 * LANES), BF16),
    ] + [jax.ShapeDtypeStruct((v.shape[0] * geo.wt, v.shape[1]), BF16) for v in weights]
    units = 1 + count * geo.wt
    dma = pltpu.SemaphoreType.DMA
    results = pl.pallas_call(
        functools.partial(forward_kernel, geo, count, rank),
        out_shape=shapes,
        in_specs=[smem, smem, any_spec, any_spec, vmem, vmem, vmem] + [any_spec] * count,
        out_specs=[any_spec] + [vmem] * 7 + [any_spec] * count,
        scratch_shapes=[
            pltpu.VMEM((geo.seq, rows, width), BF16),
            pltpu.VMEM((1, geo.keys), jnp.int32),
            pltpu.VMEM((geo.groups, rows, LANES), BF16),
            dma((4 + count,)),
            dma((Spread.KINDS, units)),
            dma((Spread.KINDS, units)),
            dma((3, geo.wt)),
            dma((3, geo.wt)),
            dma((2, max(count, 1) * geo.wt)),
            dma((max(count, 1) * geo.wt,)),
            dma((geo.groups,)),
            dma((geo.groups,)),
        ]
        + [pltpu.VMEM(v.shape, BF16) for v in weights],
        compiler_params=pltpu.CompilerParams(
            collective_id=0, has_side_effects=True, vmem_limit_bytes=VMEM_LIMIT
        ),
        name="gather_attend",
    )(lengths, ids, tokens, w_qkv, down, up, bias, *weights)
    return results[:8], results[8:]


def backward_kernel(geo, len_ref, part_ref, q_ref, k_ref, v_ref, o_ref, lse_ref, g_ref, dq_ref, dk_ref, dv_ref, dk_acc, dv_acc):
    rows = geo.rows
    part = part_ref[0, 0]
    scale = HEAD_DIM ** (-0.5)
    starts, ends = doc_bounds(len_ref)
    first_head = lax.broadcasted_iota(jnp.int32, (rows, LANES), 1) < HEAD_DIM
    dk_acc[...] = jnp.zeros_like(dk_acc)
    dv_acc[...] = jnp.zeros_like(dv_acc)

    def seg_of(position):
        seg = jnp.int32(0)
        for start in starts[1:]:
            seg = seg + (position >= start).astype(jnp.int32)
        return seg

    def pick(values, index):
        found = values[0]
        for i in range(1, len(values)):
            found = jnp.where(index == i, values[i], found)
        return found

    def query_block(b, carry):
        at = pl.ds(pl.multiple_of(b * rows, rows), rows)
        origin = (part * geo.groups + b) * rows
        query = q_ref[at, :] * jnp.asarray(scale, BF16)
        cot = g_ref[at, :]
        lse = lse_ref[at, :]
        both = cot.astype(F32) * o_ref[at, :]
        q_pos = origin + lax.broadcasted_iota(jnp.int32, (rows, 1), 0)
        q_seg = segment_from(q_pos, starts)
        heads = []
        for h in range(PAIR):
            mask = first_head if h == 0 else jnp.logical_not(first_head)
            zero = jnp.zeros_like(query)
            heads.append(
                (
                    jnp.where(mask, query, zero),
                    jnp.where(mask, cot, zero),
                    lse[:, h * HEAD_DIM : h * HEAD_DIM + 1],
                    jnp.sum(jnp.where(mask, both, 0.0), axis=1, keepdims=True),
                )
            )
        low = pick(starts, seg_of(origin)) // rows
        high = (pick(ends, seg_of(origin + rows - 1)) + rows - 1) // rows

        def key_block(c, accs):
            keys_at = pl.ds(pl.multiple_of(c * rows, rows), rows)
            key, value = k_ref[keys_at, :], v_ref[keys_at, :]
            k_pos = c * rows + lax.broadcasted_iota(jnp.int32, (1, rows), 1)
            same = q_seg == segment_from(k_pos, starts)
            new = []
            dk_parts, dv_parts = [], []
            for h in range(PAIR):
                q_head, g_head, lse_head, dot_head = heads[h]
                score = jnp.where(same, dot_nt(q_head, key), -1e30)
                prob = jnp.exp(score - lse_head)
                d_prob = dot_nt(g_head, value)
                raw = (prob * (d_prob - dot_head) * scale).astype(BF16)
                new.append(accs[h] + dot_nn(raw, key))
                dk_parts.append(dot_tn(raw, q_head))
                dv_parts.append(dot_tn(prob.astype(BF16), g_head))
            dk_acc[keys_at, :] += dk_parts[0] + dk_parts[1]
            dv_acc[keys_at, :] += dv_parts[0] + dv_parts[1]
            return tuple(new)

        zero = jnp.zeros((rows, LANES), F32)
        accs = lax.fori_loop(low, high, key_block, (zero, zero))
        dq_ref[at, :] = jnp.where(first_head, accs[0], accs[1]).astype(BF16)
        return carry

    lax.fori_loop(0, geo.groups, query_block, 0)
    dk_ref[...] = (dk_acc[...] * HEAD_DIM**0.5).astype(BF16)
    dv_ref[...] = dv_acc[...].astype(BF16)


def backward_attention(geo, lengths, part, q, k, v, o, lse, d_heads):
    smem = pl.BlockSpec(memory_space=pltpu.SMEM)
    vmem = pl.BlockSpec(memory_space=pltpu.VMEM)
    return pl.pallas_call(
        functools.partial(backward_kernel, geo),
        out_shape=[
            jax.ShapeDtypeStruct((geo.queries, LANES), BF16),
            jax.ShapeDtypeStruct((geo.keys, LANES), BF16),
            jax.ShapeDtypeStruct((geo.keys, LANES), BF16),
        ],
        in_specs=[smem, smem] + [vmem] * 6,
        out_specs=[vmem] * 3,
        scratch_shapes=[pltpu.VMEM((geo.keys, LANES), F32)] * 2,
        compiler_params=pltpu.CompilerParams(vmem_limit_bytes=VMEM_LIMIT),
        name="attend_back",
    )(lengths, part, q, k, v, o, lse, d_heads)


class Block:
    def __init__(self, geo):
        chips = geo.groups // 2
        self.nx = min(geo.nx, chips)
        self.ny = chips // self.nx


class PairSum:
    def __init__(self, count, me, core, first, w, bufs, sems, make, stage=None):
        self.count, self.me, self.core, self.first, self.w = count, me, core, first, w
        self.near_out, self.near_in, self.far_in = bufs
        self.near_send, self.near_recv, self.far_send, self.far_recv = sems
        self.make = make
        self.slots = self.near_out.shape[0]
        self.stage = stage

    def slot(self, chip):
        return ((chip + self.count - self.me + self.count - 1) % self.count) % self.slots

    def near(self, chip):
        return pltpu.make_async_remote_copy(
            src_ref=self.near_out.at[self.slot(chip)],
            dst_ref=self.near_in.at[chip],
            send_sem=self.near_send.at[chip],
            recv_sem=self.near_recv.at[chip],
            device_id=(self.first + self.me * 2 + 1 - self.core, self.w),
            device_id_type=MESH,
        )

    def far(self, chip):
        return pltpu.make_async_remote_copy(
            src_ref=self.near_in.at[chip],
            dst_ref=self.far_in.at[self.me],
            send_sem=self.far_send.at[chip],
            recv_sem=self.far_recv.at[self.me],
            device_id=(self.first + chip * 2 + self.core, self.w),
            device_id_type=MESH,
        )

    def far_arrival(self, chip):
        return pltpu.make_async_remote_copy(
            src_ref=self.far_in.at[chip],
            dst_ref=self.far_in.at[chip],
            send_sem=self.far_send.at[chip],
            recv_sem=self.far_recv.at[chip],
            device_id=(self.first + chip * 2 + self.core, self.w),
            device_id_type=MESH,
        )

    def start(self):
        def step(d, carry):
            chip = (self.me + 1 + d) % self.count
            if self.slots < self.count:

                @pl.when(d >= self.slots)
                def _():
                    self.near((self.me + 1 + d - self.slots) % self.count).wait_send()

            self.near_out[d % self.slots] = self.make(chip, 1 - self.core).astype(BF16)
            self.near(chip).start()
            return carry

        lax.fori_loop(0, self.count, step, 0)

    def send(self):
        def step(d, carry):
            chip = (self.me + 1 + d) % self.count
            own = self.make(chip, self.core)
            self.near(chip).wait_recv()
            self.near_in[chip] = (own + self.near_in[chip].astype(F32)).astype(BF16)
            self.far(chip).start()
            return carry

        lax.fori_loop(0, self.count - 1, step, 0)

    def finish(self):
        total = self.make(self.me, self.core)
        self.near(self.me).wait_recv()
        total = total + self.near_in[self.me].astype(F32)
        if self.stage is None:
            for d in range(1, self.count):
                chip = (self.me + d) % self.count
                self.far_arrival(chip).wait_recv()
                total = total + self.far_in[chip].astype(F32)
            return total
        stage, sem = self.stage

        def fetch(d):
            chip = (self.me + d) % self.count
            return pltpu.make_async_copy(self.far_in.at[chip], stage.at[d % 2], sem.at[d % 2])

        self.far_arrival((self.me + 1) % self.count).wait_recv()
        fetch(1).start()
        for d in range(1, self.count):
            if d + 1 < self.count:
                self.far_arrival((self.me + d + 1) % self.count).wait_recv()
                fetch(d + 1).start()
            fetch(d).wait()
            total = total + stage[d % 2].astype(F32)
        return total

    def drain(self):
        for d in range(self.count):
            chip = (self.me + 1 + d) % self.count
            if d >= self.count - self.slots:
                self.near(chip).wait_send()
            if d < self.count - 1:
                self.far(chip).wait_send()


def closing_kernel(
    geo,
    rank,
    len_ref,
    id_ref,
    tokens_ref,
    first_ref,
    dq_ref,
    dk_ref,
    dv_ref,
    slice_ref,
    down_ref,
    up_ref,
    small_ref,
    out_down_ref,
    out_up_ref,
    fc1_down_ref,
    fc2_up_ref,
    fc1_up_ref,
    fc2_down_ref,
    grad_ref,
    sum1_ref,
    sum2_ref,
    tok_far,
    tok_out,
    tok_in,
    tok_stage,
    small_buf,
    set1_out,
    set1_in,
    set1_far,
    set2_out,
    set2_in,
    set2_far,
    down_acc,
    up_acc,
    mine1,
    mine2,
    place_buf,
    fold_buf,
    all1,
    all2,
    places,
    done1,
    done2,
    tok_sems,
    set1_sems,
    set2_sems,
    line_send,
    line_recv,
    spread_send,
    spread_recv,
    local_sem,
    stage_sem,
    small_sem,
):
    x, y, core, w = device_here(geo)
    s = lax.axis_index("seq")
    rows, width, wt, groups, parts = geo.rows, geo.width, geo.wt, geo.groups, geo.parts
    part, g = s // groups, s % groups
    docs = len_ref.shape[1]
    doc_rows = docs * rank
    lane_count = down_ref.shape[0] // 4
    lanes = pl.ds(pl.multiple_of(g * LANES, LANES), LANES)
    starts, ends = doc_bounds(len_ref)
    ids = [id_ref[0, d] for d in range(docs)]
    fresh = []
    for d in range(docs):
        seen = jnp.bool_(False)
        for e in range(d):
            seen = seen | (ids[e] == ids[d])
        fresh.append(jnp.where(seen, 0.0, 1.0))

    greet_all(geo)

    def iota(shape, dim):
        return lax.broadcasted_iota(jnp.int32, shape, dim)

    def zero_one(condition):
        return jnp.where(condition, 1.0, 0.0).astype(BF16)

    def chosen_of(t):
        pos = t * rows + iota((rows, LANES), 0)
        return select_from(pos, starts, ends, id_ref, rank)

    def fold(j):
        a, b = iota((lane_count, LANES), 0), iota((lane_count, LANES), 1)
        return zero_one((b >= j * rank) & (b < (j + 1) * rank) & (a % rank == b - j * rank))

    def make_tokens(chip, whose):
        t = chip * 2 + whose
        at = pl.ds(pl.multiple_of(t * rows, rows), rows)
        if parts == 1:
            d_q = dq_ref[at, :]
        else:
            inner = pl.ds(pl.multiple_of((t % groups) * rows, rows), rows)
            d_q = jnp.where(t // groups == part, dq_ref[inner, :], jnp.zeros((rows, LANES), BF16))
        pieces = [d_q, dk_ref[at, :], dv_ref[at, :]]
        chosen = chosen_of(t)
        total = jnp.zeros((rows, width), F32)
        low = jnp.zeros((rows, LANES), F32)
        for j in range(3):
            total = total + dot_nt(pieces[j], slice_ref[:, j * LANES : (j + 1) * LANES])
            part_low = dot_nt(pieces[j], up_ref[pl.ds(j * lane_count, lane_count), lanes])
            low = low + dot_nn((part_low * chosen).astype(BF16), fold(j))
        return jnp.concatenate([total, low], axis=1)

    tok = PairSum(
        geo.seq // 2, s // 2, core, 0, w, (tok_out, tok_in, tok_far), [tok_sems.at[i] for i in range(4)], make_tokens,
        (tok_stage, stage_sem),
    )

    singles = [out_down_ref, out_up_ref, fc1_down_ref, fc2_up_ref, fc1_up_ref, fc2_down_ref]

    def by_document(value):
        return dot_tn(fold_buf[...], value)[:doc_rows]

    def make_set1(chip, whose):
        owner = chip * 2 + whose
        cols = []
        for ref in singles:
            wide = ref.shape[1] // groups
            cols.append(by_document(ref[:, pl.ds(pl.multiple_of(owner * wide, LANES), wide)]))
        return jnp.concatenate(cols, axis=1)

    def make_set2(chip, whose):
        owner = chip * 2 + whose
        cut = pl.ds(pl.multiple_of(owner * LANES, LANES), LANES)
        return jnp.concatenate([down_acc[j * doc_rows : (j + 1) * doc_rows, cut] for j in range(3)], axis=1)

    chips = groups // 2
    set1 = PairSum(
        chips, g // 2, core, part * groups, w, (set1_out, set1_in, set1_far), [set1_sems.at[i] for i in range(4)], make_set1
    )
    set2 = PairSum(
        chips, g // 2, core, part * groups, w, (set2_out, set2_in, set2_far), [set2_sems.at[i] for i in range(4)], make_set2
    )

    def peer(n):
        plane = (w + n) % wt
        other = (part + n // wt) % parts
        return other * groups + g, plane, other * wt + plane

    mine_at = part * wt + w

    def line_copy(kind, n, src, dst_all):
        device, plane, _ = peer(n)
        return pltpu.make_async_remote_copy(
            src_ref=src,
            dst_ref=dst_all.at[mine_at],
            send_sem=line_send.at[kind, n],
            recv_sem=line_recv.at[kind, mine_at],
            device_id=(device, plane),
            device_id_type=MESH,
        )

    def line_arrival(kind, n, dst_all):
        device, plane, at = peer(n)
        return pltpu.make_async_remote_copy(
            src_ref=dst_all.at[at],
            dst_ref=dst_all.at[at],
            send_sem=line_send.at[kind, n],
            recv_sem=line_recv.at[kind, at],
            device_id=(device, plane),
            device_id_type=MESH,
        )

    peers = range(1, wt * parts)

    block = Block(geo)
    chip_here = g // 2
    here = (chip_here % block.nx, chip_here // block.nx, core, w)

    def region_of(ref):
        def region(ux, uy, whose, half):
            one = ref.at[(uy * block.nx + ux) * 2 + whose]
            if half is None:
                return one
            return one.at[pl.ds(half * (lane_count // 2), lane_count // 2)]

        return region

    spreads = [
        Spread(block, here, region_of(ref), spread_send, spread_recv, i, part * groups)
        for i, ref in enumerate((sum1_ref, sum2_ref))
    ]
    finals = [done1, done2]
    outs = [sum1_ref, sum2_ref]

    def place(kind, mine, dst_all):
        total = dot_nn(place_buf[:, :doc_rows], mine[...])
        for n in peers:
            line_arrival(kind, n, dst_all).wait_recv()
            if kind == 0:
                line_arrival(2, n, places).wait_recv()
            at = peer(n)[2]
            total = total + dot_nn(places[at][:, :doc_rows], dst_all[at])
        finals[kind][...] = total.astype(BF16)
        for way in (0, 1, 4):
            spreads[kind].go(way, own=finals[kind])
        pltpu.make_async_copy(finals[kind], outs[kind].at[g], local_sem.at[kind]).start()

    def pass_on(kind):
        spread = spreads[kind]
        spread.wait(0)
        spread.go(2)
        spread.go(5)
        spread.wait(1)
        spread.go(3)
        spread.go(6)

    def pass_last(kind):
        spread = spreads[kind]
        spread.wait(2)
        spread.go(7)
        spread.wait(3)
        spread.go(8)

    a, b = iota((lane_count, LANES), 0), iota((lane_count, LANES), 1)
    places_all = jnp.zeros((lane_count, LANES), F32)
    places_first = jnp.zeros((lane_count, LANES), F32)
    for d in range(docs):
        hit = (a // rank == ids[d]) & (b // rank == d) & (a % rank == b % rank)
        places_all = jnp.where(hit, 1.0, places_all)
        places_first = jnp.where(hit, fresh[d], places_first)
    place_buf[...] = places_all.astype(BF16)
    fold_buf[...] = places_first.astype(BF16)
    for n in peers:
        line_copy(2, n, place_buf, places).start()

    set1.start()
    tok.start()
    set1.send()
    tok.send()

    def small_copy(t):
        return pltpu.make_async_copy(
            small_ref.at[pl.ds(pl.multiple_of(t * rows, rows), rows)], small_buf.at[t % 2], small_sem.at[t % 2]
        )

    def add_up(t, carry):
        at = pl.ds(pl.multiple_of(t * rows, rows), rows)

        @pl.when(t + 1 < geo.seq)
        def _():
            small_copy(t + 1).start()

        small_copy(t).wait()
        for j in range(3):
            cut = slice(j * LANES, (j + 1) * LANES)
            if j == 0:
                if parts == 1:
                    value = dq_ref[at, :]
                else:
                    inner = pl.ds(pl.multiple_of((t % groups) * rows, rows), rows)
                    value = jnp.where(t // groups == part, dq_ref[inner, :], jnp.zeros((rows, LANES), BF16))
            else:
                value = (dk_ref if j == 1 else dv_ref)[at, :]
            up_acc[cut, :] += dot_tn(small_buf[t % 2][:, cut], value)
        return carry

    up_acc[...] = jnp.zeros_like(up_acc)
    small_copy(0).start()
    lax.fori_loop(0, geo.seq, add_up, 0)

    mine1[...] = set1.finish().astype(BF16)
    for n in peers:
        line_copy(0, n, mine1, all1).start()

    total = tok.finish()
    low = total[:, width:].astype(BF16)
    total = total[:, :width] + first_ref[...]
    chosen = chosen_of(s)
    pos = s * rows + iota((rows, doc_rows), 0)
    doc_of = iota((rows, doc_rows), 1) // rank
    in_doc = doc_of == segment_from(pos, starts)
    tokens = tokens_ref[...]
    for j in range(3):
        a, b = iota((LANES, lane_count), 0), iota((LANES, lane_count), 1)
        widen = zero_one((a >= j * rank) & (a < (j + 1) * rank) & (b % rank == a - j * rank))
        wide = (dot_nn(low, widen) * chosen).astype(BF16)
        total = total + dot_nn(wide, down_ref[j * lane_count : (j + 1) * lane_count, :])
        by_doc = dot_nn(low, widen[:, :doc_rows])
        by_doc = jnp.where(in_doc, by_doc, 0.0).astype(BF16)
        down_acc[j * doc_rows : (j + 1) * doc_rows, :] = dot_tn(by_doc, tokens)
    set2.start()
    grad_ref[...] = total
    set2.send()
    place(0, mine1, all1)
    for j in range(3):
        mine2[:, (3 + j) * LANES : (4 + j) * LANES] = by_document(
            up_acc[j * lane_count : (j + 1) * lane_count, :].astype(BF16)
        ).astype(BF16)
    mine2[:, : 3 * LANES] = set2.finish().astype(BF16)
    for n in peers:
        line_copy(1, n, mine2, all2).start()
    pass_on(0)
    pass_last(0)
    place(1, mine2, all2)
    pass_on(1)
    pass_last(1)
    for kind in range(2):
        for way in range(4, 9):
            spreads[kind].wait(way)
        spreads[kind].wait_sends()
        pltpu.make_async_copy(finals[kind], outs[kind].at[g], local_sem.at[kind]).wait()
    for n in peers:
        line_copy(0, n, mine1, all1).wait_send()
        line_copy(1, n, mine2, all2).wait_send()
        line_copy(2, n, place_buf, places).wait_send()
    tok.drain()
    set1.drain()
    set2.drain()


def greet_all(geo):
    s, w = lax.axis_index("seq"), lax.axis_index("wt")
    barrier = pltpu.get_barrier_semaphore()
    part, g = s // geo.groups, s % geo.groups
    for d in range(1, geo.seq):
        pl.semaphore_signal(barrier, inc=1, device_id=((s + d) % geo.seq, w), device_id_type=MESH)
    count = geo.seq - 1
    for d in range(1, geo.wt):
        for q in range(geo.parts):
            other = ((part + q) % geo.parts) * geo.groups + g
            pl.semaphore_signal(barrier, inc=1, device_id=(other, (w + d) % geo.wt), device_id_type=MESH)
            count += 1
    pl.semaphore_wait(barrier, count)


def closing(geo, rank, lengths, ids, tokens, d_first, dq, dk, dv, w_slice, down, up, small, grads):
    rows, width = geo.rows, geo.width
    docs = lengths.shape[1]
    doc_rows = docs * rank
    lane_count = down.shape[0] // 4
    set1 = sum(v.shape[1] for v in grads) // geo.groups
    set2 = 6 * LANES
    chips, near = geo.seq // 2, geo.groups // 2
    peers = geo.wt * geo.parts
    smem = pl.BlockSpec(memory_space=pltpu.SMEM)
    vmem = pl.BlockSpec(memory_space=pltpu.VMEM)
    any_spec = pl.BlockSpec(memory_space=pl.ANY)
    dma = pltpu.SemaphoreType.DMA
    wide = width + LANES
    return pl.pallas_call(
        functools.partial(closing_kernel, geo, rank),
        out_shape=[
            jax.ShapeDtypeStruct((rows, width), F32),
            jax.ShapeDtypeStruct((geo.groups, lane_count, set1), BF16),
            jax.ShapeDtypeStruct((geo.groups, lane_count, set2), BF16),
            jax.ShapeDtypeStruct((chips, rows, wide), BF16),
        ],
        in_specs=[smem, smem] + [vmem] * 8 + [any_spec] + [vmem] * len(grads),
        out_specs=[vmem, any_spec, any_spec, any_spec],
        scratch_shapes=[
            pltpu.VMEM((min(chips, 4), rows, wide), BF16),
            pltpu.VMEM((chips, rows, wide), BF16),
            pltpu.VMEM((2, rows, wide), BF16),
            pltpu.VMEM((2, rows, 3 * lane_count), BF16),
            pltpu.VMEM((near, doc_rows, set1), BF16),
            pltpu.VMEM((near, doc_rows, set1), BF16),
            pltpu.VMEM((near, doc_rows, set1), BF16),
            pltpu.VMEM((near, doc_rows, 3 * LANES), BF16),
            pltpu.VMEM((near, doc_rows, 3 * LANES), BF16),
            pltpu.VMEM((near, doc_rows, 3 * LANES), BF16),
            pltpu.VMEM((3 * doc_rows, width), F32),
            pltpu.VMEM((3 * lane_count, LANES), F32),
            pltpu.VMEM((doc_rows, set1), BF16),
            pltpu.VMEM((doc_rows, set2), BF16),
            pltpu.VMEM((lane_count, LANES), BF16),
            pltpu.VMEM((lane_count, LANES), BF16),
            pltpu.VMEM((peers, doc_rows, set1), BF16),
            pltpu.VMEM((peers, doc_rows, set2), BF16),
            pltpu.VMEM((peers, lane_count, LANES), BF16),
            pltpu.VMEM((lane_count, set1), BF16),
            pltpu.VMEM((lane_count, set2), BF16),
            dma((4, chips)),
            dma((4, near)),
            dma((4, near)),
            dma((3, peers)),
            dma((3, peers)),
            dma((Spread.KINDS, 2)),
            dma((Spread.KINDS, 2)),
            dma((2,)),
            dma((2,)),
            dma((2,)),
        ],
        compiler_params=pltpu.CompilerParams(
            collective_id=1, has_side_effects=True, vmem_limit_bytes=VMEM_LIMIT
        ),
        name="close",
    )(lengths, ids, tokens, d_first, dq, dk, dv, w_slice, down, up, small, *grads)


def unpack_kernel(one_ref, two_ref, down_ref, up_ref, fc1_down_ref, fc2_up_ref, fc1_up_ref, fc2_down_ref):
    for j in range(3):
        down_ref[j] = two_ref[0, :, j * LANES : (j + 1) * LANES].astype(F32)
        up_ref[j] = two_ref[0, :, (3 + j) * LANES : (4 + j) * LANES].astype(F32)
    at = 0
    for ref in (down_ref.at[3], up_ref.at[3], fc1_down_ref, fc2_up_ref, fc1_up_ref, fc2_down_ref):
        wide = ref.shape[1]
        ref[...] = one_ref[0, :, at : at + wide].astype(F32)
        at += wide


def unpack(geo, one, two, lane_count):
    groups = geo.groups
    thick = (one.shape[2] - 4 * LANES) // 2

    def whole(wide):
        return jax.ShapeDtypeStruct((lane_count, wide * groups), F32)

    def flat(wide):
        return pl.BlockSpec((lane_count, wide), lambda i: (0, i))

    four = jax.ShapeDtypeStruct((4, lane_count, LANES * groups), F32)
    four_spec = pl.BlockSpec((4, lane_count, LANES), lambda i: (0, 0, i))
    return pl.pallas_call(
        unpack_kernel,
        grid=(groups,),
        out_shape=[four, four, whole(LANES), whole(LANES), whole(thick), whole(thick)],
        in_specs=[
            pl.BlockSpec((1,) + one.shape[1:], lambda i: (i, 0, 0)),
            pl.BlockSpec((1,) + two.shape[1:], lambda i: (i, 0, 0)),
        ],
        out_specs=[four_spec, four_spec, flat(LANES), flat(LANES), flat(thick), flat(thick)],
        compiler_params=pltpu.CompilerParams(vmem_limit_bytes=VMEM_LIMIT // 2),
        name="unpack",
    )(one, two)


def layer_norm(value, gain, shift):
    mean = jnp.mean(value, axis=-1, keepdims=True)
    centred = value - mean
    spread = jnp.mean(centred * centred, axis=-1, keepdims=True)
    return centred * lax.rsqrt(spread + 1e-05) * gain + shift


def gelu_exact(value):
    return jax.nn.gelu(value, approximate=False)


def times_transposed(grad, weight):
    return lax.dot_general(
        grad, weight, (((1,), (1,)), ((), ())), preferred_element_type=jnp.float32
    )


def left_inner(left, right):
    return lax.dot_general(
        left, right, (((0,), (0,)), ((), ())), preferred_element_type=jnp.float32
    )


def stack_down(down):
    return jnp.transpose(down, (1, 0, 2)).reshape(down.shape[1], down.shape[0] * down.shape[2])


def stack_up(up):
    return up.reshape(up.shape[0] * up.shape[1], up.shape[2])


def unstack_down(stacked, adapter_count, rank_size):
    return jnp.transpose(stacked.reshape(stacked.shape[0], adapter_count, rank_size), (1, 0, 2))


def unstack_up(stacked, adapter_count, rank_size):
    return stacked.reshape(adapter_count, rank_size, stacked.shape[1])


def segment_of(positions, starts):
    return jnp.sum((positions[:, None] >= starts[None, :]).astype(jnp.int32), axis=1) - 1


def shards(
    tokens,
    cotangent,
    w_qkv,
    qv_bias,
    w_out,
    out_bias,
    norm1_gain,
    norm1_bias,
    w_fc1,
    fc1_bias,
    w_fc2,
    fc2_bias,
    norm2_gain,
    norm2_bias,
    doc_lengths,
    adapter_ids,
    attn_down,
    attn_up,
    fc1_down,
    fc1_up,
    fc2_down,
    fc2_up,
):
    tok_rows, model_width = tokens.shape
    adapter_count = attn_down.shape[1]
    rank_size = attn_down.shape[3]
    lane_count = adapter_count * rank_size
    seq_count = lax.axis_size("seq")
    geo = Geometry(tok_rows, model_width)
    seq_index = lax.axis_index("seq")
    part_index = seq_index // geo.groups
    head_index = seq_index % geo.groups
    lengths = doc_lengths[0]
    starts = jnp.cumsum(lengths) - lengths
    local_pos = seq_index * tok_rows + jnp.arange(tok_rows, dtype=jnp.int32)
    local_seg = segment_of(local_pos, starts)
    doc_range = jnp.arange(lengths.shape[0], dtype=jnp.int32)
    chosen = jnp.sum(
        jnp.where(local_seg[:, None] == doc_range[None, :], adapter_ids[0][None, :], 0), axis=1
    )
    lane_owner = jnp.arange(lane_count, dtype=jnp.int32) // rank_size
    select = (chosen[:, None] == lane_owner[None, :]).astype(jnp.float32)
    out_down = stack_down(attn_down[3])
    out_up = stack_up(attn_up[3])
    fc1_down_all = stack_down(fc1_down)
    fc1_up_all = stack_up(fc1_up)
    fc2_down_all = stack_down(fc2_down)
    fc2_up_all = stack_up(fc2_up)
    down_rows = jnp.transpose(attn_down, (0, 1, 3, 2)).reshape(4 * lane_count, model_width)
    up_rows = attn_up.reshape(4 * lane_count, model_width)
    weights = (w_out, w_fc1, w_fc2)
    inside = [v.shape[0] % (32 * seq_count) == 0 for v in weights]
    (attended_tok, q_heads, k_heads, v_heads, o_heads, lse_heads, w_slice, small_all), gathered = forward_attention(
        geo,
        rank_size,
        doc_lengths,
        adapter_ids,
        tokens,
        w_qkv,
        down_rows,
        up_rows,
        qv_bias,
        [v for v, here in zip(weights, inside) if here],
    )
    gathered = list(gathered)
    full_out, full_fc1, full_fc2 = [
        gathered.pop(0) if here else lax.all_gather(v, "wt", axis=0, tiled=True)
        for v, here in zip(weights, inside)
    ]
    out_main = jnp.dot(attended_tok, full_out, preferred_element_type=jnp.float32)
    small_out = (
        jnp.dot(attended_tok, out_down, preferred_element_type=jnp.float32) * select
    ).astype(jnp.bfloat16)
    z_value = out_main + out_bias + jnp.dot(small_out, out_up, preferred_element_type=jnp.float32)
    first_sum = tokens.astype(jnp.float32) + z_value
    first_norm, norm1_back = jax.vjp(
        lambda value: layer_norm(value, norm1_gain, norm1_bias), first_sum
    )
    first_low = first_norm.astype(jnp.bfloat16)
    fc1_main = jnp.dot(first_low, full_fc1, preferred_element_type=jnp.float32)
    small_fc1 = (
        jnp.dot(first_low, fc1_down_all, preferred_element_type=jnp.float32) * select
    ).astype(jnp.bfloat16)
    pre_act = (
        fc1_main + fc1_bias + jnp.dot(small_fc1, fc1_up_all, preferred_element_type=jnp.float32)
    )
    act_value, gelu_back = jax.vjp(gelu_exact, pre_act)
    act_low = act_value.astype(jnp.bfloat16)
    fc2_main = jnp.dot(act_low, full_fc2, preferred_element_type=jnp.float32)
    small_fc2 = (
        jnp.dot(act_low, fc2_down_all, preferred_element_type=jnp.float32) * select
    ).astype(jnp.bfloat16)
    y_value = (
        fc2_main + fc2_bias + jnp.dot(small_fc2, fc2_up_all, preferred_element_type=jnp.float32)
    )
    output, norm2_back = jax.vjp(
        lambda value: layer_norm(value, norm2_gain, norm2_bias), first_norm + y_value
    )
    d_second = norm2_back(cotangent.astype(jnp.float32))[0]
    d_y = d_second.astype(jnp.bfloat16)
    d_act = times_transposed(d_y, full_fc2)
    low_fc2 = (times_transposed(d_y, fc2_up_all) * select).astype(jnp.bfloat16)
    d_act = d_act + times_transposed(low_fc2, fc2_down_all)
    grad_fc2_up = left_inner(small_fc2, d_y)
    grad_fc2_down = left_inner(low_fc2, act_low)
    d_pre = gelu_back(d_act)[0].astype(jnp.bfloat16)
    d_first_low = times_transposed(d_pre, full_fc1)
    low_fc1 = (times_transposed(d_pre, fc1_up_all) * select).astype(jnp.bfloat16)
    d_first_low = d_first_low + times_transposed(low_fc1, fc1_down_all)
    grad_fc1_up = left_inner(small_fc1, d_pre)
    grad_fc1_down = left_inner(low_fc1, first_low)
    d_first = norm1_back(d_second + d_first_low)[0]
    d_z = d_first.astype(jnp.bfloat16)
    d_attended = times_transposed(d_z, full_out)
    low_out = (times_transposed(d_z, out_up) * select).astype(jnp.bfloat16)
    d_attended = (d_attended + times_transposed(low_out, out_down)).astype(jnp.bfloat16)
    grad_out_up = left_inner(small_out, d_z)
    grad_out_down = left_inner(low_out, attended_tok)
    blocks = [
        [p * geo.groups + i for i in range(geo.groups)] for p in range(geo.parts)
    ]
    d_heads = lax.all_to_all(
        d_attended.reshape(tok_rows, geo.groups, LANES),
        "seq",
        split_axis=1,
        concat_axis=0,
        axis_index_groups=blocks,
        tiled=True,
    ).reshape(geo.queries, LANES)
    d_q, d_k, d_v = backward_attention(
        geo, doc_lengths, part_index.reshape(1, 1), q_heads, k_heads, v_heads, o_heads, lse_heads, d_heads
    )
    set1 = [
        v.astype(BF16) for v in (grad_out_down, grad_out_up, grad_fc1_down, grad_fc2_up, grad_fc1_up, grad_fc2_down)
    ]
    input_grad, sum1, sum2, _ = closing(
        geo,
        rank_size,
        doc_lengths,
        adapter_ids,
        tokens,
        d_first,
        d_q,
        d_k,
        d_v,
        w_slice,
        down_rows,
        up_rows,
        small_all,
        set1,
    )

    down4, up4, fc1_down_sum, fc2_up_sum, fc1_up_sum, fc2_down_sum = unpack(geo, sum1, sum2, lane_count)

    def as_up(rows):
        return rows.reshape(rows.shape[:-2] + (adapter_count, rank_size, rows.shape[-1]))

    def as_down(rows):
        return jnp.swapaxes(as_up(rows), -1, -2)

    return (
        output,
        input_grad,
        as_down(down4),
        as_up(up4),
        as_down(fc1_down_sum),
        as_up(fc1_up_sum),
        as_down(fc2_down_sum),
        as_up(fc2_up_sum),
    )


def solution(mesh):
    placed = (
        P(("wt", "seq"), None),
        P(("wt", "seq"), None),
        P("wt", None),
        P(),
        P("wt", None),
        P(),
        P(),
        P(),
        P("wt", None),
        P(),
        P("wt", None),
        P(),
        P(),
        P(),
        P("wt", None),
        P("wt", None),
        P(),
        P(),
        P(),
        P(),
        P(),
        P(),
    )
    return jax.shard_map(
        shards,
        mesh=mesh,
        in_specs=placed,
        out_specs=(P(("wt", "seq"), None), P(("wt", "seq"), None), P(), P(), P(), P(), P(), P()),
        check_vma=False,
    )
```

```python
import functools

import jax
import jax.numpy as jnp
from jax import lax
from jax.experimental import pallas as pl
from jax.experimental.pallas import tpu as pltpu
from jax.sharding import PartitionSpec as P

HEADS = 16
HEAD_DIM = 64
LANES = 128
PAIR = LANES // HEAD_DIM
MESH = pl.DeviceIdType.MESH
F32 = jnp.float32
BF16 = jnp.bfloat16
VMEM_LIMIT = 60 * 2**20


def dot_nn(a, b):
    return lax.dot_general(a, b, (((1,), (0,)), ((), ())), preferred_element_type=F32)


def dot_nt(a, b):
    return lax.dot_general(a, b, (((1,), (1,)), ((), ())), preferred_element_type=F32)


def dot_tn(a, b):
    return lax.dot_general(a, b, (((0,), (0,)), ((), ())), preferred_element_type=F32)


class Geometry:
    def __init__(self, rows, width):
        self.seq = lax.axis_size("seq")
        self.wt = lax.axis_size("wt")
        self.rows = rows
        self.width = width
        self.groups = width // LANES
        self.parts = self.seq // self.groups
        chips = self.seq // 2
        nx = 1
        while nx * nx < chips:
            nx *= 2
        self.nx = nx
        self.ny = chips // nx
        self.keys = self.seq * rows
        self.queries = self.groups * rows


def doc_bounds(len_ref):
    count = len_ref.shape[1]
    starts, ends = [], []
    at = jnp.int32(0)
    for i in range(count):
        starts.append(at)
        at = at + len_ref[0, i]
        ends.append(at)
    return starts, ends


def segment_from(positions, starts):
    seg = jnp.zeros_like(positions)
    for start in starts[1:]:
        seg = seg + (positions >= start).astype(jnp.int32)
    return seg


def select_from(positions, starts, ends, id_ref, rank):
    owner = lax.broadcasted_iota(jnp.int32, positions.shape, 1) // rank
    picked = jnp.zeros(positions.shape, F32)
    for i in range(len(starts)):
        inside = (positions >= starts[i]) & (positions < ends[i]) & (owner == id_ref[0, i])
        picked = jnp.where(inside, 1.0, picked)
    return picked


class Spread:
    KINDS = 9

    def __init__(self, geo, here, region, send, recv, unit, first=0):
        self.geo, self.here, self.region = geo, here, region
        self.send, self.recv, self.unit, self.first = send, recv, unit, first

    def copy(self, kind, src, dst, x, y, core):
        return pltpu.make_async_remote_copy(
            src_ref=src,
            dst_ref=dst,
            send_sem=self.send.at[kind, self.unit],
            recv_sem=self.recv.at[kind, self.unit],
            device_id=(self.first + ((y * self.geo.nx) + x) * 2 + core, self.here[3]),
            device_id_type=MESH,
        )

    def others(self):
        nx, ny = self.geo.nx, self.geo.ny
        x, y, core, _ = self.here
        row = [((x + d) % nx, y) for d in range(1, nx)]
        col = [(x, (y + d) % ny) for d in range(1, ny)]
        return row, col

    def plan(self):
        x, y, core, _ = self.here
        row, col = self.others()
        plan = {kind: [] for kind in range(self.KINDS)}
        for tx, ty in row:
            plan[0].append(((x, y), None, (tx, ty, core)))
        for tx, ty in col:
            plan[1].append(((x, y), None, (tx, ty, core)))
        for ux, uy in row:
            for tx, ty in col:
                plan[2].append(((ux, uy), 0, (tx, ty, core)))
        for ux, uy in col:
            for tx, ty in row:
                plan[3].append(((ux, uy), 1, (tx, ty, core)))
        plan[4].append(((x, y), None, (x, y, 1 - core)))
        for ux, uy in row:
            plan[5].append(((ux, uy), None, (x, y, 1 - core)))
        for ux, uy in col:
            plan[6].append(((ux, uy), None, (x, y, 1 - core)))
        for ux, _ in row:
            for _, uy in col:
                plan[7].append(((ux, uy), 0, (x, y, 1 - core)))
                plan[8].append(((ux, uy), 1, (x, y, 1 - core)))
        return plan

    def go(self, kind, own=None):
        core = self.here[2]
        for (ux, uy), half, (tx, ty, tcore) in self.plan()[kind]:
            dst = self.region(ux, uy, core, half)
            src = dst if own is None else own
            self.copy(kind, src, dst, tx, ty, tcore).start()

    def arrivals(self, kind):
        x, y, core, _ = self.here
        row, col = self.others()
        if kind == 0:
            return [(u, None, core) for u in row]
        if kind == 1:
            return [(u, None, core) for u in col]
        if kind in (2, 3):
            return [((ux, uy), kind - 2, core) for ux, _ in row for _, uy in col]
        if kind == 4:
            return [((x, y), None, 1 - core)]
        if kind == 5:
            return [(u, None, 1 - core) for u in row]
        if kind == 6:
            return [(u, None, 1 - core) for u in col]
        return [((ux, uy), kind - 7, 1 - core) for ux, _ in row for _, uy in col]

    def wait(self, kind):
        x, y, core, _ = self.here
        for (ux, uy), half, whose in self.arrivals(kind):
            ref = self.region(ux, uy, whose, half)
            self.copy(kind, ref, ref, x, y, 1 - core).wait_recv()

    def wait_sends(self):
        x, y, core, _ = self.here
        for kind in range(self.KINDS):
            for (ux, uy), half, _ in self.plan()[kind]:
                ref = self.region(ux, uy, core, half)
                self.copy(kind, ref, ref, x, y, 1 - core).wait_send()


def device_here(geo):
    s = lax.axis_index("seq")
    core = s % 2
    chip = s // 2
    return chip % geo.nx, chip // geo.nx, core, lax.axis_index("wt")


def greet(geo):
    s, w = lax.axis_index("seq"), lax.axis_index("wt")
    barrier = pltpu.get_barrier_semaphore()
    for d in range(1, geo.seq):
        pl.semaphore_signal(barrier, inc=1, device_id=((s + d) % geo.seq, w), device_id_type=MESH)
    for d in range(1, geo.wt):
        pl.semaphore_signal(barrier, inc=1, device_id=(s, (w + d) % geo.wt), device_id_type=MESH)
    pl.semaphore_wait(barrier, geo.seq + geo.wt - 2)


def erf(v):
    v = jnp.clip(v, -3.832506856900711, 3.832506856900711)
    sq = v * v
    top = jnp.full_like(v, 0.00022905065861350646)
    for c in (0.0034082910107109506, 0.050955695062380861, 0.18520832239976145, 1.128379143519084):
        top = top * sq + c
    low = jnp.full_like(v, -1.1791602954361697e-7)
    for c in (0.000023547966471313185, 0.0010179625278914885, 0.014070470171167667, 0.11098505178285362, 0.49746925110067538, 1.0):
        low = low * sq + c
    return v * top / low


def normed(value):
    mean = jnp.mean(value, axis=1, keepdims=True)
    centred = value - mean
    spread = lax.rsqrt(jnp.mean(centred * centred, axis=1, keepdims=True) + 1e-05)
    return centred * spread, spread


def normed_back(grad, gain, unit, spread):
    g = grad * gain
    return spread * (
        g - jnp.mean(g, axis=1, keepdims=True) - unit * jnp.mean(g * unit, axis=1, keepdims=True)
    )


class Names:
    def __init__(self, names, refs):
        self.__dict__.update(zip(names, refs))


MLP_INPUTS = (
    "w_out", "w_fc1", "w_fc2", "cotangent", "out_bias", "gain1", "shift1", "fc1_bias", "fc2_bias", "gain2", "shift2",
    "fc1_down", "fc1_up", "fc2_down", "fc2_up",
)
BASE_OUTPUTS = ("q", "k", "v", "o", "lse", "w_slice", "small")
MLP_OUTPUTS = (
    "output", "d_first", "d_heads", "g_out_down", "g_out_up", "g_fc1_down", "g_fc2_up", "g_fc1_up", "g_fc2_down",
)
BASE_SCRATCH = (
    "tok", "seg", "att_send_buf", "local_sem", "send_sem", "recv_sem", "slice_send", "slice_recv", "line_send",
    "line_recv", "att_send", "att_recv",
)
MLP_SCRATCH = (
    "att", "full_out", "full_fc1", "full_fc2", "unit1", "h1", "h1_low", "act", "slope", "d_pre", "y", "d_att_buf",
    "back_send", "back_recv",
)


def forward_kernel(geo, inside, rank, len_ref, id_ref, tokens_ref, wqkv_ref, down_ref, up_ref, bias_ref, *refs):
    in_names = MLP_INPUTS if inside else ()
    out_names = BASE_OUTPUTS + (MLP_OUTPUTS if inside else ("att",))
    scratch_names = BASE_SCRATCH + (MLP_SCRATCH if inside else ())
    r = Names(in_names + out_names + scratch_names, refs)
    weights_in = (r.w_out, r.w_fc1, r.w_fc2) if inside else ()
    weights_out = (r.full_out, r.full_fc1, r.full_fc2) if inside else ()
    weight_count = len(weights_in)
    att_ref, q_ref, k_ref, v_ref, o_ref, lse_ref, slice_ref, small_ref = (
        r.att, r.q, r.k, r.v, r.o, r.lse, r.w_slice, r.small
    )
    tok_buf, seg_buf, att_buf, local_sem = r.tok, r.seg, r.att_send_buf, r.local_sem
    send_sem, recv_sem, slice_send, slice_recv = r.send_sem, r.recv_sem, r.slice_send, r.slice_recv
    line_send, line_recv, att_send, att_recv = r.line_send, r.line_recv, r.att_send, r.att_recv
    here = device_here(geo)
    x, y, core, w = here
    s = lax.axis_index("seq")
    part, g = s // geo.groups, s % geo.groups
    rows, width, wt = geo.rows, geo.width, geo.wt
    lanes = pl.ds(pl.multiple_of(g * LANES, LANES), LANES)

    own_tok = pltpu.make_async_copy(tokens_ref, tok_buf.at[s], local_sem.at[0])
    own_tok.start()
    shard = wqkv_ref.shape[0]
    own_slices = []
    for j in range(3):
        src = wqkv_ref.at[:, pl.ds(pl.multiple_of(j * width + g * LANES, LANES), LANES)]
        dst = slice_ref.at[pl.ds(pl.multiple_of(w * shard, shard), shard), pl.ds(j * LANES, LANES)]
        own_slices.append(pltpu.make_async_copy(src, dst, local_sem.at[1 + j]))
        own_slices[-1].start()
    own_weights = []
    for m in range(weight_count):
        height = weights_in[m].shape[0]
        dst = weights_out[m].at[pl.ds(pl.multiple_of(w * height, height), height)]
        own_weights.append(pltpu.make_async_copy(weights_in[m], dst, local_sem.at[4 + m]))
        own_weights[-1].start()

    greet(geo)

    def token_region(ux, uy, whose, half):
        block = tok_buf.at[(uy * geo.nx + ux) * 2 + whose]
        if half is None:
            return block
        return block.at[pl.ds(half * (rows // 2), rows // 2)]

    tok = Spread(geo, here, token_region, send_sem, recv_sem, 0)
    tok.go(0, own=tokens_ref)
    tok.go(1, own=tokens_ref)
    tok.go(4, own=tokens_ref)

    def slice_copy(j, d):
        src = wqkv_ref.at[:, pl.ds(pl.multiple_of(j * width + g * LANES, LANES), LANES)]
        dst = slice_ref.at[pl.ds(pl.multiple_of(w * shard, shard), shard), pl.ds(j * LANES, LANES)]
        return pltpu.make_async_remote_copy(
            src_ref=src,
            dst_ref=dst,
            send_sem=slice_send.at[j, d],
            recv_sem=slice_recv.at[j, d],
            device_id=(s, (w + d) % wt),
            device_id_type=MESH,
        )

    def slice_arrival(j, d):
        origin = (w + wt - d) % wt
        dst = slice_ref.at[pl.ds(pl.multiple_of(origin * shard, shard), shard), pl.ds(j * LANES, LANES)]
        return pltpu.make_async_remote_copy(
            src_ref=dst,
            dst_ref=dst,
            send_sem=slice_send.at[j, d],
            recv_sem=slice_recv.at[j, d],
            device_id=(s, origin),
            device_id_type=MESH,
        )

    for d in range(1, wt):
        for j in range(3):
            slice_copy(j, d).start()
    starts, ends = doc_bounds(len_ref)
    seg_buf[...] = segment_from(lax.broadcasted_iota(jnp.int32, seg_buf.shape, 1), starts)

    seq = geo.seq
    mine = s

    def unit_rows(m, p, unit, half=None):
        height = weights_in[m].shape[0]
        piece = height // seq
        if half is None:
            return weights_out[m].at[pl.ds(pl.multiple_of(p * height + unit * piece, piece), piece)]
        piece = piece // 2
        return weights_out[m].at[
            pl.ds(pl.multiple_of(p * height + unit * 2 * piece + half * piece, piece), piece)
        ]

    def line_copy(m, p, up, own):
        height = weights_in[m].shape[0]
        piece = height // seq
        dst = unit_rows(m, p, mine)
        src = weights_in[m].at[pl.ds(pl.multiple_of(mine * piece, piece), piece)] if own else dst
        target = w + 1 if up else w - 1
        return pltpu.make_async_remote_copy(
            src_ref=src,
            dst_ref=dst,
            send_sem=line_send.at[0 if up else 1, m * wt + p],
            recv_sem=line_recv.at[m * wt + p],
            device_id=(s, target),
            device_id_type=MESH,
        )

    def nth_plane(j):
        below, above = w, wt - 1 - w
        both = jnp.minimum(below, above)
        in_turn = j < 2 * both
        dist = jnp.where(in_turn, j // 2 + 1, j - both + 1)
        from_below = jnp.where(in_turn, j % 2 == 0, below > above)
        return jnp.where(from_below, w - dist, w + dist)

    def weight_spread(m, p):
        def region(ux, uy, whose, half):
            return unit_rows(m, p, (uy * geo.nx + ux) * 2 + whose, half)

        return Spread(geo, here, region, send_sem, recv_sem, 1 + m * wt + p)

    units = [(m, j) for m in range(weight_count) for j in range(wt - 1)]

    def start_lines():
        for m in range(weight_count):
            @pl.when(w < wt - 1)
            def _():
                line_copy(m, w, True, True).start()

            @pl.when(w > 0)
            def _():
                line_copy(m, w, False, True).start()

    def along(i):
        if i >= len(units):
            return
        m, j = units[i]
        p = nth_plane(j)
        line_copy(m, p, True, False).wait_recv()

        @pl.when((p < w) & (w < wt - 1))
        def _():
            line_copy(m, p, True, False).start()

        @pl.when((p > w) & (w > 0))
        def _():
            line_copy(m, p, False, False).start()

    ahead = 2

    def tick(i):
        if i == 0:
            for n in range(ahead):
                along(n)
        along(i + ahead)
        if i < len(units):
            m, j = units[i]
            spread = weight_spread(m, nth_plane(j))
            spread.go(0)
            spread.go(1)
            spread.go(4)
        if 0 <= i - 1 < len(units):
            m, j = units[i - 1]
            spread = weight_spread(m, nth_plane(j))
            spread.wait(0)
            spread.go(2)
            spread.go(5)
            spread.wait(1)
            spread.go(3)
            spread.go(6)
        if 0 <= i - 2 < len(units):
            m, j = units[i - 2]
            spread = weight_spread(m, nth_plane(j))
            spread.wait(2)
            spread.go(7)
            spread.wait(3)
            spread.go(8)

    tick_count = len(units) + 2 if units else 0

    def complete(m):
        own_weights[m].wait()
        for j in range(wt - 1):
            spread = weight_spread(m, nth_plane(j))
            for kind in range(4, 9):
                spread.wait(kind)

    nx, ny = geo.nx, geo.ny
    row_n, col_n, diag_n = 2 * (nx - 1), 2 * (ny - 1), 2 * (nx - 1) * (ny - 1)

    def block_owner(i):
        r = i - 2
        c = r - row_n
        d = c - col_n
        dx_row, k_row = r % max(nx - 1, 1) + 1, r // max(nx - 1, 1)
        dy_col, k_col = c % max(ny - 1, 1) + 1, c // max(ny - 1, 1)
        half = max(diag_n // 2, 1)
        k_diag, in_diag = d // half, d % half
        dx_diag, dy_diag = in_diag % max(nx - 1, 1) + 1, in_diag // max(nx - 1, 1) + 1
        dx = jnp.where(i < 2, 0, jnp.where(i < 2 + row_n, dx_row, jnp.where(i < 2 + row_n + col_n, 0, dx_diag)))
        dy = jnp.where(i < 2 + row_n, 0, jnp.where(i < 2 + row_n + col_n, dy_col, dy_diag))
        kk = jnp.where(i < 2, i, jnp.where(i < 2 + row_n, k_row, jnp.where(i < 2 + row_n + col_n, k_col, k_diag)))
        return (((y + dy) % ny) * nx + (x + dx) % nx) * 2 + (core + kk) % 2

    def project(i, carry):
        @pl.when(i == 0)
        def _():
            own_tok.wait()
            for copy in own_slices:
                copy.wait()
            for d in range(1, wt):
                for j in range(3):
                    slice_arrival(j, d).wait_recv()
            start_lines()

        @pl.when(i == 1)
        def _():
            tok.wait(4)

        @pl.when(i == 2)
        def _():
            tok.wait(0)
            tok.go(2)
            tok.go(5)
            tok.wait(1)
            tok.go(3)
            tok.go(6)

        @pl.when(i == 2 + row_n // 2)
        def _():
            tok.wait(5)

        @pl.when(i == 2 + row_n + col_n // 2)
        def _():
            tok.wait(6)

        @pl.when(i == 2 + row_n + col_n)
        def _():
            tok.wait(2)
            tok.go(7)
            tok.wait(3)
            tok.go(8)

        @pl.when(i == 2 + row_n + col_n + diag_n // 2)
        def _():
            tok.wait(7)
            tok.wait(8)

        t = block_owner(i)
        block = tok_buf[t]
        at = pl.ds(pl.multiple_of(t * rows, rows), rows)
        pos = t * rows + lax.broadcasted_iota(jnp.int32, (rows, LANES), 0)
        chosen = select_from(pos, starts, ends, id_ref, rank)
        main = dot_nn(block, slice_ref[...])
        small = dot_nt(block, down_ref[: 3 * LANES, :])
        for j in range(3):
            cut = slice(j * LANES, (j + 1) * LANES)
            low = (small[:, cut] * chosen).astype(BF16)
            small_ref[at, cut] = low
            value = main[:, cut] + dot_nn(low, up_ref[cut, lanes])
            if j == 0:
                value = value + bias_ref[0:1, lanes]

                @pl.when(t // geo.groups == part)
                def _():
                    inner = pl.ds(pl.multiple_of((t % geo.groups) * rows, rows), rows)
                    q_ref[inner, :] = value.astype(BF16)
            elif j == 1:
                k_ref[at, :] = value.astype(BF16)
            else:
                v_ref[at, :] = (value + bias_ref[1:2, lanes]).astype(BF16)
        return carry

    lax.fori_loop(0, geo.seq, project, 0)

    scale = HEAD_DIM ** (-0.5)
    chunk = min(2048, geo.keys)
    chunks = geo.keys // chunk
    first_head = lax.broadcasted_iota(jnp.int32, (rows, LANES), 1) < HEAD_DIM

    def att_copy(b):
        return pltpu.make_async_remote_copy(
            src_ref=att_buf.at[b],
            dst_ref=att_ref.at[:, lanes],
            send_sem=att_send.at[b],
            recv_sem=att_recv.at[g],
            device_id=(part * geo.groups + b, w),
            device_id_type=MESH,
        )

    def attend(i, carry):
        for n in range(min(tick_count, geo.groups // 2)):
            @pl.when(i == 2 * n + 1)
            def _():
                tick(n)

        b = (g + 1 + i) % geo.groups
        inner = pl.ds(pl.multiple_of(b * rows, rows), rows)
        query = q_ref[inner, :] * jnp.asarray(scale, BF16)
        q_pos = (part * geo.groups + b) * rows + lax.broadcasted_iota(jnp.int32, (rows, 1), 0)
        q_seg = segment_from(q_pos, starts)
        results = []
        for h in range(PAIR):
            mask = first_head if h == 0 else jnp.logical_not(first_head)
            q_head = jnp.where(mask, query, jnp.zeros_like(query))

            def one(c, state):
                top, total, acc = state
                keys_at = pl.ds(pl.multiple_of(c * chunk, chunk), chunk)
                score = dot_nt(q_head, k_ref[keys_at, :])
                score = jnp.where(q_seg == seg_buf[:, keys_at], score, -1e30)
                peak = jnp.max(score, axis=1, keepdims=True)
                if top is not None:
                    peak = jnp.maximum(top, peak)
                weight = jnp.exp(score - peak)
                add = jnp.sum(weight, axis=1, keepdims=True)
                out = dot_nn(weight.astype(BF16), v_ref[keys_at, :])
                if top is not None:
                    fade = jnp.exp(top - peak)
                    add = add + total * fade
                    out = out + acc * fade
                return peak, add, out

            state = one(0, (None, None, None))
            if chunks > 1:
                state = lax.fori_loop(1, chunks, one, state)
            top, total, acc = state
            results.append((acc / total, top + jnp.log(total)))
        out = jnp.where(first_head, results[0][0], results[1][0])
        o_ref[inner, :] = out
        lse_ref[inner, :] = jnp.where(first_head, results[0][1], results[1][1])
        att_buf[b] = out.astype(BF16)

        @pl.when(b != g)
        def _():
            att_copy(b).start()

        return carry

    lax.fori_loop(0, geo.groups, attend, 0)
    own_att = pltpu.make_async_copy(att_buf.at[g], att_ref.at[:, lanes], local_sem.at[0])
    own_att.start()

    def att_arrivals():
        for d in range(1, geo.groups):
            other = (g + d) % geo.groups
            cut = pl.ds(pl.multiple_of(other * LANES, LANES), LANES)
            pltpu.make_async_remote_copy(
                src_ref=att_ref.at[:, cut],
                dst_ref=att_ref.at[:, cut],
                send_sem=att_send.at[other],
                recv_sem=att_recv.at[other],
                device_id=(part * geo.groups + other, w),
                device_id_type=MESH,
            ).wait_recv()
        own_att.wait()

    ticked = min(tick_count, geo.groups // 2)
    if inside:
        layer_rest(geo, rank, r, starts, ends, id_ref, down_ref, up_ref, att_arrivals, complete, tick, ticked, tick_count)
    else:
        att_arrivals()

    for d in range(1, geo.groups):
        att_copy((g + d) % geo.groups).wait_send()
    tok.wait_sends()
    for d in range(1, wt):
        for j in range(3):
            slice_copy(j, d).wait_send()
    for m in range(weight_count):
        @pl.when(w < wt - 1)
        def _():
            line_copy(m, w, True, True).wait_send()

        @pl.when(w > 0)
        def _():
            line_copy(m, w, False, True).wait_send()

    for m, j in units:
        p = nth_plane(j)

        @pl.when((p < w) & (w < wt - 1))
        def _():
            line_copy(m, p, True, False).wait_send()

        @pl.when((p > w) & (w > 0))
        def _():
            line_copy(m, p, False, False).wait_send()

        weight_spread(m, p).wait_sends()


def layer_rest(geo, rank, r, starts, ends, id_ref, down_ref, up_ref, att_arrivals, complete, tick, ticked, tick_count):
    s, w = lax.axis_index("seq"), lax.axis_index("wt")
    rows, width, groups = geo.rows, geo.width, geo.groups
    part, g = s // groups, s % groups
    hidden = r.full_fc1.shape[1]
    step = min(512, hidden)
    steps = hidden // step
    band = 2 * LANES
    bands = width // band
    lane_count = r.fc1_down.shape[0]
    out_rows = slice(3 * lane_count, 4 * lane_count)
    pos = s * rows + lax.broadcasted_iota(jnp.int32, (rows, LANES), 0)
    chosen = select_from(pos, starts, ends, id_ref, rank)

    def masked(value):
        return (value * chosen).astype(BF16)

    def at_step(i):
        return pl.ds(pl.multiple_of(i * step, step), step)

    def at_band(i):
        return pl.ds(pl.multiple_of(i * band, band), band)

    pending = list(range(ticked, tick_count))
    first_ticks, pending = pending[:1], pending[1:]
    for n in first_ticks:
        tick(n)
    att_arrivals()
    complete(0)
    att = r.att[...]
    small_out = masked(dot_nt(att, down_ref[out_rows, :]))

    def out_band(i, carry):
        cut = at_band(i)
        value = dot_nn(r.att[...], r.full_out[:, cut]) + r.out_bias[:, cut]
        value = value + dot_nn(small_out, up_ref[out_rows, cut])
        r.y[:, cut] = value + r.tok[s, :, cut].astype(F32)
        return carry

    lax.fori_loop(0, bands, out_band, 0)
    unit1, spread1 = normed(r.y[...])
    h1 = unit1 * r.gain1[...] + r.shift1[...]
    r.unit1[...] = unit1
    r.h1[...] = h1
    h1_low = h1.astype(BF16)
    r.h1_low[...] = h1_low
    small_fc1 = masked(dot_nt(h1_low, r.fc1_down[...]))

    middle = max(len(pending) - 3, 0)
    for n in pending[:middle]:
        tick(n)
    pending = pending[middle:]
    complete(1)

    def fc1_step(i, acc):
        for n, t in enumerate(pending):
            @pl.when(i == min(2 * n + 1, steps - 1))
            def _():
                tick(t)

        cut = at_step(i)
        pre = dot_nn(r.h1_low[...], r.full_fc1[:, cut]) + r.fc1_bias[:, cut]
        pre = pre + dot_nn(small_fc1, r.fc1_up[:, cut])
        share = 0.5 + 0.5 * erf(pre * 0.7071067811865476)
        act = (pre * share).astype(BF16)
        r.act[:, cut] = act
        r.slope[:, cut] = share + pre * (jnp.exp(-0.5 * pre * pre) * 0.3989422804014327)
        return acc + dot_nt(act, r.fc2_down[:, cut])

    small_fc2 = masked(lax.fori_loop(0, steps, fc1_step, jnp.zeros((rows, lane_count), F32)))
    complete(2)

    def fc2_band(i, carry):
        cut = at_band(i)
        value = dot_nn(r.act[...], r.full_fc2[:, cut]) + r.fc2_bias[:, cut]
        r.y[:, cut] = value + dot_nn(small_fc2, r.fc2_up[:, cut]) + r.h1[:, cut]
        return carry

    lax.fori_loop(0, bands, fc2_band, 0)
    unit2, spread2 = normed(r.y[...])
    r.output[...] = unit2 * r.gain2[...] + r.shift2[...]
    d_second = normed_back(r.cotangent[...].astype(F32), r.gain2[...], unit2, spread2)
    r.y[...] = d_second
    d_y = d_second.astype(BF16)
    low_fc2 = masked(dot_nt(d_y, r.fc2_up[...]))
    r.g_fc2_up[...] = dot_tn(small_fc2, d_y).astype(BF16)

    def back_step(i, acc):
        cut = at_step(i)
        d_act = dot_nt(d_y, r.full_fc2[cut, :]) + dot_nn(low_fc2, r.fc2_down[:, cut])
        d_pre = (d_act * r.slope[:, cut]).astype(BF16)
        r.d_pre[:, cut] = d_pre
        r.g_fc2_down[:, cut] = dot_tn(low_fc2, r.act[:, cut]).astype(BF16)
        r.g_fc1_up[:, cut] = dot_tn(small_fc1, d_pre).astype(BF16)
        return acc + dot_nt(d_pre, r.fc1_up[:, cut])

    low_fc1 = masked(lax.fori_loop(0, steps, back_step, jnp.zeros((rows, lane_count), F32)))
    r.g_fc1_down[...] = dot_tn(low_fc1, r.h1_low[...]).astype(BF16)

    def back_band(i, carry):
        cut = at_band(i)
        value = dot_nt(r.d_pre[...], r.full_fc1[cut, :]) + dot_nn(low_fc1, r.fc1_down[:, cut])
        r.y[:, cut] += value
        return carry

    lax.fori_loop(0, bands, back_band, 0)
    d_first = normed_back(r.y[...], r.gain1[...], r.unit1[...], spread1)
    r.d_first[...] = d_first
    d_z = d_first.astype(BF16)
    low_out = masked(dot_nt(d_z, up_ref[out_rows, :]))

    def back_copy(b):
        return pltpu.make_async_remote_copy(
            src_ref=r.d_att_buf.at[b],
            dst_ref=r.d_heads.at[pl.ds(pl.multiple_of(g * rows, rows), rows)],
            send_sem=r.back_send.at[b],
            recv_sem=r.back_recv.at[g],
            device_id=(part * groups + b, w),
            device_id_type=MESH,
        )

    def attended_band(i, carry):
        n = (g // 2 + 1 + i) % bands
        cut = at_band(n)
        value = dot_nt(d_z, r.full_out[cut, :]) + dot_nn(low_out, down_ref[out_rows, cut])
        value = value.astype(BF16)
        for h in range(2):
            b = 2 * n + h
            r.d_att_buf[b] = value[:, h * LANES : (h + 1) * LANES]

            @pl.when(b != g)
            def _():
                back_copy(b).start()

        return carry

    lax.fori_loop(0, bands, attended_band, 0)
    own = pltpu.make_async_copy(
        r.d_att_buf.at[g], r.d_heads.at[pl.ds(pl.multiple_of(g * rows, rows), rows)], r.local_sem.at[0]
    )
    own.start()
    r.g_out_down[...] = dot_tn(low_out, r.att[...]).astype(BF16)
    r.g_out_up[...] = dot_tn(small_out, d_z).astype(BF16)
    for d in range(1, groups):
        other = (g + d) % groups
        here = r.d_heads.at[pl.ds(pl.multiple_of(other * rows, rows), rows)]
        pltpu.make_async_remote_copy(
            src_ref=here,
            dst_ref=here,
            send_sem=r.back_send.at[other],
            recv_sem=r.back_recv.at[other],
            device_id=(part * groups + other, w),
            device_id_type=MESH,
        ).wait_recv()
        back_copy(other).wait_send()
    own.wait()


def forward_attention(geo, rank, lengths, ids, tokens, w_qkv, down, up, bias, mlp):
    rows, width = geo.rows, geo.width
    inside = mlp is not None
    mlp = mlp or ()
    any_spec = pl.BlockSpec(memory_space=pl.ANY)
    vmem = pl.BlockSpec(memory_space=pltpu.VMEM)
    smem = pl.BlockSpec(memory_space=pltpu.SMEM)
    lane_count = down.shape[0] // 4
    struct = jax.ShapeDtypeStruct
    shapes = [
        struct((geo.queries, LANES), BF16),
        struct((geo.keys, LANES), BF16),
        struct((geo.keys, LANES), BF16),
        struct((geo.queries, LANES), F32),
        struct((geo.queries, LANES), F32),
        struct((width, 3 * LANES), BF16),
        struct((geo.keys, 3 * LANES), BF16),
    ]
    specs = [vmem] * 7
    dma = pltpu.SemaphoreType.DMA
    count = 3 if inside else 0
    units = 1 + count * geo.wt
    scratch = [
        pltpu.VMEM((geo.seq, rows, width), BF16),
        pltpu.VMEM((1, geo.keys), jnp.int32),
        pltpu.VMEM((geo.groups, rows, LANES), BF16),
        dma((4 + count,)),
        dma((Spread.KINDS, units)),
        dma((Spread.KINDS, units)),
        dma((3, geo.wt)),
        dma((3, geo.wt)),
        dma((2, max(count, 1) * geo.wt)),
        dma((max(count, 1) * geo.wt,)),
        dma((geo.groups,)),
        dma((geo.groups,)),
    ]
    if inside:
        hidden = mlp[1].shape[1]
        shapes += [
            struct((rows, width), F32),
            struct((rows, width), F32),
            struct((geo.queries, LANES), BF16),
            struct((lane_count, width), BF16),
            struct((lane_count, width), BF16),
            struct((lane_count, width), BF16),
            struct((lane_count, width), BF16),
            struct((lane_count, hidden), BF16),
            struct((lane_count, hidden), BF16),
        ]
        specs += [vmem, vmem, any_spec] + [vmem] * 6
        scratch += [
            pltpu.VMEM((rows, width), BF16),
            pltpu.VMEM((width, width), BF16),
            pltpu.VMEM((width, hidden), BF16),
            pltpu.VMEM((hidden, width), BF16),
            pltpu.VMEM((rows, width), F32),
            pltpu.VMEM((rows, width), F32),
            pltpu.VMEM((rows, width), BF16),
            pltpu.VMEM((rows, hidden), BF16),
            pltpu.VMEM((rows, hidden), F32),
            pltpu.VMEM((rows, hidden), BF16),
            pltpu.VMEM((rows, width), F32),
            pltpu.VMEM((geo.groups, rows, LANES), BF16),
            dma((geo.groups,)),
            dma((geo.groups,)),
        ]
    else:
        shapes += [struct((rows, width), BF16)]
        specs += [any_spec]
    return pl.pallas_call(
        functools.partial(forward_kernel, geo, inside, rank),
        out_shape=shapes,
        in_specs=[smem, smem, any_spec, any_spec, vmem, vmem, vmem] + [any_spec] * count + [vmem] * (len(mlp) - count),
        out_specs=specs,
        scratch_shapes=scratch,
        compiler_params=pltpu.CompilerParams(
            collective_id=0, has_side_effects=True, vmem_limit_bytes=VMEM_LIMIT
        ),
        name="layer",
    )(lengths, ids, tokens, w_qkv, down, up, bias, *mlp)


def backward_kernel(geo, len_ref, part_ref, q_ref, k_ref, v_ref, o_ref, lse_ref, g_ref, dq_ref, dk_ref, dv_ref, dk_acc, dv_acc):
    rows = geo.rows
    part = part_ref[0, 0]
    scale = HEAD_DIM ** (-0.5)
    starts, ends = doc_bounds(len_ref)
    first_head = lax.broadcasted_iota(jnp.int32, (rows, LANES), 1) < HEAD_DIM
    dk_acc[...] = jnp.zeros_like(dk_acc)
    dv_acc[...] = jnp.zeros_like(dv_acc)

    def seg_of(position):
        seg = jnp.int32(0)
        for start in starts[1:]:
            seg = seg + (position >= start).astype(jnp.int32)
        return seg

    def pick(values, index):
        found = values[0]
        for i in range(1, len(values)):
            found = jnp.where(index == i, values[i], found)
        return found

    def query_block(b, carry):
        at = pl.ds(pl.multiple_of(b * rows, rows), rows)
        origin = (part * geo.groups + b) * rows
        query = q_ref[at, :] * jnp.asarray(scale, BF16)
        cot = g_ref[at, :]
        lse = lse_ref[at, :]
        both = cot.astype(F32) * o_ref[at, :]
        q_pos = origin + lax.broadcasted_iota(jnp.int32, (rows, 1), 0)
        q_seg = segment_from(q_pos, starts)
        heads = []
        for h in range(PAIR):
            mask = first_head if h == 0 else jnp.logical_not(first_head)
            zero = jnp.zeros_like(query)
            heads.append(
                (
                    jnp.where(mask, query, zero),
                    jnp.where(mask, cot, zero),
                    lse[:, h * HEAD_DIM : h * HEAD_DIM + 1],
                    jnp.sum(jnp.where(mask, both, 0.0), axis=1, keepdims=True),
                )
            )
        low = pick(starts, seg_of(origin)) // rows
        high = (pick(ends, seg_of(origin + rows - 1)) + rows - 1) // rows

        def key_block(c, accs):
            keys_at = pl.ds(pl.multiple_of(c * rows, rows), rows)
            key, value = k_ref[keys_at, :], v_ref[keys_at, :]
            k_pos = c * rows + lax.broadcasted_iota(jnp.int32, (1, rows), 1)
            same = q_seg == segment_from(k_pos, starts)
            new = []
            dk_parts, dv_parts = [], []
            for h in range(PAIR):
                q_head, g_head, lse_head, dot_head = heads[h]
                score = jnp.where(same, dot_nt(q_head, key), -1e30)
                prob = jnp.exp(score - lse_head)
                d_prob = dot_nt(g_head, value)
                raw = (prob * (d_prob - dot_head) * scale).astype(BF16)
                new.append(accs[h] + dot_nn(raw, key))
                dk_parts.append(dot_tn(raw, q_head))
                dv_parts.append(dot_tn(prob.astype(BF16), g_head))
            dk_acc[keys_at, :] += dk_parts[0] + dk_parts[1]
            dv_acc[keys_at, :] += dv_parts[0] + dv_parts[1]
            return tuple(new)

        zero = jnp.zeros((rows, LANES), F32)
        accs = lax.fori_loop(low, high, key_block, (zero, zero))
        dq_ref[at, :] = jnp.where(first_head, accs[0], accs[1]).astype(BF16)
        return carry

    lax.fori_loop(0, geo.groups, query_block, 0)
    dk_ref[...] = (dk_acc[...] * HEAD_DIM**0.5).astype(BF16)
    dv_ref[...] = dv_acc[...].astype(BF16)


def backward_attention(geo, lengths, part, q, k, v, o, lse, d_heads):
    smem = pl.BlockSpec(memory_space=pltpu.SMEM)
    vmem = pl.BlockSpec(memory_space=pltpu.VMEM)
    return pl.pallas_call(
        functools.partial(backward_kernel, geo),
        out_shape=[
            jax.ShapeDtypeStruct((geo.queries, LANES), BF16),
            jax.ShapeDtypeStruct((geo.keys, LANES), BF16),
            jax.ShapeDtypeStruct((geo.keys, LANES), BF16),
        ],
        in_specs=[smem, smem] + [vmem] * 6,
        out_specs=[vmem] * 3,
        scratch_shapes=[pltpu.VMEM((geo.keys, LANES), F32)] * 2,
        compiler_params=pltpu.CompilerParams(vmem_limit_bytes=VMEM_LIMIT),
        name="attend_back",
    )(lengths, part, q, k, v, o, lse, d_heads)


class Block:
    def __init__(self, geo):
        chips = geo.groups // 2
        self.nx = min(geo.nx, chips)
        self.ny = chips // self.nx


class PairSum:
    def __init__(self, count, me, core, first, w, bufs, sems, make, stage=None):
        self.count, self.me, self.core, self.first, self.w = count, me, core, first, w
        self.near_out, self.near_in, self.far_in = bufs
        self.near_send, self.near_recv, self.far_send, self.far_recv = sems
        self.make = make
        self.slots = self.near_out.shape[0]
        self.stage = stage

    def slot(self, chip):
        return ((chip + self.count - self.me + self.count - 1) % self.count) % self.slots

    def near(self, chip):
        return pltpu.make_async_remote_copy(
            src_ref=self.near_out.at[self.slot(chip)],
            dst_ref=self.near_in.at[chip],
            send_sem=self.near_send.at[chip],
            recv_sem=self.near_recv.at[chip],
            device_id=(self.first + self.me * 2 + 1 - self.core, self.w),
            device_id_type=MESH,
        )

    def far(self, chip):
        return pltpu.make_async_remote_copy(
            src_ref=self.near_in.at[chip],
            dst_ref=self.far_in.at[self.me],
            send_sem=self.far_send.at[chip],
            recv_sem=self.far_recv.at[self.me],
            device_id=(self.first + chip * 2 + self.core, self.w),
            device_id_type=MESH,
        )

    def far_arrival(self, chip):
        return pltpu.make_async_remote_copy(
            src_ref=self.far_in.at[chip],
            dst_ref=self.far_in.at[chip],
            send_sem=self.far_send.at[chip],
            recv_sem=self.far_recv.at[chip],
            device_id=(self.first + chip * 2 + self.core, self.w),
            device_id_type=MESH,
        )

    def start(self):
        def step(d, carry):
            chip = (self.me + 1 + d) % self.count
            if self.slots < self.count:

                @pl.when(d >= self.slots)
                def _():
                    self.near((self.me + 1 + d - self.slots) % self.count).wait_send()

            self.near_out[d % self.slots] = self.make(chip, 1 - self.core).astype(BF16)
            self.near(chip).start()
            return carry

        lax.fori_loop(0, self.count, step, 0)

    def send(self):
        def step(d, carry):
            chip = (self.me + 1 + d) % self.count
            own = self.make(chip, self.core)
            self.near(chip).wait_recv()
            self.near_in[chip] = (own + self.near_in[chip].astype(F32)).astype(BF16)
            self.far(chip).start()
            return carry

        lax.fori_loop(0, self.count - 1, step, 0)

    def finish(self):
        total = self.make(self.me, self.core)
        self.near(self.me).wait_recv()
        total = total + self.near_in[self.me].astype(F32)
        if self.stage is None:
            for d in range(1, self.count):
                chip = (self.me + d) % self.count
                self.far_arrival(chip).wait_recv()
                total = total + self.far_in[chip].astype(F32)
            return total
        stage, sem = self.stage

        def fetch(d):
            chip = (self.me + d) % self.count
            return pltpu.make_async_copy(self.far_in.at[chip], stage.at[d % 2], sem.at[d % 2])

        self.far_arrival((self.me + 1) % self.count).wait_recv()
        fetch(1).start()
        for d in range(1, self.count):
            if d + 1 < self.count:
                self.far_arrival((self.me + d + 1) % self.count).wait_recv()
                fetch(d + 1).start()
            fetch(d).wait()
            total = total + stage[d % 2].astype(F32)
        return total

    def drain(self):
        for d in range(self.count):
            chip = (self.me + 1 + d) % self.count
            if d >= self.count - self.slots:
                self.near(chip).wait_send()
            if d < self.count - 1:
                self.far(chip).wait_send()


def closing_kernel(
    geo,
    rank,
    len_ref,
    id_ref,
    tokens_ref,
    first_ref,
    dq_ref,
    dk_ref,
    dv_ref,
    slice_ref,
    down_ref,
    up_ref,
    small_ref,
    out_down_ref,
    out_up_ref,
    fc1_down_ref,
    fc2_up_ref,
    fc1_up_ref,
    fc2_down_ref,
    grad_ref,
    sum1_ref,
    sum2_ref,
    tok_far,
    tok_out,
    tok_in,
    tok_stage,
    small_buf,
    set1_out,
    set1_in,
    set1_far,
    set2_out,
    set2_in,
    set2_far,
    down_acc,
    up_acc,
    mine1,
    mine2,
    place_buf,
    fold_buf,
    all1,
    all2,
    places,
    done1,
    done2,
    tok_sems,
    set1_sems,
    set2_sems,
    line_send,
    line_recv,
    spread_send,
    spread_recv,
    local_sem,
    stage_sem,
    small_sem,
):
    x, y, core, w = device_here(geo)
    s = lax.axis_index("seq")
    rows, width, wt, groups, parts = geo.rows, geo.width, geo.wt, geo.groups, geo.parts
    part, g = s // groups, s % groups
    docs = len_ref.shape[1]
    doc_rows = docs * rank
    lane_count = down_ref.shape[0] // 4
    lanes = pl.ds(pl.multiple_of(g * LANES, LANES), LANES)
    starts, ends = doc_bounds(len_ref)
    ids = [id_ref[0, d] for d in range(docs)]
    fresh = []
    for d in range(docs):
        seen = jnp.bool_(False)
        for e in range(d):
            seen = seen | (ids[e] == ids[d])
        fresh.append(jnp.where(seen, 0.0, 1.0))

    greet_all(geo)

    def iota(shape, dim):
        return lax.broadcasted_iota(jnp.int32, shape, dim)

    def zero_one(condition):
        return jnp.where(condition, 1.0, 0.0).astype(BF16)

    def chosen_of(t):
        pos = t * rows + iota((rows, LANES), 0)
        return select_from(pos, starts, ends, id_ref, rank)

    def fold(j):
        a, b = iota((lane_count, LANES), 0), iota((lane_count, LANES), 1)
        return zero_one((b >= j * rank) & (b < (j + 1) * rank) & (a % rank == b - j * rank))

    def make_tokens(chip, whose):
        t = chip * 2 + whose
        at = pl.ds(pl.multiple_of(t * rows, rows), rows)
        if parts == 1:
            d_q = dq_ref[at, :]
        else:
            inner = pl.ds(pl.multiple_of((t % groups) * rows, rows), rows)
            d_q = jnp.where(t // groups == part, dq_ref[inner, :], jnp.zeros((rows, LANES), BF16))
        pieces = [d_q, dk_ref[at, :], dv_ref[at, :]]
        chosen = chosen_of(t)
        total = jnp.zeros((rows, width), F32)
        low = jnp.zeros((rows, LANES), F32)
        for j in range(3):
            total = total + dot_nt(pieces[j], slice_ref[:, j * LANES : (j + 1) * LANES])
            part_low = dot_nt(pieces[j], up_ref[pl.ds(j * lane_count, lane_count), lanes])
            low = low + dot_nn((part_low * chosen).astype(BF16), fold(j))
        return jnp.concatenate([total, low], axis=1)

    tok = PairSum(
        geo.seq // 2, s // 2, core, 0, w, (tok_out, tok_in, tok_far), [tok_sems.at[i] for i in range(4)], make_tokens,
        (tok_stage, stage_sem),
    )

    singles = [out_down_ref, out_up_ref, fc1_down_ref, fc2_up_ref, fc1_up_ref, fc2_down_ref]

    def by_document(value):
        return dot_tn(fold_buf[...], value)[:doc_rows]

    def make_set1(chip, whose):
        owner = chip * 2 + whose
        cols = []
        for ref in singles:
            wide = ref.shape[1] // groups
            cols.append(by_document(ref[:, pl.ds(pl.multiple_of(owner * wide, LANES), wide)]))
        return jnp.concatenate(cols, axis=1)

    def make_set2(chip, whose):
        owner = chip * 2 + whose
        cut = pl.ds(pl.multiple_of(owner * LANES, LANES), LANES)
        return jnp.concatenate([down_acc[j * doc_rows : (j + 1) * doc_rows, cut] for j in range(3)], axis=1)

    chips = groups // 2
    set1 = PairSum(
        chips, g // 2, core, part * groups, w, (set1_out, set1_in, set1_far), [set1_sems.at[i] for i in range(4)], make_set1
    )
    set2 = PairSum(
        chips, g // 2, core, part * groups, w, (set2_out, set2_in, set2_far), [set2_sems.at[i] for i in range(4)], make_set2
    )

    def peer(n):
        plane = (w + n) % wt
        other = (part + n // wt) % parts
        return other * groups + g, plane, other * wt + plane

    mine_at = part * wt + w

    def line_copy(kind, n, src, dst_all):
        device, plane, _ = peer(n)
        return pltpu.make_async_remote_copy(
            src_ref=src,
            dst_ref=dst_all.at[mine_at],
            send_sem=line_send.at[kind, n],
            recv_sem=line_recv.at[kind, mine_at],
            device_id=(device, plane),
            device_id_type=MESH,
        )

    def line_arrival(kind, n, dst_all):
        device, plane, at = peer(n)
        return pltpu.make_async_remote_copy(
            src_ref=dst_all.at[at],
            dst_ref=dst_all.at[at],
            send_sem=line_send.at[kind, n],
            recv_sem=line_recv.at[kind, at],
            device_id=(device, plane),
            device_id_type=MESH,
        )

    peers = range(1, wt * parts)

    block = Block(geo)
    chip_here = g // 2
    here = (chip_here % block.nx, chip_here // block.nx, core, w)

    def region_of(ref):
        def region(ux, uy, whose, half):
            one = ref.at[(uy * block.nx + ux) * 2 + whose]
            if half is None:
                return one
            return one.at[pl.ds(half * (lane_count // 2), lane_count // 2)]

        return region

    spreads = [
        Spread(block, here, region_of(ref), spread_send, spread_recv, i, part * groups)
        for i, ref in enumerate((sum1_ref, sum2_ref))
    ]
    finals = [done1, done2]
    outs = [sum1_ref, sum2_ref]

    def place(kind, mine, dst_all):
        total = dot_nn(place_buf[:, :doc_rows], mine[...])
        for n in peers:
            line_arrival(kind, n, dst_all).wait_recv()
            if kind == 0:
                line_arrival(2, n, places).wait_recv()
            at = peer(n)[2]
            total = total + dot_nn(places[at][:, :doc_rows], dst_all[at])
        finals[kind][...] = total.astype(BF16)
        for way in (0, 1, 4):
            spreads[kind].go(way, own=finals[kind])
        pltpu.make_async_copy(finals[kind], outs[kind].at[g], local_sem.at[kind]).start()

    def pass_on(kind):
        spread = spreads[kind]
        spread.wait(0)
        spread.go(2)
        spread.go(5)
        spread.wait(1)
        spread.go(3)
        spread.go(6)

    def pass_last(kind):
        spread = spreads[kind]
        spread.wait(2)
        spread.go(7)
        spread.wait(3)
        spread.go(8)

    a, b = iota((lane_count, LANES), 0), iota((lane_count, LANES), 1)
    places_all = jnp.zeros((lane_count, LANES), F32)
    places_first = jnp.zeros((lane_count, LANES), F32)
    for d in range(docs):
        hit = (a // rank == ids[d]) & (b // rank == d) & (a % rank == b % rank)
        places_all = jnp.where(hit, 1.0, places_all)
        places_first = jnp.where(hit, fresh[d], places_first)
    place_buf[...] = places_all.astype(BF16)
    fold_buf[...] = places_first.astype(BF16)
    for n in peers:
        line_copy(2, n, place_buf, places).start()

    set1.start()
    tok.start()
    set1.send()
    tok.send()

    def small_copy(t):
        return pltpu.make_async_copy(
            small_ref.at[pl.ds(pl.multiple_of(t * rows, rows), rows)], small_buf.at[t % 2], small_sem.at[t % 2]
        )

    def add_up(t, carry):
        at = pl.ds(pl.multiple_of(t * rows, rows), rows)

        @pl.when(t + 1 < geo.seq)
        def _():
            small_copy(t + 1).start()

        small_copy(t).wait()
        for j in range(3):
            cut = slice(j * LANES, (j + 1) * LANES)
            if j == 0:
                if parts == 1:
                    value = dq_ref[at, :]
                else:
                    inner = pl.ds(pl.multiple_of((t % groups) * rows, rows), rows)
                    value = jnp.where(t // groups == part, dq_ref[inner, :], jnp.zeros((rows, LANES), BF16))
            else:
                value = (dk_ref if j == 1 else dv_ref)[at, :]
            up_acc[cut, :] += dot_tn(small_buf[t % 2][:, cut], value)
        return carry

    up_acc[...] = jnp.zeros_like(up_acc)
    small_copy(0).start()
    lax.fori_loop(0, geo.seq, add_up, 0)

    mine1[...] = set1.finish().astype(BF16)
    for n in peers:
        line_copy(0, n, mine1, all1).start()

    total = tok.finish()
    low = total[:, width:].astype(BF16)
    total = total[:, :width] + first_ref[...]
    chosen = chosen_of(s)
    pos = s * rows + iota((rows, doc_rows), 0)
    doc_of = iota((rows, doc_rows), 1) // rank
    in_doc = doc_of == segment_from(pos, starts)
    tokens = tokens_ref[...]
    for j in range(3):
        a, b = iota((LANES, lane_count), 0), iota((LANES, lane_count), 1)
        widen = zero_one((a >= j * rank) & (a < (j + 1) * rank) & (b % rank == a - j * rank))
        wide = (dot_nn(low, widen) * chosen).astype(BF16)
        total = total + dot_nn(wide, down_ref[j * lane_count : (j + 1) * lane_count, :])
        by_doc = dot_nn(low, widen[:, :doc_rows])
        by_doc = jnp.where(in_doc, by_doc, 0.0).astype(BF16)
        down_acc[j * doc_rows : (j + 1) * doc_rows, :] = dot_tn(by_doc, tokens)
    set2.start()
    grad_ref[...] = total
    set2.send()
    place(0, mine1, all1)
    for j in range(3):
        mine2[:, (3 + j) * LANES : (4 + j) * LANES] = by_document(
            up_acc[j * lane_count : (j + 1) * lane_count, :].astype(BF16)
        ).astype(BF16)
    mine2[:, : 3 * LANES] = set2.finish().astype(BF16)
    for n in peers:
        line_copy(1, n, mine2, all2).start()
    pass_on(0)
    pass_last(0)
    place(1, mine2, all2)
    pass_on(1)
    pass_last(1)
    for kind in range(2):
        for way in range(4, 9):
            spreads[kind].wait(way)
        spreads[kind].wait_sends()
        pltpu.make_async_copy(finals[kind], outs[kind].at[g], local_sem.at[kind]).wait()
    for n in peers:
        line_copy(0, n, mine1, all1).wait_send()
        line_copy(1, n, mine2, all2).wait_send()
        line_copy(2, n, place_buf, places).wait_send()
    tok.drain()
    set1.drain()
    set2.drain()


def greet_all(geo):
    s, w = lax.axis_index("seq"), lax.axis_index("wt")
    barrier = pltpu.get_barrier_semaphore()
    part, g = s // geo.groups, s % geo.groups
    for d in range(1, geo.seq):
        pl.semaphore_signal(barrier, inc=1, device_id=((s + d) % geo.seq, w), device_id_type=MESH)
    count = geo.seq - 1
    for d in range(1, geo.wt):
        for q in range(geo.parts):
            other = ((part + q) % geo.parts) * geo.groups + g
            pl.semaphore_signal(barrier, inc=1, device_id=(other, (w + d) % geo.wt), device_id_type=MESH)
            count += 1
    pl.semaphore_wait(barrier, count)


def closing(geo, rank, lengths, ids, tokens, d_first, dq, dk, dv, w_slice, down, up, small, grads):
    rows, width = geo.rows, geo.width
    docs = lengths.shape[1]
    doc_rows = docs * rank
    lane_count = down.shape[0] // 4
    set1 = sum(v.shape[1] for v in grads) // geo.groups
    set2 = 6 * LANES
    chips, near = geo.seq // 2, geo.groups // 2
    peers = geo.wt * geo.parts
    smem = pl.BlockSpec(memory_space=pltpu.SMEM)
    vmem = pl.BlockSpec(memory_space=pltpu.VMEM)
    any_spec = pl.BlockSpec(memory_space=pl.ANY)
    dma = pltpu.SemaphoreType.DMA
    wide = width + LANES
    return pl.pallas_call(
        functools.partial(closing_kernel, geo, rank),
        out_shape=[
            jax.ShapeDtypeStruct((rows, width), F32),
            jax.ShapeDtypeStruct((geo.groups, lane_count, set1), BF16),
            jax.ShapeDtypeStruct((geo.groups, lane_count, set2), BF16),
            jax.ShapeDtypeStruct((chips, rows, wide), BF16),
        ],
        in_specs=[smem, smem] + [vmem] * 8 + [any_spec] + [vmem] * len(grads),
        out_specs=[vmem, any_spec, any_spec, any_spec],
        scratch_shapes=[
            pltpu.VMEM((min(chips, 4), rows, wide), BF16),
            pltpu.VMEM((chips, rows, wide), BF16),
            pltpu.VMEM((2, rows, wide), BF16),
            pltpu.VMEM((2, rows, 3 * lane_count), BF16),
            pltpu.VMEM((near, doc_rows, set1), BF16),
            pltpu.VMEM((near, doc_rows, set1), BF16),
            pltpu.VMEM((near, doc_rows, set1), BF16),
            pltpu.VMEM((near, doc_rows, 3 * LANES), BF16),
            pltpu.VMEM((near, doc_rows, 3 * LANES), BF16),
            pltpu.VMEM((near, doc_rows, 3 * LANES), BF16),
            pltpu.VMEM((3 * doc_rows, width), F32),
            pltpu.VMEM((3 * lane_count, LANES), F32),
            pltpu.VMEM((doc_rows, set1), BF16),
            pltpu.VMEM((doc_rows, set2), BF16),
            pltpu.VMEM((lane_count, LANES), BF16),
            pltpu.VMEM((lane_count, LANES), BF16),
            pltpu.VMEM((peers, doc_rows, set1), BF16),
            pltpu.VMEM((peers, doc_rows, set2), BF16),
            pltpu.VMEM((peers, lane_count, LANES), BF16),
            pltpu.VMEM((lane_count, set1), BF16),
            pltpu.VMEM((lane_count, set2), BF16),
            dma((4, chips)),
            dma((4, near)),
            dma((4, near)),
            dma((3, peers)),
            dma((3, peers)),
            dma((Spread.KINDS, 2)),
            dma((Spread.KINDS, 2)),
            dma((2,)),
            dma((2,)),
            dma((2,)),
        ],
        compiler_params=pltpu.CompilerParams(
            collective_id=1, has_side_effects=True, vmem_limit_bytes=VMEM_LIMIT
        ),
        name="close",
    )(lengths, ids, tokens, d_first, dq, dk, dv, w_slice, down, up, small, *grads)


def unpack_kernel(one_ref, two_ref, down_ref, up_ref, fc1_down_ref, fc2_up_ref, fc1_up_ref, fc2_down_ref):
    for j in range(3):
        down_ref[j] = two_ref[0, :, j * LANES : (j + 1) * LANES].astype(F32)
        up_ref[j] = two_ref[0, :, (3 + j) * LANES : (4 + j) * LANES].astype(F32)
    at = 0
    for ref in (down_ref.at[3], up_ref.at[3], fc1_down_ref, fc2_up_ref, fc1_up_ref, fc2_down_ref):
        wide = ref.shape[1]
        ref[...] = one_ref[0, :, at : at + wide].astype(F32)
        at += wide


def unpack(geo, one, two, lane_count):
    groups = geo.groups
    thick = (one.shape[2] - 4 * LANES) // 2

    def whole(wide):
        return jax.ShapeDtypeStruct((lane_count, wide * groups), F32)

    def flat(wide):
        return pl.BlockSpec((lane_count, wide), lambda i: (0, i))

    four = jax.ShapeDtypeStruct((4, lane_count, LANES * groups), F32)
    four_spec = pl.BlockSpec((4, lane_count, LANES), lambda i: (0, 0, i))
    return pl.pallas_call(
        unpack_kernel,
        grid=(groups,),
        out_shape=[four, four, whole(LANES), whole(LANES), whole(thick), whole(thick)],
        in_specs=[
            pl.BlockSpec((1,) + one.shape[1:], lambda i: (i, 0, 0)),
            pl.BlockSpec((1,) + two.shape[1:], lambda i: (i, 0, 0)),
        ],
        out_specs=[four_spec, four_spec, flat(LANES), flat(LANES), flat(thick), flat(thick)],
        compiler_params=pltpu.CompilerParams(vmem_limit_bytes=VMEM_LIMIT // 2),
        name="unpack",
    )(one, two)


def layer_norm(value, gain, shift):
    mean = jnp.mean(value, axis=-1, keepdims=True)
    centred = value - mean
    spread = jnp.mean(centred * centred, axis=-1, keepdims=True)
    return centred * lax.rsqrt(spread + 1e-05) * gain + shift


def gelu_exact(value):
    return jax.nn.gelu(value, approximate=False)


def times_transposed(grad, weight):
    return lax.dot_general(
        grad, weight, (((1,), (1,)), ((), ())), preferred_element_type=jnp.float32
    )


def left_inner(left, right):
    return lax.dot_general(
        left, right, (((0,), (0,)), ((), ())), preferred_element_type=jnp.float32
    )


def stack_down(down):
    return jnp.transpose(down, (1, 0, 2)).reshape(down.shape[1], down.shape[0] * down.shape[2])


def stack_up(up):
    return up.reshape(up.shape[0] * up.shape[1], up.shape[2])


def unstack_down(stacked, adapter_count, rank_size):
    return jnp.transpose(stacked.reshape(stacked.shape[0], adapter_count, rank_size), (1, 0, 2))


def unstack_up(stacked, adapter_count, rank_size):
    return stacked.reshape(adapter_count, rank_size, stacked.shape[1])


def segment_of(positions, starts):
    return jnp.sum((positions[:, None] >= starts[None, :]).astype(jnp.int32), axis=1) - 1


def select_local(tok_rows, lane_count, rank_size, lengths, ids):
    starts = jnp.cumsum(lengths) - lengths
    local_pos = lax.axis_index("seq") * tok_rows + jnp.arange(tok_rows, dtype=jnp.int32)
    local_seg = segment_of(local_pos, starts)
    doc_range = jnp.arange(lengths.shape[0], dtype=jnp.int32)
    chosen = jnp.sum(jnp.where(local_seg[:, None] == doc_range[None, :], ids[None, :], 0), axis=1)
    lane_owner = jnp.arange(lane_count, dtype=jnp.int32) // rank_size
    return (chosen[:, None] == lane_owner[None, :]).astype(jnp.float32)


def feed_forward(
    geo, tokens, cotangent, attended_tok, weights, vectors, attn_maps, fc1_maps, fc2_maps, select
):
    tok_rows, model_width = tokens.shape
    full_out, full_fc1, full_fc2 = [lax.all_gather(v, "wt", axis=0, tiled=True) for v in weights]
    out_bias, norm1_gain, norm1_bias, fc1_bias, fc2_bias, norm2_gain, norm2_bias = vectors
    out_down, out_up = attn_maps
    fc1_down_all, fc1_up_all = fc1_maps
    fc2_down_all, fc2_up_all = fc2_maps
    out_main = jnp.dot(attended_tok, full_out, preferred_element_type=jnp.float32)
    small_out = (
        jnp.dot(attended_tok, out_down, preferred_element_type=jnp.float32) * select
    ).astype(jnp.bfloat16)
    z_value = out_main + out_bias + jnp.dot(small_out, out_up, preferred_element_type=jnp.float32)
    first_sum = tokens.astype(jnp.float32) + z_value
    first_norm, norm1_back = jax.vjp(
        lambda value: layer_norm(value, norm1_gain, norm1_bias), first_sum
    )
    first_low = first_norm.astype(jnp.bfloat16)
    fc1_main = jnp.dot(first_low, full_fc1, preferred_element_type=jnp.float32)
    small_fc1 = (
        jnp.dot(first_low, fc1_down_all, preferred_element_type=jnp.float32) * select
    ).astype(jnp.bfloat16)
    pre_act = (
        fc1_main + fc1_bias + jnp.dot(small_fc1, fc1_up_all, preferred_element_type=jnp.float32)
    )
    act_value, gelu_back = jax.vjp(gelu_exact, pre_act)
    act_low = act_value.astype(jnp.bfloat16)
    fc2_main = jnp.dot(act_low, full_fc2, preferred_element_type=jnp.float32)
    small_fc2 = (
        jnp.dot(act_low, fc2_down_all, preferred_element_type=jnp.float32) * select
    ).astype(jnp.bfloat16)
    y_value = (
        fc2_main + fc2_bias + jnp.dot(small_fc2, fc2_up_all, preferred_element_type=jnp.float32)
    )
    output, norm2_back = jax.vjp(
        lambda value: layer_norm(value, norm2_gain, norm2_bias), first_norm + y_value
    )
    d_second = norm2_back(cotangent.astype(jnp.float32))[0]
    d_y = d_second.astype(jnp.bfloat16)
    d_act = times_transposed(d_y, full_fc2)
    low_fc2 = (times_transposed(d_y, fc2_up_all) * select).astype(jnp.bfloat16)
    d_act = d_act + times_transposed(low_fc2, fc2_down_all)
    grad_fc2_up = left_inner(small_fc2, d_y)
    grad_fc2_down = left_inner(low_fc2, act_low)
    d_pre = gelu_back(d_act)[0].astype(jnp.bfloat16)
    d_first_low = times_transposed(d_pre, full_fc1)
    low_fc1 = (times_transposed(d_pre, fc1_up_all) * select).astype(jnp.bfloat16)
    d_first_low = d_first_low + times_transposed(low_fc1, fc1_down_all)
    grad_fc1_up = left_inner(small_fc1, d_pre)
    grad_fc1_down = left_inner(low_fc1, first_low)
    d_first = norm1_back(d_second + d_first_low)[0]
    d_z = d_first.astype(jnp.bfloat16)
    d_attended = times_transposed(d_z, full_out)
    low_out = (times_transposed(d_z, out_up) * select).astype(jnp.bfloat16)
    d_attended = (d_attended + times_transposed(low_out, out_down)).astype(jnp.bfloat16)
    grad_out_up = left_inner(small_out, d_z)
    grad_out_down = left_inner(low_out, attended_tok)
    blocks = [
        [p * geo.groups + i for i in range(geo.groups)] for p in range(geo.parts)
    ]
    d_heads = lax.all_to_all(
        d_attended.reshape(tok_rows, geo.groups, LANES),
        "seq",
        split_axis=1,
        concat_axis=0,
        axis_index_groups=blocks,
        tiled=True,
    ).reshape(geo.queries, LANES)
    grads = [grad_out_down, grad_out_up, grad_fc1_down, grad_fc2_up, grad_fc1_up, grad_fc2_down]
    return output, d_first, d_heads, [v.astype(BF16) for v in grads]


def shards(
    tokens,
    cotangent,
    w_qkv,
    qv_bias,
    w_out,
    out_bias,
    norm1_gain,
    norm1_bias,
    w_fc1,
    fc1_bias,
    w_fc2,
    fc2_bias,
    norm2_gain,
    norm2_bias,
    doc_lengths,
    adapter_ids,
    attn_down,
    attn_up,
    fc1_down,
    fc1_up,
    fc2_down,
    fc2_up,
):
    tok_rows, model_width = tokens.shape
    adapter_count = attn_down.shape[1]
    rank_size = attn_down.shape[3]
    lane_count = adapter_count * rank_size
    seq_count = lax.axis_size("seq")
    geo = Geometry(tok_rows, model_width)
    part_index = lax.axis_index("seq") // geo.groups
    down_rows = jnp.transpose(attn_down, (0, 1, 3, 2)).reshape(4 * lane_count, model_width)
    up_rows = attn_up.reshape(4 * lane_count, model_width)
    weights = (w_out, w_fc1, w_fc2)
    vectors = (out_bias, norm1_gain, norm1_bias, fc1_bias, fc2_bias, norm2_gain, norm2_bias)

    def rows_of(down):
        return jnp.swapaxes(down, 1, 2).reshape(lane_count, down.shape[1])

    inside = all(v.shape[0] % (32 * seq_count) == 0 for v in weights)
    mlp = None
    if inside:
        mlp = (
            weights
            + (cotangent,)
            + tuple(v.reshape(1, -1) for v in vectors)
            + (rows_of(fc1_down), stack_up(fc1_up), rows_of(fc2_down), stack_up(fc2_up))
        )
    q_heads, k_heads, v_heads, o_heads, lse_heads, w_slice, small_all, *rest = forward_attention(
        geo, rank_size, doc_lengths, adapter_ids, tokens, w_qkv, down_rows, up_rows, qv_bias, mlp
    )
    if inside:
        output, d_first, d_heads, *set1 = rest
    else:
        output, d_first, d_heads, set1 = feed_forward(
            geo,
            tokens,
            cotangent,
            rest[0],
            weights,
            vectors,
            (stack_down(attn_down[3]), stack_up(attn_up[3])),
            (stack_down(fc1_down), stack_up(fc1_up)),
            (stack_down(fc2_down), stack_up(fc2_up)),
            select_local(tok_rows, lane_count, rank_size, doc_lengths[0], adapter_ids[0]),
        )
    d_q, d_k, d_v = backward_attention(
        geo, doc_lengths, part_index.reshape(1, 1), q_heads, k_heads, v_heads, o_heads, lse_heads, d_heads
    )
    input_grad, sum1, sum2, _ = closing(
        geo,
        rank_size,
        doc_lengths,
        adapter_ids,
        tokens,
        d_first,
        d_q,
        d_k,
        d_v,
        w_slice,
        down_rows,
        up_rows,
        small_all,
        set1,
    )

    down4, up4, fc1_down_sum, fc2_up_sum, fc1_up_sum, fc2_down_sum = unpack(geo, sum1, sum2, lane_count)

    def as_up(rows):
        return rows.reshape(rows.shape[:-2] + (adapter_count, rank_size, rows.shape[-1]))

    def as_down(rows):
        return jnp.swapaxes(as_up(rows), -1, -2)

    return (
        output,
        input_grad,
        as_down(down4),
        as_up(up4),
        as_down(fc1_down_sum),
        as_up(fc1_up_sum),
        as_down(fc2_down_sum),
        as_up(fc2_up_sum),
    )


def solution(mesh):
    placed = (
        P(("wt", "seq"), None),
        P(("wt", "seq"), None),
        P("wt", None),
        P(),
        P("wt", None),
        P(),
        P(),
        P(),
        P("wt", None),
        P(),
        P("wt", None),
        P(),
        P(),
        P(),
        P("wt", None),
        P("wt", None),
        P(),
        P(),
        P(),
        P(),
        P(),
        P(),
    )
    return jax.shard_map(
        shards,
        mesh=mesh,
        in_specs=placed,
        out_specs=(P(("wt", "seq"), None), P(("wt", "seq"), None), P(), P(), P(), P(), P(), P()),
        check_vma=False,
    )
```

```python
import functools

import jax
import jax.numpy as jnp
from jax import lax
from jax.experimental import pallas as pl
from jax.experimental.pallas import tpu as pltpu
from jax.sharding import PartitionSpec as P

HEADS = 16
HEAD_DIM = 64
LANES = 128
PAIR = LANES // HEAD_DIM
MESH = pl.DeviceIdType.MESH
F32 = jnp.float32
BF16 = jnp.bfloat16
VMEM_LIMIT = 60 * 2**20


def dot_nn(a, b):
    return lax.dot_general(a, b, (((1,), (0,)), ((), ())), preferred_element_type=F32)


def dot_nt(a, b):
    return lax.dot_general(a, b, (((1,), (1,)), ((), ())), preferred_element_type=F32)


def dot_tn(a, b):
    return lax.dot_general(a, b, (((0,), (0,)), ((), ())), preferred_element_type=F32)


class Geometry:
    def __init__(self, rows, width):
        self.seq = lax.axis_size("seq")
        self.wt = lax.axis_size("wt")
        self.rows = rows
        self.width = width
        self.groups = width // LANES
        self.parts = self.seq // self.groups
        chips = self.seq // 2
        nx = 1
        while nx * nx < chips:
            nx *= 2
        self.nx = nx
        self.ny = chips // nx
        self.keys = self.seq * rows
        self.queries = self.groups * rows


def doc_bounds(len_ref):
    count = len_ref.shape[1]
    starts, ends = [], []
    at = jnp.int32(0)
    for i in range(count):
        starts.append(at)
        at = at + len_ref[0, i]
        ends.append(at)
    return starts, ends


def segment_from(positions, starts):
    seg = jnp.zeros_like(positions)
    for start in starts[1:]:
        seg = seg + (positions >= start).astype(jnp.int32)
    return seg


def select_from(positions, starts, ends, id_ref, rank):
    owner = lax.broadcasted_iota(jnp.int32, positions.shape, 1) // rank
    picked = jnp.zeros(positions.shape, F32)
    for i in range(len(starts)):
        inside = (positions >= starts[i]) & (positions < ends[i]) & (owner == id_ref[0, i])
        picked = jnp.where(inside, 1.0, picked)
    return picked


class Spread:
    KINDS = 9

    def __init__(self, geo, here, region, send, recv, unit, first=0):
        self.geo, self.here, self.region = geo, here, region
        self.send, self.recv, self.unit, self.first = send, recv, unit, first

    def copy(self, kind, src, dst, x, y, core):
        return pltpu.make_async_remote_copy(
            src_ref=src,
            dst_ref=dst,
            send_sem=self.send.at[kind, self.unit],
            recv_sem=self.recv.at[kind, self.unit],
            device_id=(self.first + ((y * self.geo.nx) + x) * 2 + core, self.here[3]),
            device_id_type=MESH,
        )

    def others(self):
        nx, ny = self.geo.nx, self.geo.ny
        x, y, core, _ = self.here
        row = [((x + d) % nx, y) for d in range(1, nx)]
        col = [(x, (y + d) % ny) for d in range(1, ny)]
        return row, col

    def plan(self):
        x, y, core, _ = self.here
        row, col = self.others()
        plan = {kind: [] for kind in range(self.KINDS)}
        for tx, ty in row:
            plan[0].append(((x, y), None, (tx, ty, core)))
        for tx, ty in col:
            plan[1].append(((x, y), None, (tx, ty, core)))
        for ux, uy in row:
            for tx, ty in col:
                plan[2].append(((ux, uy), 0, (tx, ty, core)))
        for ux, uy in col:
            for tx, ty in row:
                plan[3].append(((ux, uy), 1, (tx, ty, core)))
        plan[4].append(((x, y), None, (x, y, 1 - core)))
        for ux, uy in row:
            plan[5].append(((ux, uy), None, (x, y, 1 - core)))
        for ux, uy in col:
            plan[6].append(((ux, uy), None, (x, y, 1 - core)))
        for ux, _ in row:
            for _, uy in col:
                plan[7].append(((ux, uy), 0, (x, y, 1 - core)))
                plan[8].append(((ux, uy), 1, (x, y, 1 - core)))
        return plan

    def go(self, kind, own=None):
        core = self.here[2]
        for (ux, uy), half, (tx, ty, tcore) in self.plan()[kind]:
            dst = self.region(ux, uy, core, half)
            src = dst if own is None else own
            self.copy(kind, src, dst, tx, ty, tcore).start()

    def arrivals(self, kind):
        x, y, core, _ = self.here
        row, col = self.others()
        if kind == 0:
            return [(u, None, core) for u in row]
        if kind == 1:
            return [(u, None, core) for u in col]
        if kind in (2, 3):
            return [((ux, uy), kind - 2, core) for ux, _ in row for _, uy in col]
        if kind == 4:
            return [((x, y), None, 1 - core)]
        if kind == 5:
            return [(u, None, 1 - core) for u in row]
        if kind == 6:
            return [(u, None, 1 - core) for u in col]
        return [((ux, uy), kind - 7, 1 - core) for ux, _ in row for _, uy in col]

    def wait(self, kind):
        x, y, core, _ = self.here
        for (ux, uy), half, whose in self.arrivals(kind):
            ref = self.region(ux, uy, whose, half)
            self.copy(kind, ref, ref, x, y, 1 - core).wait_recv()

    def wait_sends(self):
        x, y, core, _ = self.here
        for kind in range(self.KINDS):
            for (ux, uy), half, _ in self.plan()[kind]:
                ref = self.region(ux, uy, core, half)
                self.copy(kind, ref, ref, x, y, 1 - core).wait_send()


def device_here(geo):
    s = lax.axis_index("seq")
    core = s % 2
    chip = s // 2
    return chip % geo.nx, chip // geo.nx, core, lax.axis_index("wt")


def greet(geo):
    s, w = lax.axis_index("seq"), lax.axis_index("wt")
    barrier = pltpu.get_barrier_semaphore()
    for d in range(1, geo.seq):
        pl.semaphore_signal(barrier, inc=1, device_id=((s + d) % geo.seq, w), device_id_type=MESH)
    for d in range(1, geo.wt):
        pl.semaphore_signal(barrier, inc=1, device_id=(s, (w + d) % geo.wt), device_id_type=MESH)
    pl.semaphore_wait(barrier, geo.seq + geo.wt - 2)


def erf(v):
    v = jnp.clip(v, -3.832506856900711, 3.832506856900711)
    sq = v * v
    top = jnp.full_like(v, 0.00022905065861350646)
    for c in (0.0034082910107109506, 0.050955695062380861, 0.18520832239976145, 1.128379143519084):
        top = top * sq + c
    low = jnp.full_like(v, -1.1791602954361697e-7)
    for c in (0.000023547966471313185, 0.0010179625278914885, 0.014070470171167667, 0.11098505178285362, 0.49746925110067538, 1.0):
        low = low * sq + c
    return v * top / low


def normed(value):
    mean = jnp.mean(value, axis=1, keepdims=True)
    centred = value - mean
    spread = lax.rsqrt(jnp.mean(centred * centred, axis=1, keepdims=True) + 1e-05)
    return centred * spread, spread


def normed_back(grad, gain, unit, spread):
    g = grad * gain
    return spread * (
        g - jnp.mean(g, axis=1, keepdims=True) - unit * jnp.mean(g * unit, axis=1, keepdims=True)
    )


class Names:
    def __init__(self, names, refs):
        self.__dict__.update(zip(names, refs))


MLP_INPUTS = (
    "w_out", "w_fc1", "w_fc2", "cotangent", "out_bias", "gain1", "shift1", "fc1_bias", "fc2_bias", "gain2", "shift2",
    "fc1_down", "fc1_up", "fc2_down", "fc2_up",
)
BASE_OUTPUTS = ("q", "k", "v", "o", "lse", "w_slice", "small")
MLP_OUTPUTS = (
    "output", "d_first", "d_heads", "g_out_down", "g_out_up", "g_fc1_down", "g_fc2_up", "g_fc1_up", "g_fc2_down",
)
BASE_SCRATCH = (
    "tok", "seg", "att_send_buf", "local_sem", "send_sem", "recv_sem", "slice_send", "slice_recv", "line_send",
    "line_recv", "att_send", "att_recv",
)
MLP_SCRATCH = (
    "att", "full_out", "full_fc1", "full_fc2", "unit1", "h1", "h1_low", "act", "slope", "d_pre", "y", "d_att_buf",
    "back_send", "back_recv",
)


def forward_kernel(geo, inside, rank, len_ref, id_ref, tokens_ref, wqkv_ref, down_ref, up_ref, bias_ref, *refs):
    in_names = MLP_INPUTS if inside else ()
    out_names = BASE_OUTPUTS + (MLP_OUTPUTS if inside else ("att",))
    scratch_names = BASE_SCRATCH + (MLP_SCRATCH if inside else ())
    r = Names(in_names + out_names + scratch_names, refs)
    weights_in = (r.w_out, r.w_fc1, r.w_fc2) if inside else ()
    weights_out = (r.full_out, r.full_fc1, r.full_fc2) if inside else ()
    weight_count = len(weights_in)
    att_ref, q_ref, k_ref, v_ref, o_ref, lse_ref, slice_ref, small_ref = (
        r.att, r.q, r.k, r.v, r.o, r.lse, r.w_slice, r.small
    )
    tok_buf, seg_buf, att_buf, local_sem = r.tok, r.seg, r.att_send_buf, r.local_sem
    send_sem, recv_sem, slice_send, slice_recv = r.send_sem, r.recv_sem, r.slice_send, r.slice_recv
    line_send, line_recv, att_send, att_recv = r.line_send, r.line_recv, r.att_send, r.att_recv
    here = device_here(geo)
    x, y, core, w = here
    s = lax.axis_index("seq")
    part, g = s // geo.groups, s % geo.groups
    rows, width, wt = geo.rows, geo.width, geo.wt
    lanes = pl.ds(pl.multiple_of(g * LANES, LANES), LANES)

    own_tok = pltpu.make_async_copy(tokens_ref, tok_buf.at[s], local_sem.at[0])
    own_tok.start()
    shard = wqkv_ref.shape[0]
    own_slices = []
    for j in range(3):
        src = wqkv_ref.at[:, pl.ds(pl.multiple_of(j * width + g * LANES, LANES), LANES)]
        dst = slice_ref.at[pl.ds(pl.multiple_of(w * shard, shard), shard), pl.ds(j * LANES, LANES)]
        own_slices.append(pltpu.make_async_copy(src, dst, local_sem.at[1 + j]))
        own_slices[-1].start()
    own_weights = []
    for m in range(weight_count):
        height = weights_in[m].shape[0]
        dst = weights_out[m].at[pl.ds(pl.multiple_of(w * height, height), height)]
        own_weights.append(pltpu.make_async_copy(weights_in[m], dst, local_sem.at[4 + m]))
        own_weights[-1].start()

    greet(geo)

    def token_region(ux, uy, whose, half):
        block = tok_buf.at[(uy * geo.nx + ux) * 2 + whose]
        if half is None:
            return block
        return block.at[pl.ds(half * (rows // 2), rows // 2)]

    tok = Spread(geo, here, token_region, send_sem, recv_sem, 0)
    tok.go(0, own=tokens_ref)
    tok.go(1, own=tokens_ref)
    tok.go(4, own=tokens_ref)

    def slice_copy(j, p, up):
        dst = slice_ref.at[pl.ds(pl.multiple_of(p * shard, shard), shard), pl.ds(j * LANES, LANES)]
        return pltpu.make_async_remote_copy(
            src_ref=dst,
            dst_ref=dst,
            send_sem=slice_send.at[0 if up else 1, j, p],
            recv_sem=slice_recv.at[j, p],
            device_id=(s, w + 1 if up else w - 1),
            device_id_type=MESH,
        )

    starts, ends = doc_bounds(len_ref)
    seg_buf[...] = segment_from(lax.broadcasted_iota(jnp.int32, seg_buf.shape, 1), starts)

    seq = geo.seq
    mine = s

    def unit_rows(m, p, unit, half=None):
        height = weights_in[m].shape[0]
        piece = height // seq
        if half is None:
            return weights_out[m].at[pl.ds(pl.multiple_of(p * height + unit * piece, piece), piece)]
        piece = piece // 2
        return weights_out[m].at[
            pl.ds(pl.multiple_of(p * height + unit * 2 * piece + half * piece, piece), piece)
        ]

    def line_copy(m, p, up, own):
        height = weights_in[m].shape[0]
        piece = height // seq
        dst = unit_rows(m, p, mine)
        src = weights_in[m].at[pl.ds(pl.multiple_of(mine * piece, piece), piece)] if own else dst
        target = w + 1 if up else w - 1
        return pltpu.make_async_remote_copy(
            src_ref=src,
            dst_ref=dst,
            send_sem=line_send.at[0 if up else 1, m * wt + p],
            recv_sem=line_recv.at[m * wt + p],
            device_id=(s, target),
            device_id_type=MESH,
        )

    def nth_plane(j):
        below, above = w, wt - 1 - w
        both = jnp.minimum(below, above)
        in_turn = j < 2 * both
        dist = jnp.where(in_turn, j // 2 + 1, j - both + 1)
        from_below = jnp.where(in_turn, j % 2 == 0, below > above)
        return jnp.where(from_below, w - dist, w + dist)

    def weight_spread(m, p):
        def region(ux, uy, whose, half):
            return unit_rows(m, p, (uy * geo.nx + ux) * 2 + whose, half)

        return Spread(geo, here, region, send_sem, recv_sem, 1 + m * wt + p)

    units = []
    if inside:
        units = [(m, j) for j in range(wt - 1) for m in (0, 1)] + [(2, j) for j in range(wt - 1)]

    def start_lines(which):
        for m in which if inside else ():

            @pl.when(w < wt - 1)
            def _():
                line_copy(m, w, True, True).start()

            @pl.when(w > 0)
            def _():
                line_copy(m, w, False, True).start()

    def along(i):
        if i >= len(units):
            return
        m, j = units[i]
        p = nth_plane(j)
        line_copy(m, p, True, False).wait_recv()

        @pl.when((p < w) & (w < wt - 1))
        def _():
            line_copy(m, p, True, False).start()

        @pl.when((p > w) & (w > 0))
        def _():
            line_copy(m, p, False, False).start()

    def tick(i):
        if i == 0:
            along(0)
        if i == late_lines:
            start_lines((2,))
        if i < len(units):
            m, j = units[i]
            spread = weight_spread(m, nth_plane(j))
            spread.go(0)
            spread.go(1)
            spread.go(4)
        along(i + 1)
        if 0 <= i - 1 < len(units):
            m, j = units[i - 1]
            spread = weight_spread(m, nth_plane(j))
            spread.wait(0)
            spread.go(2)
            spread.go(5)
            spread.wait(1)
            spread.go(3)
            spread.go(6)
        if 0 <= i - 2 < len(units):
            m, j = units[i - 2]
            spread = weight_spread(m, nth_plane(j))
            spread.wait(2)
            spread.go(7)
            spread.wait(3)
            spread.go(8)

    tick_count = len(units) + 2 if units else 0
    late_lines = 0
    early_ticks = min(3, tick_count)
    loop_ticks = min(6, tick_count)

    def complete(m):
        own_weights[m].wait()
        for j in range(wt - 1):
            spread = weight_spread(m, nth_plane(j))
            for kind in range(4, 9):
                spread.wait(kind)

    for copy in own_slices:
        copy.wait()
    for j in range(3):

        @pl.when(w < wt - 1)
        def _():
            slice_copy(j, w, True).start()

        @pl.when(w > 0)
        def _():
            slice_copy(j, w, False).start()

    nx, ny = geo.nx, geo.ny
    row_n, col_n, diag_n = 2 * (nx - 1), 2 * (ny - 1), 2 * (nx - 1) * (ny - 1)

    def block_owner(i):
        r = i - 2
        c = r - row_n
        d = c - col_n
        dx_row, k_row = r % max(nx - 1, 1) + 1, r // max(nx - 1, 1)
        dy_col, k_col = c % max(ny - 1, 1) + 1, c // max(ny - 1, 1)
        half = max(diag_n // 2, 1)
        k_diag, in_diag = d // half, d % half
        dx_diag, dy_diag = in_diag % max(nx - 1, 1) + 1, in_diag // max(nx - 1, 1) + 1
        dx = jnp.where(i < 2, 0, jnp.where(i < 2 + row_n, dx_row, jnp.where(i < 2 + row_n + col_n, 0, dx_diag)))
        dy = jnp.where(i < 2 + row_n, 0, jnp.where(i < 2 + row_n + col_n, dy_col, dy_diag))
        kk = jnp.where(i < 2, i, jnp.where(i < 2 + row_n, k_row, jnp.where(i < 2 + row_n + col_n, k_col, k_diag)))
        return (((y + dy) % ny) * nx + (x + dx) % nx) * 2 + (core + kk) % 2

    def project(i, carry):
        @pl.when(i == 0)
        def _():
            start_lines((0, 1))
            for n in range(wt - 1):
                p = nth_plane(n)
                for j in range(3):
                    slice_copy(j, p, True).wait_recv()

                    @pl.when((p < w) & (w < wt - 1))
                    def _():
                        slice_copy(j, p, True).start()

                    @pl.when((p > w) & (w > 0))
                    def _():
                        slice_copy(j, p, False).start()

            own_tok.wait()

        @pl.when(i == 1)
        def _():
            tok.wait(4)

        @pl.when(i == 2)
        def _():
            tok.wait(0)
            tok.go(2)
            tok.go(5)
            tok.wait(1)
            tok.go(3)
            tok.go(6)

        @pl.when(i == 2 + row_n // 2)
        def _():
            tok.wait(5)

        @pl.when(i == 2 + row_n + col_n // 2)
        def _():
            tok.wait(6)

        @pl.when(i == 2 + row_n + col_n)
        def _():
            tok.wait(2)
            tok.go(7)
            tok.wait(3)
            tok.go(8)

        @pl.when(i == 2 + row_n + col_n + diag_n // 2)
        def _():
            tok.wait(7)
            tok.wait(8)

        for n in range(early_ticks):

            @pl.when(i == min(3 + 2 * n, geo.seq - 1))
            def _():
                tick(n)

        t = block_owner(i)
        block = tok_buf[t]
        at = pl.ds(pl.multiple_of(t * rows, rows), rows)
        pos = t * rows + lax.broadcasted_iota(jnp.int32, (rows, LANES), 0)
        chosen = select_from(pos, starts, ends, id_ref, rank)
        main = dot_nn(block, slice_ref[...])
        small = dot_nt(block, down_ref[: 3 * LANES, :])
        for j in range(3):
            cut = slice(j * LANES, (j + 1) * LANES)
            low = (small[:, cut] * chosen).astype(BF16)
            small_ref[at, cut] = low
            value = main[:, cut] + dot_nn(low, up_ref[cut, lanes])
            if j == 0:
                value = value + bias_ref[0:1, lanes]

                @pl.when(t // geo.groups == part)
                def _():
                    inner = pl.ds(pl.multiple_of((t % geo.groups) * rows, rows), rows)
                    q_ref[inner, :] = value.astype(BF16)
            elif j == 1:
                k_ref[at, :] = value.astype(BF16)
            else:
                v_ref[at, :] = (value + bias_ref[1:2, lanes]).astype(BF16)
        return carry

    lax.fori_loop(0, geo.seq, project, 0)

    scale = HEAD_DIM ** (-0.5)
    chunk = min(2048, geo.keys)
    chunks = geo.keys // chunk
    first_head = lax.broadcasted_iota(jnp.int32, (rows, LANES), 1) < HEAD_DIM

    def att_copy(b):
        return pltpu.make_async_remote_copy(
            src_ref=att_buf.at[b],
            dst_ref=att_ref.at[:, lanes],
            send_sem=att_send.at[b],
            recv_sem=att_recv.at[g],
            device_id=(part * geo.groups + b, w),
            device_id_type=MESH,
        )

    def attend(i, carry):
        for n in range(early_ticks, loop_ticks):

            @pl.when(i == 2 * (n - early_ticks) + 1)
            def _():
                tick(n)

        b = (g + 1 + i) % geo.groups
        inner = pl.ds(pl.multiple_of(b * rows, rows), rows)
        query = q_ref[inner, :] * jnp.asarray(scale, BF16)
        q_pos = (part * geo.groups + b) * rows + lax.broadcasted_iota(jnp.int32, (rows, 1), 0)
        q_seg = segment_from(q_pos, starts)
        results = []
        for h in range(PAIR):
            mask = first_head if h == 0 else jnp.logical_not(first_head)
            q_head = jnp.where(mask, query, jnp.zeros_like(query))

            def one(c, state):
                top, total, acc = state
                keys_at = pl.ds(pl.multiple_of(c * chunk, chunk), chunk)
                score = dot_nt(q_head, k_ref[keys_at, :])
                score = jnp.where(q_seg == seg_buf[:, keys_at], score, -1e30)
                peak = jnp.max(score, axis=1, keepdims=True)
                if top is not None:
                    peak = jnp.maximum(top, peak)
                weight = jnp.exp(score - peak)
                add = jnp.sum(weight, axis=1, keepdims=True)
                out = dot_nn(weight.astype(BF16), v_ref[keys_at, :])
                if top is not None:
                    fade = jnp.exp(top - peak)
                    add = add + total * fade
                    out = out + acc * fade
                return peak, add, out

            state = one(0, (None, None, None))
            if chunks > 1:
                state = lax.fori_loop(1, chunks, one, state)
            top, total, acc = state
            results.append((acc / total, top + jnp.log(total)))
        out = jnp.where(first_head, results[0][0], results[1][0])
        o_ref[inner, :] = out
        lse_ref[inner, :] = jnp.where(first_head, results[0][1], results[1][1])
        att_buf[b] = out.astype(BF16)

        @pl.when(b != g)
        def _():
            att_copy(b).start()

        return carry

    lax.fori_loop(0, geo.groups, attend, 0)
    own_att = pltpu.make_async_copy(att_buf.at[g], att_ref.at[:, lanes], local_sem.at[0])
    own_att.start()

    def att_arrivals():
        for d in range(1, geo.groups):
            other = (g + d) % geo.groups
            cut = pl.ds(pl.multiple_of(other * LANES, LANES), LANES)
            pltpu.make_async_remote_copy(
                src_ref=att_ref.at[:, cut],
                dst_ref=att_ref.at[:, cut],
                send_sem=att_send.at[other],
                recv_sem=att_recv.at[other],
                device_id=(part * geo.groups + other, w),
                device_id_type=MESH,
            ).wait_recv()
        own_att.wait()

    if inside:
        layer_rest(geo, rank, r, starts, ends, id_ref, down_ref, up_ref, att_arrivals, complete, tick, loop_ticks, tick_count)
    else:
        att_arrivals()

    for d in range(1, geo.groups):
        att_copy((g + d) % geo.groups).wait_send()
    tok.wait_sends()
    for j in range(3):

        @pl.when(w < wt - 1)
        def _():
            slice_copy(j, w, True).wait_send()

        @pl.when(w > 0)
        def _():
            slice_copy(j, w, False).wait_send()

        for n in range(wt - 1):
            p = nth_plane(n)

            @pl.when((p < w) & (w < wt - 1))
            def _():
                slice_copy(j, p, True).wait_send()

            @pl.when((p > w) & (w > 0))
            def _():
                slice_copy(j, p, False).wait_send()

    for m in range(weight_count):
        @pl.when(w < wt - 1)
        def _():
            line_copy(m, w, True, True).wait_send()

        @pl.when(w > 0)
        def _():
            line_copy(m, w, False, True).wait_send()

    for m, j in units:
        p = nth_plane(j)

        @pl.when((p < w) & (w < wt - 1))
        def _():
            line_copy(m, p, True, False).wait_send()

        @pl.when((p > w) & (w > 0))
        def _():
            line_copy(m, p, False, False).wait_send()

        weight_spread(m, p).wait_sends()


def layer_rest(geo, rank, r, starts, ends, id_ref, down_ref, up_ref, att_arrivals, complete, tick, ticked, tick_count):
    s, w = lax.axis_index("seq"), lax.axis_index("wt")
    rows, width, groups = geo.rows, geo.width, geo.groups
    part, g = s // groups, s % groups
    hidden = r.full_fc1.shape[1]
    step = min(512, hidden)
    steps = hidden // step
    band = 2 * LANES
    bands = width // band
    lane_count = r.fc1_down.shape[0]
    out_rows = slice(3 * lane_count, 4 * lane_count)
    pos = s * rows + lax.broadcasted_iota(jnp.int32, (rows, LANES), 0)
    chosen = select_from(pos, starts, ends, id_ref, rank)

    def masked(value):
        return (value * chosen).astype(BF16)

    def at_step(i):
        return pl.ds(pl.multiple_of(i * step, step), step)

    def at_band(i):
        return pl.ds(pl.multiple_of(i * band, band), band)

    pending = list(range(ticked, tick_count))
    first_ticks, pending = pending[:1], pending[1:]
    for n in first_ticks:
        tick(n)
    att_arrivals()
    complete(0)
    att = r.att[...]
    small_out = masked(dot_nt(att, down_ref[out_rows, :]))

    def out_band(i, carry):
        cut = at_band(i)
        value = dot_nn(r.att[...], r.full_out[:, cut]) + r.out_bias[:, cut]
        value = value + dot_nn(small_out, up_ref[out_rows, cut])
        r.y[:, cut] = value + r.tok[s, :, cut].astype(F32)
        return carry

    lax.fori_loop(0, bands, out_band, 0)
    unit1, spread1 = normed(r.y[...])
    h1 = unit1 * r.gain1[...] + r.shift1[...]
    r.unit1[...] = unit1
    r.h1[...] = h1
    h1_low = h1.astype(BF16)
    r.h1_low[...] = h1_low
    small_fc1 = masked(dot_nt(h1_low, r.fc1_down[...]))

    middle = max(len(pending) - 3, 0)
    for n in pending[:middle]:
        tick(n)
    pending = pending[middle:]
    complete(1)

    def fc1_step(i, acc):
        for n, t in enumerate(pending):
            @pl.when(i == min(2 * n + 1, steps - 1))
            def _():
                tick(t)

        cut = at_step(i)
        pre = dot_nn(r.h1_low[...], r.full_fc1[:, cut]) + r.fc1_bias[:, cut]
        pre = pre + dot_nn(small_fc1, r.fc1_up[:, cut])
        share = 0.5 + 0.5 * erf(pre * 0.7071067811865476)
        act = (pre * share).astype(BF16)
        r.act[:, cut] = act
        r.slope[:, cut] = share + pre * (jnp.exp(-0.5 * pre * pre) * 0.3989422804014327)
        return acc + dot_nt(act, r.fc2_down[:, cut])

    small_fc2 = masked(lax.fori_loop(0, steps, fc1_step, jnp.zeros((rows, lane_count), F32)))
    complete(2)

    def fc2_band(i, carry):
        cut = at_band(i)
        value = dot_nn(r.act[...], r.full_fc2[:, cut]) + r.fc2_bias[:, cut]
        r.y[:, cut] = value + dot_nn(small_fc2, r.fc2_up[:, cut]) + r.h1[:, cut]
        return carry

    lax.fori_loop(0, bands, fc2_band, 0)
    unit2, spread2 = normed(r.y[...])
    r.output[...] = unit2 * r.gain2[...] + r.shift2[...]
    d_second = normed_back(r.cotangent[...].astype(F32), r.gain2[...], unit2, spread2)
    r.y[...] = d_second
    d_y = d_second.astype(BF16)
    low_fc2 = masked(dot_nt(d_y, r.fc2_up[...]))
    r.g_fc2_up[...] = dot_tn(small_fc2, d_y).astype(BF16)

    def back_step(i, acc):
        cut = at_step(i)
        d_act = dot_nt(d_y, r.full_fc2[cut, :]) + dot_nn(low_fc2, r.fc2_down[:, cut])
        d_pre = (d_act * r.slope[:, cut]).astype(BF16)
        r.d_pre[:, cut] = d_pre
        r.g_fc2_down[:, cut] = dot_tn(low_fc2, r.act[:, cut]).astype(BF16)
        r.g_fc1_up[:, cut] = dot_tn(small_fc1, d_pre).astype(BF16)
        return acc + dot_nt(d_pre, r.fc1_up[:, cut])

    low_fc1 = masked(lax.fori_loop(0, steps, back_step, jnp.zeros((rows, lane_count), F32)))
    r.g_fc1_down[...] = dot_tn(low_fc1, r.h1_low[...]).astype(BF16)

    def back_band(i, carry):
        cut = at_band(i)
        value = dot_nt(r.d_pre[...], r.full_fc1[cut, :]) + dot_nn(low_fc1, r.fc1_down[:, cut])
        r.y[:, cut] += value
        return carry

    lax.fori_loop(0, bands, back_band, 0)
    d_first = normed_back(r.y[...], r.gain1[...], r.unit1[...], spread1)
    r.d_first[...] = d_first
    d_z = d_first.astype(BF16)
    low_out = masked(dot_nt(d_z, up_ref[out_rows, :]))

    def back_copy(b):
        return pltpu.make_async_remote_copy(
            src_ref=r.d_att_buf.at[b],
            dst_ref=r.d_heads.at[pl.ds(pl.multiple_of(g * rows, rows), rows)],
            send_sem=r.back_send.at[b],
            recv_sem=r.back_recv.at[g],
            device_id=(part * groups + b, w),
            device_id_type=MESH,
        )

    def attended_band(i, carry):
        n = (g // 2 + 1 + i) % bands
        cut = at_band(n)
        value = dot_nt(d_z, r.full_out[cut, :]) + dot_nn(low_out, down_ref[out_rows, cut])
        value = value.astype(BF16)
        for h in range(2):
            b = 2 * n + h
            r.d_att_buf[b] = value[:, h * LANES : (h + 1) * LANES]

            @pl.when(b != g)
            def _():
                back_copy(b).start()

        return carry

    lax.fori_loop(0, bands, attended_band, 0)
    own = pltpu.make_async_copy(
        r.d_att_buf.at[g], r.d_heads.at[pl.ds(pl.multiple_of(g * rows, rows), rows)], r.local_sem.at[0]
    )
    own.start()
    r.g_out_down[...] = dot_tn(low_out, r.att[...]).astype(BF16)
    r.g_out_up[...] = dot_tn(small_out, d_z).astype(BF16)
    for d in range(1, groups):
        other = (g + d) % groups
        here = r.d_heads.at[pl.ds(pl.multiple_of(other * rows, rows), rows)]
        pltpu.make_async_remote_copy(
            src_ref=here,
            dst_ref=here,
            send_sem=r.back_send.at[other],
            recv_sem=r.back_recv.at[other],
            device_id=(part * groups + other, w),
            device_id_type=MESH,
        ).wait_recv()
        back_copy(other).wait_send()
    own.wait()


def forward_attention(geo, rank, lengths, ids, tokens, w_qkv, down, up, bias, mlp):
    rows, width = geo.rows, geo.width
    inside = mlp is not None
    mlp = mlp or ()
    any_spec = pl.BlockSpec(memory_space=pl.ANY)
    vmem = pl.BlockSpec(memory_space=pltpu.VMEM)
    smem = pl.BlockSpec(memory_space=pltpu.SMEM)
    lane_count = down.shape[0] // 4
    struct = jax.ShapeDtypeStruct
    shapes = [
        struct((geo.queries, LANES), BF16),
        struct((geo.keys, LANES), BF16),
        struct((geo.keys, LANES), BF16),
        struct((geo.queries, LANES), F32),
        struct((geo.queries, LANES), F32),
        struct((width, 3 * LANES), BF16),
        struct((geo.keys, 3 * LANES), BF16),
    ]
    specs = [vmem] * 7
    dma = pltpu.SemaphoreType.DMA
    count = 3 if inside else 0
    units = 1 + count * geo.wt
    scratch = [
        pltpu.VMEM((geo.seq, rows, width), BF16),
        pltpu.VMEM((1, geo.keys), jnp.int32),
        pltpu.VMEM((geo.groups, rows, LANES), BF16),
        dma((4 + count,)),
        dma((Spread.KINDS, units)),
        dma((Spread.KINDS, units)),
        dma((2, 3, geo.wt)),
        dma((3, geo.wt)),
        dma((2, max(count, 1) * geo.wt)),
        dma((max(count, 1) * geo.wt,)),
        dma((geo.groups,)),
        dma((geo.groups,)),
    ]
    if inside:
        hidden = mlp[1].shape[1]
        shapes += [
            struct((rows, width), F32),
            struct((rows, width), F32),
            struct((geo.queries, LANES), BF16),
            struct((lane_count, width), BF16),
            struct((lane_count, width), BF16),
            struct((lane_count, width), BF16),
            struct((lane_count, width), BF16),
            struct((lane_count, hidden), BF16),
            struct((lane_count, hidden), BF16),
        ]
        specs += [vmem, vmem, any_spec] + [vmem] * 6
        scratch += [
            pltpu.VMEM((rows, width), BF16),
            pltpu.VMEM((width, width), BF16),
            pltpu.VMEM((width, hidden), BF16),
            pltpu.VMEM((hidden, width), BF16),
            pltpu.VMEM((rows, width), F32),
            pltpu.VMEM((rows, width), F32),
            pltpu.VMEM((rows, width), BF16),
            pltpu.VMEM((rows, hidden), BF16),
            pltpu.VMEM((rows, hidden), F32),
            pltpu.VMEM((rows, hidden), BF16),
            pltpu.VMEM((rows, width), F32),
            pltpu.VMEM((geo.groups, rows, LANES), BF16),
            dma((geo.groups,)),
            dma((geo.groups,)),
        ]
    else:
        shapes += [struct((rows, width), BF16)]
        specs += [any_spec]
    return pl.pallas_call(
        functools.partial(forward_kernel, geo, inside, rank),
        out_shape=shapes,
        in_specs=[smem, smem, any_spec, any_spec, vmem, vmem, vmem] + [any_spec] * count + [vmem] * (len(mlp) - count),
        out_specs=specs,
        scratch_shapes=scratch,
        compiler_params=pltpu.CompilerParams(
            collective_id=0, has_side_effects=True, vmem_limit_bytes=VMEM_LIMIT
        ),
        name="layer",
    )(lengths, ids, tokens, w_qkv, down, up, bias, *mlp)


def backward_kernel(geo, len_ref, part_ref, q_ref, k_ref, v_ref, o_ref, lse_ref, g_ref, dq_ref, dk_ref, dv_ref, dk_acc, dv_acc):
    rows = geo.rows
    part = part_ref[0, 0]
    scale = HEAD_DIM ** (-0.5)
    starts, ends = doc_bounds(len_ref)
    first_head = lax.broadcasted_iota(jnp.int32, (rows, LANES), 1) < HEAD_DIM
    dk_acc[...] = jnp.zeros_like(dk_acc)
    dv_acc[...] = jnp.zeros_like(dv_acc)

    def seg_of(position):
        seg = jnp.int32(0)
        for start in starts[1:]:
            seg = seg + (position >= start).astype(jnp.int32)
        return seg

    def pick(values, index):
        found = values[0]
        for i in range(1, len(values)):
            found = jnp.where(index == i, values[i], found)
        return found

    def query_block(b, carry):
        at = pl.ds(pl.multiple_of(b * rows, rows), rows)
        origin = (part * geo.groups + b) * rows
        query = q_ref[at, :] * jnp.asarray(scale, BF16)
        cot = g_ref[at, :]
        lse = lse_ref[at, :]
        both = cot.astype(F32) * o_ref[at, :]
        q_pos = origin + lax.broadcasted_iota(jnp.int32, (rows, 1), 0)
        q_seg = segment_from(q_pos, starts)
        heads = []
        for h in range(PAIR):
            mask = first_head if h == 0 else jnp.logical_not(first_head)
            zero = jnp.zeros_like(query)
            heads.append(
                (
                    jnp.where(mask, query, zero),
                    jnp.where(mask, cot, zero),
                    lse[:, h * HEAD_DIM : h * HEAD_DIM + 1],
                    jnp.sum(jnp.where(mask, both, 0.0), axis=1, keepdims=True),
                )
            )
        low = pick(starts, seg_of(origin)) // rows
        high = (pick(ends, seg_of(origin + rows - 1)) + rows - 1) // rows

        def key_block(c, accs):
            keys_at = pl.ds(pl.multiple_of(c * rows, rows), rows)
            key, value = k_ref[keys_at, :], v_ref[keys_at, :]
            k_pos = c * rows + lax.broadcasted_iota(jnp.int32, (1, rows), 1)
            same = q_seg == segment_from(k_pos, starts)
            new = []
            dk_parts, dv_parts = [], []
            for h in range(PAIR):
                q_head, g_head, lse_head, dot_head = heads[h]
                score = jnp.where(same, dot_nt(q_head, key), -1e30)
                prob = jnp.exp(score - lse_head)
                d_prob = dot_nt(g_head, value)
                raw = (prob * (d_prob - dot_head) * scale).astype(BF16)
                new.append(accs[h] + dot_nn(raw, key))
                dk_parts.append(dot_tn(raw, q_head))
                dv_parts.append(dot_tn(prob.astype(BF16), g_head))
            dk_acc[keys_at, :] += dk_parts[0] + dk_parts[1]
            dv_acc[keys_at, :] += dv_parts[0] + dv_parts[1]
            return tuple(new)

        zero = jnp.zeros((rows, LANES), F32)
        accs = lax.fori_loop(low, high, key_block, (zero, zero))
        dq_ref[at, :] = jnp.where(first_head, accs[0], accs[1]).astype(BF16)
        return carry

    lax.fori_loop(0, geo.groups, query_block, 0)
    dk_ref[...] = (dk_acc[...] * HEAD_DIM**0.5).astype(BF16)
    dv_ref[...] = dv_acc[...].astype(BF16)


def backward_attention(geo, lengths, part, q, k, v, o, lse, d_heads):
    smem = pl.BlockSpec(memory_space=pltpu.SMEM)
    vmem = pl.BlockSpec(memory_space=pltpu.VMEM)
    return pl.pallas_call(
        functools.partial(backward_kernel, geo),
        out_shape=[
            jax.ShapeDtypeStruct((geo.queries, LANES), BF16),
            jax.ShapeDtypeStruct((geo.keys, LANES), BF16),
            jax.ShapeDtypeStruct((geo.keys, LANES), BF16),
        ],
        in_specs=[smem, smem] + [vmem] * 6,
        out_specs=[vmem] * 3,
        scratch_shapes=[pltpu.VMEM((geo.keys, LANES), F32)] * 2,
        compiler_params=pltpu.CompilerParams(vmem_limit_bytes=VMEM_LIMIT),
        name="attend_back",
    )(lengths, part, q, k, v, o, lse, d_heads)


class Block:
    def __init__(self, geo):
        chips = geo.groups // 2
        self.nx = min(geo.nx, chips)
        self.ny = chips // self.nx


class PairSum:
    def __init__(self, count, me, core, first, w, bufs, sems, make, stage=None):
        self.count, self.me, self.core, self.first, self.w = count, me, core, first, w
        self.near_out, self.near_in, self.far_in = bufs
        self.near_send, self.near_recv, self.far_send, self.far_recv = sems
        self.make = make
        self.slots = self.near_out.shape[0]
        self.stage = stage

    def slot(self, chip):
        return ((chip + self.count - self.me + self.count - 1) % self.count) % self.slots

    def near(self, chip):
        return pltpu.make_async_remote_copy(
            src_ref=self.near_out.at[self.slot(chip)],
            dst_ref=self.near_in.at[chip],
            send_sem=self.near_send.at[chip],
            recv_sem=self.near_recv.at[chip],
            device_id=(self.first + self.me * 2 + 1 - self.core, self.w),
            device_id_type=MESH,
        )

    def far(self, chip):
        return pltpu.make_async_remote_copy(
            src_ref=self.near_in.at[chip],
            dst_ref=self.far_in.at[self.me],
            send_sem=self.far_send.at[chip],
            recv_sem=self.far_recv.at[self.me],
            device_id=(self.first + chip * 2 + self.core, self.w),
            device_id_type=MESH,
        )

    def far_arrival(self, chip):
        return pltpu.make_async_remote_copy(
            src_ref=self.far_in.at[chip],
            dst_ref=self.far_in.at[chip],
            send_sem=self.far_send.at[chip],
            recv_sem=self.far_recv.at[chip],
            device_id=(self.first + chip * 2 + self.core, self.w),
            device_id_type=MESH,
        )

    def start(self):
        def step(d, carry):
            chip = (self.me + 1 + d) % self.count
            if self.slots < self.count:

                @pl.when(d >= self.slots)
                def _():
                    self.near((self.me + 1 + d - self.slots) % self.count).wait_send()

            self.near_out[d % self.slots] = self.make(chip, 1 - self.core).astype(BF16)
            self.near(chip).start()
            return carry

        lax.fori_loop(0, self.count, step, 0)

    def send(self):
        def step(d, carry):
            chip = (self.me + 1 + d) % self.count
            own = self.make(chip, self.core)
            self.near(chip).wait_recv()
            self.near_in[chip] = (own + self.near_in[chip].astype(F32)).astype(BF16)
            self.far(chip).start()
            return carry

        lax.fori_loop(0, self.count - 1, step, 0)

    def finish(self):
        total = self.make(self.me, self.core)
        self.near(self.me).wait_recv()
        total = total + self.near_in[self.me].astype(F32)
        if self.stage is None:
            for d in range(1, self.count):
                chip = (self.me + d) % self.count
                self.far_arrival(chip).wait_recv()
                total = total + self.far_in[chip].astype(F32)
            return total
        stage, sem = self.stage

        def fetch(d):
            chip = (self.me + d) % self.count
            return pltpu.make_async_copy(self.far_in.at[chip], stage.at[d % 2], sem.at[d % 2])

        self.far_arrival((self.me + 1) % self.count).wait_recv()
        fetch(1).start()
        for d in range(1, self.count):
            if d + 1 < self.count:
                self.far_arrival((self.me + d + 1) % self.count).wait_recv()
                fetch(d + 1).start()
            fetch(d).wait()
            total = total + stage[d % 2].astype(F32)
        return total

    def drain(self):
        for d in range(self.count):
            chip = (self.me + 1 + d) % self.count
            if d >= self.count - self.slots:
                self.near(chip).wait_send()
            if d < self.count - 1:
                self.far(chip).wait_send()


def closing_kernel(
    geo,
    rank,
    len_ref,
    id_ref,
    tokens_ref,
    first_ref,
    dq_ref,
    dk_ref,
    dv_ref,
    slice_ref,
    down_ref,
    up_ref,
    small_ref,
    out_down_ref,
    out_up_ref,
    fc1_down_ref,
    fc2_up_ref,
    fc1_up_ref,
    fc2_down_ref,
    grad_ref,
    sum1_ref,
    sum2_ref,
    tok_far,
    tok_out,
    tok_in,
    tok_stage,
    small_buf,
    set1_out,
    set1_in,
    set1_far,
    set2_out,
    set2_in,
    set2_far,
    down_acc,
    up_acc,
    mine1,
    mine2,
    place_buf,
    fold_buf,
    all1,
    all2,
    places,
    done1,
    done2,
    tok_sems,
    set1_sems,
    set2_sems,
    line_send,
    line_recv,
    spread_send,
    spread_recv,
    local_sem,
    stage_sem,
    small_sem,
):
    x, y, core, w = device_here(geo)
    s = lax.axis_index("seq")
    rows, width, wt, groups, parts = geo.rows, geo.width, geo.wt, geo.groups, geo.parts
    part, g = s // groups, s % groups
    docs = len_ref.shape[1]
    doc_rows = docs * rank
    lane_count = down_ref.shape[0] // 4
    lanes = pl.ds(pl.multiple_of(g * LANES, LANES), LANES)
    starts, ends = doc_bounds(len_ref)
    ids = [id_ref[0, d] for d in range(docs)]
    fresh = []
    for d in range(docs):
        seen = jnp.bool_(False)
        for e in range(d):
            seen = seen | (ids[e] == ids[d])
        fresh.append(jnp.where(seen, 0.0, 1.0))

    greet_all(geo)

    def iota(shape, dim):
        return lax.broadcasted_iota(jnp.int32, shape, dim)

    def zero_one(condition):
        return jnp.where(condition, 1.0, 0.0).astype(BF16)

    def chosen_of(t):
        pos = t * rows + iota((rows, LANES), 0)
        return select_from(pos, starts, ends, id_ref, rank)

    def fold(j):
        a, b = iota((lane_count, LANES), 0), iota((lane_count, LANES), 1)
        return zero_one((b >= j * rank) & (b < (j + 1) * rank) & (a % rank == b - j * rank))

    def make_tokens(chip, whose):
        t = chip * 2 + whose
        at = pl.ds(pl.multiple_of(t * rows, rows), rows)
        if parts == 1:
            d_q = dq_ref[at, :]
        else:
            inner = pl.ds(pl.multiple_of((t % groups) * rows, rows), rows)
            d_q = jnp.where(t // groups == part, dq_ref[inner, :], jnp.zeros((rows, LANES), BF16))
        pieces = [d_q, dk_ref[at, :], dv_ref[at, :]]
        chosen = chosen_of(t)
        total = jnp.zeros((rows, width), F32)
        low = jnp.zeros((rows, LANES), F32)
        for j in range(3):
            total = total + dot_nt(pieces[j], slice_ref[:, j * LANES : (j + 1) * LANES])
            part_low = dot_nt(pieces[j], up_ref[pl.ds(j * lane_count, lane_count), lanes])
            low = low + dot_nn((part_low * chosen).astype(BF16), fold(j))
        return jnp.concatenate([total, low], axis=1)

    tok = PairSum(
        geo.seq // 2, s // 2, core, 0, w, (tok_out, tok_in, tok_far), [tok_sems.at[i] for i in range(4)], make_tokens,
        (tok_stage, stage_sem),
    )

    singles = [out_down_ref, out_up_ref, fc1_down_ref, fc2_up_ref, fc1_up_ref, fc2_down_ref]

    def by_document(value):
        return dot_tn(fold_buf[...], value)[:doc_rows]

    def make_set1(chip, whose):
        owner = chip * 2 + whose
        cols = []
        for ref in singles:
            wide = ref.shape[1] // groups
            cols.append(by_document(ref[:, pl.ds(pl.multiple_of(owner * wide, LANES), wide)]))
        return jnp.concatenate(cols, axis=1)

    def make_set2(chip, whose):
        owner = chip * 2 + whose
        cut = pl.ds(pl.multiple_of(owner * LANES, LANES), LANES)
        return jnp.concatenate([down_acc[j * doc_rows : (j + 1) * doc_rows, cut] for j in range(3)], axis=1)

    chips = groups // 2
    set1 = PairSum(
        chips, g // 2, core, part * groups, w, (set1_out, set1_in, set1_far), [set1_sems.at[i] for i in range(4)], make_set1
    )
    set2 = PairSum(
        chips, g // 2, core, part * groups, w, (set2_out, set2_in, set2_far), [set2_sems.at[i] for i in range(4)], make_set2
    )

    def peer(n):
        plane = (w + n) % wt
        other = (part + n // wt) % parts
        return other * groups + g, plane, other * wt + plane

    mine_at = part * wt + w

    def line_copy(kind, n, src, dst_all):
        device, plane, _ = peer(n)
        return pltpu.make_async_remote_copy(
            src_ref=src,
            dst_ref=dst_all.at[mine_at],
            send_sem=line_send.at[kind, n],
            recv_sem=line_recv.at[kind, mine_at],
            device_id=(device, plane),
            device_id_type=MESH,
        )

    def line_arrival(kind, n, dst_all):
        device, plane, at = peer(n)
        return pltpu.make_async_remote_copy(
            src_ref=dst_all.at[at],
            dst_ref=dst_all.at[at],
            send_sem=line_send.at[kind, n],
            recv_sem=line_recv.at[kind, at],
            device_id=(device, plane),
            device_id_type=MESH,
        )

    peers = range(1, wt * parts)

    block = Block(geo)
    chip_here = g // 2
    here = (chip_here % block.nx, chip_here // block.nx, core, w)

    def region_of(ref):
        def region(ux, uy, whose, half):
            one = ref.at[(uy * block.nx + ux) * 2 + whose]
            if half is None:
                return one
            return one.at[pl.ds(half * (lane_count // 2), lane_count // 2)]

        return region

    spreads = [
        Spread(block, here, region_of(ref), spread_send, spread_recv, i, part * groups)
        for i, ref in enumerate((sum1_ref, sum2_ref))
    ]
    finals = [done1, done2]
    outs = [sum1_ref, sum2_ref]

    def place(kind, mine, dst_all):
        total = dot_nn(place_buf[:, :doc_rows], mine[...])
        for n in peers:
            line_arrival(kind, n, dst_all).wait_recv()
            if kind == 0:
                line_arrival(2, n, places).wait_recv()
            at = peer(n)[2]
            total = total + dot_nn(places[at][:, :doc_rows], dst_all[at])
        finals[kind][...] = total.astype(BF16)
        for way in (0, 1, 4):
            spreads[kind].go(way, own=finals[kind])
        pltpu.make_async_copy(finals[kind], outs[kind].at[g], local_sem.at[kind]).start()

    def pass_on(kind):
        spread = spreads[kind]
        spread.wait(0)
        spread.go(2)
        spread.go(5)
        spread.wait(1)
        spread.go(3)
        spread.go(6)

    def pass_last(kind):
        spread = spreads[kind]
        spread.wait(2)
        spread.go(7)
        spread.wait(3)
        spread.go(8)

    a, b = iota((lane_count, LANES), 0), iota((lane_count, LANES), 1)
    places_all = jnp.zeros((lane_count, LANES), F32)
    places_first = jnp.zeros((lane_count, LANES), F32)
    for d in range(docs):
        hit = (a // rank == ids[d]) & (b // rank == d) & (a % rank == b % rank)
        places_all = jnp.where(hit, 1.0, places_all)
        places_first = jnp.where(hit, fresh[d], places_first)
    place_buf[...] = places_all.astype(BF16)
    fold_buf[...] = places_first.astype(BF16)
    for n in peers:
        line_copy(2, n, place_buf, places).start()

    set1.start()
    tok.start()
    set1.send()
    tok.send()

    def small_copy(t):
        return pltpu.make_async_copy(
            small_ref.at[pl.ds(pl.multiple_of(t * rows, rows), rows)], small_buf.at[t % 2], small_sem.at[t % 2]
        )

    def add_up(t, carry):
        at = pl.ds(pl.multiple_of(t * rows, rows), rows)

        @pl.when(t + 1 < geo.seq)
        def _():
            small_copy(t + 1).start()

        small_copy(t).wait()
        for j in range(3):
            cut = slice(j * LANES, (j + 1) * LANES)
            if j == 0:
                if parts == 1:
                    value = dq_ref[at, :]
                else:
                    inner = pl.ds(pl.multiple_of((t % groups) * rows, rows), rows)
                    value = jnp.where(t // groups == part, dq_ref[inner, :], jnp.zeros((rows, LANES), BF16))
            else:
                value = (dk_ref if j == 1 else dv_ref)[at, :]
            up_acc[cut, :] += dot_tn(small_buf[t % 2][:, cut], value)
        return carry

    up_acc[...] = jnp.zeros_like(up_acc)
    small_copy(0).start()
    lax.fori_loop(0, geo.seq, add_up, 0)

    mine1[...] = set1.finish().astype(BF16)
    for n in peers:
        line_copy(0, n, mine1, all1).start()

    total = tok.finish()
    low = total[:, width:].astype(BF16)
    total = total[:, :width] + first_ref[...]
    chosen = chosen_of(s)
    pos = s * rows + iota((rows, doc_rows), 0)
    doc_of = iota((rows, doc_rows), 1) // rank
    in_doc = doc_of == segment_from(pos, starts)
    tokens = tokens_ref[...]
    for j in range(3):
        a, b = iota((LANES, lane_count), 0), iota((LANES, lane_count), 1)
        widen = zero_one((a >= j * rank) & (a < (j + 1) * rank) & (b % rank == a - j * rank))
        wide = (dot_nn(low, widen) * chosen).astype(BF16)
        total = total + dot_nn(wide, down_ref[j * lane_count : (j + 1) * lane_count, :])
        by_doc = dot_nn(low, widen[:, :doc_rows])
        by_doc = jnp.where(in_doc, by_doc, 0.0).astype(BF16)
        down_acc[j * doc_rows : (j + 1) * doc_rows, :] = dot_tn(by_doc, tokens)
    set2.start()
    grad_ref[...] = total
    set2.send()
    place(0, mine1, all1)
    for j in range(3):
        mine2[:, (3 + j) * LANES : (4 + j) * LANES] = by_document(
            up_acc[j * lane_count : (j + 1) * lane_count, :].astype(BF16)
        ).astype(BF16)
    mine2[:, : 3 * LANES] = set2.finish().astype(BF16)
    for n in peers:
        line_copy(1, n, mine2, all2).start()
    pass_on(0)
    pass_last(0)
    place(1, mine2, all2)
    pass_on(1)
    pass_last(1)
    for kind in range(2):
        for way in range(4, 9):
            spreads[kind].wait(way)
        spreads[kind].wait_sends()
        pltpu.make_async_copy(finals[kind], outs[kind].at[g], local_sem.at[kind]).wait()
    for n in peers:
        line_copy(0, n, mine1, all1).wait_send()
        line_copy(1, n, mine2, all2).wait_send()
        line_copy(2, n, place_buf, places).wait_send()
    tok.drain()
    set1.drain()
    set2.drain()


def greet_all(geo):
    s, w = lax.axis_index("seq"), lax.axis_index("wt")
    barrier = pltpu.get_barrier_semaphore()
    part, g = s // geo.groups, s % geo.groups
    for d in range(1, geo.seq):
        pl.semaphore_signal(barrier, inc=1, device_id=((s + d) % geo.seq, w), device_id_type=MESH)
    count = geo.seq - 1
    for d in range(1, geo.wt):
        for q in range(geo.parts):
            other = ((part + q) % geo.parts) * geo.groups + g
            pl.semaphore_signal(barrier, inc=1, device_id=(other, (w + d) % geo.wt), device_id_type=MESH)
            count += 1
    pl.semaphore_wait(barrier, count)


def closing(geo, rank, lengths, ids, tokens, d_first, dq, dk, dv, w_slice, down, up, small, grads):
    rows, width = geo.rows, geo.width
    docs = lengths.shape[1]
    doc_rows = docs * rank
    lane_count = down.shape[0] // 4
    set1 = sum(v.shape[1] for v in grads) // geo.groups
    set2 = 6 * LANES
    chips, near = geo.seq // 2, geo.groups // 2
    peers = geo.wt * geo.parts
    smem = pl.BlockSpec(memory_space=pltpu.SMEM)
    vmem = pl.BlockSpec(memory_space=pltpu.VMEM)
    any_spec = pl.BlockSpec(memory_space=pl.ANY)
    dma = pltpu.SemaphoreType.DMA
    wide = width + LANES
    return pl.pallas_call(
        functools.partial(closing_kernel, geo, rank),
        out_shape=[
            jax.ShapeDtypeStruct((rows, width), F32),
            jax.ShapeDtypeStruct((geo.groups, lane_count, set1), BF16),
            jax.ShapeDtypeStruct((geo.groups, lane_count, set2), BF16),
            jax.ShapeDtypeStruct((chips, rows, wide), BF16),
        ],
        in_specs=[smem, smem] + [vmem] * 8 + [any_spec] + [vmem] * len(grads),
        out_specs=[vmem, any_spec, any_spec, any_spec],
        scratch_shapes=[
            pltpu.VMEM((min(chips, 4), rows, wide), BF16),
            pltpu.VMEM((chips, rows, wide), BF16),
            pltpu.VMEM((2, rows, wide), BF16),
            pltpu.VMEM((2, rows, 3 * lane_count), BF16),
            pltpu.VMEM((near, doc_rows, set1), BF16),
            pltpu.VMEM((near, doc_rows, set1), BF16),
            pltpu.VMEM((near, doc_rows, set1), BF16),
            pltpu.VMEM((near, doc_rows, 3 * LANES), BF16),
            pltpu.VMEM((near, doc_rows, 3 * LANES), BF16),
            pltpu.VMEM((near, doc_rows, 3 * LANES), BF16),
            pltpu.VMEM((3 * doc_rows, width), F32),
            pltpu.VMEM((3 * lane_count, LANES), F32),
            pltpu.VMEM((doc_rows, set1), BF16),
            pltpu.VMEM((doc_rows, set2), BF16),
            pltpu.VMEM((lane_count, LANES), BF16),
            pltpu.VMEM((lane_count, LANES), BF16),
            pltpu.VMEM((peers, doc_rows, set1), BF16),
            pltpu.VMEM((peers, doc_rows, set2), BF16),
            pltpu.VMEM((peers, lane_count, LANES), BF16),
            pltpu.VMEM((lane_count, set1), BF16),
            pltpu.VMEM((lane_count, set2), BF16),
            dma((4, chips)),
            dma((4, near)),
            dma((4, near)),
            dma((3, peers)),
            dma((3, peers)),
            dma((Spread.KINDS, 2)),
            dma((Spread.KINDS, 2)),
            dma((2,)),
            dma((2,)),
            dma((2,)),
        ],
        compiler_params=pltpu.CompilerParams(
            collective_id=1, has_side_effects=True, vmem_limit_bytes=VMEM_LIMIT
        ),
        name="close",
    )(lengths, ids, tokens, d_first, dq, dk, dv, w_slice, down, up, small, *grads)


def unpack_kernel(one_ref, two_ref, down_ref, up_ref, fc1_down_ref, fc2_up_ref, fc1_up_ref, fc2_down_ref):
    for j in range(3):
        down_ref[j] = two_ref[0, :, j * LANES : (j + 1) * LANES].astype(F32)
        up_ref[j] = two_ref[0, :, (3 + j) * LANES : (4 + j) * LANES].astype(F32)
    at = 0
    for ref in (down_ref.at[3], up_ref.at[3], fc1_down_ref, fc2_up_ref, fc1_up_ref, fc2_down_ref):
        wide = ref.shape[1]
        ref[...] = one_ref[0, :, at : at + wide].astype(F32)
        at += wide


def unpack(geo, one, two, lane_count):
    groups = geo.groups
    thick = (one.shape[2] - 4 * LANES) // 2

    def whole(wide):
        return jax.ShapeDtypeStruct((lane_count, wide * groups), F32)

    def flat(wide):
        return pl.BlockSpec((lane_count, wide), lambda i: (0, i))

    four = jax.ShapeDtypeStruct((4, lane_count, LANES * groups), F32)
    four_spec = pl.BlockSpec((4, lane_count, LANES), lambda i: (0, 0, i))
    return pl.pallas_call(
        unpack_kernel,
        grid=(groups,),
        out_shape=[four, four, whole(LANES), whole(LANES), whole(thick), whole(thick)],
        in_specs=[
            pl.BlockSpec((1,) + one.shape[1:], lambda i: (i, 0, 0)),
            pl.BlockSpec((1,) + two.shape[1:], lambda i: (i, 0, 0)),
        ],
        out_specs=[four_spec, four_spec, flat(LANES), flat(LANES), flat(thick), flat(thick)],
        compiler_params=pltpu.CompilerParams(vmem_limit_bytes=VMEM_LIMIT // 2),
        name="unpack",
    )(one, two)


def layer_norm(value, gain, shift):
    mean = jnp.mean(value, axis=-1, keepdims=True)
    centred = value - mean
    spread = jnp.mean(centred * centred, axis=-1, keepdims=True)
    return centred * lax.rsqrt(spread + 1e-05) * gain + shift


def gelu_exact(value):
    return jax.nn.gelu(value, approximate=False)


def times_transposed(grad, weight):
    return lax.dot_general(
        grad, weight, (((1,), (1,)), ((), ())), preferred_element_type=jnp.float32
    )


def left_inner(left, right):
    return lax.dot_general(
        left, right, (((0,), (0,)), ((), ())), preferred_element_type=jnp.float32
    )


def stack_down(down):
    return jnp.transpose(down, (1, 0, 2)).reshape(down.shape[1], down.shape[0] * down.shape[2])


def stack_up(up):
    return up.reshape(up.shape[0] * up.shape[1], up.shape[2])


def unstack_down(stacked, adapter_count, rank_size):
    return jnp.transpose(stacked.reshape(stacked.shape[0], adapter_count, rank_size), (1, 0, 2))


def unstack_up(stacked, adapter_count, rank_size):
    return stacked.reshape(adapter_count, rank_size, stacked.shape[1])


def segment_of(positions, starts):
    return jnp.sum((positions[:, None] >= starts[None, :]).astype(jnp.int32), axis=1) - 1


def select_local(tok_rows, lane_count, rank_size, lengths, ids):
    starts = jnp.cumsum(lengths) - lengths
    local_pos = lax.axis_index("seq") * tok_rows + jnp.arange(tok_rows, dtype=jnp.int32)
    local_seg = segment_of(local_pos, starts)
    doc_range = jnp.arange(lengths.shape[0], dtype=jnp.int32)
    chosen = jnp.sum(jnp.where(local_seg[:, None] == doc_range[None, :], ids[None, :], 0), axis=1)
    lane_owner = jnp.arange(lane_count, dtype=jnp.int32) // rank_size
    return (chosen[:, None] == lane_owner[None, :]).astype(jnp.float32)


def feed_forward(
    geo, tokens, cotangent, attended_tok, weights, vectors, attn_maps, fc1_maps, fc2_maps, select
):
    tok_rows, model_width = tokens.shape
    full_out, full_fc1, full_fc2 = [lax.all_gather(v, "wt", axis=0, tiled=True) for v in weights]
    out_bias, norm1_gain, norm1_bias, fc1_bias, fc2_bias, norm2_gain, norm2_bias = vectors
    out_down, out_up = attn_maps
    fc1_down_all, fc1_up_all = fc1_maps
    fc2_down_all, fc2_up_all = fc2_maps
    out_main = jnp.dot(attended_tok, full_out, preferred_element_type=jnp.float32)
    small_out = (
        jnp.dot(attended_tok, out_down, preferred_element_type=jnp.float32) * select
    ).astype(jnp.bfloat16)
    z_value = out_main + out_bias + jnp.dot(small_out, out_up, preferred_element_type=jnp.float32)
    first_sum = tokens.astype(jnp.float32) + z_value
    first_norm, norm1_back = jax.vjp(
        lambda value: layer_norm(value, norm1_gain, norm1_bias), first_sum
    )
    first_low = first_norm.astype(jnp.bfloat16)
    fc1_main = jnp.dot(first_low, full_fc1, preferred_element_type=jnp.float32)
    small_fc1 = (
        jnp.dot(first_low, fc1_down_all, preferred_element_type=jnp.float32) * select
    ).astype(jnp.bfloat16)
    pre_act = (
        fc1_main + fc1_bias + jnp.dot(small_fc1, fc1_up_all, preferred_element_type=jnp.float32)
    )
    act_value, gelu_back = jax.vjp(gelu_exact, pre_act)
    act_low = act_value.astype(jnp.bfloat16)
    fc2_main = jnp.dot(act_low, full_fc2, preferred_element_type=jnp.float32)
    small_fc2 = (
        jnp.dot(act_low, fc2_down_all, preferred_element_type=jnp.float32) * select
    ).astype(jnp.bfloat16)
    y_value = (
        fc2_main + fc2_bias + jnp.dot(small_fc2, fc2_up_all, preferred_element_type=jnp.float32)
    )
    output, norm2_back = jax.vjp(
        lambda value: layer_norm(value, norm2_gain, norm2_bias), first_norm + y_value
    )
    d_second = norm2_back(cotangent.astype(jnp.float32))[0]
    d_y = d_second.astype(jnp.bfloat16)
    d_act = times_transposed(d_y, full_fc2)
    low_fc2 = (times_transposed(d_y, fc2_up_all) * select).astype(jnp.bfloat16)
    d_act = d_act + times_transposed(low_fc2, fc2_down_all)
    grad_fc2_up = left_inner(small_fc2, d_y)
    grad_fc2_down = left_inner(low_fc2, act_low)
    d_pre = gelu_back(d_act)[0].astype(jnp.bfloat16)
    d_first_low = times_transposed(d_pre, full_fc1)
    low_fc1 = (times_transposed(d_pre, fc1_up_all) * select).astype(jnp.bfloat16)
    d_first_low = d_first_low + times_transposed(low_fc1, fc1_down_all)
    grad_fc1_up = left_inner(small_fc1, d_pre)
    grad_fc1_down = left_inner(low_fc1, first_low)
    d_first = norm1_back(d_second + d_first_low)[0]
    d_z = d_first.astype(jnp.bfloat16)
    d_attended = times_transposed(d_z, full_out)
    low_out = (times_transposed(d_z, out_up) * select).astype(jnp.bfloat16)
    d_attended = (d_attended + times_transposed(low_out, out_down)).astype(jnp.bfloat16)
    grad_out_up = left_inner(small_out, d_z)
    grad_out_down = left_inner(low_out, attended_tok)
    blocks = [
        [p * geo.groups + i for i in range(geo.groups)] for p in range(geo.parts)
    ]
    d_heads = lax.all_to_all(
        d_attended.reshape(tok_rows, geo.groups, LANES),
        "seq",
        split_axis=1,
        concat_axis=0,
        axis_index_groups=blocks,
        tiled=True,
    ).reshape(geo.queries, LANES)
    grads = [grad_out_down, grad_out_up, grad_fc1_down, grad_fc2_up, grad_fc1_up, grad_fc2_down]
    return output, d_first, d_heads, [v.astype(BF16) for v in grads]


def shards(
    tokens,
    cotangent,
    w_qkv,
    qv_bias,
    w_out,
    out_bias,
    norm1_gain,
    norm1_bias,
    w_fc1,
    fc1_bias,
    w_fc2,
    fc2_bias,
    norm2_gain,
    norm2_bias,
    doc_lengths,
    adapter_ids,
    attn_down,
    attn_up,
    fc1_down,
    fc1_up,
    fc2_down,
    fc2_up,
):
    tok_rows, model_width = tokens.shape
    adapter_count = attn_down.shape[1]
    rank_size = attn_down.shape[3]
    lane_count = adapter_count * rank_size
    seq_count = lax.axis_size("seq")
    geo = Geometry(tok_rows, model_width)
    part_index = lax.axis_index("seq") // geo.groups
    down_rows = jnp.transpose(attn_down, (0, 1, 3, 2)).reshape(4 * lane_count, model_width)
    up_rows = attn_up.reshape(4 * lane_count, model_width)
    weights = (w_out, w_fc1, w_fc2)
    vectors = (out_bias, norm1_gain, norm1_bias, fc1_bias, fc2_bias, norm2_gain, norm2_bias)

    def rows_of(down):
        return jnp.swapaxes(down, 1, 2).reshape(lane_count, down.shape[1])

    inside = all(v.shape[0] % (32 * seq_count) == 0 for v in weights)
    mlp = None
    if inside:
        mlp = (
            weights
            + (cotangent,)
            + tuple(v.reshape(1, -1) for v in vectors)
            + (rows_of(fc1_down), stack_up(fc1_up), rows_of(fc2_down), stack_up(fc2_up))
        )
    q_heads, k_heads, v_heads, o_heads, lse_heads, w_slice, small_all, *rest = forward_attention(
        geo, rank_size, doc_lengths, adapter_ids, tokens, w_qkv, down_rows, up_rows, qv_bias, mlp
    )
    if inside:
        output, d_first, d_heads, *set1 = rest
    else:
        output, d_first, d_heads, set1 = feed_forward(
            geo,
            tokens,
            cotangent,
            rest[0],
            weights,
            vectors,
            (stack_down(attn_down[3]), stack_up(attn_up[3])),
            (stack_down(fc1_down), stack_up(fc1_up)),
            (stack_down(fc2_down), stack_up(fc2_up)),
            select_local(tok_rows, lane_count, rank_size, doc_lengths[0], adapter_ids[0]),
        )
    d_q, d_k, d_v = backward_attention(
        geo, doc_lengths, part_index.reshape(1, 1), q_heads, k_heads, v_heads, o_heads, lse_heads, d_heads
    )
    input_grad, sum1, sum2, _ = closing(
        geo,
        rank_size,
        doc_lengths,
        adapter_ids,
        tokens,
        d_first,
        d_q,
        d_k,
        d_v,
        w_slice,
        down_rows,
        up_rows,
        small_all,
        set1,
    )

    down4, up4, fc1_down_sum, fc2_up_sum, fc1_up_sum, fc2_down_sum = unpack(geo, sum1, sum2, lane_count)

    def as_up(rows):
        return rows.reshape(rows.shape[:-2] + (adapter_count, rank_size, rows.shape[-1]))

    def as_down(rows):
        return jnp.swapaxes(as_up(rows), -1, -2)

    return (
        output,
        input_grad,
        as_down(down4),
        as_up(up4),
        as_down(fc1_down_sum),
        as_up(fc1_up_sum),
        as_down(fc2_down_sum),
        as_up(fc2_up_sum),
    )


def solution(mesh):
    placed = (
        P(("wt", "seq"), None),
        P(("wt", "seq"), None),
        P("wt", None),
        P(),
        P("wt", None),
        P(),
        P(),
        P(),
        P("wt", None),
        P(),
        P("wt", None),
        P(),
        P(),
        P(),
        P("wt", None),
        P("wt", None),
        P(),
        P(),
        P(),
        P(),
        P(),
        P(),
    )
    return jax.shard_map(
        shards,
        mesh=mesh,
        in_specs=placed,
        out_specs=(P(("wt", "seq"), None), P(("wt", "seq"), None), P(), P(), P(), P(), P(), P()),
        check_vma=False,
    )
```

```python
import functools

import jax
import jax.numpy as jnp
from jax import lax
from jax.experimental import pallas as pl
from jax.experimental.pallas import tpu as pltpu
from jax.sharding import PartitionSpec as P

HEADS = 16
HEAD_DIM = 64
LANES = 128
PAIR = LANES // HEAD_DIM
MESH = pl.DeviceIdType.MESH
F32 = jnp.float32
BF16 = jnp.bfloat16
VMEM_LIMIT = 60 * 2**20


def dot_nn(a, b):
    return lax.dot_general(a, b, (((1,), (0,)), ((), ())), preferred_element_type=F32)


def dot_nt(a, b):
    return lax.dot_general(a, b, (((1,), (1,)), ((), ())), preferred_element_type=F32)


def dot_tn(a, b):
    return lax.dot_general(a, b, (((0,), (0,)), ((), ())), preferred_element_type=F32)


class Geometry:
    def __init__(self, rows, width):
        self.seq = lax.axis_size("seq")
        self.wt = lax.axis_size("wt")
        self.rows = rows
        self.width = width
        self.groups = width // LANES
        self.parts = self.seq // self.groups
        chips = self.seq // 2
        nx = 1
        while nx * nx < chips:
            nx *= 2
        self.nx = nx
        self.ny = chips // nx
        self.keys = self.seq * rows
        self.queries = self.groups * rows


def doc_bounds(len_ref):
    count = len_ref.shape[1]
    starts, ends = [], []
    at = jnp.int32(0)
    for i in range(count):
        starts.append(at)
        at = at + len_ref[0, i]
        ends.append(at)
    return starts, ends


def segment_from(positions, starts):
    seg = jnp.zeros_like(positions)
    for start in starts[1:]:
        seg = seg + (positions >= start).astype(jnp.int32)
    return seg


def select_from(positions, starts, ends, id_ref, rank):
    owner = lax.broadcasted_iota(jnp.int32, positions.shape, 1) // rank
    picked = jnp.zeros(positions.shape, F32)
    for i in range(len(starts)):
        inside = (positions >= starts[i]) & (positions < ends[i]) & (owner == id_ref[0, i])
        picked = jnp.where(inside, 1.0, picked)
    return picked


def placement(id_ref, docs, rank, lane_count):
    a = lax.broadcasted_iota(jnp.int32, (lane_count, LANES), 0)
    b = lax.broadcasted_iota(jnp.int32, (lane_count, LANES), 1)
    every = jnp.zeros((lane_count, LANES), F32)
    first = jnp.zeros((lane_count, LANES), F32)
    for d in range(docs):
        seen = jnp.bool_(False)
        for e in range(d):
            seen = seen | (id_ref[0, e] == id_ref[0, d])
        hit = (a // rank == id_ref[0, d]) & (b // rank == d) & (a % rank == b % rank)
        every = jnp.where(hit, 1.0, every)
        first = jnp.where(hit, jnp.where(seen, 0.0, 1.0), first)
    return every.astype(BF16), first.astype(BF16)


def owner_columns(refs, owner, groups):
    cols = []
    for ref in refs:
        wide = ref.shape[1] // groups
        cols.append(ref[:, pl.ds(pl.multiple_of(owner * wide, LANES), wide)])
    return jnp.concatenate(cols, axis=1).astype(F32)


class Spread:
    KINDS = 9

    def __init__(self, geo, here, region, send, recv, unit, first=0):
        self.geo, self.here, self.region = geo, here, region
        self.send, self.recv, self.unit, self.first = send, recv, unit, first

    def copy(self, kind, src, dst, x, y, core):
        return pltpu.make_async_remote_copy(
            src_ref=src,
            dst_ref=dst,
            send_sem=self.send.at[kind, self.unit],
            recv_sem=self.recv.at[kind, self.unit],
            device_id=(self.first + ((y * self.geo.nx) + x) * 2 + core, self.here[3]),
            device_id_type=MESH,
        )

    def others(self):
        nx, ny = self.geo.nx, self.geo.ny
        x, y, core, _ = self.here
        row = [((x + d) % nx, y) for d in range(1, nx)]
        col = [(x, (y + d) % ny) for d in range(1, ny)]
        return row, col

    def plan(self):
        x, y, core, _ = self.here
        row, col = self.others()
        plan = {kind: [] for kind in range(self.KINDS)}
        for tx, ty in row:
            plan[0].append(((x, y), None, (tx, ty, core)))
        for tx, ty in col:
            plan[1].append(((x, y), None, (tx, ty, core)))
        for ux, uy in row:
            for tx, ty in col:
                plan[2].append(((ux, uy), 0, (tx, ty, core)))
        for ux, uy in col:
            for tx, ty in row:
                plan[3].append(((ux, uy), 1, (tx, ty, core)))
        plan[4].append(((x, y), None, (x, y, 1 - core)))
        for ux, uy in row:
            plan[5].append(((ux, uy), None, (x, y, 1 - core)))
        for ux, uy in col:
            plan[6].append(((ux, uy), None, (x, y, 1 - core)))
        for ux, _ in row:
            for _, uy in col:
                plan[7].append(((ux, uy), 0, (x, y, 1 - core)))
                plan[8].append(((ux, uy), 1, (x, y, 1 - core)))
        return plan

    def go(self, kind, own=None):
        core = self.here[2]
        for (ux, uy), half, (tx, ty, tcore) in self.plan()[kind]:
            dst = self.region(ux, uy, core, half)
            src = dst if own is None else own
            self.copy(kind, src, dst, tx, ty, tcore).start()

    def arrivals(self, kind):
        x, y, core, _ = self.here
        row, col = self.others()
        if kind == 0:
            return [(u, None, core) for u in row]
        if kind == 1:
            return [(u, None, core) for u in col]
        if kind in (2, 3):
            return [((ux, uy), kind - 2, core) for ux, _ in row for _, uy in col]
        if kind == 4:
            return [((x, y), None, 1 - core)]
        if kind == 5:
            return [(u, None, 1 - core) for u in row]
        if kind == 6:
            return [(u, None, 1 - core) for u in col]
        return [((ux, uy), kind - 7, 1 - core) for ux, _ in row for _, uy in col]

    def wait(self, kind):
        x, y, core, _ = self.here
        for (ux, uy), half, whose in self.arrivals(kind):
            ref = self.region(ux, uy, whose, half)
            self.copy(kind, ref, ref, x, y, 1 - core).wait_recv()

    def wait_sends(self):
        x, y, core, _ = self.here
        for kind in range(self.KINDS):
            for (ux, uy), half, _ in self.plan()[kind]:
                ref = self.region(ux, uy, core, half)
                self.copy(kind, ref, ref, x, y, 1 - core).wait_send()


def device_here(geo):
    s = lax.axis_index("seq")
    core = s % 2
    chip = s // 2
    return chip % geo.nx, chip // geo.nx, core, lax.axis_index("wt")


def greet(geo):
    s, w = lax.axis_index("seq"), lax.axis_index("wt")
    barrier = pltpu.get_barrier_semaphore()
    for d in range(1, geo.seq):
        pl.semaphore_signal(barrier, inc=1, device_id=((s + d) % geo.seq, w), device_id_type=MESH)
    for d in range(1, geo.wt):
        pl.semaphore_signal(barrier, inc=1, device_id=(s, (w + d) % geo.wt), device_id_type=MESH)
    pl.semaphore_wait(barrier, geo.seq + geo.wt - 2)


def erf(v):
    v = jnp.clip(v, -3.832506856900711, 3.832506856900711)
    sq = v * v
    top = jnp.full_like(v, 0.00022905065861350646)
    for c in (0.0034082910107109506, 0.050955695062380861, 0.18520832239976145, 1.128379143519084):
        top = top * sq + c
    low = jnp.full_like(v, -1.1791602954361697e-7)
    for c in (0.000023547966471313185, 0.0010179625278914885, 0.014070470171167667, 0.11098505178285362, 0.49746925110067538, 1.0):
        low = low * sq + c
    return v * top / low


def normed(value):
    mean = jnp.mean(value, axis=1, keepdims=True)
    centred = value - mean
    spread = lax.rsqrt(jnp.mean(centred * centred, axis=1, keepdims=True) + 1e-05)
    return centred * spread, spread


def normed_back(grad, gain, unit, spread):
    g = grad * gain
    return spread * (
        g - jnp.mean(g, axis=1, keepdims=True) - unit * jnp.mean(g * unit, axis=1, keepdims=True)
    )


class Names:
    def __init__(self, names, refs):
        self.__dict__.update(zip(names, refs))


MLP_INPUTS = (
    "w_out", "w_fc1", "w_fc2", "cotangent", "out_bias", "gain1", "shift1", "fc1_bias", "fc2_bias", "gain2", "shift2",
    "fc1_down", "fc1_up", "fc2_down", "fc2_up",
)
BASE_OUTPUTS = ("q", "k", "v", "o", "lse", "w_slice", "small")
MLP_OUTPUTS = ("output", "d_first", "d_heads", "g_out_down", "g_out_up", "g_fc1_down", "early_sum")
BASE_SCRATCH = (
    "tok", "seg", "att_send_buf", "local_sem", "send_sem", "recv_sem", "slice_send", "slice_recv", "line_send",
    "line_recv", "att_send", "att_recv",
)
MLP_SCRATCH = (
    "att", "full_out", "full_fc1", "full_fc2", "unit1", "h1", "h1_low", "act", "slope", "d_pre", "y", "d_att_buf",
    "back_send", "back_recv", "g_fc2_up", "g_fc1_up", "g_fc2_down", "set_out", "set_in", "set_far", "set_sems",
)


def forward_kernel(geo, inside, rank, len_ref, id_ref, tokens_ref, wqkv_ref, down_ref, up_ref, bias_ref, *refs):
    in_names = MLP_INPUTS if inside else ()
    out_names = BASE_OUTPUTS + (MLP_OUTPUTS if inside else ("att",))
    scratch_names = BASE_SCRATCH + (MLP_SCRATCH if inside else ())
    r = Names(in_names + out_names + scratch_names, refs)
    weights_in = (r.w_out, r.w_fc1, r.w_fc2) if inside else ()
    weights_out = (r.full_out, r.full_fc1, r.full_fc2) if inside else ()
    weight_count = len(weights_in)
    att_ref, q_ref, k_ref, v_ref, o_ref, lse_ref, slice_ref, small_ref = (
        r.att, r.q, r.k, r.v, r.o, r.lse, r.w_slice, r.small
    )
    tok_buf, seg_buf, att_buf, local_sem = r.tok, r.seg, r.att_send_buf, r.local_sem
    send_sem, recv_sem, slice_send, slice_recv = r.send_sem, r.recv_sem, r.slice_send, r.slice_recv
    line_send, line_recv, att_send, att_recv = r.line_send, r.line_recv, r.att_send, r.att_recv
    here = device_here(geo)
    x, y, core, w = here
    s = lax.axis_index("seq")
    part, g = s // geo.groups, s % geo.groups
    rows, width, wt = geo.rows, geo.width, geo.wt
    lanes = pl.ds(pl.multiple_of(g * LANES, LANES), LANES)

    own_tok = pltpu.make_async_copy(tokens_ref, tok_buf.at[s], local_sem.at[0])
    own_tok.start()
    shard = wqkv_ref.shape[0]
    own_slices = []
    for j in range(3):
        src = wqkv_ref.at[:, pl.ds(pl.multiple_of(j * width + g * LANES, LANES), LANES)]
        dst = slice_ref.at[pl.ds(pl.multiple_of(w * shard, shard), shard), pl.ds(j * LANES, LANES)]
        own_slices.append(pltpu.make_async_copy(src, dst, local_sem.at[1 + j]))
        own_slices[-1].start()
    own_weights = []
    for m in range(weight_count):
        height = weights_in[m].shape[0]
        dst = weights_out[m].at[pl.ds(pl.multiple_of(w * height, height), height)]
        own_weights.append(pltpu.make_async_copy(weights_in[m], dst, local_sem.at[4 + m]))
        own_weights[-1].start()

    greet(geo)

    def token_region(ux, uy, whose, half):
        block = tok_buf.at[(uy * geo.nx + ux) * 2 + whose]
        if half is None:
            return block
        return block.at[pl.ds(half * (rows // 2), rows // 2)]

    tok = Spread(geo, here, token_region, send_sem, recv_sem, 0)
    tok.go(0, own=tokens_ref)
    tok.go(1, own=tokens_ref)
    tok.go(4, own=tokens_ref)

    def slice_copy(j, p, up):
        dst = slice_ref.at[pl.ds(pl.multiple_of(p * shard, shard), shard), pl.ds(j * LANES, LANES)]
        return pltpu.make_async_remote_copy(
            src_ref=dst,
            dst_ref=dst,
            send_sem=slice_send.at[0 if up else 1, j, p],
            recv_sem=slice_recv.at[j, p],
            device_id=(s, w + 1 if up else w - 1),
            device_id_type=MESH,
        )

    starts, ends = doc_bounds(len_ref)
    seg_buf[...] = segment_from(lax.broadcasted_iota(jnp.int32, seg_buf.shape, 1), starts)

    seq = geo.seq
    mine = s

    def unit_rows(m, p, unit, half=None):
        height = weights_in[m].shape[0]
        piece = height // seq
        if half is None:
            return weights_out[m].at[pl.ds(pl.multiple_of(p * height + unit * piece, piece), piece)]
        piece = piece // 2
        return weights_out[m].at[
            pl.ds(pl.multiple_of(p * height + unit * 2 * piece + half * piece, piece), piece)
        ]

    def line_copy(m, p, up, own):
        height = weights_in[m].shape[0]
        piece = height // seq
        dst = unit_rows(m, p, mine)
        src = weights_in[m].at[pl.ds(pl.multiple_of(mine * piece, piece), piece)] if own else dst
        target = w + 1 if up else w - 1
        return pltpu.make_async_remote_copy(
            src_ref=src,
            dst_ref=dst,
            send_sem=line_send.at[0 if up else 1, m * wt + p],
            recv_sem=line_recv.at[m * wt + p],
            device_id=(s, target),
            device_id_type=MESH,
        )

    def nth_plane(j):
        below, above = w, wt - 1 - w
        both = jnp.minimum(below, above)
        in_turn = j < 2 * both
        dist = jnp.where(in_turn, j // 2 + 1, j - both + 1)
        from_below = jnp.where(in_turn, j % 2 == 0, below > above)
        return jnp.where(from_below, w - dist, w + dist)

    def weight_spread(m, p):
        def region(ux, uy, whose, half):
            return unit_rows(m, p, (uy * geo.nx + ux) * 2 + whose, half)

        return Spread(geo, here, region, send_sem, recv_sem, 1 + m * wt + p)

    units = []
    if inside:
        units = [(m, j) for j in range(wt - 1) for m in (0, 1)] + [(2, j) for j in range(wt - 1)]

    def start_lines(which):
        for m in which if inside else ():

            @pl.when(w < wt - 1)
            def _():
                line_copy(m, w, True, True).start()

            @pl.when(w > 0)
            def _():
                line_copy(m, w, False, True).start()

    def along(i):
        if i >= len(units):
            return
        m, j = units[i]
        p = nth_plane(j)
        line_copy(m, p, True, False).wait_recv()

        @pl.when((p < w) & (w < wt - 1))
        def _():
            line_copy(m, p, True, False).start()

        @pl.when((p > w) & (w > 0))
        def _():
            line_copy(m, p, False, False).start()

    def tick(i):
        if i == 0:
            along(0)
        if i == late_lines:
            start_lines((2,))
        if i < len(units):
            m, j = units[i]
            spread = weight_spread(m, nth_plane(j))
            spread.go(0)
            spread.go(1)
            spread.go(4)
        along(i + 1)
        if 0 <= i - 1 < len(units):
            m, j = units[i - 1]
            spread = weight_spread(m, nth_plane(j))
            spread.wait(0)
            spread.go(2)
            spread.go(5)
            spread.wait(1)
            spread.go(3)
            spread.go(6)
        if 0 <= i - 2 < len(units):
            m, j = units[i - 2]
            spread = weight_spread(m, nth_plane(j))
            spread.wait(2)
            spread.go(7)
            spread.wait(3)
            spread.go(8)

    tick_count = len(units) + 2 if units else 0
    late_lines = 0
    early_ticks = min(3, tick_count)
    loop_ticks = min(6, tick_count)

    def complete(m):
        own_weights[m].wait()
        for j in range(wt - 1):
            spread = weight_spread(m, nth_plane(j))
            for kind in range(4, 9):
                spread.wait(kind)

    for copy in own_slices:
        copy.wait()
    for j in range(3):

        @pl.when(w < wt - 1)
        def _():
            slice_copy(j, w, True).start()

        @pl.when(w > 0)
        def _():
            slice_copy(j, w, False).start()

    nx, ny = geo.nx, geo.ny
    row_n, col_n, diag_n = 2 * (nx - 1), 2 * (ny - 1), 2 * (nx - 1) * (ny - 1)

    def block_owner(i):
        r = i - 2
        c = r - row_n
        d = c - col_n
        dx_row, k_row = r % max(nx - 1, 1) + 1, r // max(nx - 1, 1)
        dy_col, k_col = c % max(ny - 1, 1) + 1, c // max(ny - 1, 1)
        half = max(diag_n // 2, 1)
        k_diag, in_diag = d // half, d % half
        dx_diag, dy_diag = in_diag % max(nx - 1, 1) + 1, in_diag // max(nx - 1, 1) + 1
        dx = jnp.where(i < 2, 0, jnp.where(i < 2 + row_n, dx_row, jnp.where(i < 2 + row_n + col_n, 0, dx_diag)))
        dy = jnp.where(i < 2 + row_n, 0, jnp.where(i < 2 + row_n + col_n, dy_col, dy_diag))
        kk = jnp.where(i < 2, i, jnp.where(i < 2 + row_n, k_row, jnp.where(i < 2 + row_n + col_n, k_col, k_diag)))
        return (((y + dy) % ny) * nx + (x + dx) % nx) * 2 + (core + kk) % 2

    def project(i, carry):
        @pl.when(i == 0)
        def _():
            start_lines((0, 1))
            for n in range(wt - 1):
                p = nth_plane(n)
                for j in range(3):
                    slice_copy(j, p, True).wait_recv()

                    @pl.when((p < w) & (w < wt - 1))
                    def _():
                        slice_copy(j, p, True).start()

                    @pl.when((p > w) & (w > 0))
                    def _():
                        slice_copy(j, p, False).start()

            own_tok.wait()

        @pl.when(i == 1)
        def _():
            tok.wait(4)

        @pl.when(i == 2)
        def _():
            tok.wait(0)
            tok.go(2)
            tok.go(5)
            tok.wait(1)
            tok.go(3)
            tok.go(6)

        @pl.when(i == 2 + row_n // 2)
        def _():
            tok.wait(5)

        @pl.when(i == 2 + row_n + col_n // 2)
        def _():
            tok.wait(6)

        @pl.when(i == 2 + row_n + col_n)
        def _():
            tok.wait(2)
            tok.go(7)
            tok.wait(3)
            tok.go(8)

        @pl.when(i == 2 + row_n + col_n + diag_n // 2)
        def _():
            tok.wait(7)
            tok.wait(8)

        for n in range(early_ticks):

            @pl.when(i == min(3 + 2 * n, geo.seq - 1))
            def _():
                tick(n)

        t = block_owner(i)
        block = tok_buf[t]
        at = pl.ds(pl.multiple_of(t * rows, rows), rows)
        pos = t * rows + lax.broadcasted_iota(jnp.int32, (rows, LANES), 0)
        chosen = select_from(pos, starts, ends, id_ref, rank)
        main = dot_nn(block, slice_ref[...])
        small = dot_nt(block, down_ref[: 3 * LANES, :])
        for j in range(3):
            cut = slice(j * LANES, (j + 1) * LANES)
            low = (small[:, cut] * chosen).astype(BF16)
            small_ref[at, cut] = low
            value = main[:, cut] + dot_nn(low, up_ref[cut, lanes])
            if j == 0:
                value = value + bias_ref[0:1, lanes]

                @pl.when(t // geo.groups == part)
                def _():
                    inner = pl.ds(pl.multiple_of((t % geo.groups) * rows, rows), rows)
                    q_ref[inner, :] = value.astype(BF16)
            elif j == 1:
                k_ref[at, :] = value.astype(BF16)
            else:
                v_ref[at, :] = (value + bias_ref[1:2, lanes]).astype(BF16)
        return carry

    lax.fori_loop(0, geo.seq, project, 0)

    scale = HEAD_DIM ** (-0.5)
    chunk = min(2048, geo.keys)
    chunks = geo.keys // chunk
    first_head = lax.broadcasted_iota(jnp.int32, (rows, LANES), 1) < HEAD_DIM

    def att_copy(b):
        return pltpu.make_async_remote_copy(
            src_ref=att_buf.at[b],
            dst_ref=att_ref.at[:, lanes],
            send_sem=att_send.at[b],
            recv_sem=att_recv.at[g],
            device_id=(part * geo.groups + b, w),
            device_id_type=MESH,
        )

    def attend(i, carry):
        for n in range(early_ticks, loop_ticks):

            @pl.when(i == 2 * (n - early_ticks) + 1)
            def _():
                tick(n)

        b = (g + 1 + i) % geo.groups
        inner = pl.ds(pl.multiple_of(b * rows, rows), rows)
        query = q_ref[inner, :] * jnp.asarray(scale, BF16)
        q_pos = (part * geo.groups + b) * rows + lax.broadcasted_iota(jnp.int32, (rows, 1), 0)
        q_seg = segment_from(q_pos, starts)
        results = []
        for h in range(PAIR):
            mask = first_head if h == 0 else jnp.logical_not(first_head)
            q_head = jnp.where(mask, query, jnp.zeros_like(query))

            def one(c, state):
                top, total, acc = state
                keys_at = pl.ds(pl.multiple_of(c * chunk, chunk), chunk)
                score = dot_nt(q_head, k_ref[keys_at, :])
                score = jnp.where(q_seg == seg_buf[:, keys_at], score, -1e30)
                peak = jnp.max(score, axis=1, keepdims=True)
                if top is not None:
                    peak = jnp.maximum(top, peak)
                weight = jnp.exp(score - peak)
                add = jnp.sum(weight, axis=1, keepdims=True)
                out = dot_nn(weight.astype(BF16), v_ref[keys_at, :])
                if top is not None:
                    fade = jnp.exp(top - peak)
                    add = add + total * fade
                    out = out + acc * fade
                return peak, add, out

            state = one(0, (None, None, None))
            if chunks > 1:
                state = lax.fori_loop(1, chunks, one, state)
            top, total, acc = state
            results.append((acc / total, top + jnp.log(total)))
        out = jnp.where(first_head, results[0][0], results[1][0])
        o_ref[inner, :] = out
        lse_ref[inner, :] = jnp.where(first_head, results[0][1], results[1][1])
        att_buf[b] = out.astype(BF16)

        @pl.when(b != g)
        def _():
            att_copy(b).start()

        return carry

    lax.fori_loop(0, geo.groups, attend, 0)
    own_att = pltpu.make_async_copy(att_buf.at[g], att_ref.at[:, lanes], local_sem.at[0])
    own_att.start()

    def att_arrivals():
        for d in range(1, geo.groups):
            other = (g + d) % geo.groups
            cut = pl.ds(pl.multiple_of(other * LANES, LANES), LANES)
            pltpu.make_async_remote_copy(
                src_ref=att_ref.at[:, cut],
                dst_ref=att_ref.at[:, cut],
                send_sem=att_send.at[other],
                recv_sem=att_recv.at[other],
                device_id=(part * geo.groups + other, w),
                device_id_type=MESH,
            ).wait_recv()
        own_att.wait()

    if inside:
        layer_rest(geo, rank, r, starts, ends, id_ref, down_ref, up_ref, att_arrivals, complete, tick, loop_ticks, tick_count, len_ref.shape[1])
    else:
        att_arrivals()

    for d in range(1, geo.groups):
        att_copy((g + d) % geo.groups).wait_send()
    tok.wait_sends()
    for j in range(3):

        @pl.when(w < wt - 1)
        def _():
            slice_copy(j, w, True).wait_send()

        @pl.when(w > 0)
        def _():
            slice_copy(j, w, False).wait_send()

        for n in range(wt - 1):
            p = nth_plane(n)

            @pl.when((p < w) & (w < wt - 1))
            def _():
                slice_copy(j, p, True).wait_send()

            @pl.when((p > w) & (w > 0))
            def _():
                slice_copy(j, p, False).wait_send()

    for m in range(weight_count):
        @pl.when(w < wt - 1)
        def _():
            line_copy(m, w, True, True).wait_send()

        @pl.when(w > 0)
        def _():
            line_copy(m, w, False, True).wait_send()

    for m, j in units:
        p = nth_plane(j)

        @pl.when((p < w) & (w < wt - 1))
        def _():
            line_copy(m, p, True, False).wait_send()

        @pl.when((p > w) & (w > 0))
        def _():
            line_copy(m, p, False, False).wait_send()

        weight_spread(m, p).wait_sends()


def layer_rest(
    geo, rank, r, starts, ends, id_ref, down_ref, up_ref, att_arrivals, complete, tick, ticked, tick_count, docs
):
    s, w = lax.axis_index("seq"), lax.axis_index("wt")
    rows, width, groups = geo.rows, geo.width, geo.groups
    part, g = s // groups, s % groups
    hidden = r.full_fc1.shape[1]
    step = min(512, hidden)
    steps = hidden // step
    band = 2 * LANES
    bands = width // band
    lane_count = r.fc1_down.shape[0]
    out_rows = slice(3 * lane_count, 4 * lane_count)
    pos = s * rows + lax.broadcasted_iota(jnp.int32, (rows, LANES), 0)
    chosen = select_from(pos, starts, ends, id_ref, rank)

    every = placement(id_ref, docs, rank, lane_count)[0]
    doc_rows = docs * rank
    in_doc = (lax.broadcasted_iota(jnp.int32, (rows, LANES), 1) // rank) == segment_from(pos, starts)

    def masked(value):
        return (value * chosen).astype(BF16)

    def by_doc(low):
        return jnp.where(in_doc, dot_nn(low, every), 0.0).astype(BF16)

    def doc_grad(low_by_doc, value):
        return dot_tn(low_by_doc, value)[:doc_rows].astype(BF16)

    def at_step(i):
        return pl.ds(pl.multiple_of(i * step, step), step)

    def at_band(i):
        return pl.ds(pl.multiple_of(i * band, band), band)

    pending = list(range(ticked, tick_count))
    first_ticks, pending = pending[:1], pending[1:]
    for n in first_ticks:
        tick(n)
    att_arrivals()
    complete(0)
    att = r.att[...]
    small_out = masked(dot_nt(att, down_ref[out_rows, :]))

    def out_band(i, carry):
        cut = at_band(i)
        value = dot_nn(r.att[...], r.full_out[:, cut]) + r.out_bias[:, cut]
        value = value + dot_nn(small_out, up_ref[out_rows, cut])
        r.y[:, cut] = value + r.tok[s, :, cut].astype(F32)
        return carry

    lax.fori_loop(0, bands, out_band, 0)
    unit1, spread1 = normed(r.y[...])
    h1 = unit1 * r.gain1[...] + r.shift1[...]
    r.unit1[...] = unit1
    r.h1[...] = h1
    h1_low = h1.astype(BF16)
    r.h1_low[...] = h1_low
    small_fc1 = masked(dot_nt(h1_low, r.fc1_down[...]))

    middle = max(len(pending) - 3, 0)
    for n in pending[:middle]:
        tick(n)
    pending = pending[middle:]
    complete(1)

    def fc1_step(i, acc):
        for n, t in enumerate(pending):
            @pl.when(i == min(2 * n + 1, steps - 1))
            def _():
                tick(t)

        cut = at_step(i)
        pre = dot_nn(r.h1_low[...], r.full_fc1[:, cut]) + r.fc1_bias[:, cut]
        pre = pre + dot_nn(small_fc1, r.fc1_up[:, cut])
        share = 0.5 + 0.5 * erf(pre * 0.7071067811865476)
        act = (pre * share).astype(BF16)
        r.act[:, cut] = act
        r.slope[:, cut] = share + pre * (jnp.exp(-0.5 * pre * pre) * 0.3989422804014327)
        return acc + dot_nt(act, r.fc2_down[:, cut])

    small_fc2 = masked(lax.fori_loop(0, steps, fc1_step, jnp.zeros((rows, lane_count), F32)))
    complete(2)

    def fc2_band(i, carry):
        cut = at_band(i)
        value = dot_nn(r.act[...], r.full_fc2[:, cut]) + r.fc2_bias[:, cut]
        r.y[:, cut] = value + dot_nn(small_fc2, r.fc2_up[:, cut]) + r.h1[:, cut]
        return carry

    lax.fori_loop(0, bands, fc2_band, 0)
    unit2, spread2 = normed(r.y[...])
    r.output[...] = unit2 * r.gain2[...] + r.shift2[...]
    d_second = normed_back(r.cotangent[...].astype(F32), r.gain2[...], unit2, spread2)
    r.y[...] = d_second
    d_y = d_second.astype(BF16)
    low_fc2 = masked(dot_nt(d_y, r.fc2_up[...]))
    r.g_fc2_up[...] = doc_grad(by_doc(small_fc2), d_y)
    low_fc2_doc, small_fc1_doc = by_doc(low_fc2), by_doc(small_fc1)

    def back_step(i, acc):
        cut = at_step(i)
        d_act = dot_nt(d_y, r.full_fc2[cut, :]) + dot_nn(low_fc2, r.fc2_down[:, cut])
        d_pre = (d_act * r.slope[:, cut]).astype(BF16)
        r.d_pre[:, cut] = d_pre
        r.g_fc2_down[:, cut] = doc_grad(low_fc2_doc, r.act[:, cut])
        r.g_fc1_up[:, cut] = doc_grad(small_fc1_doc, d_pre)
        return acc + dot_nt(d_pre, r.fc1_up[:, cut])

    low_fc1 = masked(lax.fori_loop(0, steps, back_step, jnp.zeros((rows, lane_count), F32)))

    def make_early(chip, whose):
        return owner_columns((r.g_fc2_up, r.g_fc1_up, r.g_fc2_down), chip * 2 + whose, groups)

    early = PairSum(
        groups // 2,
        g // 2,
        s % 2,
        part * groups,
        w,
        (r.set_out, r.set_in, r.set_far),
        [r.set_sems.at[i] for i in range(4)],
        make_early,
    )
    early.run()
    r.g_fc1_down[...] = doc_grad(by_doc(low_fc1), r.h1_low[...])

    def back_band(i, carry):
        cut = at_band(i)
        value = dot_nt(r.d_pre[...], r.full_fc1[cut, :]) + dot_nn(low_fc1, r.fc1_down[:, cut])
        r.y[:, cut] += value
        return carry

    lax.fori_loop(0, bands, back_band, 0)
    d_first = normed_back(r.y[...], r.gain1[...], r.unit1[...], spread1)
    r.d_first[...] = d_first
    d_z = d_first.astype(BF16)
    low_out = masked(dot_nt(d_z, up_ref[out_rows, :]))

    def back_copy(b):
        return pltpu.make_async_remote_copy(
            src_ref=r.d_att_buf.at[b],
            dst_ref=r.d_heads.at[pl.ds(pl.multiple_of(g * rows, rows), rows)],
            send_sem=r.back_send.at[b],
            recv_sem=r.back_recv.at[g],
            device_id=(part * groups + b, w),
            device_id_type=MESH,
        )

    def attended_band(i, carry):
        n = (g // 2 + 1 + i) % bands
        cut = at_band(n)
        value = dot_nt(d_z, r.full_out[cut, :]) + dot_nn(low_out, down_ref[out_rows, cut])
        value = value.astype(BF16)
        for h in range(2):
            b = 2 * n + h
            r.d_att_buf[b] = value[:, h * LANES : (h + 1) * LANES]

            @pl.when(b != g)
            def _():
                back_copy(b).start()

        return carry

    lax.fori_loop(0, bands, attended_band, 0)
    own = pltpu.make_async_copy(
        r.d_att_buf.at[g], r.d_heads.at[pl.ds(pl.multiple_of(g * rows, rows), rows)], r.local_sem.at[0]
    )
    own.start()
    r.g_out_down[...] = doc_grad(by_doc(low_out), r.att[...])
    r.g_out_up[...] = doc_grad(by_doc(small_out), d_z)
    r.early_sum[...] = early.finish().astype(BF16)
    early.drain()
    for d in range(1, groups):
        other = (g + d) % groups
        here = r.d_heads.at[pl.ds(pl.multiple_of(other * rows, rows), rows)]
        pltpu.make_async_remote_copy(
            src_ref=here,
            dst_ref=here,
            send_sem=r.back_send.at[other],
            recv_sem=r.back_recv.at[other],
            device_id=(part * groups + other, w),
            device_id_type=MESH,
        ).wait_recv()
        back_copy(other).wait_send()
    own.wait()


def forward_attention(geo, rank, lengths, ids, tokens, w_qkv, down, up, bias, mlp):
    rows, width = geo.rows, geo.width
    inside = mlp is not None
    mlp = mlp or ()
    any_spec = pl.BlockSpec(memory_space=pl.ANY)
    vmem = pl.BlockSpec(memory_space=pltpu.VMEM)
    smem = pl.BlockSpec(memory_space=pltpu.SMEM)
    lane_count = down.shape[0] // 4
    struct = jax.ShapeDtypeStruct
    shapes = [
        struct((geo.queries, LANES), BF16),
        struct((geo.keys, LANES), BF16),
        struct((geo.keys, LANES), BF16),
        struct((geo.queries, LANES), F32),
        struct((geo.queries, LANES), F32),
        struct((width, 3 * LANES), BF16),
        struct((geo.keys, 3 * LANES), BF16),
    ]
    specs = [vmem] * 7
    dma = pltpu.SemaphoreType.DMA
    count = 3 if inside else 0
    units = 1 + count * geo.wt
    scratch = [
        pltpu.VMEM((geo.seq, rows, width), BF16),
        pltpu.VMEM((1, geo.keys), jnp.int32),
        pltpu.VMEM((geo.groups, rows, LANES), BF16),
        dma((4 + count,)),
        dma((Spread.KINDS, units)),
        dma((Spread.KINDS, units)),
        dma((2, 3, geo.wt)),
        dma((3, geo.wt)),
        dma((2, max(count, 1) * geo.wt)),
        dma((max(count, 1) * geo.wt,)),
        dma((geo.groups,)),
        dma((geo.groups,)),
    ]
    if inside:
        hidden = mlp[1].shape[1]
        doc_rows = lengths.shape[1] * rank
        early = (width + 2 * hidden) // geo.groups
        near = geo.groups // 2
        shapes += [
            struct((rows, width), F32),
            struct((rows, width), F32),
            struct((geo.queries, LANES), BF16),
            struct((doc_rows, width), BF16),
            struct((doc_rows, width), BF16),
            struct((doc_rows, width), BF16),
            struct((doc_rows, early), BF16),
        ]
        specs += [vmem, vmem, any_spec] + [vmem] * 4
        scratch += [
            pltpu.VMEM((rows, width), BF16),
            pltpu.VMEM((width, width), BF16),
            pltpu.VMEM((width, hidden), BF16),
            pltpu.VMEM((hidden, width), BF16),
            pltpu.VMEM((rows, width), F32),
            pltpu.VMEM((rows, width), F32),
            pltpu.VMEM((rows, width), BF16),
            pltpu.VMEM((rows, hidden), BF16),
            pltpu.VMEM((rows, hidden), F32),
            pltpu.VMEM((rows, hidden), BF16),
            pltpu.VMEM((rows, width), F32),
            pltpu.VMEM((geo.groups, rows, LANES), BF16),
            dma((geo.groups,)),
            dma((geo.groups,)),
            pltpu.VMEM((doc_rows, width), BF16),
            pltpu.VMEM((doc_rows, hidden), BF16),
            pltpu.VMEM((doc_rows, hidden), BF16),
            pltpu.VMEM((near, doc_rows, early), BF16),
            pltpu.VMEM((near, doc_rows, early), BF16),
            pltpu.VMEM((near, doc_rows, early), BF16),
            dma((4, near)),
        ]
    else:
        shapes += [struct((rows, width), BF16)]
        specs += [any_spec]
    return pl.pallas_call(
        functools.partial(forward_kernel, geo, inside, rank),
        out_shape=shapes,
        in_specs=[smem, smem, any_spec, any_spec, vmem, vmem, vmem] + [any_spec] * count + [vmem] * (len(mlp) - count),
        out_specs=specs,
        scratch_shapes=scratch,
        compiler_params=pltpu.CompilerParams(
            collective_id=0, has_side_effects=True, vmem_limit_bytes=VMEM_LIMIT
        ),
        name="layer",
    )(lengths, ids, tokens, w_qkv, down, up, bias, *mlp)


def backward_kernel(geo, len_ref, part_ref, q_ref, k_ref, v_ref, o_ref, lse_ref, g_ref, dq_ref, dk_ref, dv_ref, dk_acc, dv_acc):
    rows = min(512, geo.queries)
    block = min(512, geo.keys)
    part = part_ref[0, 0]
    scale = HEAD_DIM ** (-0.5)
    starts, ends = doc_bounds(len_ref)
    first_head = lax.broadcasted_iota(jnp.int32, (rows, LANES), 1) < HEAD_DIM
    dk_acc[...] = jnp.zeros_like(dk_acc)
    dv_acc[...] = jnp.zeros_like(dv_acc)

    def seg_of(position):
        seg = jnp.int32(0)
        for start in starts[1:]:
            seg = seg + (position >= start).astype(jnp.int32)
        return seg

    def pick(values, index):
        found = values[0]
        for i in range(1, len(values)):
            found = jnp.where(index == i, values[i], found)
        return found

    def both_heads(value):
        zero = jnp.zeros_like(value)
        return jnp.concatenate([jnp.where(first_head, value, zero), jnp.where(first_head, zero, value)], axis=0)

    def query_block(b, carry):
        at = pl.ds(pl.multiple_of(b * rows, rows), rows)
        origin = part * geo.queries + b * rows
        query = both_heads(q_ref[at, :] * jnp.asarray(scale, BF16))
        cot = both_heads(g_ref[at, :])
        scaled = cot * jnp.asarray(scale, BF16)
        lse = jnp.concatenate([lse_ref[at, h * HEAD_DIM : h * HEAD_DIM + 1] for h in range(PAIR)], axis=0)
        out = o_ref[at, :]
        dot = jnp.sum(scaled.astype(F32) * jnp.concatenate([out, out], axis=0), axis=1, keepdims=True)
        q_pos = origin + lax.broadcasted_iota(jnp.int32, (rows, 1), 0)
        q_seg = segment_from(q_pos, starts)
        q_seg = jnp.concatenate([q_seg, q_seg], axis=0)
        low = pick(starts, seg_of(origin)) // block
        high = (pick(ends, seg_of(origin + rows - 1)) + block - 1) // block

        def key_block(c, acc):
            keys_at = pl.ds(pl.multiple_of(c * block, block), block)
            key, value = k_ref[keys_at, :], v_ref[keys_at, :]
            k_pos = c * block + lax.broadcasted_iota(jnp.int32, (1, block), 1)
            score = jnp.where(q_seg == segment_from(k_pos, starts), dot_nt(query, key), -1e30)
            prob = jnp.exp(score - lse)
            raw = (prob * (dot_nt(scaled, value) - dot)).astype(BF16)
            dk_acc[keys_at, :] += dot_tn(raw, query)
            dv_acc[keys_at, :] += dot_tn(prob.astype(BF16), cot)
            return acc + dot_nn(raw, key)

        acc = lax.fori_loop(low, high, key_block, jnp.zeros((PAIR * rows, LANES), F32))
        dq_ref[at, :] = jnp.where(first_head, acc[:rows], acc[rows:]).astype(BF16)
        return carry

    lax.fori_loop(0, geo.queries // rows, query_block, 0)
    dk_ref[...] = (dk_acc[...] * HEAD_DIM**0.5).astype(BF16)
    dv_ref[...] = dv_acc[...].astype(BF16)


def backward_attention(geo, lengths, part, q, k, v, o, lse, d_heads):
    smem = pl.BlockSpec(memory_space=pltpu.SMEM)
    vmem = pl.BlockSpec(memory_space=pltpu.VMEM)
    return pl.pallas_call(
        functools.partial(backward_kernel, geo),
        out_shape=[
            jax.ShapeDtypeStruct((geo.queries, LANES), BF16),
            jax.ShapeDtypeStruct((geo.keys, LANES), BF16),
            jax.ShapeDtypeStruct((geo.keys, LANES), BF16),
        ],
        in_specs=[smem, smem] + [vmem] * 6,
        out_specs=[vmem] * 3,
        scratch_shapes=[pltpu.VMEM((geo.keys, LANES), F32)] * 2,
        compiler_params=pltpu.CompilerParams(vmem_limit_bytes=VMEM_LIMIT),
        name="attend_back",
    )(lengths, part, q, k, v, o, lse, d_heads)


class Block:
    def __init__(self, geo):
        chips = geo.groups // 2
        self.nx = min(geo.nx, chips)
        self.ny = chips // self.nx


class PairSum:
    def __init__(self, count, me, core, first, w, bufs, sems, make, stage=None):
        self.count, self.me, self.core, self.first, self.w = count, me, core, first, w
        self.near_out, self.near_in, self.far_in = bufs
        self.near_send, self.near_recv, self.far_send, self.far_recv = sems
        self.make = make
        self.slots = self.near_out.shape[0]
        self.stage = stage

    def slot(self, chip):
        return ((chip + self.count - self.me + self.count - 1) % self.count) % self.slots

    def near(self, chip):
        return pltpu.make_async_remote_copy(
            src_ref=self.near_out.at[self.slot(chip)],
            dst_ref=self.near_in.at[chip],
            send_sem=self.near_send.at[chip],
            recv_sem=self.near_recv.at[chip],
            device_id=(self.first + self.me * 2 + 1 - self.core, self.w),
            device_id_type=MESH,
        )

    def far(self, chip):
        return pltpu.make_async_remote_copy(
            src_ref=self.near_in.at[chip],
            dst_ref=self.far_in.at[self.me],
            send_sem=self.far_send.at[chip],
            recv_sem=self.far_recv.at[self.me],
            device_id=(self.first + chip * 2 + self.core, self.w),
            device_id_type=MESH,
        )

    def far_arrival(self, chip):
        return pltpu.make_async_remote_copy(
            src_ref=self.far_in.at[chip],
            dst_ref=self.far_in.at[chip],
            send_sem=self.far_send.at[chip],
            recv_sem=self.far_recv.at[chip],
            device_id=(self.first + chip * 2 + self.core, self.w),
            device_id_type=MESH,
        )

    def run(self):
        def start(d):
            chip = (self.me + 1 + d) % self.count
            if self.slots < self.count:

                @pl.when(d >= self.slots)
                def _():
                    self.near((self.me + 1 + d - self.slots) % self.count).wait_send()

            self.near_out[d % self.slots] = self.make(chip, 1 - self.core).astype(BF16)
            self.near(chip).start()

        def send(d):
            chip = (self.me + 1 + d) % self.count
            own = self.make(chip, self.core)
            self.near(chip).wait_recv()
            self.near_in[chip] = (own + self.near_in[chip].astype(F32)).astype(BF16)
            self.far(chip).start()

        def step(d, carry):
            start(d)
            send(d - 1)
            return carry

        start(0)
        lax.fori_loop(1, self.count, step, 0)

    def finish(self):
        total = self.make(self.me, self.core)
        self.near(self.me).wait_recv()
        total = total + self.near_in[self.me].astype(F32)
        if self.stage is None:
            for d in range(1, self.count):
                chip = (self.me + d) % self.count
                self.far_arrival(chip).wait_recv()
                total = total + self.far_in[chip].astype(F32)
            return total
        stage, sem = self.stage

        def fetch(d):
            chip = (self.me + d) % self.count
            return pltpu.make_async_copy(self.far_in.at[chip], stage.at[d % 2], sem.at[d % 2])

        self.far_arrival((self.me + 1) % self.count).wait_recv()
        fetch(1).start()
        for d in range(1, self.count):
            if d + 1 < self.count:
                self.far_arrival((self.me + d + 1) % self.count).wait_recv()
                fetch(d + 1).start()
            fetch(d).wait()
            total = total + stage[d % 2].astype(F32)
        return total

    def drain(self):
        for d in range(self.count):
            chip = (self.me + 1 + d) % self.count
            if d >= self.count - self.slots:
                self.near(chip).wait_send()
            if d < self.count - 1:
                self.far(chip).wait_send()


def closing_kernel(
    geo,
    rank,
    single_count,
    early,
    len_ref,
    id_ref,
    tokens_ref,
    first_ref,
    dq_ref,
    dk_ref,
    dv_ref,
    slice_ref,
    down_ref,
    up_ref,
    small_ref,
    *refs,
):
    singles = refs[:single_count]
    early_ref = refs[single_count] if early else None
    (
        grad_ref,
        sum1_ref,
        sum2_ref,
        tok_far,
        tok_out,
        tok_in,
        tok_stage,
        small_buf,
        set1_out,
        set1_in,
        set1_far,
        set2_out,
        set2_in,
        set2_far,
        down_acc,
        up_acc,
        mine1,
        mine2,
        place_buf,
        fold_buf,
        all1,
        all2,
        places,
        done1,
        done2,
        tok_sems,
        set1_sems,
        set2_sems,
        line_send,
        line_recv,
        spread_send,
        spread_recv,
        local_sem,
        stage_sem,
        small_sem,
    ) = refs[single_count + early :]
    x, y, core, w = device_here(geo)
    s = lax.axis_index("seq")
    rows, width, wt, groups, parts = geo.rows, geo.width, geo.wt, geo.groups, geo.parts
    part, g = s // groups, s % groups
    docs = len_ref.shape[1]
    doc_rows = docs * rank
    lane_count = down_ref.shape[0] // 4
    lanes = pl.ds(pl.multiple_of(g * LANES, LANES), LANES)
    starts, ends = doc_bounds(len_ref)
    greet_all(geo)

    def iota(shape, dim):
        return lax.broadcasted_iota(jnp.int32, shape, dim)

    def zero_one(condition):
        return jnp.where(condition, 1.0, 0.0).astype(BF16)

    def chosen_of(t):
        pos = t * rows + iota((rows, LANES), 0)
        return select_from(pos, starts, ends, id_ref, rank)

    def fold(j):
        a, b = iota((lane_count, LANES), 0), iota((lane_count, LANES), 1)
        return zero_one((b >= j * rank) & (b < (j + 1) * rank) & (a % rank == b - j * rank))

    def make_tokens(chip, whose):
        t = chip * 2 + whose
        at = pl.ds(pl.multiple_of(t * rows, rows), rows)
        if parts == 1:
            d_q = dq_ref[at, :]
        else:
            inner = pl.ds(pl.multiple_of((t % groups) * rows, rows), rows)
            d_q = jnp.where(t // groups == part, dq_ref[inner, :], jnp.zeros((rows, LANES), BF16))
        pieces = [d_q, dk_ref[at, :], dv_ref[at, :]]
        chosen = chosen_of(t)
        total = jnp.zeros((rows, width), F32)
        low = jnp.zeros((rows, LANES), F32)
        for j in range(3):
            total = total + dot_nt(pieces[j], slice_ref[:, j * LANES : (j + 1) * LANES])
            part_low = dot_nt(pieces[j], up_ref[pl.ds(j * lane_count, lane_count), lanes])
            low = low + dot_nn((part_low * chosen).astype(BF16), fold(j))
        return jnp.concatenate([total, low], axis=1)

    tok = PairSum(
        geo.seq // 2, s // 2, core, 0, w, (tok_out, tok_in, tok_far), [tok_sems.at[i] for i in range(4)], make_tokens,
        (tok_stage, stage_sem),
    )

    def by_document(value):
        return dot_tn(fold_buf[...], value)[:doc_rows]

    def make_set1(chip, whose):
        return owner_columns(singles, chip * 2 + whose, groups)

    def make_set2(chip, whose):
        owner = chip * 2 + whose
        cut = pl.ds(pl.multiple_of(owner * LANES, LANES), LANES)
        return jnp.concatenate([down_acc[j * doc_rows : (j + 1) * doc_rows, cut] for j in range(3)], axis=1)

    chips = groups // 2
    set1 = PairSum(
        chips, g // 2, core, part * groups, w, (set1_out, set1_in, set1_far), [set1_sems.at[i] for i in range(4)], make_set1
    )
    set2 = PairSum(
        chips, g // 2, core, part * groups, w, (set2_out, set2_in, set2_far), [set2_sems.at[i] for i in range(4)], make_set2
    )

    def peer(n):
        plane = (w + n) % wt
        other = (part + n // wt) % parts
        return other * groups + g, plane, other * wt + plane

    mine_at = part * wt + w

    late = set1_out.shape[2]
    whole = mine1.shape[1]

    def cut_of(kind, ref):
        if kind == 0:
            return ref.at[:, pl.ds(0, late)]
        if kind == 3:
            return ref.at[:, pl.ds(late, whole - late)]
        return ref

    def line_copy(kind, n, src, dst_all):
        device, plane, _ = peer(n)
        return pltpu.make_async_remote_copy(
            src_ref=cut_of(kind, src),
            dst_ref=cut_of(kind, dst_all.at[mine_at]),
            send_sem=line_send.at[kind, n],
            recv_sem=line_recv.at[kind, mine_at],
            device_id=(device, plane),
            device_id_type=MESH,
        )

    def line_arrival(kind, n, dst_all):
        device, plane, at = peer(n)
        return pltpu.make_async_remote_copy(
            src_ref=cut_of(kind, dst_all.at[at]),
            dst_ref=cut_of(kind, dst_all.at[at]),
            send_sem=line_send.at[kind, n],
            recv_sem=line_recv.at[kind, at],
            device_id=(device, plane),
            device_id_type=MESH,
        )

    peers = range(1, wt * parts)

    block = Block(geo)
    chip_here = g // 2
    here = (chip_here % block.nx, chip_here // block.nx, core, w)

    def region_of(ref):
        def region(ux, uy, whose, half):
            one = ref.at[(uy * block.nx + ux) * 2 + whose]
            if half is None:
                return one
            return one.at[pl.ds(half * (lane_count // 2), lane_count // 2)]

        return region

    spreads = [
        Spread(block, here, region_of(ref), spread_send, spread_recv, i, part * groups)
        for i, ref in enumerate((sum1_ref, sum2_ref))
    ]
    finals = [done1, done2]
    outs = [sum1_ref, sum2_ref]

    def place(kind, mine, dst_all):
        total = dot_nn(place_buf[:, :doc_rows], mine[...])
        for n in peers:
            line_arrival(kind, n, dst_all).wait_recv()
            if kind == 0:
                line_arrival(2, n, places).wait_recv()
                if early:
                    line_arrival(3, n, dst_all).wait_recv()
            at = peer(n)[2]
            total = total + dot_nn(places[at][:, :doc_rows], dst_all[at])
        finals[kind][...] = total.astype(BF16)
        for way in (0, 1, 4):
            spreads[kind].go(way, own=finals[kind])
        pltpu.make_async_copy(finals[kind], outs[kind].at[g], local_sem.at[kind]).start()

    def pass_on(kind):
        spread = spreads[kind]
        spread.wait(0)
        spread.go(2)
        spread.go(5)
        spread.wait(1)
        spread.go(3)
        spread.go(6)

    def pass_last(kind):
        spread = spreads[kind]
        spread.wait(2)
        spread.go(7)
        spread.wait(3)
        spread.go(8)

    place_buf[...], fold_buf[...] = placement(id_ref, docs, rank, lane_count)
    for n in peers:
        line_copy(2, n, place_buf, places).start()
    if early:
        mine1[:, late:] = early_ref[...]
        for n in peers:
            line_copy(3, n, mine1, all1).start()

    set1.run()
    tok.run()

    def small_copy(t):
        return pltpu.make_async_copy(
            small_ref.at[pl.ds(pl.multiple_of(t * rows, rows), rows)], small_buf.at[t % 2], small_sem.at[t % 2]
        )

    def add_up(t, carry):
        at = pl.ds(pl.multiple_of(t * rows, rows), rows)

        @pl.when(t + 1 < geo.seq)
        def _():
            small_copy(t + 1).start()

        small_copy(t).wait()
        for j in range(3):
            cut = slice(j * LANES, (j + 1) * LANES)
            if j == 0:
                if parts == 1:
                    value = dq_ref[at, :]
                else:
                    inner = pl.ds(pl.multiple_of((t % groups) * rows, rows), rows)
                    value = jnp.where(t // groups == part, dq_ref[inner, :], jnp.zeros((rows, LANES), BF16))
            else:
                value = (dk_ref if j == 1 else dv_ref)[at, :]
            up_acc[cut, :] += dot_tn(small_buf[t % 2][:, cut], value)
        return carry

    up_acc[...] = jnp.zeros_like(up_acc)
    small_copy(0).start()
    lax.fori_loop(0, geo.seq, add_up, 0)

    mine1[:, :late] = set1.finish().astype(BF16)
    for n in peers:
        line_copy(0, n, mine1, all1).start()

    total = tok.finish()
    low = total[:, width:].astype(BF16)
    total = total[:, :width] + first_ref[...]
    chosen = chosen_of(s)
    pos = s * rows + iota((rows, doc_rows), 0)
    doc_of = iota((rows, doc_rows), 1) // rank
    in_doc = doc_of == segment_from(pos, starts)
    tokens = tokens_ref[...]
    for j in range(3):
        a, b = iota((LANES, lane_count), 0), iota((LANES, lane_count), 1)
        widen = zero_one((a >= j * rank) & (a < (j + 1) * rank) & (b % rank == a - j * rank))
        wide = (dot_nn(low, widen) * chosen).astype(BF16)
        total = total + dot_nn(wide, down_ref[j * lane_count : (j + 1) * lane_count, :])
        by_doc = dot_nn(low, widen[:, :doc_rows])
        by_doc = jnp.where(in_doc, by_doc, 0.0).astype(BF16)
        down_acc[j * doc_rows : (j + 1) * doc_rows, :] = dot_tn(by_doc, tokens)
    set2.run()
    grad_ref[...] = total
    place(0, mine1, all1)
    for j in range(3):
        mine2[:, (3 + j) * LANES : (4 + j) * LANES] = by_document(
            up_acc[j * lane_count : (j + 1) * lane_count, :].astype(BF16)
        ).astype(BF16)
    mine2[:, : 3 * LANES] = set2.finish().astype(BF16)
    for n in peers:
        line_copy(1, n, mine2, all2).start()
    pass_on(0)
    pass_last(0)
    place(1, mine2, all2)
    pass_on(1)
    pass_last(1)
    for kind in range(2):
        for way in range(4, 9):
            spreads[kind].wait(way)
        spreads[kind].wait_sends()
        pltpu.make_async_copy(finals[kind], outs[kind].at[g], local_sem.at[kind]).wait()
    for n in peers:
        line_copy(0, n, mine1, all1).wait_send()
        line_copy(1, n, mine2, all2).wait_send()
        line_copy(2, n, place_buf, places).wait_send()
        if early:
            line_copy(3, n, mine1, all1).wait_send()
    tok.drain()
    set1.drain()
    set2.drain()


def greet_all(geo):
    s, w = lax.axis_index("seq"), lax.axis_index("wt")
    barrier = pltpu.get_barrier_semaphore()
    part, g = s // geo.groups, s % geo.groups
    for d in range(1, geo.seq):
        pl.semaphore_signal(barrier, inc=1, device_id=((s + d) % geo.seq, w), device_id_type=MESH)
    count = geo.seq - 1
    for d in range(1, geo.wt):
        for q in range(geo.parts):
            other = ((part + q) % geo.parts) * geo.groups + g
            pl.semaphore_signal(barrier, inc=1, device_id=(other, (w + d) % geo.wt), device_id_type=MESH)
            count += 1
    pl.semaphore_wait(barrier, count)


def closing(geo, rank, lengths, ids, tokens, d_first, dq, dk, dv, w_slice, down, up, small, grads, early_sum):
    rows, width = geo.rows, geo.width
    docs = lengths.shape[1]
    doc_rows = docs * rank
    lane_count = down.shape[0] // 4
    early = [] if early_sum is None else [early_sum]
    late = sum(v.shape[1] for v in grads) // geo.groups
    set1 = late + sum(v.shape[1] for v in early)
    set2 = 6 * LANES
    chips, near = geo.seq // 2, geo.groups // 2
    peers = geo.wt * geo.parts
    smem = pl.BlockSpec(memory_space=pltpu.SMEM)
    vmem = pl.BlockSpec(memory_space=pltpu.VMEM)
    any_spec = pl.BlockSpec(memory_space=pl.ANY)
    dma = pltpu.SemaphoreType.DMA
    wide = width + LANES
    return pl.pallas_call(
        functools.partial(closing_kernel, geo, rank, len(grads), len(early)),
        out_shape=[
            jax.ShapeDtypeStruct((rows, width), F32),
            jax.ShapeDtypeStruct((geo.groups, lane_count, set1), BF16),
            jax.ShapeDtypeStruct((geo.groups, lane_count, set2), BF16),
            jax.ShapeDtypeStruct((chips, rows, wide), BF16),
        ],
        in_specs=[smem, smem] + [vmem] * 8 + [any_spec] + [vmem] * (len(grads) + len(early)),
        out_specs=[vmem, any_spec, any_spec, any_spec],
        scratch_shapes=[
            pltpu.VMEM((min(chips, 4), rows, wide), BF16),
            pltpu.VMEM((chips, rows, wide), BF16),
            pltpu.VMEM((2, rows, wide), BF16),
            pltpu.VMEM((2, rows, 3 * lane_count), BF16),
            pltpu.VMEM((near, doc_rows, late), BF16),
            pltpu.VMEM((near, doc_rows, late), BF16),
            pltpu.VMEM((near, doc_rows, late), BF16),
            pltpu.VMEM((near, doc_rows, 3 * LANES), BF16),
            pltpu.VMEM((near, doc_rows, 3 * LANES), BF16),
            pltpu.VMEM((near, doc_rows, 3 * LANES), BF16),
            pltpu.VMEM((3 * doc_rows, width), F32),
            pltpu.VMEM((3 * lane_count, LANES), F32),
            pltpu.VMEM((doc_rows, set1), BF16),
            pltpu.VMEM((doc_rows, set2), BF16),
            pltpu.VMEM((lane_count, LANES), BF16),
            pltpu.VMEM((lane_count, LANES), BF16),
            pltpu.VMEM((peers, doc_rows, set1), BF16),
            pltpu.VMEM((peers, doc_rows, set2), BF16),
            pltpu.VMEM((peers, lane_count, LANES), BF16),
            pltpu.VMEM((lane_count, set1), BF16),
            pltpu.VMEM((lane_count, set2), BF16),
            dma((4, chips)),
            dma((4, near)),
            dma((4, near)),
            dma((4, peers)),
            dma((4, peers)),
            dma((Spread.KINDS, 2)),
            dma((Spread.KINDS, 2)),
            dma((2,)),
            dma((2,)),
            dma((2,)),
        ],
        compiler_params=pltpu.CompilerParams(
            collective_id=1, has_side_effects=True, vmem_limit_bytes=VMEM_LIMIT
        ),
        name="close",
    )(lengths, ids, tokens, d_first, dq, dk, dv, w_slice, down, up, small, *grads, *early)


def unpack_kernel(one_ref, two_ref, down_ref, up_ref, fc1_down_ref, fc2_up_ref, fc1_up_ref, fc2_down_ref):
    for j in range(3):
        down_ref[j] = two_ref[0, :, j * LANES : (j + 1) * LANES].astype(F32)
        up_ref[j] = two_ref[0, :, (3 + j) * LANES : (4 + j) * LANES].astype(F32)
    at = 0
    for ref in (down_ref.at[3], up_ref.at[3], fc1_down_ref, fc2_up_ref, fc1_up_ref, fc2_down_ref):
        wide = ref.shape[1]
        ref[...] = one_ref[0, :, at : at + wide].astype(F32)
        at += wide


def unpack(geo, one, two, lane_count):
    groups = geo.groups
    thick = (one.shape[2] - 4 * LANES) // 2

    def whole(wide):
        return jax.ShapeDtypeStruct((lane_count, wide * groups), F32)

    def flat(wide):
        return pl.BlockSpec((lane_count, wide), lambda i: (0, i))

    four = jax.ShapeDtypeStruct((4, lane_count, LANES * groups), F32)
    four_spec = pl.BlockSpec((4, lane_count, LANES), lambda i: (0, 0, i))
    return pl.pallas_call(
        unpack_kernel,
        grid=(groups,),
        out_shape=[four, four, whole(LANES), whole(LANES), whole(thick), whole(thick)],
        in_specs=[
            pl.BlockSpec((1,) + one.shape[1:], lambda i: (i, 0, 0)),
            pl.BlockSpec((1,) + two.shape[1:], lambda i: (i, 0, 0)),
        ],
        out_specs=[four_spec, four_spec, flat(LANES), flat(LANES), flat(thick), flat(thick)],
        compiler_params=pltpu.CompilerParams(vmem_limit_bytes=VMEM_LIMIT),
        name="unpack",
    )(one, two)


def layer_norm(value, gain, shift):
    mean = jnp.mean(value, axis=-1, keepdims=True)
    centred = value - mean
    spread = jnp.mean(centred * centred, axis=-1, keepdims=True)
    return centred * lax.rsqrt(spread + 1e-05) * gain + shift


def gelu_exact(value):
    return jax.nn.gelu(value, approximate=False)


def times_transposed(grad, weight):
    return lax.dot_general(
        grad, weight, (((1,), (1,)), ((), ())), preferred_element_type=jnp.float32
    )


def left_inner(left, right):
    return lax.dot_general(
        left, right, (((0,), (0,)), ((), ())), preferred_element_type=jnp.float32
    )


def stack_down(down):
    return jnp.transpose(down, (1, 0, 2)).reshape(down.shape[1], down.shape[0] * down.shape[2])


def stack_up(up):
    return up.reshape(up.shape[0] * up.shape[1], up.shape[2])


def unstack_down(stacked, adapter_count, rank_size):
    return jnp.transpose(stacked.reshape(stacked.shape[0], adapter_count, rank_size), (1, 0, 2))


def unstack_up(stacked, adapter_count, rank_size):
    return stacked.reshape(adapter_count, rank_size, stacked.shape[1])


def segment_of(positions, starts):
    return jnp.sum((positions[:, None] >= starts[None, :]).astype(jnp.int32), axis=1) - 1


def select_local(tok_rows, lane_count, rank_size, lengths, ids):
    starts = jnp.cumsum(lengths) - lengths
    local_pos = lax.axis_index("seq") * tok_rows + jnp.arange(tok_rows, dtype=jnp.int32)
    local_seg = segment_of(local_pos, starts)
    doc_range = jnp.arange(lengths.shape[0], dtype=jnp.int32)
    chosen = jnp.sum(jnp.where(local_seg[:, None] == doc_range[None, :], ids[None, :], 0), axis=1)
    lane_owner = jnp.arange(lane_count, dtype=jnp.int32) // rank_size
    lane_rank = jnp.arange(lane_count, dtype=jnp.int32) % rank_size
    doc_owner = jnp.repeat(doc_range, rank_size)
    doc_rank = jnp.arange(doc_owner.shape[0], dtype=jnp.int32) % rank_size
    to_doc = (lane_owner[:, None] == jnp.repeat(ids, rank_size)[None, :]) & (lane_rank[:, None] == doc_rank[None, :])
    return (
        (chosen[:, None] == lane_owner[None, :]).astype(jnp.float32),
        to_doc.astype(jnp.bfloat16),
        (local_seg[:, None] == doc_owner[None, :]).astype(jnp.float32),
    )


def feed_forward(
    geo, tokens, cotangent, attended_tok, weights, vectors, attn_maps, fc1_maps, fc2_maps, select
):
    tok_rows, model_width = tokens.shape
    full_out, full_fc1, full_fc2 = [lax.all_gather(v, "wt", axis=0, tiled=True) for v in weights]
    out_bias, norm1_gain, norm1_bias, fc1_bias, fc2_bias, norm2_gain, norm2_bias = vectors
    out_down, out_up = attn_maps
    fc1_down_all, fc1_up_all = fc1_maps
    fc2_down_all, fc2_up_all = fc2_maps
    select, to_doc, in_doc = select

    def by_doc(low):
        return (jnp.dot(low, to_doc, preferred_element_type=jnp.float32) * in_doc).astype(jnp.bfloat16)

    out_main = jnp.dot(attended_tok, full_out, preferred_element_type=jnp.float32)
    small_out = (
        jnp.dot(attended_tok, out_down, preferred_element_type=jnp.float32) * select
    ).astype(jnp.bfloat16)
    z_value = out_main + out_bias + jnp.dot(small_out, out_up, preferred_element_type=jnp.float32)
    first_sum = tokens.astype(jnp.float32) + z_value
    first_norm, norm1_back = jax.vjp(
        lambda value: layer_norm(value, norm1_gain, norm1_bias), first_sum
    )
    first_low = first_norm.astype(jnp.bfloat16)
    fc1_main = jnp.dot(first_low, full_fc1, preferred_element_type=jnp.float32)
    small_fc1 = (
        jnp.dot(first_low, fc1_down_all, preferred_element_type=jnp.float32) * select
    ).astype(jnp.bfloat16)
    pre_act = (
        fc1_main + fc1_bias + jnp.dot(small_fc1, fc1_up_all, preferred_element_type=jnp.float32)
    )
    act_value, gelu_back = jax.vjp(gelu_exact, pre_act)
    act_low = act_value.astype(jnp.bfloat16)
    fc2_main = jnp.dot(act_low, full_fc2, preferred_element_type=jnp.float32)
    small_fc2 = (
        jnp.dot(act_low, fc2_down_all, preferred_element_type=jnp.float32) * select
    ).astype(jnp.bfloat16)
    y_value = (
        fc2_main + fc2_bias + jnp.dot(small_fc2, fc2_up_all, preferred_element_type=jnp.float32)
    )
    output, norm2_back = jax.vjp(
        lambda value: layer_norm(value, norm2_gain, norm2_bias), first_norm + y_value
    )
    d_second = norm2_back(cotangent.astype(jnp.float32))[0]
    d_y = d_second.astype(jnp.bfloat16)
    d_act = times_transposed(d_y, full_fc2)
    low_fc2 = (times_transposed(d_y, fc2_up_all) * select).astype(jnp.bfloat16)
    d_act = d_act + times_transposed(low_fc2, fc2_down_all)
    grad_fc2_up = left_inner(by_doc(small_fc2), d_y)
    grad_fc2_down = left_inner(by_doc(low_fc2), act_low)
    d_pre = gelu_back(d_act)[0].astype(jnp.bfloat16)
    d_first_low = times_transposed(d_pre, full_fc1)
    low_fc1 = (times_transposed(d_pre, fc1_up_all) * select).astype(jnp.bfloat16)
    d_first_low = d_first_low + times_transposed(low_fc1, fc1_down_all)
    grad_fc1_up = left_inner(by_doc(small_fc1), d_pre)
    grad_fc1_down = left_inner(by_doc(low_fc1), first_low)
    d_first = norm1_back(d_second + d_first_low)[0]
    d_z = d_first.astype(jnp.bfloat16)
    d_attended = times_transposed(d_z, full_out)
    low_out = (times_transposed(d_z, out_up) * select).astype(jnp.bfloat16)
    d_attended = (d_attended + times_transposed(low_out, out_down)).astype(jnp.bfloat16)
    grad_out_up = left_inner(by_doc(small_out), d_z)
    grad_out_down = left_inner(by_doc(low_out), attended_tok)
    blocks = [
        [p * geo.groups + i for i in range(geo.groups)] for p in range(geo.parts)
    ]
    d_heads = lax.all_to_all(
        d_attended.reshape(tok_rows, geo.groups, LANES),
        "seq",
        split_axis=1,
        concat_axis=0,
        axis_index_groups=blocks,
        tiled=True,
    ).reshape(geo.queries, LANES)
    grads = [grad_out_down, grad_out_up, grad_fc1_down, grad_fc2_up, grad_fc1_up, grad_fc2_down]
    return output, d_first, d_heads, [v.astype(BF16) for v in grads]


def shards(
    tokens,
    cotangent,
    w_qkv,
    qv_bias,
    w_out,
    out_bias,
    norm1_gain,
    norm1_bias,
    w_fc1,
    fc1_bias,
    w_fc2,
    fc2_bias,
    norm2_gain,
    norm2_bias,
    doc_lengths,
    adapter_ids,
    attn_down,
    attn_up,
    fc1_down,
    fc1_up,
    fc2_down,
    fc2_up,
):
    tok_rows, model_width = tokens.shape
    adapter_count = attn_down.shape[1]
    rank_size = attn_down.shape[3]
    lane_count = adapter_count * rank_size
    seq_count = lax.axis_size("seq")
    geo = Geometry(tok_rows, model_width)
    part_index = lax.axis_index("seq") // geo.groups
    down_rows = jnp.transpose(attn_down, (0, 1, 3, 2)).reshape(4 * lane_count, model_width)
    up_rows = attn_up.reshape(4 * lane_count, model_width)
    weights = (w_out, w_fc1, w_fc2)
    vectors = (out_bias, norm1_gain, norm1_bias, fc1_bias, fc2_bias, norm2_gain, norm2_bias)

    def rows_of(down):
        return jnp.swapaxes(down, 1, 2).reshape(lane_count, down.shape[1])

    inside = all(v.shape[0] % (32 * seq_count) == 0 for v in weights)
    mlp = None
    if inside:
        mlp = (
            weights
            + (cotangent,)
            + tuple(v.reshape(1, -1) for v in vectors)
            + (rows_of(fc1_down), stack_up(fc1_up), rows_of(fc2_down), stack_up(fc2_up))
        )
    q_heads, k_heads, v_heads, o_heads, lse_heads, w_slice, small_all, *rest = forward_attention(
        geo, rank_size, doc_lengths, adapter_ids, tokens, w_qkv, down_rows, up_rows, qv_bias, mlp
    )
    if inside:
        output, d_first, d_heads, *set1, early_sum = rest
    else:
        early_sum = None
        output, d_first, d_heads, set1 = feed_forward(
            geo,
            tokens,
            cotangent,
            rest[0],
            weights,
            vectors,
            (stack_down(attn_down[3]), stack_up(attn_up[3])),
            (stack_down(fc1_down), stack_up(fc1_up)),
            (stack_down(fc2_down), stack_up(fc2_up)),
            select_local(tok_rows, lane_count, rank_size, doc_lengths[0], adapter_ids[0]),
        )
    d_q, d_k, d_v = backward_attention(
        geo, doc_lengths, part_index.reshape(1, 1), q_heads, k_heads, v_heads, o_heads, lse_heads, d_heads
    )
    input_grad, sum1, sum2, _ = closing(
        geo,
        rank_size,
        doc_lengths,
        adapter_ids,
        tokens,
        d_first,
        d_q,
        d_k,
        d_v,
        w_slice,
        down_rows,
        up_rows,
        small_all,
        set1,
        early_sum,
    )

    down4, up4, fc1_down_sum, fc2_up_sum, fc1_up_sum, fc2_down_sum = unpack(geo, sum1, sum2, lane_count)

    def as_up(rows):
        return rows.reshape(rows.shape[:-2] + (adapter_count, rank_size, rows.shape[-1]))

    def as_down(rows):
        return jnp.swapaxes(as_up(rows), -1, -2)

    return (
        output,
        input_grad,
        as_down(down4),
        as_up(up4),
        as_down(fc1_down_sum),
        as_up(fc1_up_sum),
        as_down(fc2_down_sum),
        as_up(fc2_up_sum),
    )


def solution(mesh):
    placed = (
        P(("wt", "seq"), None),
        P(("wt", "seq"), None),
        P("wt", None),
        P(),
        P("wt", None),
        P(),
        P(),
        P(),
        P("wt", None),
        P(),
        P("wt", None),
        P(),
        P(),
        P(),
        P("wt", None),
        P("wt", None),
        P(),
        P(),
        P(),
        P(),
        P(),
        P(),
    )
    return jax.shard_map(
        shards,
        mesh=mesh,
        in_specs=placed,
        out_specs=(P(("wt", "seq"), None), P(("wt", "seq"), None), P(), P(), P(), P(), P(), P()),
        check_vma=False,
    )
```

```python
import functools

import jax
import jax.numpy as jnp
from jax import lax
from jax.experimental import pallas as pl
from jax.experimental.pallas import tpu as pltpu
from jax.sharding import PartitionSpec as P

HEADS = 16
HEAD_DIM = 64
LANES = 128
PAIR = LANES // HEAD_DIM
MESH = pl.DeviceIdType.MESH
F32 = jnp.float32
BF16 = jnp.bfloat16
VMEM_LIMIT = 60 * 2**20


def dot_nn(a, b):
    return lax.dot_general(a, b, (((1,), (0,)), ((), ())), preferred_element_type=F32)


def dot_nt(a, b):
    return lax.dot_general(a, b, (((1,), (1,)), ((), ())), preferred_element_type=F32)


def dot_tn(a, b):
    return lax.dot_general(a, b, (((0,), (0,)), ((), ())), preferred_element_type=F32)


class Geometry:
    def __init__(self, rows, width):
        self.seq = lax.axis_size("seq")
        self.wt = lax.axis_size("wt")
        self.rows = rows
        self.width = width
        self.groups = width // LANES
        self.parts = self.seq // self.groups
        chips = self.seq // 2
        nx = 1
        while nx * nx < chips:
            nx *= 2
        self.nx = nx
        self.ny = chips // nx
        self.keys = self.seq * rows
        self.queries = self.groups * rows


def doc_bounds(len_ref):
    count = len_ref.shape[1]
    starts, ends = [], []
    at = jnp.int32(0)
    for i in range(count):
        starts.append(at)
        at = at + len_ref[0, i]
        ends.append(at)
    return starts, ends


def segment_from(positions, starts):
    seg = jnp.zeros_like(positions)
    for start in starts[1:]:
        seg = seg + (positions >= start).astype(jnp.int32)
    return seg


def select_from(positions, starts, ends, id_ref, rank):
    owner = lax.broadcasted_iota(jnp.int32, positions.shape, 1) // rank
    picked = jnp.zeros(positions.shape, F32)
    for i in range(len(starts)):
        inside = (positions >= starts[i]) & (positions < ends[i]) & (owner == id_ref[0, i])
        picked = jnp.where(inside, 1.0, picked)
    return picked


def placement(id_ref, docs, rank, lane_count):
    a = lax.broadcasted_iota(jnp.int32, (lane_count, LANES), 0)
    b = lax.broadcasted_iota(jnp.int32, (lane_count, LANES), 1)
    every = jnp.zeros((lane_count, LANES), F32)
    first = jnp.zeros((lane_count, LANES), F32)
    for d in range(docs):
        seen = jnp.bool_(False)
        for e in range(d):
            seen = seen | (id_ref[0, e] == id_ref[0, d])
        hit = (a // rank == id_ref[0, d]) & (b // rank == d) & (a % rank == b % rank)
        every = jnp.where(hit, 1.0, every)
        first = jnp.where(hit, jnp.where(seen, 0.0, 1.0), first)
    return every.astype(BF16), first.astype(BF16)


def owner_columns(refs, owner, groups):
    cols = []
    for ref in refs:
        wide = ref.shape[1] // groups
        cols.append(ref[:, pl.ds(pl.multiple_of(owner * wide, LANES), wide)])
    return jnp.concatenate(cols, axis=1).astype(F32)


class Spread:
    KINDS = 9

    def __init__(self, geo, here, region, send, recv, unit, first=0):
        self.geo, self.here, self.region = geo, here, region
        self.send, self.recv, self.unit, self.first = send, recv, unit, first

    def copy(self, kind, src, dst, x, y, core):
        return pltpu.make_async_remote_copy(
            src_ref=src,
            dst_ref=dst,
            send_sem=self.send.at[kind, self.unit],
            recv_sem=self.recv.at[kind, self.unit],
            device_id=(self.first + ((y * self.geo.nx) + x) * 2 + core, self.here[3]),
            device_id_type=MESH,
        )

    def others(self):
        nx, ny = self.geo.nx, self.geo.ny
        x, y, core, _ = self.here
        row = [((x + d) % nx, y) for d in range(1, nx)]
        col = [(x, (y + d) % ny) for d in range(1, ny)]
        return row, col

    def plan(self):
        x, y, core, _ = self.here
        row, col = self.others()
        plan = {kind: [] for kind in range(self.KINDS)}
        for tx, ty in row:
            plan[0].append(((x, y), None, (tx, ty, core)))
        for tx, ty in col:
            plan[1].append(((x, y), None, (tx, ty, core)))
        for ux, uy in row:
            for tx, ty in col:
                plan[2].append(((ux, uy), 0, (tx, ty, core)))
        for ux, uy in col:
            for tx, ty in row:
                plan[3].append(((ux, uy), 1, (tx, ty, core)))
        plan[4].append(((x, y), None, (x, y, 1 - core)))
        for ux, uy in row:
            plan[5].append(((ux, uy), None, (x, y, 1 - core)))
        for ux, uy in col:
            plan[6].append(((ux, uy), None, (x, y, 1 - core)))
        for ux, _ in row:
            for _, uy in col:
                plan[7].append(((ux, uy), 0, (x, y, 1 - core)))
                plan[8].append(((ux, uy), 1, (x, y, 1 - core)))
        return plan

    def go(self, kind, own=None):
        core = self.here[2]
        for (ux, uy), half, (tx, ty, tcore) in self.plan()[kind]:
            dst = self.region(ux, uy, core, half)
            src = dst if own is None else own
            self.copy(kind, src, dst, tx, ty, tcore).start()

    def arrivals(self, kind):
        x, y, core, _ = self.here
        row, col = self.others()
        if kind == 0:
            return [(u, None, core) for u in row]
        if kind == 1:
            return [(u, None, core) for u in col]
        if kind in (2, 3):
            return [((ux, uy), kind - 2, core) for ux, _ in row for _, uy in col]
        if kind == 4:
            return [((x, y), None, 1 - core)]
        if kind == 5:
            return [(u, None, 1 - core) for u in row]
        if kind == 6:
            return [(u, None, 1 - core) for u in col]
        return [((ux, uy), kind - 7, 1 - core) for ux, _ in row for _, uy in col]

    def wait(self, kind):
        x, y, core, _ = self.here
        for (ux, uy), half, whose in self.arrivals(kind):
            ref = self.region(ux, uy, whose, half)
            self.copy(kind, ref, ref, x, y, 1 - core).wait_recv()

    def wait_sends(self):
        x, y, core, _ = self.here
        for kind in range(self.KINDS):
            for (ux, uy), half, _ in self.plan()[kind]:
                ref = self.region(ux, uy, core, half)
                self.copy(kind, ref, ref, x, y, 1 - core).wait_send()


def device_here(geo):
    s = lax.axis_index("seq")
    core = s % 2
    chip = s // 2
    return chip % geo.nx, chip // geo.nx, core, lax.axis_index("wt")


def greet(geo):
    s, w = lax.axis_index("seq"), lax.axis_index("wt")
    barrier = pltpu.get_barrier_semaphore()
    for d in range(1, geo.seq):
        pl.semaphore_signal(barrier, inc=1, device_id=((s + d) % geo.seq, w), device_id_type=MESH)
    for d in range(1, geo.wt):
        pl.semaphore_signal(barrier, inc=1, device_id=(s, (w + d) % geo.wt), device_id_type=MESH)
    pl.semaphore_wait(barrier, geo.seq + geo.wt - 2)


def erf(v):
    v = jnp.clip(v, -3.832506856900711, 3.832506856900711)
    sq = v * v
    top = jnp.full_like(v, 0.00022905065861350646)
    for c in (0.0034082910107109506, 0.050955695062380861, 0.18520832239976145, 1.128379143519084):
        top = top * sq + c
    low = jnp.full_like(v, -1.1791602954361697e-7)
    for c in (0.000023547966471313185, 0.0010179625278914885, 0.014070470171167667, 0.11098505178285362, 0.49746925110067538, 1.0):
        low = low * sq + c
    return v * top / low


def normed(value):
    mean = jnp.mean(value, axis=1, keepdims=True)
    centred = value - mean
    spread = lax.rsqrt(jnp.mean(centred * centred, axis=1, keepdims=True) + 1e-05)
    return centred * spread, spread


def normed_back(grad, gain, unit, spread):
    g = grad * gain
    return spread * (
        g - jnp.mean(g, axis=1, keepdims=True) - unit * jnp.mean(g * unit, axis=1, keepdims=True)
    )


class Names:
    def __init__(self, names, refs):
        self.__dict__.update(zip(names, refs))


MLP_INPUTS = (
    "w_out", "w_fc1", "w_fc2", "cotangent", "out_bias", "gain1", "shift1", "fc1_bias", "fc2_bias", "gain2", "shift2",
    "fc1_down", "fc1_up", "fc2_down", "fc2_up",
)
BASE_OUTPUTS = ("q", "k", "v", "o", "lse", "w_slice", "small")
MLP_OUTPUTS = ("output", "d_first", "d_heads", "g_out_down", "g_out_up", "g_fc1_down", "early_sum")
BASE_SCRATCH = (
    "tok", "seg", "att_send_buf", "local_sem", "send_sem", "recv_sem", "slice_send", "slice_recv", "line_send",
    "line_recv", "att_send", "att_recv",
)
MLP_SCRATCH = (
    "att", "full_out", "full_fc1", "full_fc2", "unit1", "h1", "h1_low", "act", "slope", "d_pre", "y", "d_att_buf",
    "back_send", "back_recv", "g_fc2_up", "g_fc1_up", "g_fc2_down", "set_out", "set_in", "set_far", "set_sems",
)


def forward_kernel(geo, inside, rank, len_ref, id_ref, tokens_ref, wqkv_ref, down_ref, up_ref, bias_ref, *refs):
    in_names = MLP_INPUTS if inside else ()
    out_names = BASE_OUTPUTS + (MLP_OUTPUTS if inside else ("att",))
    scratch_names = BASE_SCRATCH + (MLP_SCRATCH if inside else ())
    r = Names(in_names + out_names + scratch_names, refs)
    weights_in = (r.w_out, r.w_fc1, r.w_fc2) if inside else ()
    weights_out = (r.full_out, r.full_fc1, r.full_fc2) if inside else ()
    weight_count = len(weights_in)
    att_ref, q_ref, k_ref, v_ref, o_ref, lse_ref, slice_ref, small_ref = (
        r.att, r.q, r.k, r.v, r.o, r.lse, r.w_slice, r.small
    )
    tok_buf, seg_buf, att_buf, local_sem = r.tok, r.seg, r.att_send_buf, r.local_sem
    send_sem, recv_sem, slice_send, slice_recv = r.send_sem, r.recv_sem, r.slice_send, r.slice_recv
    line_send, line_recv, att_send, att_recv = r.line_send, r.line_recv, r.att_send, r.att_recv
    here = device_here(geo)
    x, y, core, w = here
    s = lax.axis_index("seq")
    part, g = s // geo.groups, s % geo.groups
    rows, width, wt = geo.rows, geo.width, geo.wt
    lanes = pl.ds(pl.multiple_of(g * LANES, LANES), LANES)

    own_tok = pltpu.make_async_copy(tokens_ref, tok_buf.at[s], local_sem.at[0])
    own_tok.start()
    shard = wqkv_ref.shape[0]
    own_slices = []
    for j in range(3):
        src = wqkv_ref.at[:, pl.ds(pl.multiple_of(j * width + g * LANES, LANES), LANES)]
        dst = slice_ref.at[pl.ds(pl.multiple_of(w * shard, shard), shard), pl.ds(j * LANES, LANES)]
        own_slices.append(pltpu.make_async_copy(src, dst, local_sem.at[1 + j]))
        own_slices[-1].start()
    own_weights = []
    for m in range(weight_count):
        height = weights_in[m].shape[0]
        dst = weights_out[m].at[pl.ds(pl.multiple_of(w * height, height), height)]
        own_weights.append(pltpu.make_async_copy(weights_in[m], dst, local_sem.at[4 + m]))
        own_weights[-1].start()

    greet(geo)

    def token_region(ux, uy, whose, half):
        block = tok_buf.at[(uy * geo.nx + ux) * 2 + whose]
        if half is None:
            return block
        return block.at[pl.ds(half * (rows // 2), rows // 2)]

    tok = Spread(geo, here, token_region, send_sem, recv_sem, 0)
    tok.go(0, own=tokens_ref)
    tok.go(1, own=tokens_ref)
    tok.go(4, own=tokens_ref)

    def slice_copy(j, p, up):
        dst = slice_ref.at[pl.ds(pl.multiple_of(p * shard, shard), shard), pl.ds(j * LANES, LANES)]
        return pltpu.make_async_remote_copy(
            src_ref=dst,
            dst_ref=dst,
            send_sem=slice_send.at[0 if up else 1, j, p],
            recv_sem=slice_recv.at[j, p],
            device_id=(s, w + 1 if up else w - 1),
            device_id_type=MESH,
        )

    starts, ends = doc_bounds(len_ref)
    seg_buf[...] = segment_from(lax.broadcasted_iota(jnp.int32, seg_buf.shape, 1), starts)

    seq = geo.seq
    mine = s

    def unit_rows(m, p, unit, half=None):
        height = weights_in[m].shape[0]
        piece = height // seq
        if half is None:
            return weights_out[m].at[pl.ds(pl.multiple_of(p * height + unit * piece, piece), piece)]
        piece = piece // 2
        return weights_out[m].at[
            pl.ds(pl.multiple_of(p * height + unit * 2 * piece + half * piece, piece), piece)
        ]

    def line_copy(m, p, up, own):
        height = weights_in[m].shape[0]
        piece = height // seq
        dst = unit_rows(m, p, mine)
        src = weights_in[m].at[pl.ds(pl.multiple_of(mine * piece, piece), piece)] if own else dst
        target = w + 1 if up else w - 1
        return pltpu.make_async_remote_copy(
            src_ref=src,
            dst_ref=dst,
            send_sem=line_send.at[0 if up else 1, m * wt + p],
            recv_sem=line_recv.at[m * wt + p],
            device_id=(s, target),
            device_id_type=MESH,
        )

    def nth_plane(j):
        below, above = w, wt - 1 - w
        both = jnp.minimum(below, above)
        in_turn = j < 2 * both
        dist = jnp.where(in_turn, j // 2 + 1, j - both + 1)
        from_below = jnp.where(in_turn, j % 2 == 0, below > above)
        return jnp.where(from_below, w - dist, w + dist)

    def weight_spread(m, p):
        def region(ux, uy, whose, half):
            return unit_rows(m, p, (uy * geo.nx + ux) * 2 + whose, half)

        return Spread(geo, here, region, send_sem, recv_sem, 1 + m * wt + p)

    units = []
    if inside:
        units = [(m, j) for j in range(wt - 1) for m in (0, 1)] + [(2, j) for j in range(wt - 1)]

    def start_lines(which):
        for m in which if inside else ():

            @pl.when(w < wt - 1)
            def _():
                line_copy(m, w, True, True).start()

            @pl.when(w > 0)
            def _():
                line_copy(m, w, False, True).start()

    def along(i):
        if i >= len(units):
            return
        m, j = units[i]
        p = nth_plane(j)
        line_copy(m, p, True, False).wait_recv()

        @pl.when((p < w) & (w < wt - 1))
        def _():
            line_copy(m, p, True, False).start()

        @pl.when((p > w) & (w > 0))
        def _():
            line_copy(m, p, False, False).start()

    def tick(i):
        if i == 0:
            along(0)
        if i == late_lines:
            start_lines((2,))
        if i < len(units):
            m, j = units[i]
            spread = weight_spread(m, nth_plane(j))
            spread.go(0)
            spread.go(1)
            spread.go(4)
        along(i + 1)
        if 0 <= i - 1 < len(units):
            m, j = units[i - 1]
            spread = weight_spread(m, nth_plane(j))
            spread.wait(0)
            spread.go(2)
            spread.go(5)
            spread.wait(1)
            spread.go(3)
            spread.go(6)
        if 0 <= i - 2 < len(units):
            m, j = units[i - 2]
            spread = weight_spread(m, nth_plane(j))
            spread.wait(2)
            spread.go(7)
            spread.wait(3)
            spread.go(8)

    tick_count = len(units) + 2 if units else 0
    late_lines = 0
    early_ticks = min(3, tick_count)
    loop_ticks = min(6, tick_count)

    def complete(m):
        own_weights[m].wait()
        for j in range(wt - 1):
            spread = weight_spread(m, nth_plane(j))
            for kind in range(4, 9):
                spread.wait(kind)

    for copy in own_slices:
        copy.wait()
    for j in range(3):

        @pl.when(w < wt - 1)
        def _():
            slice_copy(j, w, True).start()

        @pl.when(w > 0)
        def _():
            slice_copy(j, w, False).start()

    nx, ny = geo.nx, geo.ny
    row_n, col_n, diag_n = 2 * (nx - 1), 2 * (ny - 1), 2 * (nx - 1) * (ny - 1)

    def block_owner(i):
        r = i - 2
        c = r - row_n
        d = c - col_n
        dx_row, k_row = r % max(nx - 1, 1) + 1, r // max(nx - 1, 1)
        dy_col, k_col = c % max(ny - 1, 1) + 1, c // max(ny - 1, 1)
        half = max(diag_n // 2, 1)
        k_diag, in_diag = d // half, d % half
        dx_diag, dy_diag = in_diag % max(nx - 1, 1) + 1, in_diag // max(nx - 1, 1) + 1
        dx = jnp.where(i < 2, 0, jnp.where(i < 2 + row_n, dx_row, jnp.where(i < 2 + row_n + col_n, 0, dx_diag)))
        dy = jnp.where(i < 2 + row_n, 0, jnp.where(i < 2 + row_n + col_n, dy_col, dy_diag))
        kk = jnp.where(i < 2, i, jnp.where(i < 2 + row_n, k_row, jnp.where(i < 2 + row_n + col_n, k_col, k_diag)))
        return (((y + dy) % ny) * nx + (x + dx) % nx) * 2 + (core + kk) % 2

    def project(i, carry):
        @pl.when(i == 0)
        def _():
            start_lines((0, 1))
            for n in range(wt - 1):
                p = nth_plane(n)
                for j in range(3):
                    slice_copy(j, p, True).wait_recv()

                    @pl.when((p < w) & (w < wt - 1))
                    def _():
                        slice_copy(j, p, True).start()

                    @pl.when((p > w) & (w > 0))
                    def _():
                        slice_copy(j, p, False).start()

            own_tok.wait()

        @pl.when(i == 1)
        def _():
            tok.wait(4)

        @pl.when(i == 2)
        def _():
            tok.wait(0)
            tok.go(2)
            tok.go(5)
            tok.wait(1)
            tok.go(3)
            tok.go(6)

        @pl.when(i == 2 + row_n // 2)
        def _():
            tok.wait(5)

        @pl.when(i == 2 + row_n + col_n // 2)
        def _():
            tok.wait(6)

        @pl.when(i == 2 + row_n + col_n)
        def _():
            tok.wait(2)
            tok.go(7)
            tok.wait(3)
            tok.go(8)

        @pl.when(i == 2 + row_n + col_n + diag_n // 2)
        def _():
            tok.wait(7)
            tok.wait(8)

        for n in range(early_ticks):

            @pl.when(i == min(3 + 2 * n, geo.seq - 1))
            def _():
                tick(n)

        t = block_owner(i)
        block = tok_buf[t]
        at = pl.ds(pl.multiple_of(t * rows, rows), rows)
        pos = t * rows + lax.broadcasted_iota(jnp.int32, (rows, LANES), 0)
        chosen = select_from(pos, starts, ends, id_ref, rank)
        main = dot_nn(block, slice_ref[...])
        small = dot_nt(block, down_ref[: 3 * LANES, :])
        for j in range(3):
            cut = slice(j * LANES, (j + 1) * LANES)
            low = (small[:, cut] * chosen).astype(BF16)
            small_ref[at, cut] = low
            value = main[:, cut] + dot_nn(low, up_ref[cut, lanes])
            if j == 0:
                value = value + bias_ref[0:1, lanes]

                @pl.when(t // geo.groups == part)
                def _():
                    inner = pl.ds(pl.multiple_of((t % geo.groups) * rows, rows), rows)
                    q_ref[inner, :] = value.astype(BF16)
            elif j == 1:
                k_ref[at, :] = value.astype(BF16)
            else:
                v_ref[at, :] = (value + bias_ref[1:2, lanes]).astype(BF16)
        return carry

    lax.fori_loop(0, geo.seq, project, 0)

    scale = HEAD_DIM ** (-0.5)
    chunk = min(2048, geo.keys)
    chunks = geo.keys // chunk
    first_head = lax.broadcasted_iota(jnp.int32, (rows, LANES), 1) < HEAD_DIM

    def att_copy(b):
        return pltpu.make_async_remote_copy(
            src_ref=att_buf.at[b],
            dst_ref=att_ref.at[:, lanes],
            send_sem=att_send.at[b],
            recv_sem=att_recv.at[g],
            device_id=(part * geo.groups + b, w),
            device_id_type=MESH,
        )

    def attend(i, carry):
        for n in range(early_ticks, loop_ticks):

            @pl.when(i == 2 * (n - early_ticks) + 1)
            def _():
                tick(n)

        b = (g + 1 + i) % geo.groups
        inner = pl.ds(pl.multiple_of(b * rows, rows), rows)
        query = q_ref[inner, :] * jnp.asarray(scale, BF16)
        q_pos = (part * geo.groups + b) * rows + lax.broadcasted_iota(jnp.int32, (rows, 1), 0)
        q_seg = segment_from(q_pos, starts)
        results = []
        for h in range(PAIR):
            mask = first_head if h == 0 else jnp.logical_not(first_head)
            q_head = jnp.where(mask, query, jnp.zeros_like(query))

            def one(c, state):
                top, total, acc = state
                keys_at = pl.ds(pl.multiple_of(c * chunk, chunk), chunk)
                score = dot_nt(q_head, k_ref[keys_at, :])
                score = jnp.where(q_seg == seg_buf[:, keys_at], score, -1e30)
                peak = jnp.max(score, axis=1, keepdims=True)
                if top is not None:
                    peak = jnp.maximum(top, peak)
                weight = jnp.exp(score - peak)
                add = jnp.sum(weight, axis=1, keepdims=True)
                out = dot_nn(weight.astype(BF16), v_ref[keys_at, :])
                if top is not None:
                    fade = jnp.exp(top - peak)
                    add = add + total * fade
                    out = out + acc * fade
                return peak, add, out

            state = one(0, (None, None, None))
            if chunks > 1:
                state = lax.fori_loop(1, chunks, one, state)
            top, total, acc = state
            results.append((acc / total, top + jnp.log(total)))
        out = jnp.where(first_head, results[0][0], results[1][0])
        o_ref[inner, :] = out
        lse_ref[inner, :] = jnp.where(first_head, results[0][1], results[1][1])
        att_buf[b] = out.astype(BF16)

        @pl.when(b != g)
        def _():
            att_copy(b).start()

        return carry

    lax.fori_loop(0, geo.groups, attend, 0)
    own_att = pltpu.make_async_copy(att_buf.at[g], att_ref.at[:, lanes], local_sem.at[0])
    own_att.start()

    def att_arrivals():
        for d in range(1, geo.groups):
            other = (g + d) % geo.groups
            cut = pl.ds(pl.multiple_of(other * LANES, LANES), LANES)
            pltpu.make_async_remote_copy(
                src_ref=att_ref.at[:, cut],
                dst_ref=att_ref.at[:, cut],
                send_sem=att_send.at[other],
                recv_sem=att_recv.at[other],
                device_id=(part * geo.groups + other, w),
                device_id_type=MESH,
            ).wait_recv()
        own_att.wait()

    if inside:
        layer_rest(geo, rank, r, starts, ends, id_ref, down_ref, up_ref, att_arrivals, complete, tick, loop_ticks, tick_count, len_ref.shape[1])
    else:
        att_arrivals()

    for d in range(1, geo.groups):
        att_copy((g + d) % geo.groups).wait_send()
    tok.wait_sends()
    for j in range(3):

        @pl.when(w < wt - 1)
        def _():
            slice_copy(j, w, True).wait_send()

        @pl.when(w > 0)
        def _():
            slice_copy(j, w, False).wait_send()

        for n in range(wt - 1):
            p = nth_plane(n)

            @pl.when((p < w) & (w < wt - 1))
            def _():
                slice_copy(j, p, True).wait_send()

            @pl.when((p > w) & (w > 0))
            def _():
                slice_copy(j, p, False).wait_send()

    for m in range(weight_count):
        @pl.when(w < wt - 1)
        def _():
            line_copy(m, w, True, True).wait_send()

        @pl.when(w > 0)
        def _():
            line_copy(m, w, False, True).wait_send()

    for m, j in units:
        p = nth_plane(j)

        @pl.when((p < w) & (w < wt - 1))
        def _():
            line_copy(m, p, True, False).wait_send()

        @pl.when((p > w) & (w > 0))
        def _():
            line_copy(m, p, False, False).wait_send()

        weight_spread(m, p).wait_sends()


def layer_rest(
    geo, rank, r, starts, ends, id_ref, down_ref, up_ref, att_arrivals, complete, tick, ticked, tick_count, docs
):
    s, w = lax.axis_index("seq"), lax.axis_index("wt")
    rows, width, groups = geo.rows, geo.width, geo.groups
    part, g = s // groups, s % groups
    hidden = r.full_fc1.shape[1]
    step = min(512, hidden)
    steps = hidden // step
    band = 2 * LANES
    bands = width // band
    lane_count = r.fc1_down.shape[0]
    out_rows = slice(3 * lane_count, 4 * lane_count)
    pos = s * rows + lax.broadcasted_iota(jnp.int32, (rows, LANES), 0)
    chosen = select_from(pos, starts, ends, id_ref, rank)

    every = placement(id_ref, docs, rank, lane_count)[0]
    doc_rows = docs * rank
    in_doc = (lax.broadcasted_iota(jnp.int32, (rows, LANES), 1) // rank) == segment_from(pos, starts)

    def masked(value):
        return (value * chosen).astype(BF16)

    def by_doc(low):
        return jnp.where(in_doc, dot_nn(low, every), 0.0).astype(BF16)

    def doc_grad(low_by_doc, value):
        return dot_tn(low_by_doc, value)[:doc_rows].astype(BF16)

    def at_step(i):
        return pl.ds(pl.multiple_of(i * step, step), step)

    def at_band(i):
        return pl.ds(pl.multiple_of(i * band, band), band)

    pending = list(range(ticked, tick_count))
    first_ticks, pending = pending[:1], pending[1:]
    for n in first_ticks:
        tick(n)
    att_arrivals()
    complete(0)
    att = r.att[...]
    small_out = masked(dot_nt(att, down_ref[out_rows, :]))

    def out_band(i, carry):
        cut = at_band(i)
        value = dot_nn(r.att[...], r.full_out[:, cut]) + r.out_bias[:, cut]
        value = value + dot_nn(small_out, up_ref[out_rows, cut])
        r.y[:, cut] = value + r.tok[s, :, cut].astype(F32)
        return carry

    lax.fori_loop(0, bands, out_band, 0)
    unit1, spread1 = normed(r.y[...])
    h1 = unit1 * r.gain1[...] + r.shift1[...]
    r.unit1[...] = unit1
    r.h1[...] = h1
    h1_low = h1.astype(BF16)
    r.h1_low[...] = h1_low
    small_fc1 = masked(dot_nt(h1_low, r.fc1_down[...]))

    middle = max(len(pending) - 3, 0)
    for n in pending[:middle]:
        tick(n)
    pending = pending[middle:]
    complete(1)

    def fc1_step(i, acc):
        for n, t in enumerate(pending):
            @pl.when(i == min(2 * n + 1, steps - 1))
            def _():
                tick(t)

        cut = at_step(i)
        pre = dot_nn(r.h1_low[...], r.full_fc1[:, cut]) + r.fc1_bias[:, cut]
        pre = pre + dot_nn(small_fc1, r.fc1_up[:, cut])
        share = 0.5 + 0.5 * erf(pre * 0.7071067811865476)
        act = (pre * share).astype(BF16)
        r.act[:, cut] = act
        r.slope[:, cut] = share + pre * (jnp.exp(-0.5 * pre * pre) * 0.3989422804014327)
        return acc + dot_nt(act, r.fc2_down[:, cut])

    small_fc2 = masked(lax.fori_loop(0, steps, fc1_step, jnp.zeros((rows, lane_count), F32)))
    complete(2)

    def fc2_band(i, carry):
        cut = at_band(i)
        value = dot_nn(r.act[...], r.full_fc2[:, cut]) + r.fc2_bias[:, cut]
        r.y[:, cut] = value + dot_nn(small_fc2, r.fc2_up[:, cut]) + r.h1[:, cut]
        return carry

    lax.fori_loop(0, bands, fc2_band, 0)
    unit2, spread2 = normed(r.y[...])
    r.output[...] = unit2 * r.gain2[...] + r.shift2[...]
    d_second = normed_back(r.cotangent[...].astype(F32), r.gain2[...], unit2, spread2)
    r.y[...] = d_second
    d_y = d_second.astype(BF16)
    low_fc2 = masked(dot_nt(d_y, r.fc2_up[...]))
    r.g_fc2_up[...] = doc_grad(by_doc(small_fc2), d_y)
    low_fc2_doc, small_fc1_doc = by_doc(low_fc2), by_doc(small_fc1)

    def back_step(i, acc):
        cut = at_step(i)
        d_act = dot_nt(d_y, r.full_fc2[cut, :]) + dot_nn(low_fc2, r.fc2_down[:, cut])
        d_pre = (d_act * r.slope[:, cut]).astype(BF16)
        r.d_pre[:, cut] = d_pre
        r.g_fc2_down[:, cut] = doc_grad(low_fc2_doc, r.act[:, cut])
        r.g_fc1_up[:, cut] = doc_grad(small_fc1_doc, d_pre)
        return acc + dot_nt(d_pre, r.fc1_up[:, cut])

    low_fc1 = masked(lax.fori_loop(0, steps, back_step, jnp.zeros((rows, lane_count), F32)))

    def make_early(chip, whose):
        return owner_columns((r.g_fc2_up, r.g_fc1_up, r.g_fc2_down), chip * 2 + whose, groups)

    early = PairSum(
        groups // 2,
        g // 2,
        s % 2,
        part * groups,
        w,
        (r.set_out, r.set_in, r.set_far),
        [r.set_sems.at[i] for i in range(4)],
        make_early,
    )
    early.run()
    r.g_fc1_down[...] = doc_grad(by_doc(low_fc1), r.h1_low[...])

    def back_band(i, carry):
        cut = at_band(i)
        value = dot_nt(r.d_pre[...], r.full_fc1[cut, :]) + dot_nn(low_fc1, r.fc1_down[:, cut])
        r.y[:, cut] += value
        return carry

    lax.fori_loop(0, bands, back_band, 0)
    d_first = normed_back(r.y[...], r.gain1[...], r.unit1[...], spread1)
    r.d_first[...] = d_first
    d_z = d_first.astype(BF16)
    low_out = masked(dot_nt(d_z, up_ref[out_rows, :]))

    def back_copy(b):
        return pltpu.make_async_remote_copy(
            src_ref=r.d_att_buf.at[b],
            dst_ref=r.d_heads.at[pl.ds(pl.multiple_of(g * rows, rows), rows)],
            send_sem=r.back_send.at[b],
            recv_sem=r.back_recv.at[g],
            device_id=(part * groups + b, w),
            device_id_type=MESH,
        )

    def attended_band(i, carry):
        n = (g // 2 + 1 + i) % bands
        cut = at_band(n)
        value = dot_nt(d_z, r.full_out[cut, :]) + dot_nn(low_out, down_ref[out_rows, cut])
        value = value.astype(BF16)
        for h in range(2):
            b = 2 * n + h
            r.d_att_buf[b] = value[:, h * LANES : (h + 1) * LANES]

            @pl.when(b != g)
            def _():
                back_copy(b).start()

        return carry

    lax.fori_loop(0, bands, attended_band, 0)
    own = pltpu.make_async_copy(
        r.d_att_buf.at[g], r.d_heads.at[pl.ds(pl.multiple_of(g * rows, rows), rows)], r.local_sem.at[0]
    )
    own.start()
    r.g_out_down[...] = doc_grad(by_doc(low_out), r.att[...])
    r.g_out_up[...] = doc_grad(by_doc(small_out), d_z)
    r.early_sum[...] = early.finish().astype(BF16)
    early.drain()
    for d in range(1, groups):
        other = (g + d) % groups
        here = r.d_heads.at[pl.ds(pl.multiple_of(other * rows, rows), rows)]
        pltpu.make_async_remote_copy(
            src_ref=here,
            dst_ref=here,
            send_sem=r.back_send.at[other],
            recv_sem=r.back_recv.at[other],
            device_id=(part * groups + other, w),
            device_id_type=MESH,
        ).wait_recv()
        back_copy(other).wait_send()
    own.wait()


def forward_attention(geo, rank, lengths, ids, tokens, w_qkv, down, up, bias, mlp):
    rows, width = geo.rows, geo.width
    inside = mlp is not None
    mlp = mlp or ()
    any_spec = pl.BlockSpec(memory_space=pl.ANY)
    vmem = pl.BlockSpec(memory_space=pltpu.VMEM)
    smem = pl.BlockSpec(memory_space=pltpu.SMEM)
    lane_count = down.shape[0] // 4
    struct = jax.ShapeDtypeStruct
    shapes = [
        struct((geo.queries, LANES), BF16),
        struct((geo.keys, LANES), BF16),
        struct((geo.keys, LANES), BF16),
        struct((geo.queries, LANES), F32),
        struct((geo.queries, LANES), F32),
        struct((width, 3 * LANES), BF16),
        struct((geo.keys, 3 * LANES), BF16),
    ]
    specs = [vmem] * 7
    dma = pltpu.SemaphoreType.DMA
    count = 3 if inside else 0
    units = 1 + count * geo.wt
    scratch = [
        pltpu.VMEM((geo.seq, rows, width), BF16),
        pltpu.VMEM((1, geo.keys), jnp.int32),
        pltpu.VMEM((geo.groups, rows, LANES), BF16),
        dma((4 + count,)),
        dma((Spread.KINDS, units)),
        dma((Spread.KINDS, units)),
        dma((2, 3, geo.wt)),
        dma((3, geo.wt)),
        dma((2, max(count, 1) * geo.wt)),
        dma((max(count, 1) * geo.wt,)),
        dma((geo.groups,)),
        dma((geo.groups,)),
    ]
    if inside:
        hidden = mlp[1].shape[1]
        doc_rows = lengths.shape[1] * rank
        early = (width + 2 * hidden) // geo.groups
        near = geo.groups // 2
        shapes += [
            struct((rows, width), F32),
            struct((rows, width), F32),
            struct((geo.queries, LANES), BF16),
            struct((doc_rows, width), BF16),
            struct((doc_rows, width), BF16),
            struct((doc_rows, width), BF16),
            struct((doc_rows, early), BF16),
        ]
        specs += [vmem, vmem, any_spec] + [vmem] * 4
        scratch += [
            pltpu.VMEM((rows, width), BF16),
            pltpu.VMEM((width, width), BF16),
            pltpu.VMEM((width, hidden), BF16),
            pltpu.VMEM((hidden, width), BF16),
            pltpu.VMEM((rows, width), F32),
            pltpu.VMEM((rows, width), F32),
            pltpu.VMEM((rows, width), BF16),
            pltpu.VMEM((rows, hidden), BF16),
            pltpu.VMEM((rows, hidden), F32),
            pltpu.VMEM((rows, hidden), BF16),
            pltpu.VMEM((rows, width), F32),
            pltpu.VMEM((geo.groups, rows, LANES), BF16),
            dma((geo.groups,)),
            dma((geo.groups,)),
            pltpu.VMEM((doc_rows, width), BF16),
            pltpu.VMEM((doc_rows, hidden), BF16),
            pltpu.VMEM((doc_rows, hidden), BF16),
            pltpu.VMEM((near, doc_rows, early), BF16),
            pltpu.VMEM((near, doc_rows, early), BF16),
            pltpu.VMEM((near, doc_rows, early), BF16),
            dma((4, near)),
        ]
    else:
        shapes += [struct((rows, width), BF16)]
        specs += [any_spec]
    return pl.pallas_call(
        functools.partial(forward_kernel, geo, inside, rank),
        out_shape=shapes,
        in_specs=[smem, smem, any_spec, any_spec, vmem, vmem, vmem] + [any_spec] * count + [vmem] * (len(mlp) - count),
        out_specs=specs,
        scratch_shapes=scratch,
        compiler_params=pltpu.CompilerParams(
            collective_id=0, has_side_effects=True, vmem_limit_bytes=VMEM_LIMIT
        ),
        name="layer",
    )(lengths, ids, tokens, w_qkv, down, up, bias, *mlp)


def backward_kernel(geo, len_ref, part_ref, q_ref, k_ref, v_ref, o_ref, lse_ref, g_ref, dq_ref, dk_ref, dv_ref, dk_acc, dv_acc):
    rows = min(512, geo.queries)
    block = min(512, geo.keys)
    part = part_ref[0, 0]
    scale = HEAD_DIM ** (-0.5)
    starts, ends = doc_bounds(len_ref)
    first_head = lax.broadcasted_iota(jnp.int32, (rows, LANES), 1) < HEAD_DIM
    dk_acc[...] = jnp.zeros_like(dk_acc)
    dv_acc[...] = jnp.zeros_like(dv_acc)

    def seg_of(position):
        seg = jnp.int32(0)
        for start in starts[1:]:
            seg = seg + (position >= start).astype(jnp.int32)
        return seg

    def pick(values, index):
        found = values[0]
        for i in range(1, len(values)):
            found = jnp.where(index == i, values[i], found)
        return found

    def both_heads(value):
        zero = jnp.zeros_like(value)
        return jnp.concatenate([jnp.where(first_head, value, zero), jnp.where(first_head, zero, value)], axis=0)

    def query_block(b, carry):
        at = pl.ds(pl.multiple_of(b * rows, rows), rows)
        origin = part * geo.queries + b * rows
        query = both_heads(q_ref[at, :] * jnp.asarray(scale, BF16))
        cot = both_heads(g_ref[at, :])
        scaled = cot * jnp.asarray(scale, BF16)
        lse = jnp.concatenate([lse_ref[at, h * HEAD_DIM : h * HEAD_DIM + 1] for h in range(PAIR)], axis=0)
        out = o_ref[at, :]
        dot = jnp.sum(scaled.astype(F32) * jnp.concatenate([out, out], axis=0), axis=1, keepdims=True)
        q_pos = origin + lax.broadcasted_iota(jnp.int32, (rows, 1), 0)
        q_seg = segment_from(q_pos, starts)
        q_seg = jnp.concatenate([q_seg, q_seg], axis=0)
        low = pick(starts, seg_of(origin)) // block
        high = (pick(ends, seg_of(origin + rows - 1)) + block - 1) // block

        def key_block(c, acc):
            keys_at = pl.ds(pl.multiple_of(c * block, block), block)
            key, value = k_ref[keys_at, :], v_ref[keys_at, :]
            k_pos = c * block + lax.broadcasted_iota(jnp.int32, (1, block), 1)
            score = jnp.where(q_seg == segment_from(k_pos, starts), dot_nt(query, key), -1e30)
            prob = jnp.exp(score - lse)
            raw = (prob * (dot_nt(scaled, value) - dot)).astype(BF16)
            dk_acc[keys_at, :] += dot_tn(raw, query)
            dv_acc[keys_at, :] += dot_tn(prob.astype(BF16), cot)
            return acc + dot_nn(raw, key)

        acc = lax.fori_loop(low, high, key_block, jnp.zeros((PAIR * rows, LANES), F32))
        dq_ref[at, :] = jnp.where(first_head, acc[:rows], acc[rows:]).astype(BF16)
        return carry

    lax.fori_loop(0, geo.queries // rows, query_block, 0)
    dk_ref[...] = (dk_acc[...] * HEAD_DIM**0.5).astype(BF16)
    dv_ref[...] = dv_acc[...].astype(BF16)


def backward_attention(geo, lengths, part, q, k, v, o, lse, d_heads):
    smem = pl.BlockSpec(memory_space=pltpu.SMEM)
    vmem = pl.BlockSpec(memory_space=pltpu.VMEM)
    return pl.pallas_call(
        functools.partial(backward_kernel, geo),
        out_shape=[
            jax.ShapeDtypeStruct((geo.queries, LANES), BF16),
            jax.ShapeDtypeStruct((geo.keys, LANES), BF16),
            jax.ShapeDtypeStruct((geo.keys, LANES), BF16),
        ],
        in_specs=[smem, smem] + [vmem] * 6,
        out_specs=[vmem] * 3,
        scratch_shapes=[pltpu.VMEM((geo.keys, LANES), F32)] * 2,
        compiler_params=pltpu.CompilerParams(vmem_limit_bytes=VMEM_LIMIT),
        name="attend_back",
    )(lengths, part, q, k, v, o, lse, d_heads)


class Block:
    def __init__(self, geo):
        chips = geo.groups // 2
        self.nx = min(geo.nx, chips)
        self.ny = chips // self.nx


class PairSum:
    def __init__(self, count, me, core, first, w, bufs, sems, make, stage=None):
        self.count, self.me, self.core, self.first, self.w = count, me, core, first, w
        self.near_out, self.near_in, self.far_in = bufs
        self.near_send, self.near_recv, self.far_send, self.far_recv = sems
        self.make = make
        self.slots = self.near_out.shape[0]
        self.stage = stage

    def slot(self, chip):
        return ((chip + self.count - self.me + self.count - 1) % self.count) % self.slots

    def near(self, chip):
        return pltpu.make_async_remote_copy(
            src_ref=self.near_out.at[self.slot(chip)],
            dst_ref=self.near_in.at[chip],
            send_sem=self.near_send.at[chip],
            recv_sem=self.near_recv.at[chip],
            device_id=(self.first + self.me * 2 + 1 - self.core, self.w),
            device_id_type=MESH,
        )

    def far(self, chip):
        return pltpu.make_async_remote_copy(
            src_ref=self.near_in.at[chip],
            dst_ref=self.far_in.at[self.me],
            send_sem=self.far_send.at[chip],
            recv_sem=self.far_recv.at[self.me],
            device_id=(self.first + chip * 2 + self.core, self.w),
            device_id_type=MESH,
        )

    def far_arrival(self, chip):
        return pltpu.make_async_remote_copy(
            src_ref=self.far_in.at[chip],
            dst_ref=self.far_in.at[chip],
            send_sem=self.far_send.at[chip],
            recv_sem=self.far_recv.at[chip],
            device_id=(self.first + chip * 2 + self.core, self.w),
            device_id_type=MESH,
        )

    def run(self):
        def start(d):
            chip = (self.me + 1 + d) % self.count
            if self.slots < self.count:

                @pl.when(d >= self.slots)
                def _():
                    self.near((self.me + 1 + d - self.slots) % self.count).wait_send()

            self.near_out[d % self.slots] = self.make(chip, 1 - self.core).astype(BF16)
            self.near(chip).start()

        def send(d):
            chip = (self.me + 1 + d) % self.count
            own = self.make(chip, self.core)
            self.near(chip).wait_recv()
            self.near_in[chip] = (own + self.near_in[chip].astype(F32)).astype(BF16)
            self.far(chip).start()

        def step(d, carry):
            start(d)
            send(d - 1)
            return carry

        start(0)
        lax.fori_loop(1, self.count, step, 0)

    def finish(self):
        total = self.make(self.me, self.core)
        self.near(self.me).wait_recv()
        total = total + self.near_in[self.me].astype(F32)
        if self.stage is None:
            for d in range(1, self.count):
                chip = (self.me + d) % self.count
                self.far_arrival(chip).wait_recv()
                total = total + self.far_in[chip].astype(F32)
            return total
        stage, sem = self.stage

        def fetch(d):
            chip = (self.me + d) % self.count
            return pltpu.make_async_copy(self.far_in.at[chip], stage.at[d % 2], sem.at[d % 2])

        self.far_arrival((self.me + 1) % self.count).wait_recv()
        fetch(1).start()
        for d in range(1, self.count):
            if d + 1 < self.count:
                self.far_arrival((self.me + d + 1) % self.count).wait_recv()
                fetch(d + 1).start()
            fetch(d).wait()
            total = total + stage[d % 2].astype(F32)
        return total

    def drain(self):
        for d in range(self.count):
            chip = (self.me + 1 + d) % self.count
            if d >= self.count - self.slots:
                self.near(chip).wait_send()
            if d < self.count - 1:
                self.far(chip).wait_send()


class CrossSum(PairSum):
    def with_corner(self, via, via_send, via_recv):
        self.via, self.via_send, self.via_recv = via, via_send, via_recv
        x, y = self.me % 2, self.me // 2
        self.near_chips = [y * 2 + 1 - x, (1 - y) * 2 + x]
        self.corner = (1 - y) * 2 + 1 - x
        self.half = self.near_in.shape[1] // 2
        return self

    def part(self, ref, h):
        return ref.at[pl.ds(h * self.half, self.half)]

    def device(self, chip):
        return (self.first + chip * 2 + self.core, self.w)

    def corner_copy(self, h):
        return pltpu.make_async_remote_copy(
            src_ref=self.part(self.near_in.at[self.corner], h),
            dst_ref=self.via.at[h],
            send_sem=self.via_send.at[h],
            recv_sem=self.via_recv.at[h],
            device_id=self.device(self.near_chips[h]),
            device_id_type=MESH,
        )

    def near_copy(self, which, h):
        chip = self.near_chips[which]
        return pltpu.make_async_remote_copy(
            src_ref=self.part(self.near_in.at[chip], h),
            dst_ref=self.part(self.far_in.at[self.me], h),
            send_sem=self.far_send.at[which * 2 + h],
            recv_sem=self.far_recv.at[which * 2 + h],
            device_id=self.device(chip),
            device_id_type=MESH,
        )

    def near_arrival(self, which, h):
        here = self.part(self.far_in.at[self.near_chips[which]], h)
        return pltpu.make_async_remote_copy(
            src_ref=here,
            dst_ref=here,
            send_sem=self.far_send.at[which * 2 + h],
            recv_sem=self.far_recv.at[which * 2 + h],
            device_id=self.device(self.near_chips[which]),
            device_id_type=MESH,
        )

    def run(self):
        order = [self.corner] + self.near_chips + [self.me]

        def chip_at(d):
            chip = order[0]
            for i in range(1, len(order)):
                chip = jnp.where(d == i, order[i], chip)
            return chip

        def start(d):
            chip = chip_at(d)
            self.near_out[chip] = self.make(chip, 1 - self.core).astype(BF16)
            self.near(chip).start()

        start(0)

        def step(d, carry):
            start(d)
            chip = chip_at(d - 1)
            own = self.make(chip, self.core)
            self.near(chip).wait_recv()
            self.near_in[chip] = (own + self.near_in[chip].astype(F32)).astype(BF16)

            @pl.when(d == 1)
            def _():
                self.corner_copy(0).start()
                self.corner_copy(1).start()

            @pl.when(d == 2)
            def _():
                self.near_copy(0, 0).start()

            @pl.when(d == 3)
            def _():
                self.near_copy(1, 1).start()

            return carry

        lax.fori_loop(1, len(order), step, 0)
        for which in range(2):
            h = 1 - which
            self.corner_copy(h).wait_recv()
            chip = self.near_chips[which]
            rows = pl.ds(h * self.half, self.half)
            self.near_in[chip, rows, :] = (
                self.near_in[chip, rows, :].astype(F32) + self.via[h].astype(F32)
            ).astype(BF16)
            self.near_copy(which, h).start()

    def slot(self, chip):
        return chip

    def finish(self):
        stage, sem = self.stage
        total = self.make(self.me, self.core)
        self.near(self.me).wait_recv()
        total = total + self.near_in[self.me].astype(F32)
        fetches = []
        for which in range(2):
            for h in range(2):
                self.near_arrival(which, h).wait_recv()
            fetches.append(
                pltpu.make_async_copy(self.far_in.at[self.near_chips[which]], stage.at[which], sem.at[which])
            )
            fetches[-1].start()
        for which in range(2):
            fetches[which].wait()
            total = total + stage[which].astype(F32)
        return total

    def drain(self):
        for chip in [self.corner] + self.near_chips + [self.me]:
            self.near(chip).wait_send()
        for h in range(2):
            self.corner_copy(h).wait_send()
            for which in range(2):
                self.near_copy(which, h).wait_send()


def closing_kernel(
    geo,
    rank,
    single_count,
    early,
    len_ref,
    id_ref,
    tokens_ref,
    first_ref,
    dq_ref,
    dk_ref,
    dv_ref,
    slice_ref,
    down_ref,
    up_ref,
    small_ref,
    *refs,
):
    singles = refs[:single_count]
    early_ref = refs[single_count] if early else None
    (
        grad_ref,
        sum1_ref,
        sum2_ref,
        tok_far,
        tok_out,
        tok_in,
        tok_stage,
        small_buf,
        set1_out,
        set1_in,
        set1_far,
        set2_out,
        set2_in,
        set2_far,
        down_acc,
        up_acc,
        mine1,
        mine2,
        place_buf,
        fold_buf,
        all1,
        all2,
        places,
        done1,
        done2,
        tok_sems,
        set1_sems,
        set2_sems,
        line_send,
        line_recv,
        spread_send,
        spread_recv,
        local_sem,
        stage_sem,
        small_sem,
        tok_via,
        via_sems,
    ) = refs[single_count + early :]
    x, y, core, w = device_here(geo)
    s = lax.axis_index("seq")
    rows, width, wt, groups, parts = geo.rows, geo.width, geo.wt, geo.groups, geo.parts
    part, g = s // groups, s % groups
    docs = len_ref.shape[1]
    doc_rows = docs * rank
    lane_count = down_ref.shape[0] // 4
    lanes = pl.ds(pl.multiple_of(g * LANES, LANES), LANES)
    starts, ends = doc_bounds(len_ref)
    greet_all(geo)

    def iota(shape, dim):
        return lax.broadcasted_iota(jnp.int32, shape, dim)

    def zero_one(condition):
        return jnp.where(condition, 1.0, 0.0).astype(BF16)

    def chosen_of(t):
        pos = t * rows + iota((rows, LANES), 0)
        return select_from(pos, starts, ends, id_ref, rank)

    def fold(j):
        a, b = iota((lane_count, LANES), 0), iota((lane_count, LANES), 1)
        return zero_one((b >= j * rank) & (b < (j + 1) * rank) & (a % rank == b - j * rank))

    def make_tokens(chip, whose):
        t = chip * 2 + whose
        at = pl.ds(pl.multiple_of(t * rows, rows), rows)
        if parts == 1:
            d_q = dq_ref[at, :]
        else:
            inner = pl.ds(pl.multiple_of((t % groups) * rows, rows), rows)
            d_q = jnp.where(t // groups == part, dq_ref[inner, :], jnp.zeros((rows, LANES), BF16))
        pieces = [d_q, dk_ref[at, :], dv_ref[at, :]]
        chosen = chosen_of(t)
        total = jnp.zeros((rows, width), F32)
        low = jnp.zeros((rows, LANES), F32)
        for j in range(3):
            total = total + dot_nt(pieces[j], slice_ref[:, j * LANES : (j + 1) * LANES])
            part_low = dot_nt(pieces[j], up_ref[pl.ds(j * lane_count, lane_count), lanes])
            low = low + dot_nn((part_low * chosen).astype(BF16), fold(j))
        return jnp.concatenate([total, low], axis=1)

    square = geo.nx == 2 and geo.ny == 2
    tok = (CrossSum if square else PairSum)(
        geo.seq // 2, s // 2, core, 0, w, (tok_out, tok_in, tok_far), [tok_sems.at[i] for i in range(4)], make_tokens,
        (tok_stage, stage_sem),
    )
    if square:
        tok.with_corner(tok_via, via_sems.at[0], via_sems.at[1])

    def by_document(value):
        return dot_tn(fold_buf[...], value)[:doc_rows]

    def make_set1(chip, whose):
        return owner_columns(singles, chip * 2 + whose, groups)

    def make_set2(chip, whose):
        owner = chip * 2 + whose
        cut = pl.ds(pl.multiple_of(owner * LANES, LANES), LANES)
        return jnp.concatenate([down_acc[j * doc_rows : (j + 1) * doc_rows, cut] for j in range(3)], axis=1)

    chips = groups // 2
    set1 = PairSum(
        chips, g // 2, core, part * groups, w, (set1_out, set1_in, set1_far), [set1_sems.at[i] for i in range(4)], make_set1
    )
    set2 = PairSum(
        chips, g // 2, core, part * groups, w, (set2_out, set2_in, set2_far), [set2_sems.at[i] for i in range(4)], make_set2
    )

    def peer(n):
        plane = (w + n) % wt
        other = (part + n // wt) % parts
        return other * groups + g, plane, other * wt + plane

    mine_at = part * wt + w

    late = set1_out.shape[2]
    front = late + 3 * LANES
    whole = mine1.shape[1]

    def cut_of(kind, ref):
        if kind == 0:
            return ref.at[:, pl.ds(0, front)]
        if kind == 3:
            return ref.at[:, pl.ds(front, whole - front)]
        return ref

    def line_copy(kind, n, src, dst_all):
        device, plane, _ = peer(n)
        return pltpu.make_async_remote_copy(
            src_ref=cut_of(kind, src),
            dst_ref=cut_of(kind, dst_all.at[mine_at]),
            send_sem=line_send.at[kind, n],
            recv_sem=line_recv.at[kind, mine_at],
            device_id=(device, plane),
            device_id_type=MESH,
        )

    def line_arrival(kind, n, dst_all):
        device, plane, at = peer(n)
        return pltpu.make_async_remote_copy(
            src_ref=cut_of(kind, dst_all.at[at]),
            dst_ref=cut_of(kind, dst_all.at[at]),
            send_sem=line_send.at[kind, n],
            recv_sem=line_recv.at[kind, at],
            device_id=(device, plane),
            device_id_type=MESH,
        )

    peers = range(1, wt * parts)

    block = Block(geo)
    chip_here = g // 2
    here = (chip_here % block.nx, chip_here // block.nx, core, w)

    def region_of(ref):
        def region(ux, uy, whose, half):
            one = ref.at[(uy * block.nx + ux) * 2 + whose]
            if half is None:
                return one
            return one.at[pl.ds(half * (lane_count // 2), lane_count // 2)]

        return region

    spreads = [
        Spread(block, here, region_of(ref), spread_send, spread_recv, i, part * groups)
        for i, ref in enumerate((sum1_ref, sum2_ref))
    ]
    finals = [done1, done2]
    outs = [sum1_ref, sum2_ref]

    def place(kind, mine, dst_all):
        total = dot_nn(place_buf[:, :doc_rows], mine[...])
        for n in peers:
            line_arrival(kind, n, dst_all).wait_recv()
            if kind == 0:
                line_arrival(2, n, places).wait_recv()
                if early:
                    line_arrival(3, n, dst_all).wait_recv()
            at = peer(n)[2]
            total = total + dot_nn(places[at][:, :doc_rows], dst_all[at])
        finals[kind][...] = total.astype(BF16)
        for way in (0, 1, 4):
            spreads[kind].go(way, own=finals[kind])
        pltpu.make_async_copy(finals[kind], outs[kind].at[g], local_sem.at[kind]).start()

    def pass_on(kind):
        spread = spreads[kind]
        spread.wait(0)
        spread.go(2)
        spread.go(5)
        spread.wait(1)
        spread.go(3)
        spread.go(6)

    def pass_last(kind):
        spread = spreads[kind]
        spread.wait(2)
        spread.go(7)
        spread.wait(3)
        spread.go(8)

    place_buf[...], fold_buf[...] = placement(id_ref, docs, rank, lane_count)
    for n in peers:
        line_copy(2, n, place_buf, places).start()
    if early:
        mine1[:, front:] = early_ref[...]
        for n in peers:
            line_copy(3, n, mine1, all1).start()

    set1.run()
    tok.run()

    def small_copy(t):
        return pltpu.make_async_copy(
            small_ref.at[pl.ds(pl.multiple_of(t * rows, rows), rows)], small_buf.at[t % 2], small_sem.at[t % 2]
        )

    def add_up(t, carry):
        at = pl.ds(pl.multiple_of(t * rows, rows), rows)

        @pl.when(t + 1 < geo.seq)
        def _():
            small_copy(t + 1).start()

        small_copy(t).wait()
        for j in range(3):
            cut = slice(j * LANES, (j + 1) * LANES)
            if j == 0:
                if parts == 1:
                    value = dq_ref[at, :]
                else:
                    inner = pl.ds(pl.multiple_of((t % groups) * rows, rows), rows)
                    value = jnp.where(t // groups == part, dq_ref[inner, :], jnp.zeros((rows, LANES), BF16))
            else:
                value = (dk_ref if j == 1 else dv_ref)[at, :]
            up_acc[cut, :] += dot_tn(small_buf[t % 2][:, cut], value)
        return carry

    up_acc[...] = jnp.zeros_like(up_acc)
    small_copy(0).start()
    lax.fori_loop(0, geo.seq, add_up, 0)

    for j in range(3):
        mine1[:, late + j * LANES : late + (j + 1) * LANES] = by_document(
            up_acc[j * lane_count : (j + 1) * lane_count, :].astype(BF16)
        ).astype(BF16)
    mine1[:, :late] = set1.finish().astype(BF16)
    for n in peers:
        line_copy(0, n, mine1, all1).start()

    total = tok.finish()
    low = total[:, width:].astype(BF16)
    total = total[:, :width] + first_ref[...]
    chosen = chosen_of(s)
    pos = s * rows + iota((rows, doc_rows), 0)
    doc_of = iota((rows, doc_rows), 1) // rank
    in_doc = doc_of == segment_from(pos, starts)
    tokens = tokens_ref[...]
    for j in range(3):
        a, b = iota((LANES, lane_count), 0), iota((LANES, lane_count), 1)
        widen = zero_one((a >= j * rank) & (a < (j + 1) * rank) & (b % rank == a - j * rank))
        wide = (dot_nn(low, widen) * chosen).astype(BF16)
        total = total + dot_nn(wide, down_ref[j * lane_count : (j + 1) * lane_count, :])
        by_doc = dot_nn(low, widen[:, :doc_rows])
        by_doc = jnp.where(in_doc, by_doc, 0.0).astype(BF16)
        down_acc[j * doc_rows : (j + 1) * doc_rows, :] = dot_tn(by_doc, tokens)
    set2.run()
    grad_ref[...] = total
    place(0, mine1, all1)
    mine2[...] = set2.finish().astype(BF16)
    for n in peers:
        line_copy(1, n, mine2, all2).start()
    pass_on(0)
    place(1, mine2, all2)
    pass_last(0)
    pass_on(1)
    pass_last(1)
    for kind in range(2):
        for way in range(4, 9):
            spreads[kind].wait(way)
        spreads[kind].wait_sends()
        pltpu.make_async_copy(finals[kind], outs[kind].at[g], local_sem.at[kind]).wait()
    for n in peers:
        line_copy(0, n, mine1, all1).wait_send()
        line_copy(1, n, mine2, all2).wait_send()
        line_copy(2, n, place_buf, places).wait_send()
        if early:
            line_copy(3, n, mine1, all1).wait_send()
    tok.drain()
    set1.drain()
    set2.drain()


def greet_all(geo):
    s, w = lax.axis_index("seq"), lax.axis_index("wt")
    barrier = pltpu.get_barrier_semaphore()
    part, g = s // geo.groups, s % geo.groups
    for d in range(1, geo.seq):
        pl.semaphore_signal(barrier, inc=1, device_id=((s + d) % geo.seq, w), device_id_type=MESH)
    count = geo.seq - 1
    for d in range(1, geo.wt):
        for q in range(geo.parts):
            other = ((part + q) % geo.parts) * geo.groups + g
            pl.semaphore_signal(barrier, inc=1, device_id=(other, (w + d) % geo.wt), device_id_type=MESH)
            count += 1
    pl.semaphore_wait(barrier, count)


def closing(geo, rank, lengths, ids, tokens, d_first, dq, dk, dv, w_slice, down, up, small, grads, early_sum):
    rows, width = geo.rows, geo.width
    docs = lengths.shape[1]
    doc_rows = docs * rank
    lane_count = down.shape[0] // 4
    early = [] if early_sum is None else [early_sum]
    late = sum(v.shape[1] for v in grads) // geo.groups
    set1 = late + 3 * LANES + sum(v.shape[1] for v in early)
    set2 = 3 * LANES
    chips, near = geo.seq // 2, geo.groups // 2
    peers = geo.wt * geo.parts
    smem = pl.BlockSpec(memory_space=pltpu.SMEM)
    vmem = pl.BlockSpec(memory_space=pltpu.VMEM)
    any_spec = pl.BlockSpec(memory_space=pl.ANY)
    dma = pltpu.SemaphoreType.DMA
    wide = width + LANES
    return pl.pallas_call(
        functools.partial(closing_kernel, geo, rank, len(grads), len(early)),
        out_shape=[
            jax.ShapeDtypeStruct((rows, width), F32),
            jax.ShapeDtypeStruct((geo.groups, lane_count, set1), BF16),
            jax.ShapeDtypeStruct((geo.groups, lane_count, set2), BF16),
            jax.ShapeDtypeStruct((chips, rows, wide), BF16),
        ],
        in_specs=[smem, smem] + [vmem] * 8 + [any_spec] + [vmem] * (len(grads) + len(early)),
        out_specs=[vmem, any_spec, any_spec, any_spec],
        scratch_shapes=[
            pltpu.VMEM((min(chips, 4), rows, wide), BF16),
            pltpu.VMEM((chips, rows, wide), BF16),
            pltpu.VMEM((2, rows, wide), BF16),
            pltpu.VMEM((2, rows, 3 * lane_count), BF16),
            pltpu.VMEM((near, doc_rows, late), BF16),
            pltpu.VMEM((near, doc_rows, late), BF16),
            pltpu.VMEM((near, doc_rows, late), BF16),
            pltpu.VMEM((near, doc_rows, 3 * LANES), BF16),
            pltpu.VMEM((near, doc_rows, 3 * LANES), BF16),
            pltpu.VMEM((near, doc_rows, 3 * LANES), BF16),
            pltpu.VMEM((3 * doc_rows, width), F32),
            pltpu.VMEM((3 * lane_count, LANES), F32),
            pltpu.VMEM((doc_rows, set1), BF16),
            pltpu.VMEM((doc_rows, set2), BF16),
            pltpu.VMEM((lane_count, LANES), BF16),
            pltpu.VMEM((lane_count, LANES), BF16),
            pltpu.VMEM((peers, doc_rows, set1), BF16),
            pltpu.VMEM((peers, doc_rows, set2), BF16),
            pltpu.VMEM((peers, lane_count, LANES), BF16),
            pltpu.VMEM((lane_count, set1), BF16),
            pltpu.VMEM((lane_count, set2), BF16),
            dma((4, chips)),
            dma((4, near)),
            dma((4, near)),
            dma((4, peers)),
            dma((4, peers)),
            dma((Spread.KINDS, 2)),
            dma((Spread.KINDS, 2)),
            dma((2,)),
            dma((2,)),
            dma((2,)),
            pltpu.VMEM((2, rows // 2, wide) if chips == 4 else (1, 16, LANES), BF16),
            dma((2, 2)),
        ],
        compiler_params=pltpu.CompilerParams(
            collective_id=1, has_side_effects=True, vmem_limit_bytes=VMEM_LIMIT
        ),
        name="close",
    )(lengths, ids, tokens, d_first, dq, dk, dv, w_slice, down, up, small, *grads, *early)


def unpack_kernel(late, one_ref, two_ref, down_ref, up_ref, fc1_down_ref, fc2_up_ref, fc1_up_ref, fc2_down_ref):
    for j in range(3):
        down_ref[j] = two_ref[0, :, j * LANES : (j + 1) * LANES].astype(F32)
    singles = [down_ref.at[3], up_ref.at[3], fc1_down_ref, fc2_up_ref, fc1_up_ref, fc2_down_ref]
    at = 0
    for ref in singles[:late] + [up_ref.at[j] for j in range(3)] + singles[late:]:
        wide = ref.shape[1]
        ref[...] = one_ref[0, :, at : at + wide].astype(F32)
        at += wide


def unpack(geo, one, two, lane_count, late):
    groups = geo.groups
    thick = (one.shape[2] - 7 * LANES) // 2

    def whole(wide):
        return jax.ShapeDtypeStruct((lane_count, wide * groups), F32)

    def flat(wide):
        return pl.BlockSpec((lane_count, wide), lambda i: (0, i))

    four = jax.ShapeDtypeStruct((4, lane_count, LANES * groups), F32)
    four_spec = pl.BlockSpec((4, lane_count, LANES), lambda i: (0, 0, i))
    return pl.pallas_call(
        functools.partial(unpack_kernel, late),
        grid=(groups,),
        out_shape=[four, four, whole(LANES), whole(LANES), whole(thick), whole(thick)],
        in_specs=[
            pl.BlockSpec((1,) + one.shape[1:], lambda i: (i, 0, 0)),
            pl.BlockSpec((1,) + two.shape[1:], lambda i: (i, 0, 0)),
        ],
        out_specs=[four_spec, four_spec, flat(LANES), flat(LANES), flat(thick), flat(thick)],
        compiler_params=pltpu.CompilerParams(vmem_limit_bytes=VMEM_LIMIT),
        name="unpack",
    )(one, two)


def layer_norm(value, gain, shift):
    mean = jnp.mean(value, axis=-1, keepdims=True)
    centred = value - mean
    spread = jnp.mean(centred * centred, axis=-1, keepdims=True)
    return centred * lax.rsqrt(spread + 1e-05) * gain + shift


def gelu_exact(value):
    return jax.nn.gelu(value, approximate=False)


def times_transposed(grad, weight):
    return lax.dot_general(
        grad, weight, (((1,), (1,)), ((), ())), preferred_element_type=jnp.float32
    )


def left_inner(left, right):
    return lax.dot_general(
        left, right, (((0,), (0,)), ((), ())), preferred_element_type=jnp.float32
    )


def stack_down(down):
    return jnp.transpose(down, (1, 0, 2)).reshape(down.shape[1], down.shape[0] * down.shape[2])


def stack_up(up):
    return up.reshape(up.shape[0] * up.shape[1], up.shape[2])


def unstack_down(stacked, adapter_count, rank_size):
    return jnp.transpose(stacked.reshape(stacked.shape[0], adapter_count, rank_size), (1, 0, 2))


def unstack_up(stacked, adapter_count, rank_size):
    return stacked.reshape(adapter_count, rank_size, stacked.shape[1])


def segment_of(positions, starts):
    return jnp.sum((positions[:, None] >= starts[None, :]).astype(jnp.int32), axis=1) - 1


def select_local(tok_rows, lane_count, rank_size, lengths, ids):
    starts = jnp.cumsum(lengths) - lengths
    local_pos = lax.axis_index("seq") * tok_rows + jnp.arange(tok_rows, dtype=jnp.int32)
    local_seg = segment_of(local_pos, starts)
    doc_range = jnp.arange(lengths.shape[0], dtype=jnp.int32)
    chosen = jnp.sum(jnp.where(local_seg[:, None] == doc_range[None, :], ids[None, :], 0), axis=1)
    lane_owner = jnp.arange(lane_count, dtype=jnp.int32) // rank_size
    lane_rank = jnp.arange(lane_count, dtype=jnp.int32) % rank_size
    doc_owner = jnp.repeat(doc_range, rank_size)
    doc_rank = jnp.arange(doc_owner.shape[0], dtype=jnp.int32) % rank_size
    to_doc = (lane_owner[:, None] == jnp.repeat(ids, rank_size)[None, :]) & (lane_rank[:, None] == doc_rank[None, :])
    return (
        (chosen[:, None] == lane_owner[None, :]).astype(jnp.float32),
        to_doc.astype(jnp.bfloat16),
        (local_seg[:, None] == doc_owner[None, :]).astype(jnp.float32),
    )


def feed_forward(
    geo, tokens, cotangent, attended_tok, weights, vectors, attn_maps, fc1_maps, fc2_maps, select
):
    tok_rows, model_width = tokens.shape
    full_out, full_fc1, full_fc2 = [lax.all_gather(v, "wt", axis=0, tiled=True) for v in weights]
    out_bias, norm1_gain, norm1_bias, fc1_bias, fc2_bias, norm2_gain, norm2_bias = vectors
    out_down, out_up = attn_maps
    fc1_down_all, fc1_up_all = fc1_maps
    fc2_down_all, fc2_up_all = fc2_maps
    select, to_doc, in_doc = select

    def by_doc(low):
        return (jnp.dot(low, to_doc, preferred_element_type=jnp.float32) * in_doc).astype(jnp.bfloat16)

    out_main = jnp.dot(attended_tok, full_out, preferred_element_type=jnp.float32)
    small_out = (
        jnp.dot(attended_tok, out_down, preferred_element_type=jnp.float32) * select
    ).astype(jnp.bfloat16)
    z_value = out_main + out_bias + jnp.dot(small_out, out_up, preferred_element_type=jnp.float32)
    first_sum = tokens.astype(jnp.float32) + z_value
    first_norm, norm1_back = jax.vjp(
        lambda value: layer_norm(value, norm1_gain, norm1_bias), first_sum
    )
    first_low = first_norm.astype(jnp.bfloat16)
    fc1_main = jnp.dot(first_low, full_fc1, preferred_element_type=jnp.float32)
    small_fc1 = (
        jnp.dot(first_low, fc1_down_all, preferred_element_type=jnp.float32) * select
    ).astype(jnp.bfloat16)
    pre_act = (
        fc1_main + fc1_bias + jnp.dot(small_fc1, fc1_up_all, preferred_element_type=jnp.float32)
    )
    act_value, gelu_back = jax.vjp(gelu_exact, pre_act)
    act_low = act_value.astype(jnp.bfloat16)
    fc2_main = jnp.dot(act_low, full_fc2, preferred_element_type=jnp.float32)
    small_fc2 = (
        jnp.dot(act_low, fc2_down_all, preferred_element_type=jnp.float32) * select
    ).astype(jnp.bfloat16)
    y_value = (
        fc2_main + fc2_bias + jnp.dot(small_fc2, fc2_up_all, preferred_element_type=jnp.float32)
    )
    output, norm2_back = jax.vjp(
        lambda value: layer_norm(value, norm2_gain, norm2_bias), first_norm + y_value
    )
    d_second = norm2_back(cotangent.astype(jnp.float32))[0]
    d_y = d_second.astype(jnp.bfloat16)
    d_act = times_transposed(d_y, full_fc2)
    low_fc2 = (times_transposed(d_y, fc2_up_all) * select).astype(jnp.bfloat16)
    d_act = d_act + times_transposed(low_fc2, fc2_down_all)
    grad_fc2_up = left_inner(by_doc(small_fc2), d_y)
    grad_fc2_down = left_inner(by_doc(low_fc2), act_low)
    d_pre = gelu_back(d_act)[0].astype(jnp.bfloat16)
    d_first_low = times_transposed(d_pre, full_fc1)
    low_fc1 = (times_transposed(d_pre, fc1_up_all) * select).astype(jnp.bfloat16)
    d_first_low = d_first_low + times_transposed(low_fc1, fc1_down_all)
    grad_fc1_up = left_inner(by_doc(small_fc1), d_pre)
    grad_fc1_down = left_inner(by_doc(low_fc1), first_low)
    d_first = norm1_back(d_second + d_first_low)[0]
    d_z = d_first.astype(jnp.bfloat16)
    d_attended = times_transposed(d_z, full_out)
    low_out = (times_transposed(d_z, out_up) * select).astype(jnp.bfloat16)
    d_attended = (d_attended + times_transposed(low_out, out_down)).astype(jnp.bfloat16)
    grad_out_up = left_inner(by_doc(small_out), d_z)
    grad_out_down = left_inner(by_doc(low_out), attended_tok)
    blocks = [
        [p * geo.groups + i for i in range(geo.groups)] for p in range(geo.parts)
    ]
    d_heads = lax.all_to_all(
        d_attended.reshape(tok_rows, geo.groups, LANES),
        "seq",
        split_axis=1,
        concat_axis=0,
        axis_index_groups=blocks,
        tiled=True,
    ).reshape(geo.queries, LANES)
    grads = [grad_out_down, grad_out_up, grad_fc1_down, grad_fc2_up, grad_fc1_up, grad_fc2_down]
    return output, d_first, d_heads, [v.astype(BF16) for v in grads]


def shards(
    tokens,
    cotangent,
    w_qkv,
    qv_bias,
    w_out,
    out_bias,
    norm1_gain,
    norm1_bias,
    w_fc1,
    fc1_bias,
    w_fc2,
    fc2_bias,
    norm2_gain,
    norm2_bias,
    doc_lengths,
    adapter_ids,
    attn_down,
    attn_up,
    fc1_down,
    fc1_up,
    fc2_down,
    fc2_up,
):
    tok_rows, model_width = tokens.shape
    adapter_count = attn_down.shape[1]
    rank_size = attn_down.shape[3]
    lane_count = adapter_count * rank_size
    seq_count = lax.axis_size("seq")
    geo = Geometry(tok_rows, model_width)
    part_index = lax.axis_index("seq") // geo.groups
    down_rows = jnp.transpose(attn_down, (0, 1, 3, 2)).reshape(4 * lane_count, model_width)
    up_rows = attn_up.reshape(4 * lane_count, model_width)
    weights = (w_out, w_fc1, w_fc2)
    vectors = (out_bias, norm1_gain, norm1_bias, fc1_bias, fc2_bias, norm2_gain, norm2_bias)

    def rows_of(down):
        return jnp.swapaxes(down, 1, 2).reshape(lane_count, down.shape[1])

    inside = all(v.shape[0] % (32 * seq_count) == 0 for v in weights)
    mlp = None
    if inside:
        mlp = (
            weights
            + (cotangent,)
            + tuple(v.reshape(1, -1) for v in vectors)
            + (rows_of(fc1_down), stack_up(fc1_up), rows_of(fc2_down), stack_up(fc2_up))
        )
    q_heads, k_heads, v_heads, o_heads, lse_heads, w_slice, small_all, *rest = forward_attention(
        geo, rank_size, doc_lengths, adapter_ids, tokens, w_qkv, down_rows, up_rows, qv_bias, mlp
    )
    if inside:
        output, d_first, d_heads, *set1, early_sum = rest
    else:
        early_sum = None
        output, d_first, d_heads, set1 = feed_forward(
            geo,
            tokens,
            cotangent,
            rest[0],
            weights,
            vectors,
            (stack_down(attn_down[3]), stack_up(attn_up[3])),
            (stack_down(fc1_down), stack_up(fc1_up)),
            (stack_down(fc2_down), stack_up(fc2_up)),
            select_local(tok_rows, lane_count, rank_size, doc_lengths[0], adapter_ids[0]),
        )
    d_q, d_k, d_v = backward_attention(
        geo, doc_lengths, part_index.reshape(1, 1), q_heads, k_heads, v_heads, o_heads, lse_heads, d_heads
    )
    input_grad, sum1, sum2, _ = closing(
        geo,
        rank_size,
        doc_lengths,
        adapter_ids,
        tokens,
        d_first,
        d_q,
        d_k,
        d_v,
        w_slice,
        down_rows,
        up_rows,
        small_all,
        set1,
        early_sum,
    )

    down4, up4, fc1_down_sum, fc2_up_sum, fc1_up_sum, fc2_down_sum = unpack(geo, sum1, sum2, lane_count, len(set1))

    def as_up(rows):
        return rows.reshape(rows.shape[:-2] + (adapter_count, rank_size, rows.shape[-1]))

    def as_down(rows):
        return jnp.swapaxes(as_up(rows), -1, -2)

    return (
        output,
        input_grad,
        as_down(down4),
        as_up(up4),
        as_down(fc1_down_sum),
        as_up(fc1_up_sum),
        as_down(fc2_down_sum),
        as_up(fc2_up_sum),
    )


def solution(mesh):
    placed = (
        P(("wt", "seq"), None),
        P(("wt", "seq"), None),
        P("wt", None),
        P(),
        P("wt", None),
        P(),
        P(),
        P(),
        P("wt", None),
        P(),
        P("wt", None),
        P(),
        P(),
        P(),
        P("wt", None),
        P("wt", None),
        P(),
        P(),
        P(),
        P(),
        P(),
        P(),
    )
    return jax.shard_map(
        shards,
        mesh=mesh,
        in_specs=placed,
        out_specs=(P(("wt", "seq"), None), P(("wt", "seq"), None), P(), P(), P(), P(), P(), P()),
        check_vma=False,
    )
```

```python
import functools

import jax
import jax.numpy as jnp
from jax import lax
from jax.experimental import pallas as pl
from jax.experimental.pallas import tpu as pltpu
from jax.sharding import PartitionSpec as P

HEADS = 16
HEAD_DIM = 64
LANES = 128
PAIR = LANES // HEAD_DIM
MESH = pl.DeviceIdType.MESH
F32 = jnp.float32
BF16 = jnp.bfloat16
VMEM_LIMIT = 60 * 2**20


def dot_nn(a, b):
    return lax.dot_general(a, b, (((1,), (0,)), ((), ())), preferred_element_type=F32)


def dot_nt(a, b):
    return lax.dot_general(a, b, (((1,), (1,)), ((), ())), preferred_element_type=F32)


def dot_tn(a, b):
    return lax.dot_general(a, b, (((0,), (0,)), ((), ())), preferred_element_type=F32)


class Geometry:
    def __init__(self, rows, width):
        self.seq = lax.axis_size("seq")
        self.wt = lax.axis_size("wt")
        self.rows = rows
        self.width = width
        self.groups = width // LANES
        self.parts = self.seq // self.groups
        chips = self.seq // 2
        nx = 1
        while nx * nx < chips:
            nx *= 2
        self.nx = nx
        self.ny = chips // nx
        self.keys = self.seq * rows
        self.queries = self.groups * rows


def doc_bounds(len_ref):
    count = len_ref.shape[1]
    starts, ends = [], []
    at = jnp.int32(0)
    for i in range(count):
        starts.append(at)
        at = at + len_ref[0, i]
        ends.append(at)
    return starts, ends


def segment_from(positions, starts):
    seg = jnp.zeros_like(positions)
    for start in starts[1:]:
        seg = seg + (positions >= start).astype(jnp.int32)
    return seg


def select_from(positions, starts, ends, id_ref, rank):
    owner = lax.broadcasted_iota(jnp.int32, positions.shape, 1) // rank
    picked = jnp.zeros(positions.shape, F32)
    for i in range(len(starts)):
        inside = (positions >= starts[i]) & (positions < ends[i]) & (owner == id_ref[0, i])
        picked = jnp.where(inside, 1.0, picked)
    return picked


def placement(id_ref, docs, rank, lane_count):
    a = lax.broadcasted_iota(jnp.int32, (lane_count, LANES), 0)
    b = lax.broadcasted_iota(jnp.int32, (lane_count, LANES), 1)
    every = jnp.zeros((lane_count, LANES), F32)
    first = jnp.zeros((lane_count, LANES), F32)
    for d in range(docs):
        seen = jnp.bool_(False)
        for e in range(d):
            seen = seen | (id_ref[0, e] == id_ref[0, d])
        hit = (a // rank == id_ref[0, d]) & (b // rank == d) & (a % rank == b % rank)
        every = jnp.where(hit, 1.0, every)
        first = jnp.where(hit, jnp.where(seen, 0.0, 1.0), first)
    return every.astype(BF16), first.astype(BF16)


def owner_columns(refs, owner, groups):
    cols = []
    for ref in refs:
        wide = ref.shape[1] // groups
        cols.append(ref[:, pl.ds(pl.multiple_of(owner * wide, LANES), wide)])
    return jnp.concatenate(cols, axis=1).astype(F32)


class Spread:
    KINDS = 9

    def __init__(self, geo, here, region, send, recv, unit, first=0):
        self.geo, self.here, self.region = geo, here, region
        self.send, self.recv, self.unit, self.first = send, recv, unit, first

    def copy(self, kind, src, dst, x, y, core):
        return pltpu.make_async_remote_copy(
            src_ref=src,
            dst_ref=dst,
            send_sem=self.send.at[kind, self.unit],
            recv_sem=self.recv.at[kind, self.unit],
            device_id=(self.first + ((y * self.geo.nx) + x) * 2 + core, self.here[3]),
            device_id_type=MESH,
        )

    def others(self):
        nx, ny = self.geo.nx, self.geo.ny
        x, y, core, _ = self.here
        row = [((x + d) % nx, y) for d in range(1, nx)]
        col = [(x, (y + d) % ny) for d in range(1, ny)]
        return row, col

    def plan(self):
        x, y, core, _ = self.here
        row, col = self.others()
        plan = {kind: [] for kind in range(self.KINDS)}
        for tx, ty in row:
            plan[0].append(((x, y), None, (tx, ty, core)))
        for tx, ty in col:
            plan[1].append(((x, y), None, (tx, ty, core)))
        for ux, uy in row:
            for tx, ty in col:
                plan[2].append(((ux, uy), 0, (tx, ty, core)))
        for ux, uy in col:
            for tx, ty in row:
                plan[3].append(((ux, uy), 1, (tx, ty, core)))
        plan[4].append(((x, y), None, (x, y, 1 - core)))
        for ux, uy in row:
            plan[5].append(((ux, uy), None, (x, y, 1 - core)))
        for ux, uy in col:
            plan[6].append(((ux, uy), None, (x, y, 1 - core)))
        for ux, _ in row:
            for _, uy in col:
                plan[7].append(((ux, uy), 0, (x, y, 1 - core)))
                plan[8].append(((ux, uy), 1, (x, y, 1 - core)))
        return plan

    def go(self, kind, own=None):
        core = self.here[2]
        for (ux, uy), half, (tx, ty, tcore) in self.plan()[kind]:
            dst = self.region(ux, uy, core, half)
            src = dst if own is None else own
            self.copy(kind, src, dst, tx, ty, tcore).start()

    def arrivals(self, kind):
        x, y, core, _ = self.here
        row, col = self.others()
        if kind == 0:
            return [(u, None, core) for u in row]
        if kind == 1:
            return [(u, None, core) for u in col]
        if kind in (2, 3):
            return [((ux, uy), kind - 2, core) for ux, _ in row for _, uy in col]
        if kind == 4:
            return [((x, y), None, 1 - core)]
        if kind == 5:
            return [(u, None, 1 - core) for u in row]
        if kind == 6:
            return [(u, None, 1 - core) for u in col]
        return [((ux, uy), kind - 7, 1 - core) for ux, _ in row for _, uy in col]

    def wait(self, kind):
        x, y, core, _ = self.here
        for (ux, uy), half, whose in self.arrivals(kind):
            ref = self.region(ux, uy, whose, half)
            self.copy(kind, ref, ref, x, y, 1 - core).wait_recv()

    def wait_sends(self):
        x, y, core, _ = self.here
        for kind in range(self.KINDS):
            for (ux, uy), half, _ in self.plan()[kind]:
                ref = self.region(ux, uy, core, half)
                self.copy(kind, ref, ref, x, y, 1 - core).wait_send()


def device_here(geo):
    s = lax.axis_index("seq")
    core = s % 2
    chip = s // 2
    return chip % geo.nx, chip // geo.nx, core, lax.axis_index("wt")


def greet(geo):
    s, w = lax.axis_index("seq"), lax.axis_index("wt")
    barrier = pltpu.get_barrier_semaphore()
    for d in range(1, geo.seq):
        pl.semaphore_signal(barrier, inc=1, device_id=((s + d) % geo.seq, w), device_id_type=MESH)
    for d in range(1, geo.wt):
        pl.semaphore_signal(barrier, inc=1, device_id=(s, (w + d) % geo.wt), device_id_type=MESH)
    pl.semaphore_wait(barrier, geo.seq + geo.wt - 2)


def erf(v):
    v = jnp.clip(v, -3.832506856900711, 3.832506856900711)
    sq = v * v
    top = jnp.full_like(v, 0.00022905065861350646)
    for c in (0.0034082910107109506, 0.050955695062380861, 0.18520832239976145, 1.128379143519084):
        top = top * sq + c
    low = jnp.full_like(v, -1.1791602954361697e-7)
    for c in (0.000023547966471313185, 0.0010179625278914885, 0.014070470171167667, 0.11098505178285362, 0.49746925110067538, 1.0):
        low = low * sq + c
    return v * top / low


def normed(value):
    mean = jnp.mean(value, axis=1, keepdims=True)
    centred = value - mean
    spread = lax.rsqrt(jnp.mean(centred * centred, axis=1, keepdims=True) + 1e-05)
    return centred * spread, spread


def normed_back(grad, gain, unit, spread):
    g = grad * gain
    return spread * (
        g - jnp.mean(g, axis=1, keepdims=True) - unit * jnp.mean(g * unit, axis=1, keepdims=True)
    )


class Names:
    def __init__(self, names, refs):
        self.__dict__.update(zip(names, refs))


MLP_INPUTS = (
    "w_out", "w_fc1", "w_fc2", "cotangent", "out_bias", "gain1", "shift1", "fc1_bias", "fc2_bias", "gain2", "shift2",
    "fc1_down", "fc1_up", "fc2_down", "fc2_up",
)
BASE_OUTPUTS = ("q", "k", "v", "o", "lse", "w_slice", "small")
MLP_OUTPUTS = ("output", "d_first", "d_heads", "g_out_down", "g_out_up", "g_fc1_down", "early_sum")
BASE_SCRATCH = (
    "tok", "seg", "att_send_buf", "local_sem", "send_sem", "recv_sem", "slice_send", "slice_recv", "line_send",
    "line_recv", "att_send", "att_recv", "q_buf", "k_buf", "v_buf", "o_buf", "lse_buf", "slice_buf", "small_buf", "flush_sem",
)
LATER = ("cotangent", "fc1_down", "fc1_up", "fc2_down", "fc2_up")
MLP_SCRATCH = (
    "att", "full_out", "full_fc1", "full_fc2", "unit1", "h1", "h1_low", "act", "slope", "d_pre", "y", "d_att_buf",
    "back_send", "back_recv", "g_fc2_up", "g_fc1_up", "g_fc2_down", "set_out", "set_in", "set_far", "set_sems",
    "load_sem", "cotangent_buf", "fc1_down_buf", "fc1_up_buf", "fc2_down_buf", "fc2_up_buf",
)


def forward_kernel(geo, inside, rank, len_ref, id_ref, tokens_ref, wqkv_ref, down_ref, up_ref, bias_ref, *refs):
    in_names = MLP_INPUTS if inside else ()
    out_names = BASE_OUTPUTS + (MLP_OUTPUTS if inside else ("att",))
    scratch_names = BASE_SCRATCH + (MLP_SCRATCH if inside else ())
    r = Names(in_names + out_names + scratch_names, refs)
    weights_in = (r.w_out, r.w_fc1, r.w_fc2) if inside else ()
    weights_out = (r.full_out, r.full_fc1, r.full_fc2) if inside else ()
    weight_count = len(weights_in)
    att_ref, q_ref, k_ref, v_ref, o_ref, lse_ref, slice_ref, small_ref = (
        r.att, r.q_buf, r.k_buf, r.v_buf, r.o_buf, r.lse_buf, r.slice_buf, r.small_buf
    )
    results = [r.q, r.k, r.v, r.o, r.lse, r.w_slice, r.small]
    made = [q_ref, k_ref, v_ref, o_ref, lse_ref, slice_ref, small_ref]
    flushes = [pltpu.make_async_copy(made[i], results[i], r.flush_sem.at[i]) for i in range(len(made))]
    loads = []
    if inside:
        loads = [
            pltpu.make_async_copy(getattr(r, name), getattr(r, name + "_buf"), r.load_sem.at[i])
            for i, name in enumerate(LATER)
        ]
    tok_buf, seg_buf, att_buf, local_sem = r.tok, r.seg, r.att_send_buf, r.local_sem
    send_sem, recv_sem, slice_send, slice_recv = r.send_sem, r.recv_sem, r.slice_send, r.slice_recv
    line_send, line_recv, att_send, att_recv = r.line_send, r.line_recv, r.att_send, r.att_recv
    here = device_here(geo)
    x, y, core, w = here
    s = lax.axis_index("seq")
    part, g = s // geo.groups, s % geo.groups
    rows, width, wt = geo.rows, geo.width, geo.wt
    lanes = pl.ds(pl.multiple_of(g * LANES, LANES), LANES)

    own_tok = pltpu.make_async_copy(tokens_ref, tok_buf.at[s], local_sem.at[0])
    own_tok.start()
    shard = wqkv_ref.shape[0]
    own_slices = []
    for j in range(3):
        src = wqkv_ref.at[:, pl.ds(pl.multiple_of(j * width + g * LANES, LANES), LANES)]
        dst = slice_ref.at[pl.ds(pl.multiple_of(w * shard, shard), shard), pl.ds(j * LANES, LANES)]
        own_slices.append(pltpu.make_async_copy(src, dst, local_sem.at[1 + j]))
        own_slices[-1].start()
    own_weights = []
    for m in range(weight_count):
        height = weights_in[m].shape[0]
        dst = weights_out[m].at[pl.ds(pl.multiple_of(w * height, height), height)]
        own_weights.append(pltpu.make_async_copy(weights_in[m], dst, local_sem.at[4 + m]))
        own_weights[-1].start()

    greet(geo)

    def token_region(ux, uy, whose, half):
        block = tok_buf.at[(uy * geo.nx + ux) * 2 + whose]
        if half is None:
            return block
        return block.at[pl.ds(half * (rows // 2), rows // 2)]

    tok = Spread(geo, here, token_region, send_sem, recv_sem, 0)
    tok.go(0, own=tokens_ref)
    tok.go(1, own=tokens_ref)
    tok.go(4, own=tokens_ref)

    def slice_copy(j, p, up):
        dst = slice_ref.at[pl.ds(pl.multiple_of(p * shard, shard), shard), pl.ds(j * LANES, LANES)]
        return pltpu.make_async_remote_copy(
            src_ref=dst,
            dst_ref=dst,
            send_sem=slice_send.at[0 if up else 1, j, p],
            recv_sem=slice_recv.at[j, p],
            device_id=(s, w + 1 if up else w - 1),
            device_id_type=MESH,
        )

    for copy in loads:
        copy.start()

    starts, ends = doc_bounds(len_ref)
    seg_buf[...] = segment_from(lax.broadcasted_iota(jnp.int32, seg_buf.shape, 1), starts)

    seq = geo.seq
    mine = s

    def unit_rows(m, p, unit, half=None):
        height = weights_in[m].shape[0]
        piece = height // seq
        if half is None:
            return weights_out[m].at[pl.ds(pl.multiple_of(p * height + unit * piece, piece), piece)]
        piece = piece // 2
        return weights_out[m].at[
            pl.ds(pl.multiple_of(p * height + unit * 2 * piece + half * piece, piece), piece)
        ]

    def line_copy(m, p, up, own):
        height = weights_in[m].shape[0]
        piece = height // seq
        dst = unit_rows(m, p, mine)
        src = weights_in[m].at[pl.ds(pl.multiple_of(mine * piece, piece), piece)] if own else dst
        target = w + 1 if up else w - 1
        return pltpu.make_async_remote_copy(
            src_ref=src,
            dst_ref=dst,
            send_sem=line_send.at[0 if up else 1, m * wt + p],
            recv_sem=line_recv.at[m * wt + p],
            device_id=(s, target),
            device_id_type=MESH,
        )

    def nth_plane(j):
        below, above = w, wt - 1 - w
        both = jnp.minimum(below, above)
        in_turn = j < 2 * both
        dist = jnp.where(in_turn, j // 2 + 1, j - both + 1)
        from_below = jnp.where(in_turn, j % 2 == 0, below > above)
        return jnp.where(from_below, w - dist, w + dist)

    def weight_spread(m, p):
        def region(ux, uy, whose, half):
            return unit_rows(m, p, (uy * geo.nx + ux) * 2 + whose, half)

        return Spread(geo, here, region, send_sem, recv_sem, 1 + m * wt + p)

    units = []
    if inside:
        units = [(m, j) for j in range(wt - 1) for m in (0, 1)] + [(2, j) for j in range(wt - 1)]

    def start_lines(which):
        for m in which if inside else ():

            @pl.when(w < wt - 1)
            def _():
                line_copy(m, w, True, True).start()

            @pl.when(w > 0)
            def _():
                line_copy(m, w, False, True).start()

    def along(i):
        if i >= len(units):
            return
        m, j = units[i]
        p = nth_plane(j)
        line_copy(m, p, True, False).wait_recv()

        @pl.when((p < w) & (w < wt - 1))
        def _():
            line_copy(m, p, True, False).start()

        @pl.when((p > w) & (w > 0))
        def _():
            line_copy(m, p, False, False).start()

    def tick(i):
        if i == 0:
            along(0)
        if i == late_lines:
            start_lines((2,))
        if i < len(units):
            m, j = units[i]
            spread = weight_spread(m, nth_plane(j))
            spread.go(0)
            spread.go(1)
            spread.go(4)
        along(i + 1)
        if 0 <= i - 1 < len(units):
            m, j = units[i - 1]
            spread = weight_spread(m, nth_plane(j))
            spread.wait(0)
            spread.go(2)
            spread.go(5)
            spread.wait(1)
            spread.go(3)
            spread.go(6)
        if 0 <= i - 2 < len(units):
            m, j = units[i - 2]
            spread = weight_spread(m, nth_plane(j))
            spread.wait(2)
            spread.go(7)
            spread.wait(3)
            spread.go(8)

    tick_count = len(units) + 2 if units else 0
    late_lines = 0
    early_ticks = min(3, tick_count)
    loop_ticks = min(6, tick_count)

    def complete(m):
        own_weights[m].wait()
        for j in range(wt - 1):
            spread = weight_spread(m, nth_plane(j))
            for kind in range(4, 9):
                spread.wait(kind)

    for copy in own_slices:
        copy.wait()
    for j in range(3):

        @pl.when(w < wt - 1)
        def _():
            slice_copy(j, w, True).start()

        @pl.when(w > 0)
        def _():
            slice_copy(j, w, False).start()

    nx, ny = geo.nx, geo.ny
    row_n, col_n, diag_n = 2 * (nx - 1), 2 * (ny - 1), 2 * (nx - 1) * (ny - 1)

    def block_owner(i):
        r = i - 2
        c = r - row_n
        d = c - col_n
        dx_row, k_row = r % max(nx - 1, 1) + 1, r // max(nx - 1, 1)
        dy_col, k_col = c % max(ny - 1, 1) + 1, c // max(ny - 1, 1)
        half = max(diag_n // 2, 1)
        k_diag, in_diag = d // half, d % half
        dx_diag, dy_diag = in_diag % max(nx - 1, 1) + 1, in_diag // max(nx - 1, 1) + 1
        dx = jnp.where(i < 2, 0, jnp.where(i < 2 + row_n, dx_row, jnp.where(i < 2 + row_n + col_n, 0, dx_diag)))
        dy = jnp.where(i < 2 + row_n, 0, jnp.where(i < 2 + row_n + col_n, dy_col, dy_diag))
        kk = jnp.where(i < 2, i, jnp.where(i < 2 + row_n, k_row, jnp.where(i < 2 + row_n + col_n, k_col, k_diag)))
        return (((y + dy) % ny) * nx + (x + dx) % nx) * 2 + (core + kk) % 2

    def project(i, carry):
        @pl.when(i == 0)
        def _():
            start_lines((0, 1))
            for n in range(wt - 1):
                p = nth_plane(n)
                for j in range(3):
                    slice_copy(j, p, True).wait_recv()

                    @pl.when((p < w) & (w < wt - 1))
                    def _():
                        slice_copy(j, p, True).start()

                    @pl.when((p > w) & (w > 0))
                    def _():
                        slice_copy(j, p, False).start()

            own_tok.wait()

        @pl.when(i == 1)
        def _():
            tok.wait(4)

        @pl.when(i == 2)
        def _():
            tok.wait(0)
            tok.go(2)
            tok.go(5)
            tok.wait(1)
            tok.go(3)
            tok.go(6)

        @pl.when(i == 2 + row_n // 2)
        def _():
            tok.wait(5)

        @pl.when(i == 2 + row_n + col_n // 2)
        def _():
            tok.wait(6)

        @pl.when(i == 2 + row_n + col_n)
        def _():
            tok.wait(2)
            tok.go(7)
            tok.wait(3)
            tok.go(8)

        @pl.when(i == 2 + row_n + col_n + diag_n // 2)
        def _():
            tok.wait(7)
            tok.wait(8)

        for n in range(early_ticks):

            @pl.when(i == min(3 + 2 * n, geo.seq - 1))
            def _():
                tick(n)

        t = block_owner(i)
        block = tok_buf[t]
        at = pl.ds(pl.multiple_of(t * rows, rows), rows)
        pos = t * rows + lax.broadcasted_iota(jnp.int32, (rows, LANES), 0)
        chosen = select_from(pos, starts, ends, id_ref, rank)
        main = dot_nn(block, slice_ref[...])
        small = dot_nt(block, down_ref[: 3 * LANES, :])
        for j in range(3):
            cut = slice(j * LANES, (j + 1) * LANES)
            low = (small[:, cut] * chosen).astype(BF16)
            small_ref[at, cut] = low
            value = main[:, cut] + dot_nn(low, up_ref[cut, lanes])
            if j == 0:
                value = value + bias_ref[0:1, lanes]

                @pl.when(t // geo.groups == part)
                def _():
                    inner = pl.ds(pl.multiple_of((t % geo.groups) * rows, rows), rows)
                    q_ref[inner, :] = value.astype(BF16)
            elif j == 1:
                k_ref[at, :] = value.astype(BF16)
            else:
                v_ref[at, :] = (value + bias_ref[1:2, lanes]).astype(BF16)
        return carry

    lax.fori_loop(0, geo.seq, project, 0)

    scale = HEAD_DIM ** (-0.5)
    chunk = min(2048, geo.keys)
    chunks = geo.keys // chunk
    first_head = lax.broadcasted_iota(jnp.int32, (rows, LANES), 1) < HEAD_DIM

    def att_copy(b):
        return pltpu.make_async_remote_copy(
            src_ref=att_buf.at[b],
            dst_ref=att_ref.at[:, lanes],
            send_sem=att_send.at[b],
            recv_sem=att_recv.at[g],
            device_id=(part * geo.groups + b, w),
            device_id_type=MESH,
        )

    def attend(i, carry):
        for n in range(early_ticks, loop_ticks):

            @pl.when(i == 2 * (n - early_ticks) + 1)
            def _():
                tick(n)

        b = (g + 1 + i) % geo.groups
        inner = pl.ds(pl.multiple_of(b * rows, rows), rows)
        query = q_ref[inner, :] * jnp.asarray(scale, BF16)
        q_pos = (part * geo.groups + b) * rows + lax.broadcasted_iota(jnp.int32, (rows, 1), 0)
        q_seg = segment_from(q_pos, starts)
        results = []
        for h in range(PAIR):
            mask = first_head if h == 0 else jnp.logical_not(first_head)
            q_head = jnp.where(mask, query, jnp.zeros_like(query))

            def one(c, state):
                top, total, acc = state
                keys_at = pl.ds(pl.multiple_of(c * chunk, chunk), chunk)
                score = dot_nt(q_head, k_ref[keys_at, :])
                score = jnp.where(q_seg == seg_buf[:, keys_at], score, -1e30)
                peak = jnp.max(score, axis=1, keepdims=True)
                if top is not None:
                    peak = jnp.maximum(top, peak)
                weight = jnp.exp(score - peak)
                add = jnp.sum(weight, axis=1, keepdims=True)
                out = dot_nn(weight.astype(BF16), v_ref[keys_at, :])
                if top is not None:
                    fade = jnp.exp(top - peak)
                    add = add + total * fade
                    out = out + acc * fade
                return peak, add, out

            state = one(0, (None, None, None))
            if chunks > 1:
                state = lax.fori_loop(1, chunks, one, state)
            top, total, acc = state
            results.append((acc / total, top + jnp.log(total)))
        out = jnp.where(first_head, results[0][0], results[1][0])
        o_ref[inner, :] = out
        lse_ref[inner, :] = jnp.where(first_head, results[0][1], results[1][1])
        att_buf[b] = out.astype(BF16)

        @pl.when(b != g)
        def _():
            att_copy(b).start()

        return carry

    lax.fori_loop(0, geo.groups, attend, 0)
    for copy in flushes:
        copy.start()
    own_att = pltpu.make_async_copy(att_buf.at[g], att_ref.at[:, lanes], local_sem.at[0])
    own_att.start()

    def att_arrivals():
        for d in range(1, geo.groups):
            other = (g + d) % geo.groups
            cut = pl.ds(pl.multiple_of(other * LANES, LANES), LANES)
            pltpu.make_async_remote_copy(
                src_ref=att_ref.at[:, cut],
                dst_ref=att_ref.at[:, cut],
                send_sem=att_send.at[other],
                recv_sem=att_recv.at[other],
                device_id=(part * geo.groups + other, w),
                device_id_type=MESH,
            ).wait_recv()
        own_att.wait()

    if inside:
        for copy in loads:
            copy.wait()
        for name in LATER:
            setattr(r, name, getattr(r, name + "_buf"))
        layer_rest(geo, rank, r, starts, ends, id_ref, down_ref, up_ref, att_arrivals, complete, tick, loop_ticks, tick_count, len_ref.shape[1])
    else:
        att_arrivals()

    for copy in flushes:
        copy.wait()
    for d in range(1, geo.groups):
        att_copy((g + d) % geo.groups).wait_send()
    tok.wait_sends()
    for j in range(3):

        @pl.when(w < wt - 1)
        def _():
            slice_copy(j, w, True).wait_send()

        @pl.when(w > 0)
        def _():
            slice_copy(j, w, False).wait_send()

        for n in range(wt - 1):
            p = nth_plane(n)

            @pl.when((p < w) & (w < wt - 1))
            def _():
                slice_copy(j, p, True).wait_send()

            @pl.when((p > w) & (w > 0))
            def _():
                slice_copy(j, p, False).wait_send()

    for m in range(weight_count):
        @pl.when(w < wt - 1)
        def _():
            line_copy(m, w, True, True).wait_send()

        @pl.when(w > 0)
        def _():
            line_copy(m, w, False, True).wait_send()

    for m, j in units:
        p = nth_plane(j)

        @pl.when((p < w) & (w < wt - 1))
        def _():
            line_copy(m, p, True, False).wait_send()

        @pl.when((p > w) & (w > 0))
        def _():
            line_copy(m, p, False, False).wait_send()

        weight_spread(m, p).wait_sends()


def layer_rest(
    geo, rank, r, starts, ends, id_ref, down_ref, up_ref, att_arrivals, complete, tick, ticked, tick_count, docs
):
    s, w = lax.axis_index("seq"), lax.axis_index("wt")
    rows, width, groups = geo.rows, geo.width, geo.groups
    part, g = s // groups, s % groups
    hidden = r.full_fc1.shape[1]
    step = min(512, hidden)
    steps = hidden // step
    band = 2 * LANES
    bands = width // band
    lane_count = r.fc1_down.shape[0]
    out_rows = slice(3 * lane_count, 4 * lane_count)
    pos = s * rows + lax.broadcasted_iota(jnp.int32, (rows, LANES), 0)
    chosen = select_from(pos, starts, ends, id_ref, rank)

    every = placement(id_ref, docs, rank, lane_count)[0]
    doc_rows = docs * rank
    in_doc = (lax.broadcasted_iota(jnp.int32, (rows, LANES), 1) // rank) == segment_from(pos, starts)

    def masked(value):
        return (value * chosen).astype(BF16)

    def by_doc(low):
        return jnp.where(in_doc, dot_nn(low, every), 0.0).astype(BF16)

    def doc_grad(low_by_doc, value):
        return dot_tn(low_by_doc, value)[:doc_rows].astype(BF16)

    def at_step(i):
        return pl.ds(pl.multiple_of(i * step, step), step)

    def at_band(i):
        return pl.ds(pl.multiple_of(i * band, band), band)

    pending = list(range(ticked, tick_count))
    first_ticks, pending = pending[:1], pending[1:]
    for n in first_ticks:
        tick(n)
    att_arrivals()
    complete(0)
    att = r.att[...]
    small_out = masked(dot_nt(att, down_ref[out_rows, :]))

    def out_band(i, carry):
        cut = at_band(i)
        value = dot_nn(r.att[...], r.full_out[:, cut]) + r.out_bias[:, cut]
        value = value + dot_nn(small_out, up_ref[out_rows, cut])
        r.y[:, cut] = value + r.tok[s, :, cut].astype(F32)
        return carry

    lax.fori_loop(0, bands, out_band, 0)
    unit1, spread1 = normed(r.y[...])
    h1 = unit1 * r.gain1[...] + r.shift1[...]
    r.unit1[...] = unit1
    r.h1[...] = h1
    h1_low = h1.astype(BF16)
    r.h1_low[...] = h1_low
    small_fc1 = masked(dot_nt(h1_low, r.fc1_down[...]))

    middle = max(len(pending) - 3, 0)
    for n in pending[:middle]:
        tick(n)
    pending = pending[middle:]
    complete(1)

    def fc1_step(i, acc):
        for n, t in enumerate(pending):
            @pl.when(i == min(2 * n + 1, steps - 1))
            def _():
                tick(t)

        cut = at_step(i)
        pre = dot_nn(r.h1_low[...], r.full_fc1[:, cut]) + r.fc1_bias[:, cut]
        pre = pre + dot_nn(small_fc1, r.fc1_up[:, cut])
        share = 0.5 + 0.5 * erf(pre * 0.7071067811865476)
        act = (pre * share).astype(BF16)
        r.act[:, cut] = act
        r.slope[:, cut] = share + pre * (jnp.exp(-0.5 * pre * pre) * 0.3989422804014327)
        return acc + dot_nt(act, r.fc2_down[:, cut])

    small_fc2 = masked(lax.fori_loop(0, steps, fc1_step, jnp.zeros((rows, lane_count), F32)))
    complete(2)

    def fc2_band(i, carry):
        cut = at_band(i)
        value = dot_nn(r.act[...], r.full_fc2[:, cut]) + r.fc2_bias[:, cut]
        r.y[:, cut] = value + dot_nn(small_fc2, r.fc2_up[:, cut]) + r.h1[:, cut]
        return carry

    lax.fori_loop(0, bands, fc2_band, 0)
    unit2, spread2 = normed(r.y[...])
    r.output[...] = unit2 * r.gain2[...] + r.shift2[...]
    d_second = normed_back(r.cotangent[...].astype(F32), r.gain2[...], unit2, spread2)
    r.y[...] = d_second
    d_y = d_second.astype(BF16)
    low_fc2 = masked(dot_nt(d_y, r.fc2_up[...]))
    r.g_fc2_up[...] = doc_grad(by_doc(small_fc2), d_y)
    low_fc2_doc, small_fc1_doc = by_doc(low_fc2), by_doc(small_fc1)

    def back_step(i, acc):
        cut = at_step(i)
        d_act = dot_nt(d_y, r.full_fc2[cut, :]) + dot_nn(low_fc2, r.fc2_down[:, cut])
        d_pre = (d_act * r.slope[:, cut]).astype(BF16)
        r.d_pre[:, cut] = d_pre
        r.g_fc2_down[:, cut] = doc_grad(low_fc2_doc, r.act[:, cut])
        r.g_fc1_up[:, cut] = doc_grad(small_fc1_doc, d_pre)
        return acc + dot_nt(d_pre, r.fc1_up[:, cut])

    low_fc1 = masked(lax.fori_loop(0, steps, back_step, jnp.zeros((rows, lane_count), F32)))

    def make_early(chip, whose):
        return owner_columns((r.g_fc2_up, r.g_fc1_up, r.g_fc2_down), chip * 2 + whose, groups)

    early = PairSum(
        groups // 2,
        g // 2,
        s % 2,
        part * groups,
        w,
        (r.set_out, r.set_in, r.set_far),
        [r.set_sems.at[i] for i in range(4)],
        make_early,
    )
    early.run()
    r.g_fc1_down[...] = doc_grad(by_doc(low_fc1), r.h1_low[...])

    def back_band(i, carry):
        cut = at_band(i)
        value = dot_nt(r.d_pre[...], r.full_fc1[cut, :]) + dot_nn(low_fc1, r.fc1_down[:, cut])
        r.y[:, cut] += value
        return carry

    lax.fori_loop(0, bands, back_band, 0)
    d_first = normed_back(r.y[...], r.gain1[...], r.unit1[...], spread1)
    r.d_first[...] = d_first
    d_z = d_first.astype(BF16)
    low_out = masked(dot_nt(d_z, up_ref[out_rows, :]))

    def back_copy(b):
        return pltpu.make_async_remote_copy(
            src_ref=r.d_att_buf.at[b],
            dst_ref=r.d_heads.at[pl.ds(pl.multiple_of(g * rows, rows), rows)],
            send_sem=r.back_send.at[b],
            recv_sem=r.back_recv.at[g],
            device_id=(part * groups + b, w),
            device_id_type=MESH,
        )

    def attended_band(i, carry):
        n = (g // 2 + 1 + i) % bands
        cut = at_band(n)
        value = dot_nt(d_z, r.full_out[cut, :]) + dot_nn(low_out, down_ref[out_rows, cut])
        value = value.astype(BF16)
        for h in range(2):
            b = 2 * n + h
            r.d_att_buf[b] = value[:, h * LANES : (h + 1) * LANES]

            @pl.when(b != g)
            def _():
                back_copy(b).start()

        return carry

    lax.fori_loop(0, bands, attended_band, 0)
    own = pltpu.make_async_copy(
        r.d_att_buf.at[g], r.d_heads.at[pl.ds(pl.multiple_of(g * rows, rows), rows)], r.local_sem.at[0]
    )
    own.start()
    r.g_out_down[...] = doc_grad(by_doc(low_out), r.att[...])
    r.g_out_up[...] = doc_grad(by_doc(small_out), d_z)
    r.early_sum[...] = early.finish().astype(BF16)
    early.drain()
    for d in range(1, groups):
        other = (g + d) % groups
        here = r.d_heads.at[pl.ds(pl.multiple_of(other * rows, rows), rows)]
        pltpu.make_async_remote_copy(
            src_ref=here,
            dst_ref=here,
            send_sem=r.back_send.at[other],
            recv_sem=r.back_recv.at[other],
            device_id=(part * groups + other, w),
            device_id_type=MESH,
        ).wait_recv()
        back_copy(other).wait_send()
    own.wait()


def forward_attention(geo, rank, lengths, ids, tokens, w_qkv, down, up, bias, mlp):
    rows, width = geo.rows, geo.width
    inside = mlp is not None
    mlp = mlp or ()
    any_spec = pl.BlockSpec(memory_space=pl.ANY)
    vmem = pl.BlockSpec(memory_space=pltpu.VMEM)
    smem = pl.BlockSpec(memory_space=pltpu.SMEM)
    lane_count = down.shape[0] // 4
    struct = jax.ShapeDtypeStruct
    shapes = [
        struct((geo.queries, LANES), BF16),
        struct((geo.keys, LANES), BF16),
        struct((geo.keys, LANES), BF16),
        struct((geo.queries, LANES), F32),
        struct((geo.queries, LANES), F32),
        struct((width, 3 * LANES), BF16),
        struct((geo.keys, 3 * LANES), BF16),
    ]
    specs = [any_spec] * 7
    dma = pltpu.SemaphoreType.DMA
    count = 3 if inside else 0
    units = 1 + count * geo.wt
    scratch = [
        pltpu.VMEM((geo.seq, rows, width), BF16),
        pltpu.VMEM((1, geo.keys), jnp.int32),
        pltpu.VMEM((geo.groups, rows, LANES), BF16),
        dma((4 + count,)),
        dma((Spread.KINDS, units)),
        dma((Spread.KINDS, units)),
        dma((2, 3, geo.wt)),
        dma((3, geo.wt)),
        dma((2, max(count, 1) * geo.wt)),
        dma((max(count, 1) * geo.wt,)),
        dma((geo.groups,)),
        dma((geo.groups,)),
    ]
    scratch += [pltpu.VMEM(v.shape, v.dtype) for v in shapes] + [dma((len(shapes),))]
    if inside:
        hidden = mlp[1].shape[1]
        doc_rows = lengths.shape[1] * rank
        early = (width + 2 * hidden) // geo.groups
        near = geo.groups // 2
        shapes += [
            struct((rows, width), F32),
            struct((rows, width), F32),
            struct((geo.queries, LANES), BF16),
            struct((doc_rows, width), BF16),
            struct((doc_rows, width), BF16),
            struct((doc_rows, width), BF16),
            struct((doc_rows, early), BF16),
        ]
        specs += [vmem, vmem, any_spec] + [vmem] * 4
        scratch += [
            pltpu.VMEM((rows, width), BF16),
            pltpu.VMEM((width, width), BF16),
            pltpu.VMEM((width, hidden), BF16),
            pltpu.VMEM((hidden, width), BF16),
            pltpu.VMEM((rows, width), F32),
            pltpu.VMEM((rows, width), F32),
            pltpu.VMEM((rows, width), BF16),
            pltpu.VMEM((rows, hidden), BF16),
            pltpu.VMEM((rows, hidden), F32),
            pltpu.VMEM((rows, hidden), BF16),
            pltpu.VMEM((rows, width), F32),
            pltpu.VMEM((geo.groups, rows, LANES), BF16),
            dma((geo.groups,)),
            dma((geo.groups,)),
            pltpu.VMEM((doc_rows, width), BF16),
            pltpu.VMEM((doc_rows, hidden), BF16),
            pltpu.VMEM((doc_rows, hidden), BF16),
            pltpu.VMEM((near, doc_rows, early), BF16),
            pltpu.VMEM((near, doc_rows, early), BF16),
            pltpu.VMEM((near, doc_rows, early), BF16),
            dma((4, near)),
            dma((len(LATER),)),
        ]
        scratch += [pltpu.VMEM(v.shape, v.dtype) for name, v in zip(MLP_INPUTS, mlp) if name in LATER]
    else:
        shapes += [struct((rows, width), BF16)]
        specs += [any_spec]
    return pl.pallas_call(
        functools.partial(forward_kernel, geo, inside, rank),
        out_shape=shapes,
        in_specs=[smem, smem, any_spec, any_spec, vmem, vmem, vmem] + [
            any_spec if i < count or name in LATER else vmem for i, name in enumerate(MLP_INPUTS[: len(mlp)])
        ],
        out_specs=specs,
        scratch_shapes=scratch,
        compiler_params=pltpu.CompilerParams(
            collective_id=0, has_side_effects=True, vmem_limit_bytes=VMEM_LIMIT
        ),
        name="layer",
    )(lengths, ids, tokens, w_qkv, down, up, bias, *mlp)


def backward_kernel(
    geo, len_ref, part_ref, q_ref, k_ref, v_ref, o_ref, lse_ref, g_ref, pass_ref, dq_ref, dk_ref, dv_ref, passed_ref,
    dk_acc, dv_acc, pass_buf, pass_sem,
):
    rows = min(512, geo.queries)
    block = min(512, geo.keys)
    part = part_ref[0, 0]
    scale = HEAD_DIM ** (-0.5)
    starts, ends = doc_bounds(len_ref)
    first_head = lax.broadcasted_iota(jnp.int32, (rows, LANES), 1) < HEAD_DIM
    fetch = pltpu.make_async_copy(pass_ref, pass_buf, pass_sem.at[0])
    store = pltpu.make_async_copy(pass_buf, passed_ref, pass_sem.at[1])
    fetch.start()
    dk_acc[...] = jnp.zeros_like(dk_acc)
    dv_acc[...] = jnp.zeros_like(dv_acc)

    def seg_of(position):
        seg = jnp.int32(0)
        for start in starts[1:]:
            seg = seg + (position >= start).astype(jnp.int32)
        return seg

    def pick(values, index):
        found = values[0]
        for i in range(1, len(values)):
            found = jnp.where(index == i, values[i], found)
        return found

    def both_heads(value):
        zero = jnp.zeros_like(value)
        return jnp.concatenate([jnp.where(first_head, value, zero), jnp.where(first_head, zero, value)], axis=0)

    def query_block(b, carry):
        at = pl.ds(pl.multiple_of(b * rows, rows), rows)
        origin = part * geo.queries + b * rows
        query = both_heads(q_ref[at, :] * jnp.asarray(scale, BF16))
        cot = both_heads(g_ref[at, :])
        scaled = cot * jnp.asarray(scale, BF16)
        lse = jnp.concatenate([lse_ref[at, h * HEAD_DIM : h * HEAD_DIM + 1] for h in range(PAIR)], axis=0)
        out = o_ref[at, :]
        dot = jnp.sum(scaled.astype(F32) * jnp.concatenate([out, out], axis=0), axis=1, keepdims=True)
        q_pos = origin + lax.broadcasted_iota(jnp.int32, (rows, 1), 0)
        q_seg = segment_from(q_pos, starts)
        q_seg = jnp.concatenate([q_seg, q_seg], axis=0)
        low = pick(starts, seg_of(origin)) // block
        high = (pick(ends, seg_of(origin + rows - 1)) + block - 1) // block

        def key_block(c, acc):
            keys_at = pl.ds(pl.multiple_of(c * block, block), block)
            key, value = k_ref[keys_at, :], v_ref[keys_at, :]
            k_pos = c * block + lax.broadcasted_iota(jnp.int32, (1, block), 1)
            score = jnp.where(q_seg == segment_from(k_pos, starts), dot_nt(query, key), -1e30)
            prob = jnp.exp(score - lse)
            raw = (prob * (dot_nt(scaled, value) - dot)).astype(BF16)
            dk_acc[keys_at, :] += dot_tn(raw, query)
            dv_acc[keys_at, :] += dot_tn(prob.astype(BF16), cot)
            return acc + dot_nn(raw, key)

        acc = lax.fori_loop(low, high, key_block, jnp.zeros((PAIR * rows, LANES), F32))
        dq_ref[at, :] = jnp.where(first_head, acc[:rows], acc[rows:]).astype(BF16)
        return carry

    query_block(0, 0)
    fetch.wait()
    store.start()
    lax.fori_loop(1, geo.queries // rows, query_block, 0)
    dk_ref[...] = (dk_acc[...] * HEAD_DIM**0.5).astype(BF16)
    dv_ref[...] = dv_acc[...].astype(BF16)
    store.wait()


def backward_attention(geo, lengths, part, q, k, v, o, lse, d_heads, output):
    any_spec = pl.BlockSpec(memory_space=pl.ANY)
    smem = pl.BlockSpec(memory_space=pltpu.SMEM)
    vmem = pl.BlockSpec(memory_space=pltpu.VMEM)
    return pl.pallas_call(
        functools.partial(backward_kernel, geo),
        out_shape=[
            jax.ShapeDtypeStruct((geo.queries, LANES), BF16),
            jax.ShapeDtypeStruct((geo.keys, LANES), BF16),
            jax.ShapeDtypeStruct((geo.keys, LANES), BF16),
            jax.ShapeDtypeStruct(output.shape, F32),
        ],
        in_specs=[smem, smem] + [vmem] * 6 + [any_spec],
        out_specs=[vmem] * 3 + [any_spec],
        scratch_shapes=[pltpu.VMEM((geo.keys, LANES), F32)] * 2
        + [pltpu.VMEM(output.shape, F32), pltpu.SemaphoreType.DMA((2,))],
        compiler_params=pltpu.CompilerParams(vmem_limit_bytes=VMEM_LIMIT),
        name="attend_back",
    )(lengths, part, q, k, v, o, lse, d_heads, output)


class Block:
    def __init__(self, geo):
        chips = geo.groups // 2
        self.nx = min(geo.nx, chips)
        self.ny = chips // self.nx


class PairSum:
    def __init__(self, count, me, core, first, w, bufs, sems, make, stage=None):
        self.count, self.me, self.core, self.first, self.w = count, me, core, first, w
        self.near_out, self.near_in, self.far_in = bufs
        self.near_send, self.near_recv, self.far_send, self.far_recv = sems
        self.make = make
        self.slots = self.near_out.shape[0]
        self.stage = stage

    def slot(self, chip):
        return ((chip + self.count - self.me + self.count - 1) % self.count) % self.slots

    def near(self, chip):
        return pltpu.make_async_remote_copy(
            src_ref=self.near_out.at[self.slot(chip)],
            dst_ref=self.near_in.at[chip],
            send_sem=self.near_send.at[chip],
            recv_sem=self.near_recv.at[chip],
            device_id=(self.first + self.me * 2 + 1 - self.core, self.w),
            device_id_type=MESH,
        )

    def far(self, chip):
        return pltpu.make_async_remote_copy(
            src_ref=self.near_in.at[chip],
            dst_ref=self.far_in.at[self.me],
            send_sem=self.far_send.at[chip],
            recv_sem=self.far_recv.at[self.me],
            device_id=(self.first + chip * 2 + self.core, self.w),
            device_id_type=MESH,
        )

    def far_arrival(self, chip):
        return pltpu.make_async_remote_copy(
            src_ref=self.far_in.at[chip],
            dst_ref=self.far_in.at[chip],
            send_sem=self.far_send.at[chip],
            recv_sem=self.far_recv.at[chip],
            device_id=(self.first + chip * 2 + self.core, self.w),
            device_id_type=MESH,
        )

    def run(self):
        def start(d):
            chip = (self.me + 1 + d) % self.count
            if self.slots < self.count:

                @pl.when(d >= self.slots)
                def _():
                    self.near((self.me + 1 + d - self.slots) % self.count).wait_send()

            self.near_out[d % self.slots] = self.make(chip, 1 - self.core).astype(BF16)
            self.near(chip).start()

        def send(d):
            chip = (self.me + 1 + d) % self.count
            own = self.make(chip, self.core)
            self.near(chip).wait_recv()
            self.near_in[chip] = (own + self.near_in[chip].astype(F32)).astype(BF16)
            self.far(chip).start()

        def step(d, carry):
            start(d)
            send(d - 1)
            return carry

        start(0)
        lax.fori_loop(1, self.count, step, 0)

    def finish(self):
        total = self.make(self.me, self.core)
        self.near(self.me).wait_recv()
        total = total + self.near_in[self.me].astype(F32)
        if self.stage is None:
            for d in range(1, self.count):
                chip = (self.me + d) % self.count
                self.far_arrival(chip).wait_recv()
                total = total + self.far_in[chip].astype(F32)
            return total
        stage, sem = self.stage

        def fetch(d):
            chip = (self.me + d) % self.count
            return pltpu.make_async_copy(self.far_in.at[chip], stage.at[d % 2], sem.at[d % 2])

        self.far_arrival((self.me + 1) % self.count).wait_recv()
        fetch(1).start()
        for d in range(1, self.count):
            if d + 1 < self.count:
                self.far_arrival((self.me + d + 1) % self.count).wait_recv()
                fetch(d + 1).start()
            fetch(d).wait()
            total = total + stage[d % 2].astype(F32)
        return total

    def drain(self):
        for d in range(self.count):
            chip = (self.me + 1 + d) % self.count
            if d >= self.count - self.slots:
                self.near(chip).wait_send()
            if d < self.count - 1:
                self.far(chip).wait_send()


class CrossSum(PairSum):
    def with_corner(self, via, via_send, via_recv):
        self.via, self.via_send, self.via_recv = via, via_send, via_recv
        x, y = self.me % 2, self.me // 2
        self.near_chips = [y * 2 + 1 - x, (1 - y) * 2 + x]
        self.corner = (1 - y) * 2 + 1 - x
        self.half = self.near_in.shape[1] // 2
        return self

    def part(self, ref, h):
        return ref.at[pl.ds(h * self.half, self.half)]

    def device(self, chip):
        return (self.first + chip * 2 + self.core, self.w)

    def corner_copy(self, h):
        return pltpu.make_async_remote_copy(
            src_ref=self.part(self.near_in.at[self.corner], h),
            dst_ref=self.via.at[h],
            send_sem=self.via_send.at[h],
            recv_sem=self.via_recv.at[h],
            device_id=self.device(self.near_chips[h]),
            device_id_type=MESH,
        )

    def near_copy(self, which, h):
        chip = self.near_chips[which]
        return pltpu.make_async_remote_copy(
            src_ref=self.part(self.near_in.at[chip], h),
            dst_ref=self.part(self.far_in.at[self.me], h),
            send_sem=self.far_send.at[which * 2 + h],
            recv_sem=self.far_recv.at[which * 2 + h],
            device_id=self.device(chip),
            device_id_type=MESH,
        )

    def near_arrival(self, which, h):
        here = self.part(self.far_in.at[self.near_chips[which]], h)
        return pltpu.make_async_remote_copy(
            src_ref=here,
            dst_ref=here,
            send_sem=self.far_send.at[which * 2 + h],
            recv_sem=self.far_recv.at[which * 2 + h],
            device_id=self.device(self.near_chips[which]),
            device_id_type=MESH,
        )

    def run(self):
        order = [self.corner] + self.near_chips + [self.me]

        def chip_at(d):
            chip = order[0]
            for i in range(1, len(order)):
                chip = jnp.where(d == i, order[i], chip)
            return chip

        def start(d):
            chip = chip_at(d)
            self.near_out[chip] = self.make(chip, 1 - self.core).astype(BF16)
            self.near(chip).start()

        start(0)

        def step(d, carry):
            start(d)
            chip = chip_at(d - 1)
            own = self.make(chip, self.core)
            self.near(chip).wait_recv()
            self.near_in[chip] = (own + self.near_in[chip].astype(F32)).astype(BF16)

            @pl.when(d == 1)
            def _():
                self.corner_copy(0).start()
                self.corner_copy(1).start()

            @pl.when(d == 2)
            def _():
                self.near_copy(0, 0).start()

            @pl.when(d == 3)
            def _():
                self.near_copy(1, 1).start()

            return carry

        lax.fori_loop(1, len(order), step, 0)
        for which in range(2):
            h = 1 - which
            self.corner_copy(h).wait_recv()
            chip = self.near_chips[which]
            rows = pl.ds(h * self.half, self.half)
            self.near_in[chip, rows, :] = (
                self.near_in[chip, rows, :].astype(F32) + self.via[h].astype(F32)
            ).astype(BF16)
            self.near_copy(which, h).start()

    def slot(self, chip):
        return chip

    def finish(self):
        stage, sem = self.stage
        total = self.make(self.me, self.core)
        self.near(self.me).wait_recv()
        total = total + self.near_in[self.me].astype(F32)
        fetches = []
        for which in range(2):
            for h in range(2):
                self.near_arrival(which, h).wait_recv()
            fetches.append(
                pltpu.make_async_copy(self.far_in.at[self.near_chips[which]], stage.at[which], sem.at[which])
            )
            fetches[-1].start()
        for which in range(2):
            fetches[which].wait()
            total = total + stage[which].astype(F32)
        return total

    def drain(self):
        for chip in [self.corner] + self.near_chips + [self.me]:
            self.near(chip).wait_send()
        for h in range(2):
            self.corner_copy(h).wait_send()
            for which in range(2):
                self.near_copy(which, h).wait_send()


def closing_kernel(
    geo,
    rank,
    single_count,
    early,
    len_ref,
    id_ref,
    tokens_ref,
    first_ref,
    dq_ref,
    dk_ref,
    dv_ref,
    slice_ref,
    down_ref,
    up_ref,
    small_ref,
    *refs,
):
    singles = refs[:single_count]
    early_ref = refs[single_count] if early else None
    (
        grad_ref,
        sum1_ref,
        sum2_ref,
        tok_far,
        tok_out,
        tok_in,
        tok_stage,
        small_buf,
        set1_out,
        set1_in,
        set1_far,
        set2_out,
        set2_in,
        set2_far,
        down_acc,
        up_acc,
        mine1,
        mine2,
        place_buf,
        fold_buf,
        all1,
        all2,
        places,
        done1,
        done2,
        tok_sems,
        set1_sems,
        set2_sems,
        line_send,
        line_recv,
        spread_send,
        spread_recv,
        local_sem,
        stage_sem,
        small_sem,
        tok_via,
        via_sems,
    ) = refs[single_count + early :]
    x, y, core, w = device_here(geo)
    s = lax.axis_index("seq")
    rows, width, wt, groups, parts = geo.rows, geo.width, geo.wt, geo.groups, geo.parts
    part, g = s // groups, s % groups
    docs = len_ref.shape[1]
    doc_rows = docs * rank
    lane_count = down_ref.shape[0] // 4
    lanes = pl.ds(pl.multiple_of(g * LANES, LANES), LANES)
    starts, ends = doc_bounds(len_ref)
    greet_all(geo)

    def iota(shape, dim):
        return lax.broadcasted_iota(jnp.int32, shape, dim)

    def zero_one(condition):
        return jnp.where(condition, 1.0, 0.0).astype(BF16)

    def chosen_of(t):
        pos = t * rows + iota((rows, LANES), 0)
        return select_from(pos, starts, ends, id_ref, rank)

    def fold(j):
        a, b = iota((lane_count, LANES), 0), iota((lane_count, LANES), 1)
        return zero_one((b >= j * rank) & (b < (j + 1) * rank) & (a % rank == b - j * rank))

    def make_tokens(chip, whose):
        t = chip * 2 + whose
        at = pl.ds(pl.multiple_of(t * rows, rows), rows)
        if parts == 1:
            d_q = dq_ref[at, :]
        else:
            inner = pl.ds(pl.multiple_of((t % groups) * rows, rows), rows)
            d_q = jnp.where(t // groups == part, dq_ref[inner, :], jnp.zeros((rows, LANES), BF16))
        pieces = [d_q, dk_ref[at, :], dv_ref[at, :]]
        chosen = chosen_of(t)
        total = jnp.zeros((rows, width), F32)
        low = jnp.zeros((rows, LANES), F32)
        for j in range(3):
            total = total + dot_nt(pieces[j], slice_ref[:, j * LANES : (j + 1) * LANES])
            part_low = dot_nt(pieces[j], up_ref[pl.ds(j * lane_count, lane_count), lanes])
            low = low + dot_nn((part_low * chosen).astype(BF16), fold(j))
        return jnp.concatenate([total, low], axis=1)

    square = geo.nx == 2 and geo.ny == 2
    tok = (CrossSum if square else PairSum)(
        geo.seq // 2, s // 2, core, 0, w, (tok_out, tok_in, tok_far), [tok_sems.at[i] for i in range(4)], make_tokens,
        (tok_stage, stage_sem),
    )
    if square:
        tok.with_corner(tok_via, via_sems.at[0], via_sems.at[1])

    def by_document(value):
        return dot_tn(fold_buf[...], value)[:doc_rows]

    def make_set1(chip, whose):
        return owner_columns(singles, chip * 2 + whose, groups)

    def make_set2(chip, whose):
        owner = chip * 2 + whose
        cut = pl.ds(pl.multiple_of(owner * LANES, LANES), LANES)
        return jnp.concatenate([down_acc[j * doc_rows : (j + 1) * doc_rows, cut] for j in range(3)], axis=1)

    chips = groups // 2
    set1 = PairSum(
        chips, g // 2, core, part * groups, w, (set1_out, set1_in, set1_far), [set1_sems.at[i] for i in range(4)], make_set1
    )
    set2 = PairSum(
        chips, g // 2, core, part * groups, w, (set2_out, set2_in, set2_far), [set2_sems.at[i] for i in range(4)], make_set2
    )

    def peer(n):
        plane = (w + n) % wt
        other = (part + n // wt) % parts
        return other * groups + g, plane, other * wt + plane

    mine_at = part * wt + w

    late = set1_out.shape[2]
    front = late + 3 * LANES
    whole = mine1.shape[1]

    def cut_of(kind, ref):
        if kind == 0:
            return ref.at[:, pl.ds(0, front)]
        if kind == 3:
            return ref.at[:, pl.ds(front, whole - front)]
        return ref

    def line_copy(kind, n, src, dst_all):
        device, plane, _ = peer(n)
        return pltpu.make_async_remote_copy(
            src_ref=cut_of(kind, src),
            dst_ref=cut_of(kind, dst_all.at[mine_at]),
            send_sem=line_send.at[kind, n],
            recv_sem=line_recv.at[kind, mine_at],
            device_id=(device, plane),
            device_id_type=MESH,
        )

    def line_arrival(kind, n, dst_all):
        device, plane, at = peer(n)
        return pltpu.make_async_remote_copy(
            src_ref=cut_of(kind, dst_all.at[at]),
            dst_ref=cut_of(kind, dst_all.at[at]),
            send_sem=line_send.at[kind, n],
            recv_sem=line_recv.at[kind, at],
            device_id=(device, plane),
            device_id_type=MESH,
        )

    peers = range(1, wt * parts)

    block = Block(geo)
    chip_here = g // 2
    here = (chip_here % block.nx, chip_here // block.nx, core, w)

    def region_of(ref):
        def region(ux, uy, whose, half):
            one = ref.at[(uy * block.nx + ux) * 2 + whose]
            if half is None:
                return one
            return one.at[pl.ds(half * (lane_count // 2), lane_count // 2)]

        return region

    spreads = [
        Spread(block, here, region_of(ref), spread_send, spread_recv, i, part * groups)
        for i, ref in enumerate((sum1_ref, sum2_ref))
    ]
    finals = [done1, done2]
    outs = [sum1_ref, sum2_ref]

    def place(kind, mine, dst_all):
        total = dot_nn(place_buf[:, :doc_rows], mine[...])
        for n in peers:
            line_arrival(kind, n, dst_all).wait_recv()
            if kind == 0:
                line_arrival(2, n, places).wait_recv()
                if early:
                    line_arrival(3, n, dst_all).wait_recv()
            at = peer(n)[2]
            total = total + dot_nn(places[at][:, :doc_rows], dst_all[at])
        finals[kind][...] = total.astype(BF16)
        for way in (0, 1, 4):
            spreads[kind].go(way, own=finals[kind])
        pltpu.make_async_copy(finals[kind], outs[kind].at[g], local_sem.at[kind]).start()

    def pass_on(kind):
        spread = spreads[kind]
        spread.wait(0)
        spread.go(2)
        spread.go(5)
        spread.wait(1)
        spread.go(3)
        spread.go(6)

    def pass_last(kind):
        spread = spreads[kind]
        spread.wait(2)
        spread.go(7)
        spread.wait(3)
        spread.go(8)

    place_buf[...], fold_buf[...] = placement(id_ref, docs, rank, lane_count)
    for n in peers:
        line_copy(2, n, place_buf, places).start()
    if early:
        mine1[:, front:] = early_ref[...]
        for n in peers:
            line_copy(3, n, mine1, all1).start()

    set1.run()
    tok.run()

    def small_copy(t):
        return pltpu.make_async_copy(
            small_ref.at[pl.ds(pl.multiple_of(t * rows, rows), rows)], small_buf.at[t % 2], small_sem.at[t % 2]
        )

    def add_up(t, carry):
        at = pl.ds(pl.multiple_of(t * rows, rows), rows)

        @pl.when(t + 1 < geo.seq)
        def _():
            small_copy(t + 1).start()

        small_copy(t).wait()
        for j in range(3):
            cut = slice(j * LANES, (j + 1) * LANES)
            if j == 0:
                if parts == 1:
                    value = dq_ref[at, :]
                else:
                    inner = pl.ds(pl.multiple_of((t % groups) * rows, rows), rows)
                    value = jnp.where(t // groups == part, dq_ref[inner, :], jnp.zeros((rows, LANES), BF16))
            else:
                value = (dk_ref if j == 1 else dv_ref)[at, :]
            up_acc[cut, :] += dot_tn(small_buf[t % 2][:, cut], value)
        return carry

    up_acc[...] = jnp.zeros_like(up_acc)
    small_copy(0).start()
    lax.fori_loop(0, geo.seq, add_up, 0)

    for j in range(3):
        mine1[:, late + j * LANES : late + (j + 1) * LANES] = by_document(
            up_acc[j * lane_count : (j + 1) * lane_count, :].astype(BF16)
        ).astype(BF16)
    mine1[:, :late] = set1.finish().astype(BF16)
    for n in peers:
        line_copy(0, n, mine1, all1).start()

    total = tok.finish()
    low = total[:, width:].astype(BF16)
    total = total[:, :width] + first_ref[...]
    chosen = chosen_of(s)
    pos = s * rows + iota((rows, doc_rows), 0)
    doc_of = iota((rows, doc_rows), 1) // rank
    in_doc = doc_of == segment_from(pos, starts)
    tokens = tokens_ref[...]
    for j in range(3):
        a, b = iota((LANES, lane_count), 0), iota((LANES, lane_count), 1)
        widen = zero_one((a >= j * rank) & (a < (j + 1) * rank) & (b % rank == a - j * rank))
        wide = (dot_nn(low, widen) * chosen).astype(BF16)
        total = total + dot_nn(wide, down_ref[j * lane_count : (j + 1) * lane_count, :])
        by_doc = dot_nn(low, widen[:, :doc_rows])
        by_doc = jnp.where(in_doc, by_doc, 0.0).astype(BF16)
        down_acc[j * doc_rows : (j + 1) * doc_rows, :] = dot_tn(by_doc, tokens)
    set2.run()
    grad_ref[...] = total
    place(0, mine1, all1)
    mine2[...] = set2.finish().astype(BF16)
    for n in peers:
        line_copy(1, n, mine2, all2).start()
    pass_on(0)
    place(1, mine2, all2)
    pass_last(0)
    pass_on(1)
    pass_last(1)
    for kind in range(2):
        for way in range(4, 9):
            spreads[kind].wait(way)
        spreads[kind].wait_sends()
        pltpu.make_async_copy(finals[kind], outs[kind].at[g], local_sem.at[kind]).wait()
    for n in peers:
        line_copy(0, n, mine1, all1).wait_send()
        line_copy(1, n, mine2, all2).wait_send()
        line_copy(2, n, place_buf, places).wait_send()
        if early:
            line_copy(3, n, mine1, all1).wait_send()
    tok.drain()
    set1.drain()
    set2.drain()


def greet_all(geo):
    s, w = lax.axis_index("seq"), lax.axis_index("wt")
    barrier = pltpu.get_barrier_semaphore()
    part, g = s // geo.groups, s % geo.groups
    for d in range(1, geo.seq):
        pl.semaphore_signal(barrier, inc=1, device_id=((s + d) % geo.seq, w), device_id_type=MESH)
    count = geo.seq - 1
    for d in range(1, geo.wt):
        for q in range(geo.parts):
            other = ((part + q) % geo.parts) * geo.groups + g
            pl.semaphore_signal(barrier, inc=1, device_id=(other, (w + d) % geo.wt), device_id_type=MESH)
            count += 1
    pl.semaphore_wait(barrier, count)


def closing(geo, rank, lengths, ids, tokens, d_first, dq, dk, dv, w_slice, down, up, small, grads, early_sum):
    rows, width = geo.rows, geo.width
    docs = lengths.shape[1]
    doc_rows = docs * rank
    lane_count = down.shape[0] // 4
    early = [] if early_sum is None else [early_sum]
    late = sum(v.shape[1] for v in grads) // geo.groups
    set1 = late + 3 * LANES + sum(v.shape[1] for v in early)
    set2 = 3 * LANES
    chips, near = geo.seq // 2, geo.groups // 2
    peers = geo.wt * geo.parts
    smem = pl.BlockSpec(memory_space=pltpu.SMEM)
    vmem = pl.BlockSpec(memory_space=pltpu.VMEM)
    any_spec = pl.BlockSpec(memory_space=pl.ANY)
    dma = pltpu.SemaphoreType.DMA
    wide = width + LANES
    return pl.pallas_call(
        functools.partial(closing_kernel, geo, rank, len(grads), len(early)),
        out_shape=[
            jax.ShapeDtypeStruct((rows, width), F32),
            jax.ShapeDtypeStruct((geo.groups, lane_count, set1), BF16),
            jax.ShapeDtypeStruct((geo.groups, lane_count, set2), BF16),
            jax.ShapeDtypeStruct((chips, rows, wide), BF16),
        ],
        in_specs=[smem, smem] + [vmem] * 8 + [any_spec] + [vmem] * (len(grads) + len(early)),
        out_specs=[vmem, any_spec, any_spec, any_spec],
        scratch_shapes=[
            pltpu.VMEM((min(chips, 4), rows, wide), BF16),
            pltpu.VMEM((chips, rows, wide), BF16),
            pltpu.VMEM((2, rows, wide), BF16),
            pltpu.VMEM((2, rows, 3 * lane_count), BF16),
            pltpu.VMEM((near, doc_rows, late), BF16),
            pltpu.VMEM((near, doc_rows, late), BF16),
            pltpu.VMEM((near, doc_rows, late), BF16),
            pltpu.VMEM((near, doc_rows, 3 * LANES), BF16),
            pltpu.VMEM((near, doc_rows, 3 * LANES), BF16),
            pltpu.VMEM((near, doc_rows, 3 * LANES), BF16),
            pltpu.VMEM((3 * doc_rows, width), F32),
            pltpu.VMEM((3 * lane_count, LANES), F32),
            pltpu.VMEM((doc_rows, set1), BF16),
            pltpu.VMEM((doc_rows, set2), BF16),
            pltpu.VMEM((lane_count, LANES), BF16),
            pltpu.VMEM((lane_count, LANES), BF16),
            pltpu.VMEM((peers, doc_rows, set1), BF16),
            pltpu.VMEM((peers, doc_rows, set2), BF16),
            pltpu.VMEM((peers, lane_count, LANES), BF16),
            pltpu.VMEM((lane_count, set1), BF16),
            pltpu.VMEM((lane_count, set2), BF16),
            dma((4, chips)),
            dma((4, near)),
            dma((4, near)),
            dma((4, peers)),
            dma((4, peers)),
            dma((Spread.KINDS, 2)),
            dma((Spread.KINDS, 2)),
            dma((2,)),
            dma((2,)),
            dma((2,)),
            pltpu.VMEM((2, rows // 2, wide) if chips == 4 else (1, 16, LANES), BF16),
            dma((2, 2)),
        ],
        compiler_params=pltpu.CompilerParams(
            collective_id=1, has_side_effects=True, vmem_limit_bytes=VMEM_LIMIT
        ),
        name="close",
    )(lengths, ids, tokens, d_first, dq, dk, dv, w_slice, down, up, small, *grads, *early)


def unpack_kernel(late, one_ref, two_ref, down_ref, up_ref, fc1_down_ref, fc2_up_ref, fc1_up_ref, fc2_down_ref):
    for j in range(3):
        down_ref[j] = two_ref[0, :, j * LANES : (j + 1) * LANES].astype(F32)
    singles = [down_ref.at[3], up_ref.at[3], fc1_down_ref, fc2_up_ref, fc1_up_ref, fc2_down_ref]
    at = 0
    for ref in singles[:late] + [up_ref.at[j] for j in range(3)] + singles[late:]:
        wide = ref.shape[1]
        ref[...] = one_ref[0, :, at : at + wide].astype(F32)
        at += wide


def unpack(geo, one, two, lane_count, late):
    groups = geo.groups
    thick = (one.shape[2] - 7 * LANES) // 2

    def whole(wide):
        return jax.ShapeDtypeStruct((lane_count, wide * groups), F32)

    def flat(wide):
        return pl.BlockSpec((lane_count, wide), lambda i: (0, i))

    four = jax.ShapeDtypeStruct((4, lane_count, LANES * groups), F32)
    four_spec = pl.BlockSpec((4, lane_count, LANES), lambda i: (0, 0, i))
    return pl.pallas_call(
        functools.partial(unpack_kernel, late),
        grid=(groups,),
        out_shape=[four, four, whole(LANES), whole(LANES), whole(thick), whole(thick)],
        in_specs=[
            pl.BlockSpec((1,) + one.shape[1:], lambda i: (i, 0, 0)),
            pl.BlockSpec((1,) + two.shape[1:], lambda i: (i, 0, 0)),
        ],
        out_specs=[four_spec, four_spec, flat(LANES), flat(LANES), flat(thick), flat(thick)],
        compiler_params=pltpu.CompilerParams(vmem_limit_bytes=VMEM_LIMIT),
        name="unpack",
    )(one, two)


def layer_norm(value, gain, shift):
    mean = jnp.mean(value, axis=-1, keepdims=True)
    centred = value - mean
    spread = jnp.mean(centred * centred, axis=-1, keepdims=True)
    return centred * lax.rsqrt(spread + 1e-05) * gain + shift


def gelu_exact(value):
    return jax.nn.gelu(value, approximate=False)


def times_transposed(grad, weight):
    return lax.dot_general(
        grad, weight, (((1,), (1,)), ((), ())), preferred_element_type=jnp.float32
    )


def left_inner(left, right):
    return lax.dot_general(
        left, right, (((0,), (0,)), ((), ())), preferred_element_type=jnp.float32
    )


def stack_down(down):
    return jnp.transpose(down, (1, 0, 2)).reshape(down.shape[1], down.shape[0] * down.shape[2])


def stack_up(up):
    return up.reshape(up.shape[0] * up.shape[1], up.shape[2])


def unstack_down(stacked, adapter_count, rank_size):
    return jnp.transpose(stacked.reshape(stacked.shape[0], adapter_count, rank_size), (1, 0, 2))


def unstack_up(stacked, adapter_count, rank_size):
    return stacked.reshape(adapter_count, rank_size, stacked.shape[1])


def segment_of(positions, starts):
    return jnp.sum((positions[:, None] >= starts[None, :]).astype(jnp.int32), axis=1) - 1


def select_local(tok_rows, lane_count, rank_size, lengths, ids):
    starts = jnp.cumsum(lengths) - lengths
    local_pos = lax.axis_index("seq") * tok_rows + jnp.arange(tok_rows, dtype=jnp.int32)
    local_seg = segment_of(local_pos, starts)
    doc_range = jnp.arange(lengths.shape[0], dtype=jnp.int32)
    chosen = jnp.sum(jnp.where(local_seg[:, None] == doc_range[None, :], ids[None, :], 0), axis=1)
    lane_owner = jnp.arange(lane_count, dtype=jnp.int32) // rank_size
    lane_rank = jnp.arange(lane_count, dtype=jnp.int32) % rank_size
    doc_owner = jnp.repeat(doc_range, rank_size)
    doc_rank = jnp.arange(doc_owner.shape[0], dtype=jnp.int32) % rank_size
    to_doc = (lane_owner[:, None] == jnp.repeat(ids, rank_size)[None, :]) & (lane_rank[:, None] == doc_rank[None, :])
    return (
        (chosen[:, None] == lane_owner[None, :]).astype(jnp.float32),
        to_doc.astype(jnp.bfloat16),
        (local_seg[:, None] == doc_owner[None, :]).astype(jnp.float32),
    )


def feed_forward(
    geo, tokens, cotangent, attended_tok, weights, vectors, attn_maps, fc1_maps, fc2_maps, select
):
    tok_rows, model_width = tokens.shape
    full_out, full_fc1, full_fc2 = [lax.all_gather(v, "wt", axis=0, tiled=True) for v in weights]
    out_bias, norm1_gain, norm1_bias, fc1_bias, fc2_bias, norm2_gain, norm2_bias = vectors
    out_down, out_up = attn_maps
    fc1_down_all, fc1_up_all = fc1_maps
    fc2_down_all, fc2_up_all = fc2_maps
    select, to_doc, in_doc = select

    def by_doc(low):
        return (jnp.dot(low, to_doc, preferred_element_type=jnp.float32) * in_doc).astype(jnp.bfloat16)

    out_main = jnp.dot(attended_tok, full_out, preferred_element_type=jnp.float32)
    small_out = (
        jnp.dot(attended_tok, out_down, preferred_element_type=jnp.float32) * select
    ).astype(jnp.bfloat16)
    z_value = out_main + out_bias + jnp.dot(small_out, out_up, preferred_element_type=jnp.float32)
    first_sum = tokens.astype(jnp.float32) + z_value
    first_norm, norm1_back = jax.vjp(
        lambda value: layer_norm(value, norm1_gain, norm1_bias), first_sum
    )
    first_low = first_norm.astype(jnp.bfloat16)
    fc1_main = jnp.dot(first_low, full_fc1, preferred_element_type=jnp.float32)
    small_fc1 = (
        jnp.dot(first_low, fc1_down_all, preferred_element_type=jnp.float32) * select
    ).astype(jnp.bfloat16)
    pre_act = (
        fc1_main + fc1_bias + jnp.dot(small_fc1, fc1_up_all, preferred_element_type=jnp.float32)
    )
    act_value, gelu_back = jax.vjp(gelu_exact, pre_act)
    act_low = act_value.astype(jnp.bfloat16)
    fc2_main = jnp.dot(act_low, full_fc2, preferred_element_type=jnp.float32)
    small_fc2 = (
        jnp.dot(act_low, fc2_down_all, preferred_element_type=jnp.float32) * select
    ).astype(jnp.bfloat16)
    y_value = (
        fc2_main + fc2_bias + jnp.dot(small_fc2, fc2_up_all, preferred_element_type=jnp.float32)
    )
    output, norm2_back = jax.vjp(
        lambda value: layer_norm(value, norm2_gain, norm2_bias), first_norm + y_value
    )
    d_second = norm2_back(cotangent.astype(jnp.float32))[0]
    d_y = d_second.astype(jnp.bfloat16)
    d_act = times_transposed(d_y, full_fc2)
    low_fc2 = (times_transposed(d_y, fc2_up_all) * select).astype(jnp.bfloat16)
    d_act = d_act + times_transposed(low_fc2, fc2_down_all)
    grad_fc2_up = left_inner(by_doc(small_fc2), d_y)
    grad_fc2_down = left_inner(by_doc(low_fc2), act_low)
    d_pre = gelu_back(d_act)[0].astype(jnp.bfloat16)
    d_first_low = times_transposed(d_pre, full_fc1)
    low_fc1 = (times_transposed(d_pre, fc1_up_all) * select).astype(jnp.bfloat16)
    d_first_low = d_first_low + times_transposed(low_fc1, fc1_down_all)
    grad_fc1_up = left_inner(by_doc(small_fc1), d_pre)
    grad_fc1_down = left_inner(by_doc(low_fc1), first_low)
    d_first = norm1_back(d_second + d_first_low)[0]
    d_z = d_first.astype(jnp.bfloat16)
    d_attended = times_transposed(d_z, full_out)
    low_out = (times_transposed(d_z, out_up) * select).astype(jnp.bfloat16)
    d_attended = (d_attended + times_transposed(low_out, out_down)).astype(jnp.bfloat16)
    grad_out_up = left_inner(by_doc(small_out), d_z)
    grad_out_down = left_inner(by_doc(low_out), attended_tok)
    blocks = [
        [p * geo.groups + i for i in range(geo.groups)] for p in range(geo.parts)
    ]
    d_heads = lax.all_to_all(
        d_attended.reshape(tok_rows, geo.groups, LANES),
        "seq",
        split_axis=1,
        concat_axis=0,
        axis_index_groups=blocks,
        tiled=True,
    ).reshape(geo.queries, LANES)
    grads = [grad_out_down, grad_out_up, grad_fc1_down, grad_fc2_up, grad_fc1_up, grad_fc2_down]
    return output, d_first, d_heads, [v.astype(BF16) for v in grads]


def shards(
    tokens,
    cotangent,
    w_qkv,
    qv_bias,
    w_out,
    out_bias,
    norm1_gain,
    norm1_bias,
    w_fc1,
    fc1_bias,
    w_fc2,
    fc2_bias,
    norm2_gain,
    norm2_bias,
    doc_lengths,
    adapter_ids,
    attn_down,
    attn_up,
    fc1_down,
    fc1_up,
    fc2_down,
    fc2_up,
):
    tok_rows, model_width = tokens.shape
    adapter_count = attn_down.shape[1]
    rank_size = attn_down.shape[3]
    lane_count = adapter_count * rank_size
    seq_count = lax.axis_size("seq")
    geo = Geometry(tok_rows, model_width)
    part_index = lax.axis_index("seq") // geo.groups
    down_rows = jnp.transpose(attn_down, (0, 1, 3, 2)).reshape(4 * lane_count, model_width)
    up_rows = attn_up.reshape(4 * lane_count, model_width)
    weights = (w_out, w_fc1, w_fc2)
    vectors = (out_bias, norm1_gain, norm1_bias, fc1_bias, fc2_bias, norm2_gain, norm2_bias)

    def rows_of(down):
        return jnp.swapaxes(down, 1, 2).reshape(lane_count, down.shape[1])

    inside = all(v.shape[0] % (32 * seq_count) == 0 for v in weights)
    mlp = None
    if inside:
        mlp = (
            weights
            + (cotangent,)
            + tuple(v.reshape(1, -1) for v in vectors)
            + (rows_of(fc1_down), stack_up(fc1_up), rows_of(fc2_down), stack_up(fc2_up))
        )
    q_heads, k_heads, v_heads, o_heads, lse_heads, w_slice, small_all, *rest = forward_attention(
        geo, rank_size, doc_lengths, adapter_ids, tokens, w_qkv, down_rows, up_rows, qv_bias, mlp
    )
    if inside:
        output, d_first, d_heads, *set1, early_sum = rest
    else:
        early_sum = None
        output, d_first, d_heads, set1 = feed_forward(
            geo,
            tokens,
            cotangent,
            rest[0],
            weights,
            vectors,
            (stack_down(attn_down[3]), stack_up(attn_up[3])),
            (stack_down(fc1_down), stack_up(fc1_up)),
            (stack_down(fc2_down), stack_up(fc2_up)),
            select_local(tok_rows, lane_count, rank_size, doc_lengths[0], adapter_ids[0]),
        )
    d_q, d_k, d_v, output = backward_attention(
        geo, doc_lengths, part_index.reshape(1, 1), q_heads, k_heads, v_heads, o_heads, lse_heads, d_heads, output
    )
    input_grad, sum1, sum2, _ = closing(
        geo,
        rank_size,
        doc_lengths,
        adapter_ids,
        tokens,
        d_first,
        d_q,
        d_k,
        d_v,
        w_slice,
        down_rows,
        up_rows,
        small_all,
        set1,
        early_sum,
    )

    down4, up4, fc1_down_sum, fc2_up_sum, fc1_up_sum, fc2_down_sum = unpack(geo, sum1, sum2, lane_count, len(set1))

    def as_up(rows):
        return rows.reshape(rows.shape[:-2] + (adapter_count, rank_size, rows.shape[-1]))

    def as_down(rows):
        return jnp.swapaxes(as_up(rows), -1, -2)

    return (
        output,
        input_grad,
        as_down(down4),
        as_up(up4),
        as_down(fc1_down_sum),
        as_up(fc1_up_sum),
        as_down(fc2_down_sum),
        as_up(fc2_up_sum),
    )


def solution(mesh):
    placed = (
        P(("wt", "seq"), None),
        P(("wt", "seq"), None),
        P("wt", None),
        P(),
        P("wt", None),
        P(),
        P(),
        P(),
        P("wt", None),
        P(),
        P("wt", None),
        P(),
        P(),
        P(),
        P("wt", None),
        P("wt", None),
        P(),
        P(),
        P(),
        P(),
        P(),
        P(),
    )
    return jax.shard_map(
        shards,
        mesh=mesh,
        in_specs=placed,
        out_specs=(P(("wt", "seq"), None), P(("wt", "seq"), None), P(), P(), P(), P(), P(), P()),
        check_vma=False,
    )
```

```python
import functools

import jax
import jax.numpy as jnp
from jax import lax
from jax.experimental import pallas as pl
from jax.experimental.pallas import tpu as pltpu
from jax.sharding import PartitionSpec as P

HEADS = 16
HEAD_DIM = 64
LANES = 128
PAIR = LANES // HEAD_DIM
MESH = pl.DeviceIdType.MESH
F32 = jnp.float32
BF16 = jnp.bfloat16
VMEM_LIMIT = 60 * 2**20


def dot_nn(a, b):
    return lax.dot_general(a, b, (((1,), (0,)), ((), ())), preferred_element_type=F32)


def dot_nt(a, b):
    return lax.dot_general(a, b, (((1,), (1,)), ((), ())), preferred_element_type=F32)


def dot_tn(a, b):
    return lax.dot_general(a, b, (((0,), (0,)), ((), ())), preferred_element_type=F32)


class Geometry:
    def __init__(self, rows, width):
        self.seq = lax.axis_size("seq")
        self.wt = lax.axis_size("wt")
        self.rows = rows
        self.width = width
        self.groups = width // LANES
        self.parts = self.seq // self.groups
        chips = self.seq // 2
        nx = 1
        while nx * nx < chips:
            nx *= 2
        self.nx = nx
        self.ny = chips // nx
        self.keys = self.seq * rows
        self.queries = self.groups * rows


def doc_bounds(len_ref):
    count = len_ref.shape[1]
    starts, ends = [], []
    at = jnp.int32(0)
    for i in range(count):
        starts.append(at)
        at = at + len_ref[0, i]
        ends.append(at)
    return starts, ends


def segment_from(positions, starts):
    seg = jnp.zeros_like(positions)
    for start in starts[1:]:
        seg = seg + (positions >= start).astype(jnp.int32)
    return seg


def select_from(positions, starts, ends, id_ref, rank):
    owner = lax.broadcasted_iota(jnp.int32, positions.shape, 1) // rank
    picked = jnp.zeros(positions.shape, F32)
    for i in range(len(starts)):
        inside = (positions >= starts[i]) & (positions < ends[i]) & (owner == id_ref[0, i])
        picked = jnp.where(inside, 1.0, picked)
    return picked


def placement(id_ref, docs, rank, lane_count):
    a = lax.broadcasted_iota(jnp.int32, (lane_count, LANES), 0)
    b = lax.broadcasted_iota(jnp.int32, (lane_count, LANES), 1)
    every = jnp.zeros((lane_count, LANES), F32)
    first = jnp.zeros((lane_count, LANES), F32)
    for d in range(docs):
        seen = jnp.bool_(False)
        for e in range(d):
            seen = seen | (id_ref[0, e] == id_ref[0, d])
        hit = (a // rank == id_ref[0, d]) & (b // rank == d) & (a % rank == b % rank)
        every = jnp.where(hit, 1.0, every)
        first = jnp.where(hit, jnp.where(seen, 0.0, 1.0), first)
    return every.astype(BF16), first.astype(BF16)


def owner_columns(refs, owner, groups):
    cols = []
    for ref in refs:
        wide = ref.shape[1] // groups
        cols.append(ref[:, pl.ds(pl.multiple_of(owner * wide, LANES), wide)])
    return jnp.concatenate(cols, axis=1).astype(F32)


class Spread:
    KINDS = 9

    def __init__(self, geo, here, region, send, recv, unit, first=0):
        self.geo, self.here, self.region = geo, here, region
        self.send, self.recv, self.unit, self.first = send, recv, unit, first

    def copy(self, kind, src, dst, x, y, core):
        return pltpu.make_async_remote_copy(
            src_ref=src,
            dst_ref=dst,
            send_sem=self.send.at[kind, self.unit],
            recv_sem=self.recv.at[kind, self.unit],
            device_id=(self.first + ((y * self.geo.nx) + x) * 2 + core, self.here[3]),
            device_id_type=MESH,
        )

    def others(self):
        nx, ny = self.geo.nx, self.geo.ny
        x, y, core, _ = self.here
        row = [((x + d) % nx, y) for d in range(1, nx)]
        col = [(x, (y + d) % ny) for d in range(1, ny)]
        return row, col

    def plan(self):
        x, y, core, _ = self.here
        row, col = self.others()
        plan = {kind: [] for kind in range(self.KINDS)}
        for tx, ty in row:
            plan[0].append(((x, y), None, (tx, ty, core)))
        for tx, ty in col:
            plan[1].append(((x, y), None, (tx, ty, core)))
        for ux, uy in row:
            for tx, ty in col:
                plan[2].append(((ux, uy), 0, (tx, ty, core)))
        for ux, uy in col:
            for tx, ty in row:
                plan[3].append(((ux, uy), 1, (tx, ty, core)))
        plan[4].append(((x, y), None, (x, y, 1 - core)))
        for ux, uy in row:
            plan[5].append(((ux, uy), None, (x, y, 1 - core)))
        for ux, uy in col:
            plan[6].append(((ux, uy), None, (x, y, 1 - core)))
        for ux, _ in row:
            for _, uy in col:
                plan[7].append(((ux, uy), 0, (x, y, 1 - core)))
                plan[8].append(((ux, uy), 1, (x, y, 1 - core)))
        return plan

    def go(self, kind, own=None):
        core = self.here[2]
        for (ux, uy), half, (tx, ty, tcore) in self.plan()[kind]:
            dst = self.region(ux, uy, core, half)
            src = dst if own is None else own
            self.copy(kind, src, dst, tx, ty, tcore).start()

    def arrivals(self, kind):
        x, y, core, _ = self.here
        row, col = self.others()
        if kind == 0:
            return [(u, None, core) for u in row]
        if kind == 1:
            return [(u, None, core) for u in col]
        if kind in (2, 3):
            return [((ux, uy), kind - 2, core) for ux, _ in row for _, uy in col]
        if kind == 4:
            return [((x, y), None, 1 - core)]
        if kind == 5:
            return [(u, None, 1 - core) for u in row]
        if kind == 6:
            return [(u, None, 1 - core) for u in col]
        return [((ux, uy), kind - 7, 1 - core) for ux, _ in row for _, uy in col]

    def wait(self, kind):
        x, y, core, _ = self.here
        for (ux, uy), half, whose in self.arrivals(kind):
            ref = self.region(ux, uy, whose, half)
            self.copy(kind, ref, ref, x, y, 1 - core).wait_recv()

    def wait_sends(self):
        x, y, core, _ = self.here
        for kind in range(self.KINDS):
            for (ux, uy), half, _ in self.plan()[kind]:
                ref = self.region(ux, uy, core, half)
                self.copy(kind, ref, ref, x, y, 1 - core).wait_send()


def device_here(geo):
    s = lax.axis_index("seq")
    core = s % 2
    chip = s // 2
    return chip % geo.nx, chip // geo.nx, core, lax.axis_index("wt")


def greet(geo):
    s, w = lax.axis_index("seq"), lax.axis_index("wt")
    barrier = pltpu.get_barrier_semaphore()
    for d in range(1, geo.seq):
        pl.semaphore_signal(barrier, inc=1, device_id=((s + d) % geo.seq, w), device_id_type=MESH)
    for d in range(1, geo.wt):
        pl.semaphore_signal(barrier, inc=1, device_id=(s, (w + d) % geo.wt), device_id_type=MESH)
    pl.semaphore_wait(barrier, geo.seq + geo.wt - 2)


def erf(v):
    v = jnp.clip(v, -3.832506856900711, 3.832506856900711)
    sq = v * v
    top = jnp.full_like(v, 0.00022905065861350646)
    for c in (0.0034082910107109506, 0.050955695062380861, 0.18520832239976145, 1.128379143519084):
        top = top * sq + c
    low = jnp.full_like(v, -1.1791602954361697e-7)
    for c in (0.000023547966471313185, 0.0010179625278914885, 0.014070470171167667, 0.11098505178285362, 0.49746925110067538, 1.0):
        low = low * sq + c
    return v * top / low


def normed(value):
    mean = jnp.mean(value, axis=1, keepdims=True)
    centred = value - mean
    spread = lax.rsqrt(jnp.mean(centred * centred, axis=1, keepdims=True) + 1e-05)
    return centred * spread, spread


def normed_back(grad, gain, unit, spread):
    g = grad * gain
    return spread * (
        g - jnp.mean(g, axis=1, keepdims=True) - unit * jnp.mean(g * unit, axis=1, keepdims=True)
    )


class Names:
    def __init__(self, names, refs):
        self.__dict__.update(zip(names, refs))


MLP_INPUTS = (
    "w_out", "w_fc1", "w_fc2", "cotangent", "out_bias", "gain1", "shift1", "fc1_bias", "fc2_bias", "gain2", "shift2",
    "fc1_down", "fc1_up", "fc2_down", "fc2_up",
)
BASE_OUTPUTS = ("q", "k", "v", "o", "lse", "w_slice", "small")
MLP_OUTPUTS = ("output", "d_first", "d_heads", "g_out_down", "g_out_up", "g_fc1_down", "early_sum")
BASE_SCRATCH = (
    "tok", "seg", "att_send_buf", "local_sem", "send_sem", "recv_sem", "slice_send", "slice_recv", "line_send",
    "line_recv", "att_send", "att_recv", "q_buf", "k_buf", "v_buf", "o_buf", "lse_buf", "slice_buf", "small_buf", "flush_sem",
)
LATER = ("cotangent", "fc1_down", "fc1_up", "fc2_down", "fc2_up")
MLP_SCRATCH = (
    "att", "full_out", "full_fc1", "full_fc2", "unit1", "h1", "h1_low", "act", "slope", "d_pre", "y", "d_att_buf",
    "back_send", "back_recv", "g_fc2_up", "g_fc1_up", "g_fc2_down", "set_out", "set_in", "set_far", "set_sems",
    "load_sem", "cotangent_buf", "fc1_down_buf", "fc1_up_buf", "fc2_down_buf", "fc2_up_buf",
)


def forward_kernel(geo, inside, rank, len_ref, id_ref, tokens_ref, wqkv_ref, down_ref, up_ref, bias_ref, *refs):
    in_names = MLP_INPUTS if inside else ()
    out_names = BASE_OUTPUTS + (MLP_OUTPUTS if inside else ("att",))
    scratch_names = BASE_SCRATCH + (MLP_SCRATCH if inside else ())
    r = Names(in_names + out_names + scratch_names, refs)
    weights_in = (r.w_out, r.w_fc1, r.w_fc2) if inside else ()
    weights_out = (r.full_out, r.full_fc1, r.full_fc2) if inside else ()
    weight_count = len(weights_in)
    att_ref, q_ref, k_ref, v_ref, o_ref, lse_ref, slice_ref, small_ref = (
        r.att, r.q_buf, r.k_buf, r.v_buf, r.o_buf, r.lse_buf, r.slice_buf, r.small_buf
    )
    results = [r.q, r.k, r.v, r.o, r.lse, r.w_slice, r.small]
    made = [q_ref, k_ref, v_ref, o_ref, lse_ref, slice_ref, small_ref]
    flushes = [pltpu.make_async_copy(made[i], results[i], r.flush_sem.at[i]) for i in range(len(made))]
    loads = []
    if inside:
        loads = [
            pltpu.make_async_copy(getattr(r, name), getattr(r, name + "_buf"), r.load_sem.at[i])
            for i, name in enumerate(LATER)
        ]
    tok_buf, seg_buf, att_buf, local_sem = r.tok, r.seg, r.att_send_buf, r.local_sem
    send_sem, recv_sem, slice_send, slice_recv = r.send_sem, r.recv_sem, r.slice_send, r.slice_recv
    line_send, line_recv, att_send, att_recv = r.line_send, r.line_recv, r.att_send, r.att_recv
    here = device_here(geo)
    x, y, core, w = here
    s = lax.axis_index("seq")
    part, g = s // geo.groups, s % geo.groups
    rows, width, wt = geo.rows, geo.width, geo.wt
    lanes = pl.ds(pl.multiple_of(g * LANES, LANES), LANES)

    own_tok = pltpu.make_async_copy(tokens_ref, tok_buf.at[s], local_sem.at[0])
    own_tok.start()
    shard = wqkv_ref.shape[0]
    own_slices = []
    for j in range(3):
        src = wqkv_ref.at[:, pl.ds(pl.multiple_of(j * width + g * LANES, LANES), LANES)]
        dst = slice_ref.at[pl.ds(pl.multiple_of(w * shard, shard), shard), pl.ds(j * LANES, LANES)]
        own_slices.append(pltpu.make_async_copy(src, dst, local_sem.at[1 + j]))
        own_slices[-1].start()
    own_weights = []
    for m in range(weight_count):
        height = weights_in[m].shape[0]
        dst = weights_out[m].at[pl.ds(pl.multiple_of(w * height, height), height)]
        own_weights.append(pltpu.make_async_copy(weights_in[m], dst, local_sem.at[4 + m]))
        own_weights[-1].start()

    greet(geo)

    def token_region(ux, uy, whose, half):
        block = tok_buf.at[(uy * geo.nx + ux) * 2 + whose]
        if half is None:
            return block
        return block.at[pl.ds(half * (rows // 2), rows // 2)]

    tok = Spread(geo, here, token_region, send_sem, recv_sem, 0)
    tok.go(0, own=tokens_ref)
    tok.go(1, own=tokens_ref)
    tok.go(4, own=tokens_ref)

    def slice_copy(j, p, up):
        dst = slice_ref.at[pl.ds(pl.multiple_of(p * shard, shard), shard), pl.ds(j * LANES, LANES)]
        return pltpu.make_async_remote_copy(
            src_ref=dst,
            dst_ref=dst,
            send_sem=slice_send.at[0 if up else 1, j, p],
            recv_sem=slice_recv.at[j, p],
            device_id=(s, w + 1 if up else w - 1),
            device_id_type=MESH,
        )

    for copy in loads:
        copy.start()

    starts, ends = doc_bounds(len_ref)
    seg_buf[...] = segment_from(lax.broadcasted_iota(jnp.int32, seg_buf.shape, 1), starts)

    seq = geo.seq
    mine = s

    def unit_rows(m, p, unit, half=None):
        height = weights_in[m].shape[0]
        piece = height // seq
        if half is None:
            return weights_out[m].at[pl.ds(pl.multiple_of(p * height + unit * piece, piece), piece)]
        piece = piece // 2
        return weights_out[m].at[
            pl.ds(pl.multiple_of(p * height + unit * 2 * piece + half * piece, piece), piece)
        ]

    def line_copy(m, p, up, own):
        height = weights_in[m].shape[0]
        piece = height // seq
        dst = unit_rows(m, p, mine)
        src = weights_in[m].at[pl.ds(pl.multiple_of(mine * piece, piece), piece)] if own else dst
        target = w + 1 if up else w - 1
        return pltpu.make_async_remote_copy(
            src_ref=src,
            dst_ref=dst,
            send_sem=line_send.at[0 if up else 1, m * wt + p],
            recv_sem=line_recv.at[m * wt + p],
            device_id=(s, target),
            device_id_type=MESH,
        )

    def nth_plane(j):
        below, above = w, wt - 1 - w
        both = jnp.minimum(below, above)
        in_turn = j < 2 * both
        dist = jnp.where(in_turn, j // 2 + 1, j - both + 1)
        from_below = jnp.where(in_turn, j % 2 == 0, below > above)
        return jnp.where(from_below, w - dist, w + dist)

    def weight_spread(m, p):
        def region(ux, uy, whose, half):
            return unit_rows(m, p, (uy * geo.nx + ux) * 2 + whose, half)

        return Spread(geo, here, region, send_sem, recv_sem, 1 + m * wt + p)

    units = []
    if inside:
        units = [(m, j) for j in range(wt - 1) for m in (0, 1)] + [(2, j) for j in range(wt - 1)]

    def start_lines(which):
        for m in which if inside else ():

            @pl.when(w < wt - 1)
            def _():
                line_copy(m, w, True, True).start()

            @pl.when(w > 0)
            def _():
                line_copy(m, w, False, True).start()

    def along(i):
        if i >= len(units):
            return
        m, j = units[i]
        p = nth_plane(j)
        line_copy(m, p, True, False).wait_recv()

        @pl.when((p < w) & (w < wt - 1))
        def _():
            line_copy(m, p, True, False).start()

        @pl.when((p > w) & (w > 0))
        def _():
            line_copy(m, p, False, False).start()

    def tick(i):
        if i == 0:
            along(0)
        if i == late_lines:
            start_lines((2,))
        if i < len(units):
            m, j = units[i]
            spread = weight_spread(m, nth_plane(j))
            spread.go(0)
            spread.go(1)
            spread.go(4)
        along(i + 1)
        if 0 <= i - 1 < len(units):
            m, j = units[i - 1]
            spread = weight_spread(m, nth_plane(j))
            spread.wait(0)
            spread.go(2)
            spread.go(5)
            spread.wait(1)
            spread.go(3)
            spread.go(6)
        if 0 <= i - 2 < len(units):
            m, j = units[i - 2]
            spread = weight_spread(m, nth_plane(j))
            spread.wait(2)
            spread.go(7)
            spread.wait(3)
            spread.go(8)

    tick_count = len(units) + 2 if units else 0
    late_lines = 0
    early_ticks = min(3, tick_count)
    loop_ticks = min(6, tick_count)

    def complete(m):
        own_weights[m].wait()
        for j in range(wt - 1):
            spread = weight_spread(m, nth_plane(j))
            for kind in range(4, 9):
                spread.wait(kind)

    for copy in own_slices:
        copy.wait()
    for j in range(3):

        @pl.when(w < wt - 1)
        def _():
            slice_copy(j, w, True).start()

        @pl.when(w > 0)
        def _():
            slice_copy(j, w, False).start()

    nx, ny = geo.nx, geo.ny
    row_n, col_n, diag_n = 2 * (nx - 1), 2 * (ny - 1), 2 * (nx - 1) * (ny - 1)

    def block_owner(i):
        r = i - 2
        c = r - row_n
        d = c - col_n
        dx_row, k_row = r % max(nx - 1, 1) + 1, r // max(nx - 1, 1)
        dy_col, k_col = c % max(ny - 1, 1) + 1, c // max(ny - 1, 1)
        half = max(diag_n // 2, 1)
        k_diag, in_diag = d // half, d % half
        dx_diag, dy_diag = in_diag % max(nx - 1, 1) + 1, in_diag // max(nx - 1, 1) + 1
        dx = jnp.where(i < 2, 0, jnp.where(i < 2 + row_n, dx_row, jnp.where(i < 2 + row_n + col_n, 0, dx_diag)))
        dy = jnp.where(i < 2 + row_n, 0, jnp.where(i < 2 + row_n + col_n, dy_col, dy_diag))
        kk = jnp.where(i < 2, i, jnp.where(i < 2 + row_n, k_row, jnp.where(i < 2 + row_n + col_n, k_col, k_diag)))
        return (((y + dy) % ny) * nx + (x + dx) % nx) * 2 + (core + kk) % 2

    def project(i, carry):
        @pl.when(i == 0)
        def _():
            for n in range(wt - 1):
                p = nth_plane(n)
                for j in range(3):
                    slice_copy(j, p, True).wait_recv()

                    @pl.when((p < w) & (w < wt - 1))
                    def _():
                        slice_copy(j, p, True).start()

                    @pl.when((p > w) & (w > 0))
                    def _():
                        slice_copy(j, p, False).start()

            start_lines((0, 1))
            own_tok.wait()

        @pl.when(i == 1)
        def _():
            tok.wait(4)

        @pl.when(i == 2)
        def _():
            tok.wait(0)
            tok.go(2)
            tok.go(5)
            tok.wait(1)
            tok.go(3)
            tok.go(6)

        @pl.when(i == 2 + row_n // 2)
        def _():
            tok.wait(5)

        @pl.when(i == 2 + row_n + col_n // 2)
        def _():
            tok.wait(6)

        @pl.when(i == 2 + row_n + col_n)
        def _():
            tok.wait(2)
            tok.go(7)
            tok.wait(3)
            tok.go(8)

        @pl.when(i == 2 + row_n + col_n + diag_n // 2)
        def _():
            tok.wait(7)
            tok.wait(8)

        for n in range(early_ticks):

            @pl.when(i == min(3 + 2 * n, geo.seq - 1))
            def _():
                tick(n)

        t = block_owner(i)
        block = tok_buf[t]
        at = pl.ds(pl.multiple_of(t * rows, rows), rows)
        pos = t * rows + lax.broadcasted_iota(jnp.int32, (rows, LANES), 0)
        chosen = select_from(pos, starts, ends, id_ref, rank)
        main = dot_nn(block, slice_ref[...])
        small = dot_nt(block, down_ref[: 3 * LANES, :])
        for j in range(3):
            cut = slice(j * LANES, (j + 1) * LANES)
            low = (small[:, cut] * chosen).astype(BF16)
            small_ref[at, cut] = low
            value = main[:, cut] + dot_nn(low, up_ref[cut, lanes])
            if j == 0:
                value = value + bias_ref[0:1, lanes]

                @pl.when(t // geo.groups == part)
                def _():
                    inner = pl.ds(pl.multiple_of((t % geo.groups) * rows, rows), rows)
                    q_ref[inner, :] = value.astype(BF16)
            elif j == 1:
                k_ref[at, :] = value.astype(BF16)
            else:
                v_ref[at, :] = (value + bias_ref[1:2, lanes]).astype(BF16)
        return carry

    lax.fori_loop(0, geo.seq, project, 0)

    scale = HEAD_DIM ** (-0.5)
    chunk = min(2048, geo.keys)
    chunks = geo.keys // chunk
    first_head = lax.broadcasted_iota(jnp.int32, (rows, LANES), 1) < HEAD_DIM

    def att_copy(b):
        return pltpu.make_async_remote_copy(
            src_ref=att_buf.at[b],
            dst_ref=att_ref.at[:, lanes],
            send_sem=att_send.at[b],
            recv_sem=att_recv.at[g],
            device_id=(part * geo.groups + b, w),
            device_id_type=MESH,
        )

    def attend(i, carry):
        for n in range(early_ticks, loop_ticks):

            @pl.when(i == 2 * (n - early_ticks) + 1)
            def _():
                tick(n)

        b = (g + 1 + i) % geo.groups
        inner = pl.ds(pl.multiple_of(b * rows, rows), rows)
        query = q_ref[inner, :] * jnp.asarray(scale, BF16)
        q_pos = (part * geo.groups + b) * rows + lax.broadcasted_iota(jnp.int32, (rows, 1), 0)
        q_seg = segment_from(q_pos, starts)
        results = []
        for h in range(PAIR):
            mask = first_head if h == 0 else jnp.logical_not(first_head)
            q_head = jnp.where(mask, query, jnp.zeros_like(query))

            def one(c, state):
                top, total, acc = state
                keys_at = pl.ds(pl.multiple_of(c * chunk, chunk), chunk)
                score = dot_nt(q_head, k_ref[keys_at, :])
                score = jnp.where(q_seg == seg_buf[:, keys_at], score, -1e30)
                peak = jnp.max(score, axis=1, keepdims=True)
                if top is not None:
                    peak = jnp.maximum(top, peak)
                weight = jnp.exp(score - peak)
                add = jnp.sum(weight, axis=1, keepdims=True)
                out = dot_nn(weight.astype(BF16), v_ref[keys_at, :])
                if top is not None:
                    fade = jnp.exp(top - peak)
                    add = add + total * fade
                    out = out + acc * fade
                return peak, add, out

            state = one(0, (None, None, None))
            if chunks > 1:
                state = lax.fori_loop(1, chunks, one, state)
            top, total, acc = state
            results.append((acc / total, top + jnp.log(total)))
        out = jnp.where(first_head, results[0][0], results[1][0])
        o_ref[inner, :] = out
        lse_ref[inner, :] = jnp.where(first_head, results[0][1], results[1][1])
        att_buf[b] = out.astype(BF16)

        @pl.when(b != g)
        def _():
            att_copy(b).start()

        return carry

    lax.fori_loop(0, geo.groups, attend, 0)
    for copy in flushes:
        copy.start()
    own_att = pltpu.make_async_copy(att_buf.at[g], att_ref.at[:, lanes], local_sem.at[0])
    own_att.start()

    def att_arrivals():
        for d in range(1, geo.groups):
            other = (g + d) % geo.groups
            cut = pl.ds(pl.multiple_of(other * LANES, LANES), LANES)
            pltpu.make_async_remote_copy(
                src_ref=att_ref.at[:, cut],
                dst_ref=att_ref.at[:, cut],
                send_sem=att_send.at[other],
                recv_sem=att_recv.at[other],
                device_id=(part * geo.groups + other, w),
                device_id_type=MESH,
            ).wait_recv()
        own_att.wait()

    if inside:
        for copy in loads:
            copy.wait()
        for name in LATER:
            setattr(r, name, getattr(r, name + "_buf"))
        layer_rest(geo, rank, r, starts, ends, id_ref, down_ref, up_ref, att_arrivals, complete, tick, loop_ticks, tick_count, len_ref.shape[1])
    else:
        att_arrivals()

    for copy in flushes:
        copy.wait()
    for d in range(1, geo.groups):
        att_copy((g + d) % geo.groups).wait_send()
    tok.wait_sends()
    for j in range(3):

        @pl.when(w < wt - 1)
        def _():
            slice_copy(j, w, True).wait_send()

        @pl.when(w > 0)
        def _():
            slice_copy(j, w, False).wait_send()

        for n in range(wt - 1):
            p = nth_plane(n)

            @pl.when((p < w) & (w < wt - 1))
            def _():
                slice_copy(j, p, True).wait_send()

            @pl.when((p > w) & (w > 0))
            def _():
                slice_copy(j, p, False).wait_send()

    for m in range(weight_count):
        @pl.when(w < wt - 1)
        def _():
            line_copy(m, w, True, True).wait_send()

        @pl.when(w > 0)
        def _():
            line_copy(m, w, False, True).wait_send()

    for m, j in units:
        p = nth_plane(j)

        @pl.when((p < w) & (w < wt - 1))
        def _():
            line_copy(m, p, True, False).wait_send()

        @pl.when((p > w) & (w > 0))
        def _():
            line_copy(m, p, False, False).wait_send()

        weight_spread(m, p).wait_sends()


def layer_rest(
    geo, rank, r, starts, ends, id_ref, down_ref, up_ref, att_arrivals, complete, tick, ticked, tick_count, docs
):
    s, w = lax.axis_index("seq"), lax.axis_index("wt")
    rows, width, groups = geo.rows, geo.width, geo.groups
    part, g = s // groups, s % groups
    hidden = r.full_fc1.shape[1]
    step = min(512, hidden)
    steps = hidden // step
    band = 2 * LANES
    bands = width // band
    lane_count = r.fc1_down.shape[0]
    out_rows = slice(3 * lane_count, 4 * lane_count)
    pos = s * rows + lax.broadcasted_iota(jnp.int32, (rows, LANES), 0)
    chosen = select_from(pos, starts, ends, id_ref, rank)

    every = placement(id_ref, docs, rank, lane_count)[0]
    doc_rows = docs * rank
    in_doc = (lax.broadcasted_iota(jnp.int32, (rows, LANES), 1) // rank) == segment_from(pos, starts)

    def masked(value):
        return (value * chosen).astype(BF16)

    def by_doc(low):
        return jnp.where(in_doc, dot_nn(low, every), 0.0).astype(BF16)

    def doc_grad(low_by_doc, value):
        return dot_tn(low_by_doc, value)[:doc_rows].astype(BF16)

    def at_step(i):
        return pl.ds(pl.multiple_of(i * step, step), step)

    def at_band(i):
        return pl.ds(pl.multiple_of(i * band, band), band)

    pending = list(range(ticked, tick_count))
    first_ticks, pending = pending[:1], pending[1:]
    for n in first_ticks:
        tick(n)
    att_arrivals()
    complete(0)
    att = r.att[...]
    small_out = masked(dot_nt(att, down_ref[out_rows, :]))

    def out_band(i, carry):
        cut = at_band(i)
        value = dot_nn(r.att[...], r.full_out[:, cut]) + r.out_bias[:, cut]
        value = value + dot_nn(small_out, up_ref[out_rows, cut])
        r.y[:, cut] = value + r.tok[s, :, cut].astype(F32)
        return carry

    lax.fori_loop(0, bands, out_band, 0)
    unit1, spread1 = normed(r.y[...])
    h1 = unit1 * r.gain1[...] + r.shift1[...]
    r.unit1[...] = unit1
    r.h1[...] = h1
    h1_low = h1.astype(BF16)
    r.h1_low[...] = h1_low
    small_fc1 = masked(dot_nt(h1_low, r.fc1_down[...]))

    middle = max(len(pending) - 3, 0)
    for n in pending[:middle]:
        tick(n)
    pending = pending[middle:]
    complete(1)

    def fc1_step(i, acc):
        for n, t in enumerate(pending):
            @pl.when(i == min(2 * n + 1, steps - 1))
            def _():
                tick(t)

        cut = at_step(i)
        pre = dot_nn(r.h1_low[...], r.full_fc1[:, cut]) + r.fc1_bias[:, cut]
        pre = pre + dot_nn(small_fc1, r.fc1_up[:, cut])
        share = 0.5 + 0.5 * erf(pre * 0.7071067811865476)
        act = (pre * share).astype(BF16)
        r.act[:, cut] = act
        r.slope[:, cut] = share + pre * (jnp.exp(-0.5 * pre * pre) * 0.3989422804014327)
        return acc + dot_nt(act, r.fc2_down[:, cut])

    small_fc2 = masked(lax.fori_loop(0, steps, fc1_step, jnp.zeros((rows, lane_count), F32)))
    complete(2)

    def fc2_band(i, carry):
        cut = at_band(i)
        value = dot_nn(r.act[...], r.full_fc2[:, cut]) + r.fc2_bias[:, cut]
        r.y[:, cut] = value + dot_nn(small_fc2, r.fc2_up[:, cut]) + r.h1[:, cut]
        return carry

    lax.fori_loop(0, bands, fc2_band, 0)
    unit2, spread2 = normed(r.y[...])
    r.output[...] = unit2 * r.gain2[...] + r.shift2[...]
    d_second = normed_back(r.cotangent[...].astype(F32), r.gain2[...], unit2, spread2)
    r.y[...] = d_second
    d_y = d_second.astype(BF16)
    low_fc2 = masked(dot_nt(d_y, r.fc2_up[...]))
    r.g_fc2_up[...] = doc_grad(by_doc(small_fc2), d_y)
    low_fc2_doc, small_fc1_doc = by_doc(low_fc2), by_doc(small_fc1)

    def back_step(i, acc):
        cut = at_step(i)
        d_act = dot_nt(d_y, r.full_fc2[cut, :]) + dot_nn(low_fc2, r.fc2_down[:, cut])
        d_pre = (d_act * r.slope[:, cut]).astype(BF16)
        r.d_pre[:, cut] = d_pre
        r.g_fc2_down[:, cut] = doc_grad(low_fc2_doc, r.act[:, cut])
        r.g_fc1_up[:, cut] = doc_grad(small_fc1_doc, d_pre)
        return acc + dot_nt(d_pre, r.fc1_up[:, cut])

    low_fc1 = masked(lax.fori_loop(0, steps, back_step, jnp.zeros((rows, lane_count), F32)))

    def make_early(chip, whose):
        return owner_columns((r.g_fc2_up, r.g_fc1_up, r.g_fc2_down), chip * 2 + whose, groups)

    early = PairSum(
        groups // 2,
        g // 2,
        s % 2,
        part * groups,
        w,
        (r.set_out, r.set_in, r.set_far),
        [r.set_sems.at[i] for i in range(4)],
        make_early,
    )
    early.run()
    r.g_fc1_down[...] = doc_grad(by_doc(low_fc1), r.h1_low[...])

    def back_band(i, carry):
        cut = at_band(i)
        value = dot_nt(r.d_pre[...], r.full_fc1[cut, :]) + dot_nn(low_fc1, r.fc1_down[:, cut])
        r.y[:, cut] += value
        return carry

    lax.fori_loop(0, bands, back_band, 0)
    d_first = normed_back(r.y[...], r.gain1[...], r.unit1[...], spread1)
    r.d_first[...] = d_first
    d_z = d_first.astype(BF16)
    low_out = masked(dot_nt(d_z, up_ref[out_rows, :]))

    def back_copy(b):
        return pltpu.make_async_remote_copy(
            src_ref=r.d_att_buf.at[b],
            dst_ref=r.d_heads.at[pl.ds(pl.multiple_of(g * rows, rows), rows)],
            send_sem=r.back_send.at[b],
            recv_sem=r.back_recv.at[g],
            device_id=(part * groups + b, w),
            device_id_type=MESH,
        )

    def attended_band(i, carry):
        n = (g // 2 + 1 + i) % bands
        cut = at_band(n)
        value = dot_nt(d_z, r.full_out[cut, :]) + dot_nn(low_out, down_ref[out_rows, cut])
        value = value.astype(BF16)
        for h in range(2):
            b = 2 * n + h
            r.d_att_buf[b] = value[:, h * LANES : (h + 1) * LANES]

            @pl.when(b != g)
            def _():
                back_copy(b).start()

        return carry

    lax.fori_loop(0, bands, attended_band, 0)
    own = pltpu.make_async_copy(
        r.d_att_buf.at[g], r.d_heads.at[pl.ds(pl.multiple_of(g * rows, rows), rows)], r.local_sem.at[0]
    )
    own.start()
    r.g_out_down[...] = doc_grad(by_doc(low_out), r.att[...])
    r.g_out_up[...] = doc_grad(by_doc(small_out), d_z)
    r.early_sum[...] = early.finish().astype(BF16)
    early.drain()
    for d in range(1, groups):
        other = (g + d) % groups
        here = r.d_heads.at[pl.ds(pl.multiple_of(other * rows, rows), rows)]
        pltpu.make_async_remote_copy(
            src_ref=here,
            dst_ref=here,
            send_sem=r.back_send.at[other],
            recv_sem=r.back_recv.at[other],
            device_id=(part * groups + other, w),
            device_id_type=MESH,
        ).wait_recv()
        back_copy(other).wait_send()
    own.wait()


def forward_attention(geo, rank, lengths, ids, tokens, w_qkv, down, up, bias, mlp):
    rows, width = geo.rows, geo.width
    inside = mlp is not None
    mlp = mlp or ()
    any_spec = pl.BlockSpec(memory_space=pl.ANY)
    vmem = pl.BlockSpec(memory_space=pltpu.VMEM)
    smem = pl.BlockSpec(memory_space=pltpu.SMEM)
    lane_count = down.shape[0] // 4
    struct = jax.ShapeDtypeStruct
    shapes = [
        struct((geo.queries, LANES), BF16),
        struct((geo.keys, LANES), BF16),
        struct((geo.keys, LANES), BF16),
        struct((geo.queries, LANES), F32),
        struct((geo.queries, LANES), F32),
        struct((width, 3 * LANES), BF16),
        struct((geo.keys, 3 * LANES), BF16),
    ]
    specs = [any_spec] * 7
    dma = pltpu.SemaphoreType.DMA
    count = 3 if inside else 0
    units = 1 + count * geo.wt
    scratch = [
        pltpu.VMEM((geo.seq, rows, width), BF16),
        pltpu.VMEM((1, geo.keys), jnp.int32),
        pltpu.VMEM((geo.groups, rows, LANES), BF16),
        dma((4 + count,)),
        dma((Spread.KINDS, units)),
        dma((Spread.KINDS, units)),
        dma((2, 3, geo.wt)),
        dma((3, geo.wt)),
        dma((2, max(count, 1) * geo.wt)),
        dma((max(count, 1) * geo.wt,)),
        dma((geo.groups,)),
        dma((geo.groups,)),
    ]
    scratch += [pltpu.VMEM(v.shape, v.dtype) for v in shapes] + [dma((len(shapes),))]
    if inside:
        hidden = mlp[1].shape[1]
        doc_rows = lengths.shape[1] * rank
        early = (width + 2 * hidden) // geo.groups
        near = geo.groups // 2
        shapes += [
            struct((rows, width), F32),
            struct((rows, width), F32),
            struct((geo.queries, LANES), BF16),
            struct((doc_rows, width), BF16),
            struct((doc_rows, width), BF16),
            struct((doc_rows, width), BF16),
            struct((doc_rows, early), BF16),
        ]
        specs += [vmem, vmem, any_spec] + [vmem] * 4
        scratch += [
            pltpu.VMEM((rows, width), BF16),
            pltpu.VMEM((width, width), BF16),
            pltpu.VMEM((width, hidden), BF16),
            pltpu.VMEM((hidden, width), BF16),
            pltpu.VMEM((rows, width), F32),
            pltpu.VMEM((rows, width), F32),
            pltpu.VMEM((rows, width), BF16),
            pltpu.VMEM((rows, hidden), BF16),
            pltpu.VMEM((rows, hidden), F32),
            pltpu.VMEM((rows, hidden), BF16),
            pltpu.VMEM((rows, width), F32),
            pltpu.VMEM((geo.groups, rows, LANES), BF16),
            dma((geo.groups,)),
            dma((geo.groups,)),
            pltpu.VMEM((doc_rows, width), BF16),
            pltpu.VMEM((doc_rows, hidden), BF16),
            pltpu.VMEM((doc_rows, hidden), BF16),
            pltpu.VMEM((near, doc_rows, early), BF16),
            pltpu.VMEM((near, doc_rows, early), BF16),
            pltpu.VMEM((near, doc_rows, early), BF16),
            dma((4, near)),
            dma((len(LATER),)),
        ]
        scratch += [pltpu.VMEM(v.shape, v.dtype) for name, v in zip(MLP_INPUTS, mlp) if name in LATER]
    else:
        shapes += [struct((rows, width), BF16)]
        specs += [any_spec]
    return pl.pallas_call(
        functools.partial(forward_kernel, geo, inside, rank),
        out_shape=shapes,
        in_specs=[smem, smem, any_spec, any_spec, vmem, vmem, vmem] + [
            any_spec if i < count or name in LATER else vmem for i, name in enumerate(MLP_INPUTS[: len(mlp)])
        ],
        out_specs=specs,
        scratch_shapes=scratch,
        compiler_params=pltpu.CompilerParams(
            collective_id=0, has_side_effects=True, vmem_limit_bytes=VMEM_LIMIT
        ),
        name="layer",
    )(lengths, ids, tokens, w_qkv, down, up, bias, *mlp)


def backward_kernel(
    geo, len_ref, part_ref, q_ref, k_ref, v_ref, o_ref, lse_ref, g_ref, pass_ref, dq_ref, dk_ref, dv_ref, passed_ref,
    dk_acc, dv_acc, pass_buf, pass_sem,
):
    rows = min(512, geo.queries)
    block = min(512, geo.keys)
    part = part_ref[0, 0]
    scale = HEAD_DIM ** (-0.5)
    starts, ends = doc_bounds(len_ref)
    first_head = lax.broadcasted_iota(jnp.int32, (rows, LANES), 1) < HEAD_DIM
    fetch = pltpu.make_async_copy(pass_ref, pass_buf, pass_sem.at[0])
    store = pltpu.make_async_copy(pass_buf, passed_ref, pass_sem.at[1])
    fetch.start()
    dk_acc[...] = jnp.zeros_like(dk_acc)
    dv_acc[...] = jnp.zeros_like(dv_acc)

    def seg_of(position):
        seg = jnp.int32(0)
        for start in starts[1:]:
            seg = seg + (position >= start).astype(jnp.int32)
        return seg

    def pick(values, index):
        found = values[0]
        for i in range(1, len(values)):
            found = jnp.where(index == i, values[i], found)
        return found

    def both_heads(value):
        zero = jnp.zeros_like(value)
        return jnp.concatenate([jnp.where(first_head, value, zero), jnp.where(first_head, zero, value)], axis=0)

    def query_block(b, carry):
        at = pl.ds(pl.multiple_of(b * rows, rows), rows)
        origin = part * geo.queries + b * rows
        query = both_heads(q_ref[at, :] * jnp.asarray(scale, BF16))
        cot = both_heads(g_ref[at, :])
        scaled = cot * jnp.asarray(scale, BF16)
        lse = jnp.concatenate([lse_ref[at, h * HEAD_DIM : h * HEAD_DIM + 1] for h in range(PAIR)], axis=0)
        out = o_ref[at, :]
        dot = jnp.sum(scaled.astype(F32) * jnp.concatenate([out, out], axis=0), axis=1, keepdims=True)
        q_pos = origin + lax.broadcasted_iota(jnp.int32, (rows, 1), 0)
        q_seg = segment_from(q_pos, starts)
        q_seg = jnp.concatenate([q_seg, q_seg], axis=0)
        low = pick(starts, seg_of(origin)) // block
        high = (pick(ends, seg_of(origin + rows - 1)) + block - 1) // block

        def key_block(c, acc):
            keys_at = pl.ds(pl.multiple_of(c * block, block), block)
            key, value = k_ref[keys_at, :], v_ref[keys_at, :]
            k_pos = c * block + lax.broadcasted_iota(jnp.int32, (1, block), 1)
            score = jnp.where(q_seg == segment_from(k_pos, starts), dot_nt(query, key), -1e30)
            prob = jnp.exp(score - lse)
            raw = (prob * (dot_nt(scaled, value) - dot)).astype(BF16)
            dk_acc[keys_at, :] += dot_tn(raw, query)
            dv_acc[keys_at, :] += dot_tn(prob.astype(BF16), cot)
            return acc + dot_nn(raw, key)

        acc = lax.fori_loop(low, high, key_block, jnp.zeros((PAIR * rows, LANES), F32))
        dq_ref[at, :] = jnp.where(first_head, acc[:rows], acc[rows:]).astype(BF16)
        return carry

    query_block(0, 0)
    fetch.wait()
    store.start()
    lax.fori_loop(1, geo.queries // rows, query_block, 0)
    dk_ref[...] = (dk_acc[...] * HEAD_DIM**0.5).astype(BF16)
    dv_ref[...] = dv_acc[...].astype(BF16)
    store.wait()


def backward_attention(geo, lengths, part, q, k, v, o, lse, d_heads, output):
    any_spec = pl.BlockSpec(memory_space=pl.ANY)
    smem = pl.BlockSpec(memory_space=pltpu.SMEM)
    vmem = pl.BlockSpec(memory_space=pltpu.VMEM)
    return pl.pallas_call(
        functools.partial(backward_kernel, geo),
        out_shape=[
            jax.ShapeDtypeStruct((geo.queries, LANES), BF16),
            jax.ShapeDtypeStruct((geo.keys, LANES), BF16),
            jax.ShapeDtypeStruct((geo.keys, LANES), BF16),
            jax.ShapeDtypeStruct(output.shape, F32),
        ],
        in_specs=[smem, smem] + [vmem] * 6 + [any_spec],
        out_specs=[vmem] * 3 + [any_spec],
        scratch_shapes=[pltpu.VMEM((geo.keys, LANES), F32)] * 2
        + [pltpu.VMEM(output.shape, F32), pltpu.SemaphoreType.DMA((2,))],
        compiler_params=pltpu.CompilerParams(vmem_limit_bytes=VMEM_LIMIT),
        name="attend_back",
    )(lengths, part, q, k, v, o, lse, d_heads, output)


class Block:
    def __init__(self, geo):
        chips = geo.groups // 2
        self.nx = min(geo.nx, chips)
        self.ny = chips // self.nx


class PairSum:
    def __init__(self, count, me, core, first, w, bufs, sems, make, stage=None):
        self.count, self.me, self.core, self.first, self.w = count, me, core, first, w
        self.near_out, self.near_in, self.far_in = bufs
        self.near_send, self.near_recv, self.far_send, self.far_recv = sems
        self.make = make
        self.slots = self.near_out.shape[0]
        self.stage = stage

    def slot(self, chip):
        return ((chip + self.count - self.me + self.count - 1) % self.count) % self.slots

    def near(self, chip):
        return pltpu.make_async_remote_copy(
            src_ref=self.near_out.at[self.slot(chip)],
            dst_ref=self.near_in.at[chip],
            send_sem=self.near_send.at[chip],
            recv_sem=self.near_recv.at[chip],
            device_id=(self.first + self.me * 2 + 1 - self.core, self.w),
            device_id_type=MESH,
        )

    def far(self, chip):
        return pltpu.make_async_remote_copy(
            src_ref=self.near_in.at[chip],
            dst_ref=self.far_in.at[self.me],
            send_sem=self.far_send.at[chip],
            recv_sem=self.far_recv.at[self.me],
            device_id=(self.first + chip * 2 + self.core, self.w),
            device_id_type=MESH,
        )

    def far_arrival(self, chip):
        return pltpu.make_async_remote_copy(
            src_ref=self.far_in.at[chip],
            dst_ref=self.far_in.at[chip],
            send_sem=self.far_send.at[chip],
            recv_sem=self.far_recv.at[chip],
            device_id=(self.first + chip * 2 + self.core, self.w),
            device_id_type=MESH,
        )

    def run(self):
        def start(d):
            chip = (self.me + 1 + d) % self.count
            if self.slots < self.count:

                @pl.when(d >= self.slots)
                def _():
                    self.near((self.me + 1 + d - self.slots) % self.count).wait_send()

            self.near_out[d % self.slots] = self.make(chip, 1 - self.core).astype(BF16)
            self.near(chip).start()

        def send(d):
            chip = (self.me + 1 + d) % self.count
            own = self.make(chip, self.core)
            self.near(chip).wait_recv()
            self.near_in[chip] = (own + self.near_in[chip].astype(F32)).astype(BF16)
            self.far(chip).start()

        def step(d, carry):
            start(d)
            send(d - 1)
            return carry

        start(0)
        lax.fori_loop(1, self.count, step, 0)

    def finish(self):
        total = self.make(self.me, self.core)
        self.near(self.me).wait_recv()
        total = total + self.near_in[self.me].astype(F32)
        if self.stage is None:
            for d in range(1, self.count):
                chip = (self.me + d) % self.count
                self.far_arrival(chip).wait_recv()
                total = total + self.far_in[chip].astype(F32)
            return total
        stage, sem = self.stage

        def fetch(d):
            chip = (self.me + d) % self.count
            return pltpu.make_async_copy(self.far_in.at[chip], stage.at[d % 2], sem.at[d % 2])

        self.far_arrival((self.me + 1) % self.count).wait_recv()
        fetch(1).start()
        for d in range(1, self.count):
            if d + 1 < self.count:
                self.far_arrival((self.me + d + 1) % self.count).wait_recv()
                fetch(d + 1).start()
            fetch(d).wait()
            total = total + stage[d % 2].astype(F32)
        return total

    def drain(self):
        for d in range(self.count):
            chip = (self.me + 1 + d) % self.count
            if d >= self.count - self.slots:
                self.near(chip).wait_send()
            if d < self.count - 1:
                self.far(chip).wait_send()


class CrossSum(PairSum):
    def with_corner(self, via, via_send, via_recv):
        self.via, self.via_send, self.via_recv = via, via_send, via_recv
        x, y = self.me % 2, self.me // 2
        self.near_chips = [y * 2 + 1 - x, (1 - y) * 2 + x]
        self.corner = (1 - y) * 2 + 1 - x
        self.half = self.near_in.shape[1] // 2
        return self

    def part(self, ref, h):
        return ref.at[pl.ds(h * self.half, self.half)]

    def device(self, chip):
        return (self.first + chip * 2 + self.core, self.w)

    def corner_copy(self, h):
        return pltpu.make_async_remote_copy(
            src_ref=self.part(self.near_in.at[self.corner], h),
            dst_ref=self.via.at[h],
            send_sem=self.via_send.at[h],
            recv_sem=self.via_recv.at[h],
            device_id=self.device(self.near_chips[h]),
            device_id_type=MESH,
        )

    def near_copy(self, which, h):
        chip = self.near_chips[which]
        return pltpu.make_async_remote_copy(
            src_ref=self.part(self.near_in.at[chip], h),
            dst_ref=self.part(self.far_in.at[self.me], h),
            send_sem=self.far_send.at[which * 2 + h],
            recv_sem=self.far_recv.at[which * 2 + h],
            device_id=self.device(chip),
            device_id_type=MESH,
        )

    def near_arrival(self, which, h):
        here = self.part(self.far_in.at[self.near_chips[which]], h)
        return pltpu.make_async_remote_copy(
            src_ref=here,
            dst_ref=here,
            send_sem=self.far_send.at[which * 2 + h],
            recv_sem=self.far_recv.at[which * 2 + h],
            device_id=self.device(self.near_chips[which]),
            device_id_type=MESH,
        )

    def run(self):
        order = [self.corner] + self.near_chips + [self.me]

        def chip_at(d):
            chip = order[0]
            for i in range(1, len(order)):
                chip = jnp.where(d == i, order[i], chip)
            return chip

        def start(d):
            chip = chip_at(d)
            self.near_out[chip] = self.make(chip, 1 - self.core).astype(BF16)
            self.near(chip).start()

        start(0)

        def step(d, carry):
            start(d)
            chip = chip_at(d - 1)
            own = self.make(chip, self.core)
            self.near(chip).wait_recv()
            self.near_in[chip] = (own + self.near_in[chip].astype(F32)).astype(BF16)

            @pl.when(d == 1)
            def _():
                self.corner_copy(0).start()
                self.corner_copy(1).start()

            @pl.when(d == 2)
            def _():
                self.near_copy(0, 0).start()

            @pl.when(d == 3)
            def _():
                self.near_copy(1, 1).start()

            return carry

        lax.fori_loop(1, len(order), step, 0)
        for which in range(2):
            h = 1 - which
            self.corner_copy(h).wait_recv()
            chip = self.near_chips[which]
            rows = pl.ds(h * self.half, self.half)
            self.near_in[chip, rows, :] = (
                self.near_in[chip, rows, :].astype(F32) + self.via[h].astype(F32)
            ).astype(BF16)
            self.near_copy(which, h).start()

    def slot(self, chip):
        return chip

    def finish(self):
        stage, sem = self.stage
        total = self.make(self.me, self.core)
        self.near(self.me).wait_recv()
        total = total + self.near_in[self.me].astype(F32)
        fetches = []
        for which in range(2):
            for h in range(2):
                self.near_arrival(which, h).wait_recv()
            fetches.append(
                pltpu.make_async_copy(self.far_in.at[self.near_chips[which]], stage.at[which], sem.at[which])
            )
            fetches[-1].start()
        for which in range(2):
            fetches[which].wait()
            total = total + stage[which].astype(F32)
        return total

    def drain(self):
        for chip in [self.corner] + self.near_chips + [self.me]:
            self.near(chip).wait_send()
        for h in range(2):
            self.corner_copy(h).wait_send()
            for which in range(2):
                self.near_copy(which, h).wait_send()


def closing_kernel(
    geo,
    rank,
    single_count,
    early,
    len_ref,
    id_ref,
    tokens_ref,
    first_ref,
    dq_ref,
    dk_ref,
    dv_ref,
    slice_ref,
    down_ref,
    up_ref,
    small_ref,
    *refs,
):
    singles = refs[:single_count]
    early_ref = refs[single_count] if early else None
    (
        grad_ref,
        sum1_ref,
        sum2_ref,
        tok_far,
        tok_out,
        tok_in,
        tok_stage,
        small_buf,
        set1_out,
        set1_in,
        set1_far,
        set2_out,
        set2_in,
        set2_far,
        down_acc,
        up_acc,
        mine1,
        mine2,
        place_buf,
        fold_buf,
        all1,
        all2,
        places,
        done1,
        done2,
        tok_sems,
        set1_sems,
        set2_sems,
        line_send,
        line_recv,
        spread_send,
        spread_recv,
        local_sem,
        stage_sem,
        small_sem,
        tok_via,
        via_sems,
    ) = refs[single_count + early :]
    x, y, core, w = device_here(geo)
    s = lax.axis_index("seq")
    rows, width, wt, groups, parts = geo.rows, geo.width, geo.wt, geo.groups, geo.parts
    part, g = s // groups, s % groups
    docs = len_ref.shape[1]
    doc_rows = docs * rank
    lane_count = down_ref.shape[0] // 4
    lanes = pl.ds(pl.multiple_of(g * LANES, LANES), LANES)
    starts, ends = doc_bounds(len_ref)
    greet_all(geo)

    def iota(shape, dim):
        return lax.broadcasted_iota(jnp.int32, shape, dim)

    def zero_one(condition):
        return jnp.where(condition, 1.0, 0.0).astype(BF16)

    def chosen_of(t):
        pos = t * rows + iota((rows, LANES), 0)
        return select_from(pos, starts, ends, id_ref, rank)

    def fold(j):
        a, b = iota((lane_count, LANES), 0), iota((lane_count, LANES), 1)
        return zero_one((b >= j * rank) & (b < (j + 1) * rank) & (a % rank == b - j * rank))

    def make_tokens(chip, whose):
        t = chip * 2 + whose
        at = pl.ds(pl.multiple_of(t * rows, rows), rows)
        if parts == 1:
            d_q = dq_ref[at, :]
        else:
            inner = pl.ds(pl.multiple_of((t % groups) * rows, rows), rows)
            d_q = jnp.where(t // groups == part, dq_ref[inner, :], jnp.zeros((rows, LANES), BF16))
        pieces = [d_q, dk_ref[at, :], dv_ref[at, :]]
        chosen = chosen_of(t)
        total = jnp.zeros((rows, width), F32)
        low = jnp.zeros((rows, LANES), F32)
        for j in range(3):
            total = total + dot_nt(pieces[j], slice_ref[:, j * LANES : (j + 1) * LANES])
            part_low = dot_nt(pieces[j], up_ref[pl.ds(j * lane_count, lane_count), lanes])
            low = low + dot_nn((part_low * chosen).astype(BF16), fold(j))
        return jnp.concatenate([total, low], axis=1)

    square = geo.nx == 2 and geo.ny == 2
    tok = (CrossSum if square else PairSum)(
        geo.seq // 2, s // 2, core, 0, w, (tok_out, tok_in, tok_far), [tok_sems.at[i] for i in range(4)], make_tokens,
        (tok_stage, stage_sem),
    )
    if square:
        tok.with_corner(tok_via, via_sems.at[0], via_sems.at[1])

    def by_document(value):
        return dot_tn(fold_buf[...], value)[:doc_rows]

    def make_set1(chip, whose):
        return owner_columns(singles, chip * 2 + whose, groups)

    def make_set2(chip, whose):
        owner = chip * 2 + whose
        cut = pl.ds(pl.multiple_of(owner * LANES, LANES), LANES)
        return jnp.concatenate([down_acc[j * doc_rows : (j + 1) * doc_rows, cut] for j in range(3)], axis=1)

    chips = groups // 2
    set1 = PairSum(
        chips, g // 2, core, part * groups, w, (set1_out, set1_in, set1_far), [set1_sems.at[i] for i in range(4)], make_set1
    )
    set2 = PairSum(
        chips, g // 2, core, part * groups, w, (set2_out, set2_in, set2_far), [set2_sems.at[i] for i in range(4)], make_set2
    )

    def peer(n):
        plane = (w + n) % wt
        other = (part + n // wt) % parts
        return other * groups + g, plane, other * wt + plane

    mine_at = part * wt + w

    late = set1_out.shape[2]
    front = late + 3 * LANES
    whole = mine1.shape[1]

    def cut_of(kind, ref):
        if kind == 0:
            return ref.at[:, pl.ds(0, front)]
        if kind == 3:
            return ref.at[:, pl.ds(front, whole - front)]
        return ref

    def line_copy(kind, n, src, dst_all):
        device, plane, _ = peer(n)
        return pltpu.make_async_remote_copy(
            src_ref=cut_of(kind, src),
            dst_ref=cut_of(kind, dst_all.at[mine_at]),
            send_sem=line_send.at[kind, n],
            recv_sem=line_recv.at[kind, mine_at],
            device_id=(device, plane),
            device_id_type=MESH,
        )

    def line_arrival(kind, n, dst_all):
        device, plane, at = peer(n)
        return pltpu.make_async_remote_copy(
            src_ref=cut_of(kind, dst_all.at[at]),
            dst_ref=cut_of(kind, dst_all.at[at]),
            send_sem=line_send.at[kind, n],
            recv_sem=line_recv.at[kind, at],
            device_id=(device, plane),
            device_id_type=MESH,
        )

    peers = range(1, wt * parts)

    block = Block(geo)
    chip_here = g // 2
    here = (chip_here % block.nx, chip_here // block.nx, core, w)

    def region_of(ref):
        def region(ux, uy, whose, half):
            one = ref.at[(uy * block.nx + ux) * 2 + whose]
            if half is None:
                return one
            return one.at[pl.ds(half * (lane_count // 2), lane_count // 2)]

        return region

    spreads = [
        Spread(block, here, region_of(ref), spread_send, spread_recv, i, part * groups)
        for i, ref in enumerate((sum1_ref, sum2_ref))
    ]
    finals = [done1, done2]
    outs = [sum1_ref, sum2_ref]

    def place(kind, mine, dst_all):
        total = dot_nn(place_buf[:, :doc_rows], mine[...])
        for n in peers:
            line_arrival(kind, n, dst_all).wait_recv()
            if kind == 0:
                line_arrival(2, n, places).wait_recv()
                if early:
                    line_arrival(3, n, dst_all).wait_recv()
            at = peer(n)[2]
            total = total + dot_nn(places[at][:, :doc_rows], dst_all[at])
        finals[kind][...] = total.astype(BF16)
        for way in (0, 1, 4):
            spreads[kind].go(way, own=finals[kind])
        pltpu.make_async_copy(finals[kind], outs[kind].at[g], local_sem.at[kind]).start()

    def pass_on(kind):
        spread = spreads[kind]
        spread.wait(0)
        spread.go(2)
        spread.go(5)
        spread.wait(1)
        spread.go(3)
        spread.go(6)

    def pass_last(kind):
        spread = spreads[kind]
        spread.wait(2)
        spread.go(7)
        spread.wait(3)
        spread.go(8)

    place_buf[...], fold_buf[...] = placement(id_ref, docs, rank, lane_count)
    for n in peers:
        line_copy(2, n, place_buf, places).start()
    if early:
        mine1[:, front:] = early_ref[...]
        for n in peers:
            line_copy(3, n, mine1, all1).start()

    set1.run()
    tok.run()

    def small_copy(t):
        return pltpu.make_async_copy(
            small_ref.at[pl.ds(pl.multiple_of(t * rows, rows), rows)], small_buf.at[t % 2], small_sem.at[t % 2]
        )

    def add_up(t, carry):
        at = pl.ds(pl.multiple_of(t * rows, rows), rows)

        @pl.when(t + 1 < geo.seq)
        def _():
            small_copy(t + 1).start()

        small_copy(t).wait()
        for j in range(3):
            cut = slice(j * LANES, (j + 1) * LANES)
            if j == 0:
                if parts == 1:
                    value = dq_ref[at, :]
                else:
                    inner = pl.ds(pl.multiple_of((t % groups) * rows, rows), rows)
                    value = jnp.where(t // groups == part, dq_ref[inner, :], jnp.zeros((rows, LANES), BF16))
            else:
                value = (dk_ref if j == 1 else dv_ref)[at, :]
            up_acc[cut, :] += dot_tn(small_buf[t % 2][:, cut], value)
        return carry

    up_acc[...] = jnp.zeros_like(up_acc)
    small_copy(0).start()
    lax.fori_loop(0, geo.seq, add_up, 0)

    for j in range(3):
        mine1[:, late + j * LANES : late + (j + 1) * LANES] = by_document(
            up_acc[j * lane_count : (j + 1) * lane_count, :].astype(BF16)
        ).astype(BF16)
    mine1[:, :late] = set1.finish().astype(BF16)
    for n in peers:
        line_copy(0, n, mine1, all1).start()

    total = tok.finish()
    low = total[:, width:].astype(BF16)
    total = total[:, :width] + first_ref[...]
    chosen = chosen_of(s)
    pos = s * rows + iota((rows, doc_rows), 0)
    doc_of = iota((rows, doc_rows), 1) // rank
    in_doc = doc_of == segment_from(pos, starts)
    tokens = tokens_ref[...]
    for j in range(3):
        a, b = iota((LANES, lane_count), 0), iota((LANES, lane_count), 1)
        widen = zero_one((a >= j * rank) & (a < (j + 1) * rank) & (b % rank == a - j * rank))
        wide = (dot_nn(low, widen) * chosen).astype(BF16)
        total = total + dot_nn(wide, down_ref[j * lane_count : (j + 1) * lane_count, :])
        by_doc = dot_nn(low, widen[:, :doc_rows])
        by_doc = jnp.where(in_doc, by_doc, 0.0).astype(BF16)
        down_acc[j * doc_rows : (j + 1) * doc_rows, :] = dot_tn(by_doc, tokens)
    set2.run()
    grad_ref[...] = total
    place(0, mine1, all1)
    mine2[...] = set2.finish().astype(BF16)
    for n in peers:
        line_copy(1, n, mine2, all2).start()
    pass_on(0)
    place(1, mine2, all2)
    pass_last(0)
    pass_on(1)
    pass_last(1)
    for kind in range(2):
        for way in range(4, 9):
            spreads[kind].wait(way)
        spreads[kind].wait_sends()
        pltpu.make_async_copy(finals[kind], outs[kind].at[g], local_sem.at[kind]).wait()
    for n in peers:
        line_copy(0, n, mine1, all1).wait_send()
        line_copy(1, n, mine2, all2).wait_send()
        line_copy(2, n, place_buf, places).wait_send()
        if early:
            line_copy(3, n, mine1, all1).wait_send()
    tok.drain()
    set1.drain()
    set2.drain()


def greet_all(geo):
    s, w = lax.axis_index("seq"), lax.axis_index("wt")
    barrier = pltpu.get_barrier_semaphore()
    part, g = s // geo.groups, s % geo.groups
    for d in range(1, geo.seq):
        pl.semaphore_signal(barrier, inc=1, device_id=((s + d) % geo.seq, w), device_id_type=MESH)
    count = geo.seq - 1
    for d in range(1, geo.wt):
        for q in range(geo.parts):
            other = ((part + q) % geo.parts) * geo.groups + g
            pl.semaphore_signal(barrier, inc=1, device_id=(other, (w + d) % geo.wt), device_id_type=MESH)
            count += 1
    pl.semaphore_wait(barrier, count)


def closing(geo, rank, lengths, ids, tokens, d_first, dq, dk, dv, w_slice, down, up, small, grads, early_sum):
    rows, width = geo.rows, geo.width
    docs = lengths.shape[1]
    doc_rows = docs * rank
    lane_count = down.shape[0] // 4
    early = [] if early_sum is None else [early_sum]
    late = sum(v.shape[1] for v in grads) // geo.groups
    set1 = late + 3 * LANES + sum(v.shape[1] for v in early)
    set2 = 3 * LANES
    chips, near = geo.seq // 2, geo.groups // 2
    peers = geo.wt * geo.parts
    smem = pl.BlockSpec(memory_space=pltpu.SMEM)
    vmem = pl.BlockSpec(memory_space=pltpu.VMEM)
    any_spec = pl.BlockSpec(memory_space=pl.ANY)
    dma = pltpu.SemaphoreType.DMA
    wide = width + LANES
    return pl.pallas_call(
        functools.partial(closing_kernel, geo, rank, len(grads), len(early)),
        out_shape=[
            jax.ShapeDtypeStruct((rows, width), F32),
            jax.ShapeDtypeStruct((geo.groups, lane_count, set1), BF16),
            jax.ShapeDtypeStruct((geo.groups, lane_count, set2), BF16),
            jax.ShapeDtypeStruct((chips, rows, wide), BF16),
        ],
        in_specs=[smem, smem] + [vmem] * 8 + [any_spec] + [vmem] * (len(grads) + len(early)),
        out_specs=[vmem, any_spec, any_spec, any_spec],
        scratch_shapes=[
            pltpu.VMEM((min(chips, 4), rows, wide), BF16),
            pltpu.VMEM((chips, rows, wide), BF16),
            pltpu.VMEM((2, rows, wide), BF16),
            pltpu.VMEM((2, rows, 3 * lane_count), BF16),
            pltpu.VMEM((near, doc_rows, late), BF16),
            pltpu.VMEM((near, doc_rows, late), BF16),
            pltpu.VMEM((near, doc_rows, late), BF16),
            pltpu.VMEM((near, doc_rows, 3 * LANES), BF16),
            pltpu.VMEM((near, doc_rows, 3 * LANES), BF16),
            pltpu.VMEM((near, doc_rows, 3 * LANES), BF16),
            pltpu.VMEM((3 * doc_rows, width), F32),
            pltpu.VMEM((3 * lane_count, LANES), F32),
            pltpu.VMEM((doc_rows, set1), BF16),
            pltpu.VMEM((doc_rows, set2), BF16),
            pltpu.VMEM((lane_count, LANES), BF16),
            pltpu.VMEM((lane_count, LANES), BF16),
            pltpu.VMEM((peers, doc_rows, set1), BF16),
            pltpu.VMEM((peers, doc_rows, set2), BF16),
            pltpu.VMEM((peers, lane_count, LANES), BF16),
            pltpu.VMEM((lane_count, set1), BF16),
            pltpu.VMEM((lane_count, set2), BF16),
            dma((4, chips)),
            dma((4, near)),
            dma((4, near)),
            dma((4, peers)),
            dma((4, peers)),
            dma((Spread.KINDS, 2)),
            dma((Spread.KINDS, 2)),
            dma((2,)),
            dma((2,)),
            dma((2,)),
            pltpu.VMEM((2, rows // 2, wide) if chips == 4 else (1, 16, LANES), BF16),
            dma((2, 2)),
        ],
        compiler_params=pltpu.CompilerParams(
            collective_id=1, has_side_effects=True, vmem_limit_bytes=VMEM_LIMIT
        ),
        name="close",
    )(lengths, ids, tokens, d_first, dq, dk, dv, w_slice, down, up, small, *grads, *early)


def unpack_kernel(
    late, one_ref, two_ref, grad_ref, down_ref, up_ref, fc1_down_ref, fc2_up_ref, fc1_up_ref, fc2_down_ref, passed_ref
):
    passed_ref[...] = grad_ref[...]
    count = one_ref.shape[0]
    for i in range(count):
        for j in range(3):
            down_ref[j, :, i * LANES : (i + 1) * LANES] = two_ref[i, :, j * LANES : (j + 1) * LANES].astype(F32)
        singles = [down_ref.at[3], up_ref.at[3], fc1_down_ref, fc2_up_ref, fc1_up_ref, fc2_down_ref]
        at = 0
        for ref in singles[:late] + [up_ref.at[j] for j in range(3)] + singles[late:]:
            wide = ref.shape[1] // count
            ref[:, i * wide : (i + 1) * wide] = one_ref[i, :, at : at + wide].astype(F32)
            at += wide


def unpack(geo, one, two, grad, lane_count, late):
    groups = geo.groups
    thick = (one.shape[2] - 7 * LANES) // 2
    count = 2
    steps = groups // count

    def whole(wide):
        return jax.ShapeDtypeStruct((lane_count, wide * groups), F32)

    def flat(wide):
        return pl.BlockSpec((lane_count, count * wide), lambda i: (0, i))

    four = jax.ShapeDtypeStruct((4, lane_count, LANES * groups), F32)
    four_spec = pl.BlockSpec((4, lane_count, count * LANES), lambda i: (0, 0, i))
    grad_spec = pl.BlockSpec((grad.shape[0] // steps, grad.shape[1]), lambda i: (i, 0))
    return pl.pallas_call(
        functools.partial(unpack_kernel, late),
        grid=(steps,),
        out_shape=[
            four, four, whole(LANES), whole(LANES), whole(thick), whole(thick), jax.ShapeDtypeStruct(grad.shape, F32)
        ],
        in_specs=[
            pl.BlockSpec((count,) + one.shape[1:], lambda i: (i, 0, 0)),
            pl.BlockSpec((count,) + two.shape[1:], lambda i: (i, 0, 0)),
            grad_spec,
        ],
        out_specs=[four_spec, four_spec, flat(LANES), flat(LANES), flat(thick), flat(thick), grad_spec],
        compiler_params=pltpu.CompilerParams(vmem_limit_bytes=VMEM_LIMIT),
        name="unpack",
    )(one, two, grad)


def layer_norm(value, gain, shift):
    mean = jnp.mean(value, axis=-1, keepdims=True)
    centred = value - mean
    spread = jnp.mean(centred * centred, axis=-1, keepdims=True)
    return centred * lax.rsqrt(spread + 1e-05) * gain + shift


def gelu_exact(value):
    return jax.nn.gelu(value, approximate=False)


def times_transposed(grad, weight):
    return lax.dot_general(
        grad, weight, (((1,), (1,)), ((), ())), preferred_element_type=jnp.float32
    )


def left_inner(left, right):
    return lax.dot_general(
        left, right, (((0,), (0,)), ((), ())), preferred_element_type=jnp.float32
    )


def stack_down(down):
    return jnp.transpose(down, (1, 0, 2)).reshape(down.shape[1], down.shape[0] * down.shape[2])


def stack_up(up):
    return up.reshape(up.shape[0] * up.shape[1], up.shape[2])


def unstack_down(stacked, adapter_count, rank_size):
    return jnp.transpose(stacked.reshape(stacked.shape[0], adapter_count, rank_size), (1, 0, 2))


def unstack_up(stacked, adapter_count, rank_size):
    return stacked.reshape(adapter_count, rank_size, stacked.shape[1])


def segment_of(positions, starts):
    return jnp.sum((positions[:, None] >= starts[None, :]).astype(jnp.int32), axis=1) - 1


def select_local(tok_rows, lane_count, rank_size, lengths, ids):
    starts = jnp.cumsum(lengths) - lengths
    local_pos = lax.axis_index("seq") * tok_rows + jnp.arange(tok_rows, dtype=jnp.int32)
    local_seg = segment_of(local_pos, starts)
    doc_range = jnp.arange(lengths.shape[0], dtype=jnp.int32)
    chosen = jnp.sum(jnp.where(local_seg[:, None] == doc_range[None, :], ids[None, :], 0), axis=1)
    lane_owner = jnp.arange(lane_count, dtype=jnp.int32) // rank_size
    lane_rank = jnp.arange(lane_count, dtype=jnp.int32) % rank_size
    doc_owner = jnp.repeat(doc_range, rank_size)
    doc_rank = jnp.arange(doc_owner.shape[0], dtype=jnp.int32) % rank_size
    to_doc = (lane_owner[:, None] == jnp.repeat(ids, rank_size)[None, :]) & (lane_rank[:, None] == doc_rank[None, :])
    return (
        (chosen[:, None] == lane_owner[None, :]).astype(jnp.float32),
        to_doc.astype(jnp.bfloat16),
        (local_seg[:, None] == doc_owner[None, :]).astype(jnp.float32),
    )


def feed_forward(
    geo, tokens, cotangent, attended_tok, weights, vectors, attn_maps, fc1_maps, fc2_maps, select
):
    tok_rows, model_width = tokens.shape
    full_out, full_fc1, full_fc2 = [lax.all_gather(v, "wt", axis=0, tiled=True) for v in weights]
    out_bias, norm1_gain, norm1_bias, fc1_bias, fc2_bias, norm2_gain, norm2_bias = vectors
    out_down, out_up = attn_maps
    fc1_down_all, fc1_up_all = fc1_maps
    fc2_down_all, fc2_up_all = fc2_maps
    select, to_doc, in_doc = select

    def by_doc(low):
        return (jnp.dot(low, to_doc, preferred_element_type=jnp.float32) * in_doc).astype(jnp.bfloat16)

    out_main = jnp.dot(attended_tok, full_out, preferred_element_type=jnp.float32)
    small_out = (
        jnp.dot(attended_tok, out_down, preferred_element_type=jnp.float32) * select
    ).astype(jnp.bfloat16)
    z_value = out_main + out_bias + jnp.dot(small_out, out_up, preferred_element_type=jnp.float32)
    first_sum = tokens.astype(jnp.float32) + z_value
    first_norm, norm1_back = jax.vjp(
        lambda value: layer_norm(value, norm1_gain, norm1_bias), first_sum
    )
    first_low = first_norm.astype(jnp.bfloat16)
    fc1_main = jnp.dot(first_low, full_fc1, preferred_element_type=jnp.float32)
    small_fc1 = (
        jnp.dot(first_low, fc1_down_all, preferred_element_type=jnp.float32) * select
    ).astype(jnp.bfloat16)
    pre_act = (
        fc1_main + fc1_bias + jnp.dot(small_fc1, fc1_up_all, preferred_element_type=jnp.float32)
    )
    act_value, gelu_back = jax.vjp(gelu_exact, pre_act)
    act_low = act_value.astype(jnp.bfloat16)
    fc2_main = jnp.dot(act_low, full_fc2, preferred_element_type=jnp.float32)
    small_fc2 = (
        jnp.dot(act_low, fc2_down_all, preferred_element_type=jnp.float32) * select
    ).astype(jnp.bfloat16)
    y_value = (
        fc2_main + fc2_bias + jnp.dot(small_fc2, fc2_up_all, preferred_element_type=jnp.float32)
    )
    output, norm2_back = jax.vjp(
        lambda value: layer_norm(value, norm2_gain, norm2_bias), first_norm + y_value
    )
    d_second = norm2_back(cotangent.astype(jnp.float32))[0]
    d_y = d_second.astype(jnp.bfloat16)
    d_act = times_transposed(d_y, full_fc2)
    low_fc2 = (times_transposed(d_y, fc2_up_all) * select).astype(jnp.bfloat16)
    d_act = d_act + times_transposed(low_fc2, fc2_down_all)
    grad_fc2_up = left_inner(by_doc(small_fc2), d_y)
    grad_fc2_down = left_inner(by_doc(low_fc2), act_low)
    d_pre = gelu_back(d_act)[0].astype(jnp.bfloat16)
    d_first_low = times_transposed(d_pre, full_fc1)
    low_fc1 = (times_transposed(d_pre, fc1_up_all) * select).astype(jnp.bfloat16)
    d_first_low = d_first_low + times_transposed(low_fc1, fc1_down_all)
    grad_fc1_up = left_inner(by_doc(small_fc1), d_pre)
    grad_fc1_down = left_inner(by_doc(low_fc1), first_low)
    d_first = norm1_back(d_second + d_first_low)[0]
    d_z = d_first.astype(jnp.bfloat16)
    d_attended = times_transposed(d_z, full_out)
    low_out = (times_transposed(d_z, out_up) * select).astype(jnp.bfloat16)
    d_attended = (d_attended + times_transposed(low_out, out_down)).astype(jnp.bfloat16)
    grad_out_up = left_inner(by_doc(small_out), d_z)
    grad_out_down = left_inner(by_doc(low_out), attended_tok)
    blocks = [
        [p * geo.groups + i for i in range(geo.groups)] for p in range(geo.parts)
    ]
    d_heads = lax.all_to_all(
        d_attended.reshape(tok_rows, geo.groups, LANES),
        "seq",
        split_axis=1,
        concat_axis=0,
        axis_index_groups=blocks,
        tiled=True,
    ).reshape(geo.queries, LANES)
    grads = [grad_out_down, grad_out_up, grad_fc1_down, grad_fc2_up, grad_fc1_up, grad_fc2_down]
    return output, d_first, d_heads, [v.astype(BF16) for v in grads]


def shards(
    tokens,
    cotangent,
    w_qkv,
    qv_bias,
    w_out,
    out_bias,
    norm1_gain,
    norm1_bias,
    w_fc1,
    fc1_bias,
    w_fc2,
    fc2_bias,
    norm2_gain,
    norm2_bias,
    doc_lengths,
    adapter_ids,
    attn_down,
    attn_up,
    fc1_down,
    fc1_up,
    fc2_down,
    fc2_up,
):
    tok_rows, model_width = tokens.shape
    adapter_count = attn_down.shape[1]
    rank_size = attn_down.shape[3]
    lane_count = adapter_count * rank_size
    seq_count = lax.axis_size("seq")
    geo = Geometry(tok_rows, model_width)
    part_index = lax.axis_index("seq") // geo.groups
    down_rows = jnp.transpose(attn_down, (0, 1, 3, 2)).reshape(4 * lane_count, model_width)
    up_rows = attn_up.reshape(4 * lane_count, model_width)
    weights = (w_out, w_fc1, w_fc2)
    vectors = (out_bias, norm1_gain, norm1_bias, fc1_bias, fc2_bias, norm2_gain, norm2_bias)

    def rows_of(down):
        return jnp.swapaxes(down, 1, 2).reshape(lane_count, down.shape[1])

    inside = all(v.shape[0] % (32 * seq_count) == 0 for v in weights)
    mlp = None
    if inside:
        mlp = (
            weights
            + (cotangent,)
            + tuple(v.reshape(1, -1) for v in vectors)
            + (rows_of(fc1_down), stack_up(fc1_up), rows_of(fc2_down), stack_up(fc2_up))
        )
    q_heads, k_heads, v_heads, o_heads, lse_heads, w_slice, small_all, *rest = forward_attention(
        geo, rank_size, doc_lengths, adapter_ids, tokens, w_qkv, down_rows, up_rows, qv_bias, mlp
    )
    if inside:
        output, d_first, d_heads, *set1, early_sum = rest
    else:
        early_sum = None
        output, d_first, d_heads, set1 = feed_forward(
            geo,
            tokens,
            cotangent,
            rest[0],
            weights,
            vectors,
            (stack_down(attn_down[3]), stack_up(attn_up[3])),
            (stack_down(fc1_down), stack_up(fc1_up)),
            (stack_down(fc2_down), stack_up(fc2_up)),
            select_local(tok_rows, lane_count, rank_size, doc_lengths[0], adapter_ids[0]),
        )
    d_q, d_k, d_v, output = backward_attention(
        geo, doc_lengths, part_index.reshape(1, 1), q_heads, k_heads, v_heads, o_heads, lse_heads, d_heads, output
    )
    input_grad, sum1, sum2, _ = closing(
        geo,
        rank_size,
        doc_lengths,
        adapter_ids,
        tokens,
        d_first,
        d_q,
        d_k,
        d_v,
        w_slice,
        down_rows,
        up_rows,
        small_all,
        set1,
        early_sum,
    )

    down4, up4, fc1_down_sum, fc2_up_sum, fc1_up_sum, fc2_down_sum, input_grad = unpack(
        geo, sum1, sum2, input_grad, lane_count, len(set1)
    )

    def as_up(rows):
        return rows.reshape(rows.shape[:-2] + (adapter_count, rank_size, rows.shape[-1]))

    def as_down(rows):
        return jnp.swapaxes(as_up(rows), -1, -2)

    return (
        output,
        input_grad,
        as_down(down4),
        as_up(up4),
        as_down(fc1_down_sum),
        as_up(fc1_up_sum),
        as_down(fc2_down_sum),
        as_up(fc2_up_sum),
    )


def solution(mesh):
    placed = (
        P(("wt", "seq"), None),
        P(("wt", "seq"), None),
        P("wt", None),
        P(),
        P("wt", None),
        P(),
        P(),
        P(),
        P("wt", None),
        P(),
        P("wt", None),
        P(),
        P(),
        P(),
        P("wt", None),
        P("wt", None),
        P(),
        P(),
        P(),
        P(),
        P(),
        P(),
    )
    return jax.shard_map(
        shards,
        mesh=mesh,
        in_specs=placed,
        out_specs=(P(("wt", "seq"), None), P(("wt", "seq"), None), P(), P(), P(), P(), P(), P()),
        check_vma=False,
    )
```

```python
import functools

import jax
import jax.numpy as jnp
from jax import lax
from jax.experimental import pallas as pl
from jax.experimental.pallas import tpu as pltpu
from jax.sharding import PartitionSpec as P

HEADS = 16
HEAD_DIM = 64
LANES = 128
PAIR = LANES // HEAD_DIM
MESH = pl.DeviceIdType.MESH
F32 = jnp.float32
BF16 = jnp.bfloat16
VMEM_LIMIT = 60 * 2**20


def dot_nn(a, b):
    return lax.dot_general(a, b, (((1,), (0,)), ((), ())), preferred_element_type=F32)


def dot_nt(a, b):
    return lax.dot_general(a, b, (((1,), (1,)), ((), ())), preferred_element_type=F32)


def dot_tn(a, b):
    return lax.dot_general(a, b, (((0,), (0,)), ((), ())), preferred_element_type=F32)


class Geometry:
    def __init__(self, rows, width):
        self.seq = lax.axis_size("seq")
        self.wt = lax.axis_size("wt")
        self.rows = rows
        self.width = width
        self.groups = width // LANES
        self.parts = self.seq // self.groups
        chips = self.seq // 2
        nx = 1
        while nx * nx < chips:
            nx *= 2
        self.nx = nx
        self.ny = chips // nx
        self.keys = self.seq * rows
        self.queries = self.groups * rows


def doc_bounds(len_ref):
    count = len_ref.shape[1]
    starts, ends = [], []
    at = jnp.int32(0)
    for i in range(count):
        starts.append(at)
        at = at + len_ref[0, i]
        ends.append(at)
    return starts, ends


def segment_from(positions, starts):
    seg = jnp.zeros_like(positions)
    for start in starts[1:]:
        seg = seg + (positions >= start).astype(jnp.int32)
    return seg


def select_from(positions, starts, ends, id_ref, rank):
    owner = lax.broadcasted_iota(jnp.int32, positions.shape, 1) // rank
    picked = jnp.zeros(positions.shape, F32)
    for i in range(len(starts)):
        inside = (positions >= starts[i]) & (positions < ends[i]) & (owner == id_ref[0, i])
        picked = jnp.where(inside, 1.0, picked)
    return picked


def placement(id_ref, docs, rank, lane_count):
    a = lax.broadcasted_iota(jnp.int32, (lane_count, LANES), 0)
    b = lax.broadcasted_iota(jnp.int32, (lane_count, LANES), 1)
    every = jnp.zeros((lane_count, LANES), F32)
    first = jnp.zeros((lane_count, LANES), F32)
    for d in range(docs):
        seen = jnp.bool_(False)
        for e in range(d):
            seen = seen | (id_ref[0, e] == id_ref[0, d])
        hit = (a // rank == id_ref[0, d]) & (b // rank == d) & (a % rank == b % rank)
        every = jnp.where(hit, 1.0, every)
        first = jnp.where(hit, jnp.where(seen, 0.0, 1.0), first)
    return every.astype(BF16), first.astype(BF16)


def owner_columns(refs, owner, groups):
    cols = []
    for ref in refs:
        wide = ref.shape[1] // groups
        cols.append(ref[:, pl.ds(pl.multiple_of(owner * wide, LANES), wide)])
    return jnp.concatenate(cols, axis=1).astype(F32)


class Spread:
    KINDS = 9

    def __init__(self, geo, here, region, send, recv, unit, first=0):
        self.geo, self.here, self.region = geo, here, region
        self.send, self.recv, self.unit, self.first = send, recv, unit, first

    def copy(self, kind, src, dst, x, y, core):
        return pltpu.make_async_remote_copy(
            src_ref=src,
            dst_ref=dst,
            send_sem=self.send.at[kind, self.unit],
            recv_sem=self.recv.at[kind, self.unit],
            device_id=(self.first + ((y * self.geo.nx) + x) * 2 + core, self.here[3]),
            device_id_type=MESH,
        )

    def others(self):
        nx, ny = self.geo.nx, self.geo.ny
        x, y, core, _ = self.here
        row = [((x + d) % nx, y) for d in range(1, nx)]
        col = [(x, (y + d) % ny) for d in range(1, ny)]
        return row, col

    def plan(self):
        x, y, core, _ = self.here
        row, col = self.others()
        plan = {kind: [] for kind in range(self.KINDS)}
        for tx, ty in row:
            plan[0].append(((x, y), None, (tx, ty, core)))
        for tx, ty in col:
            plan[1].append(((x, y), None, (tx, ty, core)))
        for ux, uy in row:
            for tx, ty in col:
                plan[2].append(((ux, uy), 0, (tx, ty, core)))
        for ux, uy in col:
            for tx, ty in row:
                plan[3].append(((ux, uy), 1, (tx, ty, core)))
        plan[4].append(((x, y), None, (x, y, 1 - core)))
        for ux, uy in row:
            plan[5].append(((ux, uy), None, (x, y, 1 - core)))
        for ux, uy in col:
            plan[6].append(((ux, uy), None, (x, y, 1 - core)))
        for ux, _ in row:
            for _, uy in col:
                plan[7].append(((ux, uy), 0, (x, y, 1 - core)))
                plan[8].append(((ux, uy), 1, (x, y, 1 - core)))
        return plan

    def go(self, kind, own=None):
        core = self.here[2]
        for (ux, uy), half, (tx, ty, tcore) in self.plan()[kind]:
            dst = self.region(ux, uy, core, half)
            src = dst if own is None else own
            self.copy(kind, src, dst, tx, ty, tcore).start()

    def arrivals(self, kind):
        x, y, core, _ = self.here
        row, col = self.others()
        if kind == 0:
            return [(u, None, core) for u in row]
        if kind == 1:
            return [(u, None, core) for u in col]
        if kind in (2, 3):
            return [((ux, uy), kind - 2, core) for ux, _ in row for _, uy in col]
        if kind == 4:
            return [((x, y), None, 1 - core)]
        if kind == 5:
            return [(u, None, 1 - core) for u in row]
        if kind == 6:
            return [(u, None, 1 - core) for u in col]
        return [((ux, uy), kind - 7, 1 - core) for ux, _ in row for _, uy in col]

    def wait(self, kind):
        x, y, core, _ = self.here
        for (ux, uy), half, whose in self.arrivals(kind):
            ref = self.region(ux, uy, whose, half)
            self.copy(kind, ref, ref, x, y, 1 - core).wait_recv()

    def wait_sends(self):
        x, y, core, _ = self.here
        for kind in range(self.KINDS):
            for (ux, uy), half, _ in self.plan()[kind]:
                ref = self.region(ux, uy, core, half)
                self.copy(kind, ref, ref, x, y, 1 - core).wait_send()


def device_here(geo):
    s = lax.axis_index("seq")
    core = s % 2
    chip = s // 2
    return chip % geo.nx, chip // geo.nx, core, lax.axis_index("wt")


def greet(geo):
    s, w = lax.axis_index("seq"), lax.axis_index("wt")
    barrier = pltpu.get_barrier_semaphore()
    for d in range(1, geo.seq):
        pl.semaphore_signal(barrier, inc=1, device_id=((s + d) % geo.seq, w), device_id_type=MESH)
    for d in range(1, geo.wt):
        pl.semaphore_signal(barrier, inc=1, device_id=(s, (w + d) % geo.wt), device_id_type=MESH)
    pl.semaphore_wait(barrier, geo.seq + geo.wt - 2)


def erf(v):
    v = jnp.clip(v, -3.832506856900711, 3.832506856900711)
    sq = v * v
    top = jnp.full_like(v, 0.00022905065861350646)
    for c in (0.0034082910107109506, 0.050955695062380861, 0.18520832239976145, 1.128379143519084):
        top = top * sq + c
    low = jnp.full_like(v, -1.1791602954361697e-7)
    for c in (0.000023547966471313185, 0.0010179625278914885, 0.014070470171167667, 0.11098505178285362, 0.49746925110067538, 1.0):
        low = low * sq + c
    return v * top / low


def normed(value):
    mean = jnp.mean(value, axis=1, keepdims=True)
    centred = value - mean
    spread = lax.rsqrt(jnp.mean(centred * centred, axis=1, keepdims=True) + 1e-05)
    return centred * spread, spread


def normed_back(grad, gain, unit, spread):
    g = grad * gain
    return spread * (
        g - jnp.mean(g, axis=1, keepdims=True) - unit * jnp.mean(g * unit, axis=1, keepdims=True)
    )


class Names:
    def __init__(self, names, refs):
        self.__dict__.update(zip(names, refs))


MLP_INPUTS = (
    "w_out", "w_fc1", "w_fc2", "cotangent", "out_bias", "gain1", "shift1", "fc1_bias", "fc2_bias", "gain2", "shift2",
    "fc1_down", "fc1_up", "fc2_down", "fc2_up",
)
BASE_OUTPUTS = ("q", "k", "v", "o", "lse", "w_slice", "small")
MLP_OUTPUTS = ("output", "d_first", "d_heads", "g_out_down", "g_out_up", "g_fc1_down", "early_sum")
BASE_SCRATCH = (
    "tok", "seg", "att_send_buf", "local_sem", "send_sem", "recv_sem", "slice_send", "slice_recv", "line_send",
    "line_recv", "att_send", "att_recv", "q_buf", "k_buf", "v_buf", "o_buf", "lse_buf", "slice_buf", "small_buf", "flush_sem",
)
LATER = ("cotangent", "fc1_down", "fc1_up", "fc2_down", "fc2_up")
MLP_SCRATCH = (
    "att", "full_out", "full_fc1", "full_fc2", "unit1", "h1", "h1_low", "act", "slope", "d_pre", "y", "d_att_buf",
    "back_send", "back_recv", "g_fc2_up", "g_fc1_up", "g_fc2_down", "set_out", "set_in", "set_far", "set_sems",
    "load_sem", "cotangent_buf", "fc1_down_buf", "fc1_up_buf", "fc2_down_buf", "fc2_up_buf",
)


def forward_kernel(geo, inside, rank, len_ref, id_ref, tokens_ref, wqkv_ref, down_ref, up_ref, bias_ref, *refs):
    in_names = MLP_INPUTS if inside else ()
    out_names = BASE_OUTPUTS + (MLP_OUTPUTS if inside else ("att",))
    scratch_names = BASE_SCRATCH + (MLP_SCRATCH if inside else ())
    r = Names(in_names + out_names + scratch_names, refs)
    weights_in = (r.w_out, r.w_fc1, r.w_fc2) if inside else ()
    weights_out = (r.full_out, r.full_fc1, r.full_fc2) if inside else ()
    weight_count = len(weights_in)
    att_ref, q_ref, k_ref, v_ref, o_ref, lse_ref, slice_ref, small_ref = (
        r.att, r.q_buf, r.k_buf, r.v_buf, r.o_buf, r.lse_buf, r.slice_buf, r.small_buf
    )
    results = [r.q, r.k, r.v, r.o, r.lse, r.w_slice, r.small]
    made = [q_ref, k_ref, v_ref, o_ref, lse_ref, slice_ref, small_ref]
    flushes = [pltpu.make_async_copy(made[i], results[i], r.flush_sem.at[i]) for i in range(len(made))]
    loads = []
    if inside:
        loads = [
            pltpu.make_async_copy(getattr(r, name), getattr(r, name + "_buf"), r.load_sem.at[i])
            for i, name in enumerate(LATER)
        ]
    tok_buf, seg_buf, att_buf, local_sem = r.tok, r.seg, r.att_send_buf, r.local_sem
    send_sem, recv_sem, slice_send, slice_recv = r.send_sem, r.recv_sem, r.slice_send, r.slice_recv
    line_send, line_recv, att_send, att_recv = r.line_send, r.line_recv, r.att_send, r.att_recv
    here = device_here(geo)
    x, y, core, w = here
    s = lax.axis_index("seq")
    part, g = s // geo.groups, s % geo.groups
    rows, width, wt = geo.rows, geo.width, geo.wt
    lanes = pl.ds(pl.multiple_of(g * LANES, LANES), LANES)

    own_tok = pltpu.make_async_copy(tokens_ref, tok_buf.at[s], local_sem.at[0])
    own_tok.start()
    shard = wqkv_ref.shape[0]
    own_slices = []
    for j in range(3):
        src = wqkv_ref.at[:, pl.ds(pl.multiple_of(j * width + g * LANES, LANES), LANES)]
        dst = slice_ref.at[pl.ds(pl.multiple_of(w * shard, shard), shard), pl.ds(j * LANES, LANES)]
        own_slices.append(pltpu.make_async_copy(src, dst, local_sem.at[1 + j]))
        own_slices[-1].start()
    own_weights = []
    for m in range(weight_count):
        height = weights_in[m].shape[0]
        dst = weights_out[m].at[pl.ds(pl.multiple_of(w * height, height), height)]
        own_weights.append(pltpu.make_async_copy(weights_in[m], dst, local_sem.at[4 + m]))
        own_weights[-1].start()

    greet(geo)

    def token_region(ux, uy, whose, half):
        block = tok_buf.at[(uy * geo.nx + ux) * 2 + whose]
        if half is None:
            return block
        return block.at[pl.ds(half * (rows // 2), rows // 2)]

    tok = Spread(geo, here, token_region, send_sem, recv_sem, 0)
    tok.go(0, own=tokens_ref)
    tok.go(1, own=tokens_ref)
    tok.go(4, own=tokens_ref)

    def slice_copy(j, p, up):
        dst = slice_ref.at[pl.ds(pl.multiple_of(p * shard, shard), shard), pl.ds(j * LANES, LANES)]
        return pltpu.make_async_remote_copy(
            src_ref=dst,
            dst_ref=dst,
            send_sem=slice_send.at[0 if up else 1, j, p],
            recv_sem=slice_recv.at[j, p],
            device_id=(s, (w + 1) % wt if up else (w + wt - 1) % wt),
            device_id_type=MESH,
        )

    for copy in loads:
        copy.start()

    starts, ends = doc_bounds(len_ref)
    seg_buf[...] = segment_from(lax.broadcasted_iota(jnp.int32, seg_buf.shape, 1), starts)

    seq = geo.seq
    mine = s

    def unit_rows(m, p, unit, half=None):
        height = weights_in[m].shape[0]
        piece = height // seq
        if half is None:
            return weights_out[m].at[pl.ds(pl.multiple_of(p * height + unit * piece, piece), piece)]
        piece = piece // 2
        return weights_out[m].at[
            pl.ds(pl.multiple_of(p * height + unit * 2 * piece + half * piece, piece), piece)
        ]

    def line_copy(m, p, up, own):
        height = weights_in[m].shape[0]
        piece = height // seq
        dst = unit_rows(m, p, mine)
        src = weights_in[m].at[pl.ds(pl.multiple_of(mine * piece, piece), piece)] if own else dst
        target = (w + 1) % wt if up else (w + wt - 1) % wt
        return pltpu.make_async_remote_copy(
            src_ref=src,
            dst_ref=dst,
            send_sem=line_send.at[0 if up else 1, m * wt + p],
            recv_sem=line_recv.at[m * wt + p],
            device_id=(s, target),
            device_id_type=MESH,
        )

    def nth_plane(j):
        below, above = w, wt - 1 - w
        both = jnp.minimum(below, above)
        in_turn = j < 2 * both
        dist = jnp.where(in_turn, j // 2 + 1, j - both + 1)
        from_below = jnp.where(in_turn, j % 2 == 0, below > above)
        return jnp.where(from_below, w - dist, w + dist)

    def weight_spread(m, p):
        def region(ux, uy, whose, half):
            return unit_rows(m, p, (uy * geo.nx + ux) * 2 + whose, half)

        return Spread(geo, here, region, send_sem, recv_sem, 1 + m * wt + p)

    units = []
    if inside:
        units = [(m, j) for j in range(wt - 1) for m in (0, 1)] + [(2, j) for j in range(wt - 1)]

    def start_lines(which):
        for m in which if inside else ():

            @pl.when(w < wt - 1)
            def _():
                line_copy(m, w, True, True).start()

            @pl.when(w > 0)
            def _():
                line_copy(m, w, False, True).start()

    def along(i):
        if i >= len(units):
            return
        m, j = units[i]
        p = nth_plane(j)
        line_copy(m, p, True, False).wait_recv()

        @pl.when((p < w) & (w < wt - 1))
        def _():
            line_copy(m, p, True, False).start()

        @pl.when((p > w) & (w > 0))
        def _():
            line_copy(m, p, False, False).start()

    def tick(i):
        if i == 0:
            along(0)
        if i == late_lines:
            start_lines((2,))
        if i < len(units):
            m, j = units[i]
            spread = weight_spread(m, nth_plane(j))
            spread.go(0)
            spread.go(1)
            spread.go(4)
        along(i + 1)
        if 0 <= i - 1 < len(units):
            m, j = units[i - 1]
            spread = weight_spread(m, nth_plane(j))
            spread.wait(0)
            spread.go(2)
            spread.go(5)
            spread.wait(1)
            spread.go(3)
            spread.go(6)
        if 0 <= i - 2 < len(units):
            m, j = units[i - 2]
            spread = weight_spread(m, nth_plane(j))
            spread.wait(2)
            spread.go(7)
            spread.wait(3)
            spread.go(8)

    tick_count = len(units) + 2 if units else 0
    late_lines = 1
    early_ticks = min(3, tick_count)
    loop_ticks = min(6, tick_count)

    def complete(m):
        own_weights[m].wait()
        for j in range(wt - 1):
            spread = weight_spread(m, nth_plane(j))
            for kind in range(4, 9):
                spread.wait(kind)

    for copy in own_slices:
        copy.wait()
    for j in range(3):

        @pl.when(w < wt - 1)
        def _():
            slice_copy(j, w, True).start()

        @pl.when(w > 0)
        def _():
            slice_copy(j, w, False).start()

    nx, ny = geo.nx, geo.ny
    row_n, col_n, diag_n = 2 * (nx - 1), 2 * (ny - 1), 2 * (nx - 1) * (ny - 1)

    def block_owner(i):
        r = i - 2
        c = r - row_n
        d = c - col_n
        dx_row, k_row = r % max(nx - 1, 1) + 1, r // max(nx - 1, 1)
        dy_col, k_col = c % max(ny - 1, 1) + 1, c // max(ny - 1, 1)
        half = max(diag_n // 2, 1)
        k_diag, in_diag = d // half, d % half
        dx_diag, dy_diag = in_diag % max(nx - 1, 1) + 1, in_diag // max(nx - 1, 1) + 1
        dx = jnp.where(i < 2, 0, jnp.where(i < 2 + row_n, dx_row, jnp.where(i < 2 + row_n + col_n, 0, dx_diag)))
        dy = jnp.where(i < 2 + row_n, 0, jnp.where(i < 2 + row_n + col_n, dy_col, dy_diag))
        kk = jnp.where(i < 2, i, jnp.where(i < 2 + row_n, k_row, jnp.where(i < 2 + row_n + col_n, k_col, k_diag)))
        return (((y + dy) % ny) * nx + (x + dx) % nx) * 2 + (core + kk) % 2

    def project(i, carry):
        @pl.when(i == 0)
        def _():
            for n in range(wt - 1):
                p = nth_plane(n)
                for j in range(3):
                    slice_copy(j, p, True).wait_recv()

                    @pl.when((p < w) & (w < wt - 1))
                    def _():
                        slice_copy(j, p, True).start()

                    @pl.when((p > w) & (w > 0))
                    def _():
                        slice_copy(j, p, False).start()

            start_lines((0, 1))
            own_tok.wait()

        @pl.when(i == 1)
        def _():
            tok.wait(4)

        @pl.when(i == 2)
        def _():
            tok.wait(0)
            tok.go(2)
            tok.go(5)
            tok.wait(1)
            tok.go(3)
            tok.go(6)

        @pl.when(i == 2 + row_n // 2)
        def _():
            tok.wait(5)

        @pl.when(i == 2 + row_n + col_n // 2)
        def _():
            tok.wait(6)

        @pl.when(i == 2 + row_n + col_n)
        def _():
            tok.wait(2)
            tok.go(7)
            tok.wait(3)
            tok.go(8)

        @pl.when(i == 2 + row_n + col_n + diag_n // 2)
        def _():
            tok.wait(7)
            tok.wait(8)

        for n in range(early_ticks):

            @pl.when(i == min(3 + 2 * n, geo.seq - 1))
            def _():
                tick(n)

        t = block_owner(i)
        block = tok_buf[t]
        at = pl.ds(pl.multiple_of(t * rows, rows), rows)
        pos = t * rows + lax.broadcasted_iota(jnp.int32, (rows, LANES), 0)
        chosen = select_from(pos, starts, ends, id_ref, rank)
        main = dot_nn(block, slice_ref[...])
        small = dot_nt(block, down_ref[: 3 * LANES, :])
        for j in range(3):
            cut = slice(j * LANES, (j + 1) * LANES)
            low = (small[:, cut] * chosen).astype(BF16)
            small_ref[at, cut] = low
            value = main[:, cut] + dot_nn(low, up_ref[cut, lanes])
            if j == 0:
                value = value + bias_ref[0:1, lanes]

                @pl.when(t // geo.groups == part)
                def _():
                    inner = pl.ds(pl.multiple_of((t % geo.groups) * rows, rows), rows)
                    q_ref[inner, :] = value.astype(BF16)
            elif j == 1:
                k_ref[at, :] = value.astype(BF16)
            else:
                v_ref[at, :] = (value + bias_ref[1:2, lanes]).astype(BF16)
        return carry

    lax.fori_loop(0, geo.seq, project, 0)

    scale = HEAD_DIM ** (-0.5)
    chunk = min(2048, geo.keys)
    chunks = geo.keys // chunk
    first_head = lax.broadcasted_iota(jnp.int32, (rows, LANES), 1) < HEAD_DIM

    def att_copy(b):
        return pltpu.make_async_remote_copy(
            src_ref=att_buf.at[b],
            dst_ref=att_ref.at[:, lanes],
            send_sem=att_send.at[b],
            recv_sem=att_recv.at[g],
            device_id=(part * geo.groups + b, w),
            device_id_type=MESH,
        )

    def attend(i, carry):
        for n in range(early_ticks, loop_ticks):

            @pl.when(i == 2 * (n - early_ticks) + 1)
            def _():
                tick(n)

        b = (g + 1 + i) % geo.groups
        inner = pl.ds(pl.multiple_of(b * rows, rows), rows)
        query = q_ref[inner, :] * jnp.asarray(scale, BF16)
        q_pos = (part * geo.groups + b) * rows + lax.broadcasted_iota(jnp.int32, (rows, 1), 0)
        q_seg = segment_from(q_pos, starts)
        results = []
        for h in range(PAIR):
            mask = first_head if h == 0 else jnp.logical_not(first_head)
            q_head = jnp.where(mask, query, jnp.zeros_like(query))

            def one(c, state):
                top, total, acc = state
                keys_at = pl.ds(pl.multiple_of(c * chunk, chunk), chunk)
                score = dot_nt(q_head, k_ref[keys_at, :])
                score = jnp.where(q_seg == seg_buf[:, keys_at], score, -1e30)
                peak = jnp.max(score, axis=1, keepdims=True)
                if top is not None:
                    peak = jnp.maximum(top, peak)
                weight = jnp.exp(score - peak)
                add = jnp.sum(weight, axis=1, keepdims=True)
                out = dot_nn(weight.astype(BF16), v_ref[keys_at, :])
                if top is not None:
                    fade = jnp.exp(top - peak)
                    add = add + total * fade
                    out = out + acc * fade
                return peak, add, out

            state = one(0, (None, None, None))
            if chunks > 1:
                state = lax.fori_loop(1, chunks, one, state)
            top, total, acc = state
            results.append((acc / total, top + jnp.log(total)))
        out = jnp.where(first_head, results[0][0], results[1][0])
        o_ref[inner, :] = out
        lse_ref[inner, :] = jnp.where(first_head, results[0][1], results[1][1])
        att_buf[b] = out.astype(BF16)

        @pl.when(b != g)
        def _():
            att_copy(b).start()

        return carry

    lax.fori_loop(0, geo.groups, attend, 0)
    for copy in flushes:
        copy.start()
    own_att = pltpu.make_async_copy(att_buf.at[g], att_ref.at[:, lanes], local_sem.at[0])
    own_att.start()

    def att_arrivals():
        for d in range(1, geo.groups):
            other = (g + d) % geo.groups
            cut = pl.ds(pl.multiple_of(other * LANES, LANES), LANES)
            pltpu.make_async_remote_copy(
                src_ref=att_ref.at[:, cut],
                dst_ref=att_ref.at[:, cut],
                send_sem=att_send.at[other],
                recv_sem=att_recv.at[other],
                device_id=(part * geo.groups + other, w),
                device_id_type=MESH,
            ).wait_recv()
        own_att.wait()

    if inside:
        for copy in loads:
            copy.wait()
        for name in LATER:
            setattr(r, name, getattr(r, name + "_buf"))
        layer_rest(geo, rank, r, starts, ends, id_ref, down_ref, up_ref, att_arrivals, complete, tick, loop_ticks, tick_count, len_ref.shape[1])
    else:
        att_arrivals()

    for copy in flushes:
        copy.wait()
    for d in range(1, geo.groups):
        att_copy((g + d) % geo.groups).wait_send()
    tok.wait_sends()
    for j in range(3):

        @pl.when(w < wt - 1)
        def _():
            slice_copy(j, w, True).wait_send()

        @pl.when(w > 0)
        def _():
            slice_copy(j, w, False).wait_send()

        for n in range(wt - 1):
            p = nth_plane(n)

            @pl.when((p < w) & (w < wt - 1))
            def _():
                slice_copy(j, p, True).wait_send()

            @pl.when((p > w) & (w > 0))
            def _():
                slice_copy(j, p, False).wait_send()

    for m in range(weight_count):
        @pl.when(w < wt - 1)
        def _():
            line_copy(m, w, True, True).wait_send()

        @pl.when(w > 0)
        def _():
            line_copy(m, w, False, True).wait_send()

    for m, j in units:
        p = nth_plane(j)

        @pl.when((p < w) & (w < wt - 1))
        def _():
            line_copy(m, p, True, False).wait_send()

        @pl.when((p > w) & (w > 0))
        def _():
            line_copy(m, p, False, False).wait_send()

        weight_spread(m, p).wait_sends()


def layer_rest(
    geo, rank, r, starts, ends, id_ref, down_ref, up_ref, att_arrivals, complete, tick, ticked, tick_count, docs
):
    s, w = lax.axis_index("seq"), lax.axis_index("wt")
    rows, width, groups = geo.rows, geo.width, geo.groups
    part, g = s // groups, s % groups
    hidden = r.full_fc1.shape[1]
    step = min(512, hidden)
    steps = hidden // step
    band = 2 * LANES
    bands = width // band
    lane_count = r.fc1_down.shape[0]
    out_rows = slice(3 * lane_count, 4 * lane_count)
    pos = s * rows + lax.broadcasted_iota(jnp.int32, (rows, LANES), 0)
    chosen = select_from(pos, starts, ends, id_ref, rank)

    every = placement(id_ref, docs, rank, lane_count)[0]
    doc_rows = docs * rank
    in_doc = (lax.broadcasted_iota(jnp.int32, (rows, LANES), 1) // rank) == segment_from(pos, starts)

    def masked(value):
        return (value * chosen).astype(BF16)

    def by_doc(low):
        return jnp.where(in_doc, dot_nn(low, every), 0.0).astype(BF16)

    def doc_grad(low_by_doc, value):
        return dot_tn(low_by_doc, value)[:doc_rows].astype(BF16)

    def at_step(i):
        return pl.ds(pl.multiple_of(i * step, step), step)

    def at_band(i):
        return pl.ds(pl.multiple_of(i * band, band), band)

    pending = list(range(ticked, tick_count))
    first_ticks, pending = pending[:1], pending[1:]
    for n in first_ticks:
        tick(n)
    att_arrivals()
    complete(0)
    att = r.att[...]
    small_out = masked(dot_nt(att, down_ref[out_rows, :]))

    def out_band(i, carry):
        cut = at_band(i)
        value = dot_nn(r.att[...], r.full_out[:, cut]) + r.out_bias[:, cut]
        value = value + dot_nn(small_out, up_ref[out_rows, cut])
        r.y[:, cut] = value + r.tok[s, :, cut].astype(F32)
        return carry

    lax.fori_loop(0, bands, out_band, 0)
    unit1, spread1 = normed(r.y[...])
    h1 = unit1 * r.gain1[...] + r.shift1[...]
    r.unit1[...] = unit1
    r.h1[...] = h1
    h1_low = h1.astype(BF16)
    r.h1_low[...] = h1_low
    small_fc1 = masked(dot_nt(h1_low, r.fc1_down[...]))

    middle = max(len(pending) - 3, 0)
    for n in pending[:middle]:
        tick(n)
    pending = pending[middle:]
    complete(1)

    def fc1_step(i, acc):
        for n, t in enumerate(pending):
            @pl.when(i == min(2 * n + 1, steps - 1))
            def _():
                tick(t)

        cut = at_step(i)
        pre = dot_nn(r.h1_low[...], r.full_fc1[:, cut]) + r.fc1_bias[:, cut]
        pre = pre + dot_nn(small_fc1, r.fc1_up[:, cut])
        share = 0.5 + 0.5 * erf(pre * 0.7071067811865476)
        act = (pre * share).astype(BF16)
        r.act[:, cut] = act
        r.slope[:, cut] = share + pre * (jnp.exp(-0.5 * pre * pre) * 0.3989422804014327)
        return acc + dot_nt(act, r.fc2_down[:, cut])

    small_fc2 = masked(lax.fori_loop(0, steps, fc1_step, jnp.zeros((rows, lane_count), F32)))
    complete(2)

    def fc2_band(i, carry):
        cut = at_band(i)
        value = dot_nn(r.act[...], r.full_fc2[:, cut]) + r.fc2_bias[:, cut]
        r.y[:, cut] = value + dot_nn(small_fc2, r.fc2_up[:, cut]) + r.h1[:, cut]
        return carry

    lax.fori_loop(0, bands, fc2_band, 0)
    unit2, spread2 = normed(r.y[...])
    r.output[...] = unit2 * r.gain2[...] + r.shift2[...]
    d_second = normed_back(r.cotangent[...].astype(F32), r.gain2[...], unit2, spread2)
    r.y[...] = d_second
    d_y = d_second.astype(BF16)
    low_fc2 = masked(dot_nt(d_y, r.fc2_up[...]))
    r.g_fc2_up[...] = doc_grad(by_doc(small_fc2), d_y)
    low_fc2_doc, small_fc1_doc = by_doc(low_fc2), by_doc(small_fc1)

    def back_step(i, acc):
        cut = at_step(i)
        d_act = dot_nt(d_y, r.full_fc2[cut, :]) + dot_nn(low_fc2, r.fc2_down[:, cut])
        d_pre = (d_act * r.slope[:, cut]).astype(BF16)
        r.d_pre[:, cut] = d_pre
        r.g_fc2_down[:, cut] = doc_grad(low_fc2_doc, r.act[:, cut])
        r.g_fc1_up[:, cut] = doc_grad(small_fc1_doc, d_pre)
        return acc + dot_nt(d_pre, r.fc1_up[:, cut])

    low_fc1 = masked(lax.fori_loop(0, steps, back_step, jnp.zeros((rows, lane_count), F32)))

    def make_early(chip, whose):
        return owner_columns((r.g_fc2_up, r.g_fc1_up, r.g_fc2_down), chip * 2 + whose, groups)

    early = PairSum(
        groups // 2,
        g // 2,
        s % 2,
        part * groups,
        w,
        (r.set_out, r.set_in, r.set_far),
        [r.set_sems.at[i] for i in range(4)],
        make_early,
    )
    early.run()
    r.g_fc1_down[...] = doc_grad(by_doc(low_fc1), r.h1_low[...])

    def back_band(i, carry):
        cut = at_band(i)
        value = dot_nt(r.d_pre[...], r.full_fc1[cut, :]) + dot_nn(low_fc1, r.fc1_down[:, cut])
        r.y[:, cut] += value
        return carry

    lax.fori_loop(0, bands, back_band, 0)
    d_first = normed_back(r.y[...], r.gain1[...], r.unit1[...], spread1)
    r.d_first[...] = d_first
    d_z = d_first.astype(BF16)
    low_out = masked(dot_nt(d_z, up_ref[out_rows, :]))

    def back_copy(b):
        return pltpu.make_async_remote_copy(
            src_ref=r.d_att_buf.at[b],
            dst_ref=r.d_heads.at[pl.ds(pl.multiple_of(g * rows, rows), rows)],
            send_sem=r.back_send.at[b],
            recv_sem=r.back_recv.at[g],
            device_id=(part * groups + b, w),
            device_id_type=MESH,
        )

    def attended_band(i, carry):
        n = (g // 2 + 1 + i) % bands
        cut = at_band(n)
        value = dot_nt(d_z, r.full_out[cut, :]) + dot_nn(low_out, down_ref[out_rows, cut])
        value = value.astype(BF16)
        for h in range(2):
            b = 2 * n + h
            r.d_att_buf[b] = value[:, h * LANES : (h + 1) * LANES]

            @pl.when(b != g)
            def _():
                back_copy(b).start()

        return carry

    lax.fori_loop(0, bands, attended_band, 0)
    own = pltpu.make_async_copy(
        r.d_att_buf.at[g], r.d_heads.at[pl.ds(pl.multiple_of(g * rows, rows), rows)], r.local_sem.at[0]
    )
    own.start()
    r.g_out_down[...] = doc_grad(by_doc(low_out), r.att[...])
    r.g_out_up[...] = doc_grad(by_doc(small_out), d_z)
    r.early_sum[...] = early.finish().astype(BF16)
    early.drain()
    for d in range(1, groups):
        other = (g + d) % groups
        here = r.d_heads.at[pl.ds(pl.multiple_of(other * rows, rows), rows)]
        pltpu.make_async_remote_copy(
            src_ref=here,
            dst_ref=here,
            send_sem=r.back_send.at[other],
            recv_sem=r.back_recv.at[other],
            device_id=(part * groups + other, w),
            device_id_type=MESH,
        ).wait_recv()
        back_copy(other).wait_send()
    own.wait()


def forward_attention(geo, rank, lengths, ids, tokens, w_qkv, down, up, bias, mlp):
    rows, width = geo.rows, geo.width
    inside = mlp is not None
    mlp = mlp or ()
    any_spec = pl.BlockSpec(memory_space=pl.ANY)
    vmem = pl.BlockSpec(memory_space=pltpu.VMEM)
    smem = pl.BlockSpec(memory_space=pltpu.SMEM)
    lane_count = down.shape[0] // 4
    struct = jax.ShapeDtypeStruct
    shapes = [
        struct((geo.queries, LANES), BF16),
        struct((geo.keys, LANES), BF16),
        struct((geo.keys, LANES), BF16),
        struct((geo.queries, LANES), F32),
        struct((geo.queries, LANES), F32),
        struct((width, 3 * LANES), BF16),
        struct((geo.keys, 3 * LANES), BF16),
    ]
    specs = [any_spec] * 7
    dma = pltpu.SemaphoreType.DMA
    count = 3 if inside else 0
    units = 1 + count * geo.wt
    scratch = [
        pltpu.VMEM((geo.seq, rows, width), BF16),
        pltpu.VMEM((1, geo.keys), jnp.int32),
        pltpu.VMEM((geo.groups, rows, LANES), BF16),
        dma((4 + count,)),
        dma((Spread.KINDS, units)),
        dma((Spread.KINDS, units)),
        dma((2, 3, geo.wt)),
        dma((3, geo.wt)),
        dma((2, max(count, 1) * geo.wt)),
        dma((max(count, 1) * geo.wt,)),
        dma((geo.groups,)),
        dma((geo.groups,)),
    ]
    scratch += [pltpu.VMEM(v.shape, v.dtype) for v in shapes] + [dma((len(shapes),))]
    if inside:
        hidden = mlp[1].shape[1]
        doc_rows = lengths.shape[1] * rank
        early = (width + 2 * hidden) // geo.groups
        near = geo.groups // 2
        shapes += [
            struct((rows, width), F32),
            struct((rows, width), F32),
            struct((geo.queries, LANES), BF16),
            struct((doc_rows, width), BF16),
            struct((doc_rows, width), BF16),
            struct((doc_rows, width), BF16),
            struct((doc_rows, early), BF16),
        ]
        specs += [vmem, vmem, any_spec] + [vmem] * 4
        scratch += [
            pltpu.VMEM((rows, width), BF16),
            pltpu.VMEM((width, width), BF16),
            pltpu.VMEM((width, hidden), BF16),
            pltpu.VMEM((hidden, width), BF16),
            pltpu.VMEM((rows, width), F32),
            pltpu.VMEM((rows, width), F32),
            pltpu.VMEM((rows, width), BF16),
            pltpu.VMEM((rows, hidden), BF16),
            pltpu.VMEM((rows, hidden), F32),
            pltpu.VMEM((rows, hidden), BF16),
            pltpu.VMEM((rows, width), F32),
            pltpu.VMEM((geo.groups, rows, LANES), BF16),
            dma((geo.groups,)),
            dma((geo.groups,)),
            pltpu.VMEM((doc_rows, width), BF16),
            pltpu.VMEM((doc_rows, hidden), BF16),
            pltpu.VMEM((doc_rows, hidden), BF16),
            pltpu.VMEM((near, doc_rows, early), BF16),
            pltpu.VMEM((near, doc_rows, early), BF16),
            pltpu.VMEM((near, doc_rows, early), BF16),
            dma((4, near)),
            dma((len(LATER),)),
        ]
        scratch += [pltpu.VMEM(v.shape, v.dtype) for name, v in zip(MLP_INPUTS, mlp) if name in LATER]
    else:
        shapes += [struct((rows, width), BF16)]
        specs += [any_spec]
    return pl.pallas_call(
        functools.partial(forward_kernel, geo, inside, rank),
        out_shape=shapes,
        in_specs=[smem, smem, any_spec, any_spec, vmem, vmem, vmem] + [
            any_spec if i < count or name in LATER else vmem for i, name in enumerate(MLP_INPUTS[: len(mlp)])
        ],
        out_specs=specs,
        scratch_shapes=scratch,
        compiler_params=pltpu.CompilerParams(
            collective_id=0, has_side_effects=True, vmem_limit_bytes=VMEM_LIMIT
        ),
        name="layer",
    )(lengths, ids, tokens, w_qkv, down, up, bias, *mlp)


def backward_kernel(
    geo, len_ref, part_ref, q_ref, k_ref, v_ref, o_ref, lse_ref, g_ref, pass_ref, dq_ref, dk_ref, dv_ref, passed_ref,
    dk_acc, dv_acc, pass_buf, pass_sem,
):
    rows = min(512, geo.queries)
    block = min(512, geo.keys)
    part = part_ref[0, 0]
    scale = HEAD_DIM ** (-0.5)
    starts, ends = doc_bounds(len_ref)
    first_head = lax.broadcasted_iota(jnp.int32, (rows, LANES), 1) < HEAD_DIM
    fetch = pltpu.make_async_copy(pass_ref, pass_buf, pass_sem.at[0])
    store = pltpu.make_async_copy(pass_buf, passed_ref, pass_sem.at[1])
    fetch.start()
    dk_acc[...] = jnp.zeros_like(dk_acc)
    dv_acc[...] = jnp.zeros_like(dv_acc)

    def seg_of(position):
        seg = jnp.int32(0)
        for start in starts[1:]:
            seg = seg + (position >= start).astype(jnp.int32)
        return seg

    def pick(values, index):
        found = values[0]
        for i in range(1, len(values)):
            found = jnp.where(index == i, values[i], found)
        return found

    def both_heads(value):
        zero = jnp.zeros_like(value)
        return jnp.concatenate([jnp.where(first_head, value, zero), jnp.where(first_head, zero, value)], axis=0)

    def query_block(b, carry):
        at = pl.ds(pl.multiple_of(b * rows, rows), rows)
        origin = part * geo.queries + b * rows
        query = both_heads(q_ref[at, :] * jnp.asarray(scale, BF16))
        cot = both_heads(g_ref[at, :])
        scaled = cot * jnp.asarray(scale, BF16)
        lse = jnp.concatenate([lse_ref[at, h * HEAD_DIM : h * HEAD_DIM + 1] for h in range(PAIR)], axis=0)
        out = o_ref[at, :]
        dot = jnp.sum(scaled.astype(F32) * jnp.concatenate([out, out], axis=0), axis=1, keepdims=True)
        q_pos = origin + lax.broadcasted_iota(jnp.int32, (rows, 1), 0)
        q_seg = segment_from(q_pos, starts)
        q_seg = jnp.concatenate([q_seg, q_seg], axis=0)
        low = pick(starts, seg_of(origin)) // block
        high = (pick(ends, seg_of(origin + rows - 1)) + block - 1) // block

        def key_block(c, acc):
            keys_at = pl.ds(pl.multiple_of(c * block, block), block)
            key, value = k_ref[keys_at, :], v_ref[keys_at, :]
            k_pos = c * block + lax.broadcasted_iota(jnp.int32, (1, block), 1)
            score = jnp.where(q_seg == segment_from(k_pos, starts), dot_nt(query, key), -1e30)
            prob = jnp.exp(score - lse)
            raw = (prob * (dot_nt(scaled, value) - dot)).astype(BF16)
            dk_acc[keys_at, :] += dot_tn(raw, query)
            dv_acc[keys_at, :] += dot_tn(prob.astype(BF16), cot)
            return acc + dot_nn(raw, key)

        acc = lax.fori_loop(low, high, key_block, jnp.zeros((PAIR * rows, LANES), F32))
        dq_ref[at, :] = jnp.where(first_head, acc[:rows], acc[rows:]).astype(BF16)
        return carry

    query_block(0, 0)
    fetch.wait()
    store.start()
    lax.fori_loop(1, geo.queries // rows, query_block, 0)
    dk_ref[...] = (dk_acc[...] * HEAD_DIM**0.5).astype(BF16)
    dv_ref[...] = dv_acc[...].astype(BF16)
    store.wait()


def backward_attention(geo, lengths, part, q, k, v, o, lse, d_heads, output):
    any_spec = pl.BlockSpec(memory_space=pl.ANY)
    smem = pl.BlockSpec(memory_space=pltpu.SMEM)
    vmem = pl.BlockSpec(memory_space=pltpu.VMEM)
    return pl.pallas_call(
        functools.partial(backward_kernel, geo),
        out_shape=[
            jax.ShapeDtypeStruct((geo.queries, LANES), BF16),
            jax.ShapeDtypeStruct((geo.keys, LANES), BF16),
            jax.ShapeDtypeStruct((geo.keys, LANES), BF16),
            jax.ShapeDtypeStruct(output.shape, F32),
        ],
        in_specs=[smem, smem] + [vmem] * 6 + [any_spec],
        out_specs=[vmem] * 3 + [any_spec],
        scratch_shapes=[pltpu.VMEM((geo.keys, LANES), F32)] * 2
        + [pltpu.VMEM(output.shape, F32), pltpu.SemaphoreType.DMA((2,))],
        compiler_params=pltpu.CompilerParams(vmem_limit_bytes=VMEM_LIMIT),
        name="attend_back",
    )(lengths, part, q, k, v, o, lse, d_heads, output)


class Block:
    def __init__(self, geo):
        chips = geo.groups // 2
        self.nx = min(geo.nx, chips)
        self.ny = chips // self.nx


class PairSum:
    def __init__(self, count, me, core, first, w, bufs, sems, make, stage=None):
        self.count, self.me, self.core, self.first, self.w = count, me, core, first, w
        self.near_out, self.near_in, self.far_in = bufs
        self.near_send, self.near_recv, self.far_send, self.far_recv = sems
        self.make = make
        self.slots = self.near_out.shape[0]
        self.stage = stage

    def slot(self, chip):
        return ((chip + self.count - self.me + self.count - 1) % self.count) % self.slots

    def near(self, chip):
        return pltpu.make_async_remote_copy(
            src_ref=self.near_out.at[self.slot(chip)],
            dst_ref=self.near_in.at[chip],
            send_sem=self.near_send.at[chip],
            recv_sem=self.near_recv.at[chip],
            device_id=(self.first + self.me * 2 + 1 - self.core, self.w),
            device_id_type=MESH,
        )

    def far(self, chip):
        return pltpu.make_async_remote_copy(
            src_ref=self.near_in.at[chip],
            dst_ref=self.far_in.at[self.me],
            send_sem=self.far_send.at[chip],
            recv_sem=self.far_recv.at[self.me],
            device_id=(self.first + chip * 2 + self.core, self.w),
            device_id_type=MESH,
        )

    def far_arrival(self, chip):
        return pltpu.make_async_remote_copy(
            src_ref=self.far_in.at[chip],
            dst_ref=self.far_in.at[chip],
            send_sem=self.far_send.at[chip],
            recv_sem=self.far_recv.at[chip],
            device_id=(self.first + chip * 2 + self.core, self.w),
            device_id_type=MESH,
        )

    def run(self):
        def start(d):
            chip = (self.me + 1 + d) % self.count
            if self.slots < self.count:

                @pl.when(d >= self.slots)
                def _():
                    self.near((self.me + 1 + d - self.slots) % self.count).wait_send()

            self.near_out[d % self.slots] = self.make(chip, 1 - self.core).astype(BF16)
            self.near(chip).start()

        def send(d):
            chip = (self.me + 1 + d) % self.count
            own = self.make(chip, self.core)
            self.near(chip).wait_recv()
            self.near_in[chip] = (own + self.near_in[chip].astype(F32)).astype(BF16)
            self.far(chip).start()

        def step(d, carry):
            start(d)
            send(d - 1)
            return carry

        start(0)
        lax.fori_loop(1, self.count, step, 0)

    def finish(self):
        total = self.make(self.me, self.core)
        self.near(self.me).wait_recv()
        total = total + self.near_in[self.me].astype(F32)
        if self.stage is None:
            for d in range(1, self.count):
                chip = (self.me + d) % self.count
                self.far_arrival(chip).wait_recv()
                total = total + self.far_in[chip].astype(F32)
            return total
        stage, sem = self.stage

        def fetch(d):
            chip = (self.me + d) % self.count
            return pltpu.make_async_copy(self.far_in.at[chip], stage.at[d % 2], sem.at[d % 2])

        self.far_arrival((self.me + 1) % self.count).wait_recv()
        fetch(1).start()
        for d in range(1, self.count):
            if d + 1 < self.count:
                self.far_arrival((self.me + d + 1) % self.count).wait_recv()
                fetch(d + 1).start()
            fetch(d).wait()
            total = total + stage[d % 2].astype(F32)
        return total

    def drain(self):
        for d in range(self.count):
            chip = (self.me + 1 + d) % self.count
            if d >= self.count - self.slots:
                self.near(chip).wait_send()
            if d < self.count - 1:
                self.far(chip).wait_send()


class CrossSum(PairSum):
    def with_corner(self, via, via_send, via_recv):
        self.via, self.via_send, self.via_recv = via, via_send, via_recv
        x, y = self.me % 2, self.me // 2
        self.near_chips = [y * 2 + 1 - x, (1 - y) * 2 + x]
        self.corner = (1 - y) * 2 + 1 - x
        self.half = self.near_in.shape[1] // 2
        return self

    def part(self, ref, h):
        return ref.at[pl.ds(h * self.half, self.half)]

    def device(self, chip):
        return (self.first + chip * 2 + self.core, self.w)

    def corner_copy(self, h):
        return pltpu.make_async_remote_copy(
            src_ref=self.part(self.near_in.at[self.corner], h),
            dst_ref=self.via.at[h],
            send_sem=self.via_send.at[h],
            recv_sem=self.via_recv.at[h],
            device_id=self.device(self.near_chips[h]),
            device_id_type=MESH,
        )

    def near_copy(self, which, h):
        chip = self.near_chips[which]
        return pltpu.make_async_remote_copy(
            src_ref=self.part(self.near_in.at[chip], h),
            dst_ref=self.part(self.far_in.at[self.me], h),
            send_sem=self.far_send.at[which * 2 + h],
            recv_sem=self.far_recv.at[which * 2 + h],
            device_id=self.device(chip),
            device_id_type=MESH,
        )

    def near_arrival(self, which, h):
        here = self.part(self.far_in.at[self.near_chips[which]], h)
        return pltpu.make_async_remote_copy(
            src_ref=here,
            dst_ref=here,
            send_sem=self.far_send.at[which * 2 + h],
            recv_sem=self.far_recv.at[which * 2 + h],
            device_id=self.device(self.near_chips[which]),
            device_id_type=MESH,
        )

    def run(self):
        order = [self.corner] + self.near_chips + [self.me]

        def chip_at(d):
            chip = order[0]
            for i in range(1, len(order)):
                chip = jnp.where(d == i, order[i], chip)
            return chip

        def start(d):
            chip = chip_at(d)
            self.near_out[chip] = self.make(chip, 1 - self.core).astype(BF16)
            self.near(chip).start()

        start(0)

        def step(d, carry):
            start(d)
            chip = chip_at(d - 1)
            own = self.make(chip, self.core)
            self.near(chip).wait_recv()
            self.near_in[chip] = (own + self.near_in[chip].astype(F32)).astype(BF16)

            @pl.when(d == 1)
            def _():
                self.corner_copy(0).start()
                self.corner_copy(1).start()

            @pl.when(d == 2)
            def _():
                self.near_copy(0, 0).start()

            @pl.when(d == 3)
            def _():
                self.near_copy(1, 1).start()

            return carry

        lax.fori_loop(1, len(order), step, 0)
        for which in range(2):
            h = 1 - which
            self.corner_copy(h).wait_recv()
            chip = self.near_chips[which]
            rows = pl.ds(h * self.half, self.half)
            self.near_in[chip, rows, :] = (
                self.near_in[chip, rows, :].astype(F32) + self.via[h].astype(F32)
            ).astype(BF16)
            self.near_copy(which, h).start()

    def slot(self, chip):
        return chip

    def finish(self):
        stage, sem = self.stage
        total = self.make(self.me, self.core)
        self.near(self.me).wait_recv()
        total = total + self.near_in[self.me].astype(F32)
        fetches = []
        for which in range(2):
            for h in range(2):
                self.near_arrival(which, h).wait_recv()
            fetches.append(
                pltpu.make_async_copy(self.far_in.at[self.near_chips[which]], stage.at[which], sem.at[which])
            )
            fetches[-1].start()
        for which in range(2):
            fetches[which].wait()
            total = total + stage[which].astype(F32)
        return total

    def drain(self):
        for chip in [self.corner] + self.near_chips + [self.me]:
            self.near(chip).wait_send()
        for h in range(2):
            self.corner_copy(h).wait_send()
            for which in range(2):
                self.near_copy(which, h).wait_send()


def closing_kernel(
    geo,
    rank,
    single_count,
    early,
    len_ref,
    id_ref,
    tokens_ref,
    first_ref,
    dq_ref,
    dk_ref,
    dv_ref,
    slice_ref,
    down_ref,
    up_ref,
    small_ref,
    *refs,
):
    singles = refs[:single_count]
    early_ref = refs[single_count] if early else None
    (
        grad_ref,
        sum1_ref,
        sum2_ref,
        tok_far,
        tok_out,
        tok_in,
        tok_stage,
        small_buf,
        set1_out,
        set1_in,
        set1_far,
        set2_out,
        set2_in,
        set2_far,
        down_acc,
        up_acc,
        mine1,
        mine2,
        place_buf,
        fold_buf,
        all1,
        all2,
        places,
        done1,
        done2,
        tok_sems,
        set1_sems,
        set2_sems,
        line_send,
        line_recv,
        spread_send,
        spread_recv,
        local_sem,
        stage_sem,
        small_sem,
        tok_via,
        via_sems,
    ) = refs[single_count + early :]
    x, y, core, w = device_here(geo)
    s = lax.axis_index("seq")
    rows, width, wt, groups, parts = geo.rows, geo.width, geo.wt, geo.groups, geo.parts
    part, g = s // groups, s % groups
    docs = len_ref.shape[1]
    doc_rows = docs * rank
    lane_count = down_ref.shape[0] // 4
    lanes = pl.ds(pl.multiple_of(g * LANES, LANES), LANES)
    starts, ends = doc_bounds(len_ref)
    greet_all(geo)

    def iota(shape, dim):
        return lax.broadcasted_iota(jnp.int32, shape, dim)

    def zero_one(condition):
        return jnp.where(condition, 1.0, 0.0).astype(BF16)

    def chosen_of(t):
        pos = t * rows + iota((rows, LANES), 0)
        return select_from(pos, starts, ends, id_ref, rank)

    def fold(j):
        a, b = iota((lane_count, LANES), 0), iota((lane_count, LANES), 1)
        return zero_one((b >= j * rank) & (b < (j + 1) * rank) & (a % rank == b - j * rank))

    def make_tokens(chip, whose):
        t = chip * 2 + whose
        at = pl.ds(pl.multiple_of(t * rows, rows), rows)
        if parts == 1:
            d_q = dq_ref[at, :]
        else:
            inner = pl.ds(pl.multiple_of((t % groups) * rows, rows), rows)
            d_q = jnp.where(t // groups == part, dq_ref[inner, :], jnp.zeros((rows, LANES), BF16))
        pieces = [d_q, dk_ref[at, :], dv_ref[at, :]]
        chosen = chosen_of(t)
        total = jnp.zeros((rows, width), F32)
        low = jnp.zeros((rows, LANES), F32)
        for j in range(3):
            total = total + dot_nt(pieces[j], slice_ref[:, j * LANES : (j + 1) * LANES])
            part_low = dot_nt(pieces[j], up_ref[pl.ds(j * lane_count, lane_count), lanes])
            low = low + dot_nn((part_low * chosen).astype(BF16), fold(j))
        return jnp.concatenate([total, low], axis=1)

    square = geo.nx == 2 and geo.ny == 2
    tok = (CrossSum if square else PairSum)(
        geo.seq // 2, s // 2, core, 0, w, (tok_out, tok_in, tok_far), [tok_sems.at[i] for i in range(4)], make_tokens,
        (tok_stage, stage_sem),
    )
    if square:
        tok.with_corner(tok_via, via_sems.at[0], via_sems.at[1])

    def by_document(value):
        return dot_tn(fold_buf[...], value)[:doc_rows]

    def make_set1(chip, whose):
        return owner_columns(singles, chip * 2 + whose, groups)

    def make_set2(chip, whose):
        owner = chip * 2 + whose
        cut = pl.ds(pl.multiple_of(owner * LANES, LANES), LANES)
        return jnp.concatenate([down_acc[j * doc_rows : (j + 1) * doc_rows, cut] for j in range(3)], axis=1)

    chips = groups // 2
    set1 = PairSum(
        chips, g // 2, core, part * groups, w, (set1_out, set1_in, set1_far), [set1_sems.at[i] for i in range(4)], make_set1
    )
    set2 = PairSum(
        chips, g // 2, core, part * groups, w, (set2_out, set2_in, set2_far), [set2_sems.at[i] for i in range(4)], make_set2
    )

    def peer(n):
        plane = (w + n) % wt
        other = (part + n // wt) % parts
        return other * groups + g, plane, other * wt + plane

    mine_at = part * wt + w

    late = set1_out.shape[2]
    front = late + 3 * LANES
    whole = mine1.shape[1]

    def cut_of(kind, ref):
        if kind == 0:
            return ref.at[:, pl.ds(0, front)]
        if kind == 3:
            return ref.at[:, pl.ds(front, whole - front)]
        return ref

    def line_copy(kind, n, src, dst_all):
        device, plane, _ = peer(n)
        return pltpu.make_async_remote_copy(
            src_ref=cut_of(kind, src),
            dst_ref=cut_of(kind, dst_all.at[mine_at]),
            send_sem=line_send.at[kind, n],
            recv_sem=line_recv.at[kind, mine_at],
            device_id=(device, plane),
            device_id_type=MESH,
        )

    def line_arrival(kind, n, dst_all):
        device, plane, at = peer(n)
        return pltpu.make_async_remote_copy(
            src_ref=cut_of(kind, dst_all.at[at]),
            dst_ref=cut_of(kind, dst_all.at[at]),
            send_sem=line_send.at[kind, n],
            recv_sem=line_recv.at[kind, at],
            device_id=(device, plane),
            device_id_type=MESH,
        )

    peers = range(1, wt * parts)

    block = Block(geo)
    chip_here = g // 2
    here = (chip_here % block.nx, chip_here // block.nx, core, w)

    def region_of(ref):
        def region(ux, uy, whose, half):
            one = ref.at[(uy * block.nx + ux) * 2 + whose]
            if half is None:
                return one
            return one.at[pl.ds(half * (lane_count // 2), lane_count // 2)]

        return region

    spreads = [
        Spread(block, here, region_of(ref), spread_send, spread_recv, i, part * groups)
        for i, ref in enumerate((sum1_ref, sum2_ref))
    ]
    finals = [done1, done2]
    outs = [sum1_ref, sum2_ref]

    def place(kind, mine, dst_all):
        total = dot_nn(place_buf[:, :doc_rows], mine[...])
        for n in peers:
            line_arrival(kind, n, dst_all).wait_recv()
            if kind == 0:
                line_arrival(2, n, places).wait_recv()
                if early:
                    line_arrival(3, n, dst_all).wait_recv()
            at = peer(n)[2]
            total = total + dot_nn(places[at][:, :doc_rows], dst_all[at])
        finals[kind][...] = total.astype(BF16)
        for way in (0, 1, 4):
            spreads[kind].go(way, own=finals[kind])
        pltpu.make_async_copy(finals[kind], outs[kind].at[g], local_sem.at[kind]).start()

    def pass_on(kind):
        spread = spreads[kind]
        spread.wait(0)
        spread.go(2)
        spread.go(5)
        spread.wait(1)
        spread.go(3)
        spread.go(6)

    def pass_last(kind):
        spread = spreads[kind]
        spread.wait(2)
        spread.go(7)
        spread.wait(3)
        spread.go(8)

    place_buf[...], fold_buf[...] = placement(id_ref, docs, rank, lane_count)
    for n in peers:
        line_copy(2, n, place_buf, places).start()
    if early:
        mine1[:, front:] = early_ref[...]
        for n in peers:
            line_copy(3, n, mine1, all1).start()

    set1.run()
    tok.run()

    def small_copy(t):
        return pltpu.make_async_copy(
            small_ref.at[pl.ds(pl.multiple_of(t * rows, rows), rows)], small_buf.at[t % 2], small_sem.at[t % 2]
        )

    def add_up(t, carry):
        at = pl.ds(pl.multiple_of(t * rows, rows), rows)

        @pl.when(t + 1 < geo.seq)
        def _():
            small_copy(t + 1).start()

        small_copy(t).wait()
        for j in range(3):
            cut = slice(j * LANES, (j + 1) * LANES)
            if j == 0:
                if parts == 1:
                    value = dq_ref[at, :]
                else:
                    inner = pl.ds(pl.multiple_of((t % groups) * rows, rows), rows)
                    value = jnp.where(t // groups == part, dq_ref[inner, :], jnp.zeros((rows, LANES), BF16))
            else:
                value = (dk_ref if j == 1 else dv_ref)[at, :]
            up_acc[cut, :] += dot_tn(small_buf[t % 2][:, cut], value)
        return carry

    up_acc[...] = jnp.zeros_like(up_acc)
    small_copy(0).start()
    lax.fori_loop(0, geo.seq, add_up, 0)

    for j in range(3):
        mine1[:, late + j * LANES : late + (j + 1) * LANES] = by_document(
            up_acc[j * lane_count : (j + 1) * lane_count, :].astype(BF16)
        ).astype(BF16)
    mine1[:, :late] = set1.finish().astype(BF16)
    for n in peers:
        line_copy(0, n, mine1, all1).start()

    total = tok.finish()
    low = total[:, width:].astype(BF16)
    total = total[:, :width] + first_ref[...]
    chosen = chosen_of(s)
    pos = s * rows + iota((rows, doc_rows), 0)
    doc_of = iota((rows, doc_rows), 1) // rank
    in_doc = doc_of == segment_from(pos, starts)
    tokens = tokens_ref[...]
    for j in range(3):
        a, b = iota((LANES, lane_count), 0), iota((LANES, lane_count), 1)
        widen = zero_one((a >= j * rank) & (a < (j + 1) * rank) & (b % rank == a - j * rank))
        wide = (dot_nn(low, widen) * chosen).astype(BF16)
        total = total + dot_nn(wide, down_ref[j * lane_count : (j + 1) * lane_count, :])
        by_doc = dot_nn(low, widen[:, :doc_rows])
        by_doc = jnp.where(in_doc, by_doc, 0.0).astype(BF16)
        down_acc[j * doc_rows : (j + 1) * doc_rows, :] = dot_tn(by_doc, tokens)
    set2.run()
    grad_ref[...] = total
    place(0, mine1, all1)
    mine2[...] = set2.finish().astype(BF16)
    for n in peers:
        line_copy(1, n, mine2, all2).start()
    pass_on(0)
    place(1, mine2, all2)
    pass_last(0)
    pass_on(1)
    pass_last(1)
    for kind in range(2):
        for way in range(4, 9):
            spreads[kind].wait(way)
        spreads[kind].wait_sends()
        pltpu.make_async_copy(finals[kind], outs[kind].at[g], local_sem.at[kind]).wait()
    for n in peers:
        line_copy(0, n, mine1, all1).wait_send()
        line_copy(1, n, mine2, all2).wait_send()
        line_copy(2, n, place_buf, places).wait_send()
        if early:
            line_copy(3, n, mine1, all1).wait_send()
    tok.drain()
    set1.drain()
    set2.drain()


def greet_all(geo):
    s, w = lax.axis_index("seq"), lax.axis_index("wt")
    barrier = pltpu.get_barrier_semaphore()
    part, g = s // geo.groups, s % geo.groups
    for d in range(1, geo.seq):
        pl.semaphore_signal(barrier, inc=1, device_id=((s + d) % geo.seq, w), device_id_type=MESH)
    count = geo.seq - 1
    for d in range(1, geo.wt):
        for q in range(geo.parts):
            other = ((part + q) % geo.parts) * geo.groups + g
            pl.semaphore_signal(barrier, inc=1, device_id=(other, (w + d) % geo.wt), device_id_type=MESH)
            count += 1
    pl.semaphore_wait(barrier, count)


def closing(geo, rank, lengths, ids, tokens, d_first, dq, dk, dv, w_slice, down, up, small, grads, early_sum):
    rows, width = geo.rows, geo.width
    docs = lengths.shape[1]
    doc_rows = docs * rank
    lane_count = down.shape[0] // 4
    early = [] if early_sum is None else [early_sum]
    late = sum(v.shape[1] for v in grads) // geo.groups
    set1 = late + 3 * LANES + sum(v.shape[1] for v in early)
    set2 = 3 * LANES
    chips, near = geo.seq // 2, geo.groups // 2
    peers = geo.wt * geo.parts
    smem = pl.BlockSpec(memory_space=pltpu.SMEM)
    vmem = pl.BlockSpec(memory_space=pltpu.VMEM)
    any_spec = pl.BlockSpec(memory_space=pl.ANY)
    dma = pltpu.SemaphoreType.DMA
    wide = width + LANES
    return pl.pallas_call(
        functools.partial(closing_kernel, geo, rank, len(grads), len(early)),
        out_shape=[
            jax.ShapeDtypeStruct((rows, width), F32),
            jax.ShapeDtypeStruct((geo.groups, lane_count, set1), BF16),
            jax.ShapeDtypeStruct((geo.groups, lane_count, set2), BF16),
            jax.ShapeDtypeStruct((chips, rows, wide), BF16),
        ],
        in_specs=[smem, smem] + [vmem] * 8 + [any_spec] + [vmem] * (len(grads) + len(early)),
        out_specs=[vmem, any_spec, any_spec, any_spec],
        scratch_shapes=[
            pltpu.VMEM((min(chips, 4), rows, wide), BF16),
            pltpu.VMEM((chips, rows, wide), BF16),
            pltpu.VMEM((2, rows, wide), BF16),
            pltpu.VMEM((2, rows, 3 * lane_count), BF16),
            pltpu.VMEM((near, doc_rows, late), BF16),
            pltpu.VMEM((near, doc_rows, late), BF16),
            pltpu.VMEM((near, doc_rows, late), BF16),
            pltpu.VMEM((near, doc_rows, 3 * LANES), BF16),
            pltpu.VMEM((near, doc_rows, 3 * LANES), BF16),
            pltpu.VMEM((near, doc_rows, 3 * LANES), BF16),
            pltpu.VMEM((3 * doc_rows, width), F32),
            pltpu.VMEM((3 * lane_count, LANES), F32),
            pltpu.VMEM((doc_rows, set1), BF16),
            pltpu.VMEM((doc_rows, set2), BF16),
            pltpu.VMEM((lane_count, LANES), BF16),
            pltpu.VMEM((lane_count, LANES), BF16),
            pltpu.VMEM((peers, doc_rows, set1), BF16),
            pltpu.VMEM((peers, doc_rows, set2), BF16),
            pltpu.VMEM((peers, lane_count, LANES), BF16),
            pltpu.VMEM((lane_count, set1), BF16),
            pltpu.VMEM((lane_count, set2), BF16),
            dma((4, chips)),
            dma((4, near)),
            dma((4, near)),
            dma((4, peers)),
            dma((4, peers)),
            dma((Spread.KINDS, 2)),
            dma((Spread.KINDS, 2)),
            dma((2,)),
            dma((2,)),
            dma((2,)),
            pltpu.VMEM((2, rows // 2, wide) if chips == 4 else (1, 16, LANES), BF16),
            dma((2, 2)),
        ],
        compiler_params=pltpu.CompilerParams(
            collective_id=1, has_side_effects=True, vmem_limit_bytes=VMEM_LIMIT
        ),
        name="close",
    )(lengths, ids, tokens, d_first, dq, dk, dv, w_slice, down, up, small, *grads, *early)


def unpack_kernel(
    late, one_ref, two_ref, grad_ref, down_ref, up_ref, fc1_down_ref, fc2_up_ref, fc1_up_ref, fc2_down_ref, passed_ref
):
    passed_ref[...] = grad_ref[...]
    count = one_ref.shape[0]
    for i in range(count):
        for j in range(3):
            down_ref[j, :, i * LANES : (i + 1) * LANES] = two_ref[i, :, j * LANES : (j + 1) * LANES].astype(F32)
        singles = [down_ref.at[3], up_ref.at[3], fc1_down_ref, fc2_up_ref, fc1_up_ref, fc2_down_ref]
        at = 0
        for ref in singles[:late] + [up_ref.at[j] for j in range(3)] + singles[late:]:
            wide = ref.shape[1] // count
            ref[:, i * wide : (i + 1) * wide] = one_ref[i, :, at : at + wide].astype(F32)
            at += wide


def unpack(geo, one, two, grad, lane_count, late):
    groups = geo.groups
    thick = (one.shape[2] - 7 * LANES) // 2
    count = 2
    steps = groups // count

    def whole(wide):
        return jax.ShapeDtypeStruct((lane_count, wide * groups), F32)

    def flat(wide):
        return pl.BlockSpec((lane_count, count * wide), lambda i: (0, i))

    four = jax.ShapeDtypeStruct((4, lane_count, LANES * groups), F32)
    four_spec = pl.BlockSpec((4, lane_count, count * LANES), lambda i: (0, 0, i))
    grad_spec = pl.BlockSpec((grad.shape[0] // steps, grad.shape[1]), lambda i: (i, 0))
    return pl.pallas_call(
        functools.partial(unpack_kernel, late),
        grid=(steps,),
        out_shape=[
            four, four, whole(LANES), whole(LANES), whole(thick), whole(thick), jax.ShapeDtypeStruct(grad.shape, F32)
        ],
        in_specs=[
            pl.BlockSpec((count,) + one.shape[1:], lambda i: (i, 0, 0)),
            pl.BlockSpec((count,) + two.shape[1:], lambda i: (i, 0, 0)),
            grad_spec,
        ],
        out_specs=[four_spec, four_spec, flat(LANES), flat(LANES), flat(thick), flat(thick), grad_spec],
        compiler_params=pltpu.CompilerParams(vmem_limit_bytes=VMEM_LIMIT),
        name="unpack",
    )(one, two, grad)


def layer_norm(value, gain, shift):
    mean = jnp.mean(value, axis=-1, keepdims=True)
    centred = value - mean
    spread = jnp.mean(centred * centred, axis=-1, keepdims=True)
    return centred * lax.rsqrt(spread + 1e-05) * gain + shift


def gelu_exact(value):
    return jax.nn.gelu(value, approximate=False)


def times_transposed(grad, weight):
    return lax.dot_general(
        grad, weight, (((1,), (1,)), ((), ())), preferred_element_type=jnp.float32
    )


def left_inner(left, right):
    return lax.dot_general(
        left, right, (((0,), (0,)), ((), ())), preferred_element_type=jnp.float32
    )


def stack_down(down):
    return jnp.transpose(down, (1, 0, 2)).reshape(down.shape[1], down.shape[0] * down.shape[2])


def stack_up(up):
    return up.reshape(up.shape[0] * up.shape[1], up.shape[2])


def unstack_down(stacked, adapter_count, rank_size):
    return jnp.transpose(stacked.reshape(stacked.shape[0], adapter_count, rank_size), (1, 0, 2))


def unstack_up(stacked, adapter_count, rank_size):
    return stacked.reshape(adapter_count, rank_size, stacked.shape[1])


def segment_of(positions, starts):
    return jnp.sum((positions[:, None] >= starts[None, :]).astype(jnp.int32), axis=1) - 1


def select_local(tok_rows, lane_count, rank_size, lengths, ids):
    starts = jnp.cumsum(lengths) - lengths
    local_pos = lax.axis_index("seq") * tok_rows + jnp.arange(tok_rows, dtype=jnp.int32)
    local_seg = segment_of(local_pos, starts)
    doc_range = jnp.arange(lengths.shape[0], dtype=jnp.int32)
    chosen = jnp.sum(jnp.where(local_seg[:, None] == doc_range[None, :], ids[None, :], 0), axis=1)
    lane_owner = jnp.arange(lane_count, dtype=jnp.int32) // rank_size
    lane_rank = jnp.arange(lane_count, dtype=jnp.int32) % rank_size
    doc_owner = jnp.repeat(doc_range, rank_size)
    doc_rank = jnp.arange(doc_owner.shape[0], dtype=jnp.int32) % rank_size
    to_doc = (lane_owner[:, None] == jnp.repeat(ids, rank_size)[None, :]) & (lane_rank[:, None] == doc_rank[None, :])
    return (
        (chosen[:, None] == lane_owner[None, :]).astype(jnp.float32),
        to_doc.astype(jnp.bfloat16),
        (local_seg[:, None] == doc_owner[None, :]).astype(jnp.float32),
    )


def feed_forward(
    geo, tokens, cotangent, attended_tok, weights, vectors, attn_maps, fc1_maps, fc2_maps, select
):
    tok_rows, model_width = tokens.shape
    full_out, full_fc1, full_fc2 = [lax.all_gather(v, "wt", axis=0, tiled=True) for v in weights]
    out_bias, norm1_gain, norm1_bias, fc1_bias, fc2_bias, norm2_gain, norm2_bias = vectors
    out_down, out_up = attn_maps
    fc1_down_all, fc1_up_all = fc1_maps
    fc2_down_all, fc2_up_all = fc2_maps
    select, to_doc, in_doc = select

    def by_doc(low):
        return (jnp.dot(low, to_doc, preferred_element_type=jnp.float32) * in_doc).astype(jnp.bfloat16)

    out_main = jnp.dot(attended_tok, full_out, preferred_element_type=jnp.float32)
    small_out = (
        jnp.dot(attended_tok, out_down, preferred_element_type=jnp.float32) * select
    ).astype(jnp.bfloat16)
    z_value = out_main + out_bias + jnp.dot(small_out, out_up, preferred_element_type=jnp.float32)
    first_sum = tokens.astype(jnp.float32) + z_value
    first_norm, norm1_back = jax.vjp(
        lambda value: layer_norm(value, norm1_gain, norm1_bias), first_sum
    )
    first_low = first_norm.astype(jnp.bfloat16)
    fc1_main = jnp.dot(first_low, full_fc1, preferred_element_type=jnp.float32)
    small_fc1 = (
        jnp.dot(first_low, fc1_down_all, preferred_element_type=jnp.float32) * select
    ).astype(jnp.bfloat16)
    pre_act = (
        fc1_main + fc1_bias + jnp.dot(small_fc1, fc1_up_all, preferred_element_type=jnp.float32)
    )
    act_value, gelu_back = jax.vjp(gelu_exact, pre_act)
    act_low = act_value.astype(jnp.bfloat16)
    fc2_main = jnp.dot(act_low, full_fc2, preferred_element_type=jnp.float32)
    small_fc2 = (
        jnp.dot(act_low, fc2_down_all, preferred_element_type=jnp.float32) * select
    ).astype(jnp.bfloat16)
    y_value = (
        fc2_main + fc2_bias + jnp.dot(small_fc2, fc2_up_all, preferred_element_type=jnp.float32)
    )
    output, norm2_back = jax.vjp(
        lambda value: layer_norm(value, norm2_gain, norm2_bias), first_norm + y_value
    )
    d_second = norm2_back(cotangent.astype(jnp.float32))[0]
    d_y = d_second.astype(jnp.bfloat16)
    d_act = times_transposed(d_y, full_fc2)
    low_fc2 = (times_transposed(d_y, fc2_up_all) * select).astype(jnp.bfloat16)
    d_act = d_act + times_transposed(low_fc2, fc2_down_all)
    grad_fc2_up = left_inner(by_doc(small_fc2), d_y)
    grad_fc2_down = left_inner(by_doc(low_fc2), act_low)
    d_pre = gelu_back(d_act)[0].astype(jnp.bfloat16)
    d_first_low = times_transposed(d_pre, full_fc1)
    low_fc1 = (times_transposed(d_pre, fc1_up_all) * select).astype(jnp.bfloat16)
    d_first_low = d_first_low + times_transposed(low_fc1, fc1_down_all)
    grad_fc1_up = left_inner(by_doc(small_fc1), d_pre)
    grad_fc1_down = left_inner(by_doc(low_fc1), first_low)
    d_first = norm1_back(d_second + d_first_low)[0]
    d_z = d_first.astype(jnp.bfloat16)
    d_attended = times_transposed(d_z, full_out)
    low_out = (times_transposed(d_z, out_up) * select).astype(jnp.bfloat16)
    d_attended = (d_attended + times_transposed(low_out, out_down)).astype(jnp.bfloat16)
    grad_out_up = left_inner(by_doc(small_out), d_z)
    grad_out_down = left_inner(by_doc(low_out), attended_tok)
    blocks = [
        [p * geo.groups + i for i in range(geo.groups)] for p in range(geo.parts)
    ]
    d_heads = lax.all_to_all(
        d_attended.reshape(tok_rows, geo.groups, LANES),
        "seq",
        split_axis=1,
        concat_axis=0,
        axis_index_groups=blocks,
        tiled=True,
    ).reshape(geo.queries, LANES)
    grads = [grad_out_down, grad_out_up, grad_fc1_down, grad_fc2_up, grad_fc1_up, grad_fc2_down]
    return output, d_first, d_heads, [v.astype(BF16) for v in grads]


def shards(
    tokens,
    cotangent,
    w_qkv,
    qv_bias,
    w_out,
    out_bias,
    norm1_gain,
    norm1_bias,
    w_fc1,
    fc1_bias,
    w_fc2,
    fc2_bias,
    norm2_gain,
    norm2_bias,
    doc_lengths,
    adapter_ids,
    attn_down,
    attn_up,
    fc1_down,
    fc1_up,
    fc2_down,
    fc2_up,
):
    tok_rows, model_width = tokens.shape
    adapter_count = attn_down.shape[1]
    rank_size = attn_down.shape[3]
    lane_count = adapter_count * rank_size
    seq_count = lax.axis_size("seq")
    geo = Geometry(tok_rows, model_width)
    part_index = lax.axis_index("seq") // geo.groups
    down_rows = jnp.transpose(attn_down, (0, 1, 3, 2)).reshape(4 * lane_count, model_width)
    up_rows = attn_up.reshape(4 * lane_count, model_width)
    weights = (w_out, w_fc1, w_fc2)
    vectors = (out_bias, norm1_gain, norm1_bias, fc1_bias, fc2_bias, norm2_gain, norm2_bias)

    def rows_of(down):
        return jnp.swapaxes(down, 1, 2).reshape(lane_count, down.shape[1])

    inside = all(v.shape[0] % (32 * seq_count) == 0 for v in weights)
    mlp = None
    if inside:
        mlp = (
            weights
            + (cotangent,)
            + tuple(v.reshape(1, -1) for v in vectors)
            + (rows_of(fc1_down), stack_up(fc1_up), rows_of(fc2_down), stack_up(fc2_up))
        )
    q_heads, k_heads, v_heads, o_heads, lse_heads, w_slice, small_all, *rest = forward_attention(
        geo, rank_size, doc_lengths, adapter_ids, tokens, w_qkv, down_rows, up_rows, qv_bias, mlp
    )
    if inside:
        output, d_first, d_heads, *set1, early_sum = rest
    else:
        early_sum = None
        output, d_first, d_heads, set1 = feed_forward(
            geo,
            tokens,
            cotangent,
            rest[0],
            weights,
            vectors,
            (stack_down(attn_down[3]), stack_up(attn_up[3])),
            (stack_down(fc1_down), stack_up(fc1_up)),
            (stack_down(fc2_down), stack_up(fc2_up)),
            select_local(tok_rows, lane_count, rank_size, doc_lengths[0], adapter_ids[0]),
        )
    d_q, d_k, d_v, output = backward_attention(
        geo, doc_lengths, part_index.reshape(1, 1), q_heads, k_heads, v_heads, o_heads, lse_heads, d_heads, output
    )
    input_grad, sum1, sum2, _ = closing(
        geo,
        rank_size,
        doc_lengths,
        adapter_ids,
        tokens,
        d_first,
        d_q,
        d_k,
        d_v,
        w_slice,
        down_rows,
        up_rows,
        small_all,
        set1,
        early_sum,
    )

    down4, up4, fc1_down_sum, fc2_up_sum, fc1_up_sum, fc2_down_sum, input_grad = unpack(
        geo, sum1, sum2, input_grad, lane_count, len(set1)
    )

    def as_up(rows):
        return rows.reshape(rows.shape[:-2] + (adapter_count, rank_size, rows.shape[-1]))

    def as_down(rows):
        return jnp.swapaxes(as_up(rows), -1, -2)

    return (
        output,
        input_grad,
        as_down(down4),
        as_up(up4),
        as_down(fc1_down_sum),
        as_up(fc1_up_sum),
        as_down(fc2_down_sum),
        as_up(fc2_up_sum),
    )


def solution(mesh):
    placed = (
        P(("wt", "seq"), None),
        P(("wt", "seq"), None),
        P("wt", None),
        P(),
        P("wt", None),
        P(),
        P(),
        P(),
        P("wt", None),
        P(),
        P("wt", None),
        P(),
        P(),
        P(),
        P("wt", None),
        P("wt", None),
        P(),
        P(),
        P(),
        P(),
        P(),
        P(),
    )
    return jax.shard_map(
        shards,
        mesh=mesh,
        in_specs=placed,
        out_specs=(P(("wt", "seq"), None), P(("wt", "seq"), None), P(), P(), P(), P(), P(), P()),
        check_vma=False,
    )
```
